32 devices in a mesh: fsdp: 32 (over z, y, x, core).
Axes of the slice: x: 2, y: 2, z: 4, core: 2. Of those that a mesh axis runs over, the one named last changes fastest.
Arguments:
- tokens: bfloat16 [12288, 1024], P('fsdp'), may hold values from -6 to 6
- seq_lengths: int32 [96], replicated, may hold values from 0 to 384, as said below
- seq_owner: int32 [96], replicated, may hold values from 0 to 31, as said below
- g_attn: bfloat16 [1024], P('fsdp'), may hold values from 0.099609375 to 1.8984375
- w_query: bfloat16 [1024, 2048], P('fsdp'), may hold values from -0.1875 to 0.1875
- key_projection: bfloat16 [1024, 1024], P('fsdp'), may hold values from -0.1875 to 0.1875
- value_projection: bfloat16 [1024, 1024], P('fsdp'), may hold values from -0.1875 to 0.1875
- query_norm_gain: bfloat16 [128], P('fsdp'), may hold values from 0.099609375 to 1.8984375
- g_key: bfloat16 [128], P('fsdp'), may hold values from 0.099609375 to 1.8984375
- w_out: bfloat16 [2048, 1024], P('fsdp'), may hold values from -0.625 to 0.625
- g_ffn: bfloat16 [1024], P('fsdp'), may hold values from 0.099609375 to 1.8984375
- w_gate: bfloat16 [1024, 3072], P('fsdp'), may hold values from -0.1875 to 0.1875
- w_up: bfloat16 [1024, 3072], P('fsdp'), may hold values from -0.1875 to 0.1875
- w_down: bfloat16 [3072, 1024], P('fsdp'), may hold values from -0.109375 to 0.109375
- cotangent: bfloat16 [12288, 1024], P('fsdp'), may hold values from -6 to 6
Outputs:
- mixed: bfloat16 [12288, 1024], P('fsdp')
- grad_tokens: bfloat16 [12288, 1024], P('fsdp')
- grad_g_attn: float32 [1024], P('fsdp')
- grad_w_query: float32 [1024, 2048], P('fsdp')
- grad_w_key: float32 [1024, 1024], P('fsdp')
- grad_w_value: float32 [1024, 1024], P('fsdp')
- grad_g_query: float32 [128], P('fsdp')
- grad_g_key: float32 [128], P('fsdp')
- grad_w_out: float32 [2048, 1024], P('fsdp')
- grad_g_ffn: float32 [1024], P('fsdp')
- grad_w_gate: float32 [1024, 3072], P('fsdp')
- grad_w_up: float32 [1024, 3072], P('fsdp')
- grad_w_down: float32 [3072, 1024], P('fsdp')
The draws below stay inside these ranges and needn't reach their ends.
Inputs may be any that keep to these rules, and one draw needn't show every extreme that they name: `seq_lengths`: the slots of each device have lengths that add up to exactly 384; some slot is 384 long. `seq_owner`: every device holds exactly 3 slots.
All inputs are finite; a program needn't handle non-finite values.
Results may differ from the reference program's by a relative error of at most 0.015.
Values may be sent and summed in bfloat16 or wider, within the bound.
No kernel may reach another device: no remote copies, remote signals or barrier semaphores. Data moves between devices by JAX's collectives and lax.ppermute only.
A program may use at most 256 MiB of HBM per device.

```python
import math
import jax
import jax.numpy as jnp
from jax import lax

MODEL_WIDTH = 1024
QUERY_HEADS = 16
KEY_VALUE_HEADS = 8
HEAD_SIZE = 128
FF = 3072
DEVICE_ROWS = 384
SEQ_DEV = 3
TOKENS = 12288
SEQS = 96
N_FSDP = 32


def seq_layout(key):
    key_cuts, key_full, key_order = jax.random.split(key, 3)
    cuts = jax.random.randint(key_cuts, (N_FSDP, 2), 0, DEVICE_ROWS + 1)
    lower = jnp.minimum(cuts[:, 0], cuts[:, 1])
    upper = jnp.maximum(cuts[:, 0], cuts[:, 1])
    full_device = jax.random.randint(key_full, (), 0, N_FSDP)
    chosen = jnp.arange(N_FSDP) == full_device
    lower = jnp.where(chosen, DEVICE_ROWS, lower)
    upper = jnp.where(chosen, DEVICE_ROWS, upper)
    slots = jnp.stack([lower, upper - lower, DEVICE_ROWS - upper], axis=1).reshape(-1)
    holders = jnp.repeat(jnp.arange(N_FSDP), SEQ_DEV)
    ordering = jax.random.permutation(key_order, N_FSDP * SEQ_DEV)
    inverse = jnp.argsort(ordering)
    return (slots[inverse].astype(jnp.int32), holders[inverse].astype(jnp.int32))


def draw_seq_lengths(key, part):
    lengths, owners = seq_layout(key)
    return lengths


def draw_seq_owner(key, part):
    lengths, owners = seq_layout(key)
    return owners


def block_levels(rng, dims, shards, least, high):
    def one(position, shards_of):
        heights = jax.random.uniform(jax.random.fold_in(jax.random.fold_in(rng, 6), position), (shards_of,), jnp.float32, least / len(shards), high / len(shards))
        return jnp.repeat(jnp.exp(heights), dims[position] // shards_of).reshape((-1,) + (1,) * (len(dims) - position - 1))

    loudness = one(*shards[0])
    for cut in shards[1:]:
        loudness = loudness * one(*cut)
    return loudness


def scatter_about(key, dims, scale, limit, cuts=(), kind=jnp.bfloat16):
    values = jax.random.normal(key, dims, jnp.float32) * scale
    if len(cuts) > 0:
        values = block_levels(key, dims, cuts, -0.22, 0.18) * values
    return jnp.clip(values, min=-limit, max=limit).astype(kind)


def setup_inputs(seed: int = 0) -> dict:
    splits = jax.random.split(jax.random.key(seed), 16)
    tokens = scatter_about(splits[0], (TOKENS, MODEL_WIDTH), 1.0, 6.0, ((0, 32),))
    seq_lengths = draw_seq_lengths(jax.random.fold_in(splits[15], 71), 0)
    seq_owner = draw_seq_owner(jax.random.fold_in(splits[15], 71), 0)
    g_attn = jnp.clip(1.0 + 0.18 * jax.random.normal(splits[3], (MODEL_WIDTH,), jnp.float32), 0.099609375, 1.8984375).astype(jnp.bfloat16)
    w_query = scatter_about(splits[4], (MODEL_WIDTH, QUERY_HEADS * HEAD_SIZE), MODEL_WIDTH ** -0.5, 0.1875, ((0, 32),))
    key_projection = scatter_about(splits[5], (MODEL_WIDTH, KEY_VALUE_HEADS * HEAD_SIZE), MODEL_WIDTH ** -0.5, 0.1875, ((0, 32),))
    value_projection = scatter_about(splits[6], (MODEL_WIDTH, KEY_VALUE_HEADS * HEAD_SIZE), MODEL_WIDTH ** -0.5, 0.1875, ((0, 32),))
    query_norm_gain = jnp.clip(1.0 + 0.18 * jax.random.normal(splits[7], (HEAD_SIZE,), jnp.float32), 0.099609375, 1.8984375).astype(jnp.bfloat16)
    g_key = jnp.clip(1.0 + 0.18 * jax.random.normal(splits[8], (HEAD_SIZE,), jnp.float32), 0.099609375, 1.8984375).astype(jnp.bfloat16)
    w_out = scatter_about(splits[9], (QUERY_HEADS * HEAD_SIZE, MODEL_WIDTH), (QUERY_HEADS * HEAD_SIZE * 16 // DEVICE_ROWS) ** -0.5, 0.625, ((0, 32),))
    g_ffn = jnp.clip(1.0 + 0.18 * jax.random.normal(splits[10], (MODEL_WIDTH,), jnp.float32), 0.099609375, 1.8984375).astype(jnp.bfloat16)
    w_gate = scatter_about(splits[11], (MODEL_WIDTH, FF), MODEL_WIDTH ** -0.5, 0.1875, ((0, 32),))
    w_up = scatter_about(splits[12], (MODEL_WIDTH, FF), MODEL_WIDTH ** -0.5, 0.1875, ((0, 32),))
    w_down = scatter_about(splits[13], (FF, MODEL_WIDTH), FF ** -0.5, 0.109375, ((0, 32),))
    cotangent = scatter_about(splits[14], (TOKENS, MODEL_WIDTH), 1.0, 6.0, ((0, 32),))
    return {"tokens": tokens, "seq_lengths": seq_lengths, "seq_owner": seq_owner, "g_attn": g_attn, "w_query": w_query, "key_projection": key_projection, "value_projection": value_projection, "query_norm_gain": query_norm_gain, "g_key": g_key, "w_out": w_out, "g_ffn": g_ffn, "w_gate": w_gate, "w_up": w_up, "w_down": w_down, "cotangent": cotangent}


@jax.custom_vjp
def lowered_values(v):
    return lax.optimization_barrier(v.astype(jnp.bfloat16)).astype(jnp.float32)

@jax.custom_vjp
def lowered_reverse(v):
    return v

def low_keep(v):
    return (lowered_values(v), None)

def low_pass(kept, grad):
    return (grad,)

def back_keep(v):
    return (v, None)

def back_low(kept, grad):
    return (lowered_values(grad),)
lowered_values.defvjp(low_keep, low_pass)
lowered_reverse.defvjp(back_keep, back_low)
epsilon = 1e-06
rope_base = 1000000.0
top_precision = lax.Precision.HIGHEST

def layout(seq_lengths, seq_owner, device):
    seq_index = jnp.arange(SEQS, dtype=jnp.int32)
    same_owner = seq_owner[:, None] == seq_owner[None, :]
    before = seq_index[None, :] < seq_index[:, None]
    starts = lax.optimization_barrier(jnp.sum(jnp.where(same_owner & before, seq_lengths[None, :], 0), axis=1)).astype(jnp.int32)
    places = jnp.arange(DEVICE_ROWS, dtype=jnp.int32)
    member = (seq_owner[None, :] == device) & (starts[None, :] <= places[:, None]) & (places[:, None] < (starts + seq_lengths)[None, :])
    seq_id = lax.optimization_barrier(jnp.sum(jnp.where(member, seq_index[None, :], 0), axis=1)).astype(jnp.int32)
    token_position = lax.optimization_barrier(jnp.sum(jnp.where(member, places[:, None] - starts[None, :], 0), axis=1)).astype(jnp.int32)
    return (seq_id, token_position)

def root_mean_scale(values, gain):
    return values * lax.rsqrt(lax.optimization_barrier(jnp.mean(values * values, axis=-1, keepdims=True)) + epsilon) * gain

def rotation_table(values, token_position):
    half_width = HEAD_SIZE // 2
    frequency = jnp.exp(jnp.arange(half_width, dtype=jnp.float32) * (-2.0 * math.log(rope_base) / HEAD_SIZE))
    angles = token_position.astype(jnp.float32)[:, None] * frequency[None, :]
    cosine = jnp.cos(angles)[:, None, :]
    sine_part = jnp.sin(angles)[:, None, :]
    first_half = values[..., :half_width]
    second = values[..., half_width:]
    return jnp.concatenate([first_half * cosine - second * sine_part, second * cosine + first_half * sine_part], axis=-1)

def block_layer(block_rows, seq_id, token_position, g_attn, w_query, key_projection, value_projection, query_norm_gain, g_key, w_out, g_ffn, w_gate, w_up, w_down):
    places = jnp.arange(DEVICE_ROWS, dtype=jnp.int32)
    allowed = (seq_id[:, None] == seq_id[None, :]) & (places[None, :] <= places[:, None])
    normalized_input = lowered_values(root_mean_scale(block_rows, g_attn))
    query_unnormed = lowered_reverse(jnp.dot(normalized_input, w_query, precision=top_precision)).reshape(DEVICE_ROWS, QUERY_HEADS, HEAD_SIZE)
    key_unnormed = lowered_reverse(jnp.dot(normalized_input, key_projection, precision=top_precision)).reshape(DEVICE_ROWS, KEY_VALUE_HEADS, HEAD_SIZE)
    value_row_matrix = lowered_values(lowered_reverse(jnp.dot(normalized_input, value_projection, precision=top_precision))).reshape(DEVICE_ROWS, KEY_VALUE_HEADS, HEAD_SIZE)
    query_matrix = lowered_values(rotation_table(root_mean_scale(query_unnormed, query_norm_gain), token_position)).reshape(DEVICE_ROWS, KEY_VALUE_HEADS, QUERY_HEADS // KEY_VALUE_HEADS, HEAD_SIZE)
    keys = lowered_values(rotation_table(root_mean_scale(key_unnormed, g_key), token_position))
    scores = lowered_reverse(jnp.einsum('qkgd,skd->kgqs', query_matrix, keys, precision=top_precision) * (1.0 / math.sqrt(HEAD_SIZE)))
    scores = jnp.where(allowed[None, None], scores, -1e+30)
    weights = lowered_values(jax.nn.softmax(scores, axis=-1))
    heads_out = jnp.einsum('kgqs,skd->qkgd', weights, value_row_matrix, precision=top_precision).reshape(DEVICE_ROWS, QUERY_HEADS * HEAD_SIZE)
    attended = lowered_values(lowered_reverse(heads_out))
    residual = block_rows + lowered_reverse(jnp.dot(attended, w_out, precision=top_precision))
    normed_two = lowered_values(root_mean_scale(residual, g_ffn))
    gate_rows = lowered_reverse(jnp.dot(normed_two, w_gate, precision=top_precision))
    up_rows = lowered_reverse(jnp.dot(normed_two, w_up, precision=top_precision))
    hidden = lowered_values(jax.nn.silu(gate_rows) * up_rows)
    return residual + lowered_reverse(jnp.dot(hidden, w_down, precision=top_precision))

def reference(tokens, seq_lengths, seq_owner, g_attn, w_query, key_projection, value_projection, query_norm_gain, g_key, w_out, g_ffn, w_gate, w_up, w_down, cotangent):
    devices = jnp.arange(N_FSDP, dtype=jnp.int32)
    seq_ids, positions = lax.map(lambda device: layout(seq_lengths, seq_owner, device), devices)
    floats = (tokens.astype(jnp.float32), g_attn.astype(jnp.float32), w_query.astype(jnp.float32), key_projection.astype(jnp.float32), value_projection.astype(jnp.float32), query_norm_gain.astype(jnp.float32), g_key.astype(jnp.float32), w_out.astype(jnp.float32), g_ffn.astype(jnp.float32), w_gate.astype(jnp.float32), w_up.astype(jnp.float32), w_down.astype(jnp.float32))

    def whole_layer(inputs, *params):
        slabs = inputs.reshape(N_FSDP, DEVICE_ROWS, MODEL_WIDTH)

        def scan_step(scan_carry, slab_rows):
            return (scan_carry, jax.checkpoint(block_layer)(slab_rows[0], slab_rows[1], slab_rows[2], *params))
        scan_carry, results = lax.scan(scan_step, jnp.zeros((), jnp.float32), (slabs, seq_ids, positions))
        return results.reshape(TOKENS, MODEL_WIDTH)
    output, pullback = jax.vjp(whole_layer, *floats)
    gradients = pullback(cotangent.astype(jnp.float32))
    return (output.astype(jnp.bfloat16), gradients[0].astype(jnp.bfloat16), gradients[1], gradients[2], gradients[3], gradients[4], gradients[5], gradients[6], gradients[7], gradients[8], gradients[9], gradients[10], gradients[11])
```

```python
import math

import jax
import jax.numpy as jnp
from jax import lax
from jax.sharding import PartitionSpec as P

QUERY_HEADS = 16
KEY_VALUE_HEADS = 8
HEAD_SIZE = 128


epsilon = 1e-06
rope_base = 1000000.0


def layout(seq_lengths, seq_owner, device, row_total_count):
    seq_index = jnp.arange(seq_lengths.shape[0], dtype=jnp.int32)
    same_owner = seq_owner[:, None] == seq_owner[None, :]
    before = seq_index[None, :] < seq_index[:, None]
    starts = jnp.sum(jnp.where(same_owner & before, seq_lengths[None, :], 0), axis=1)
    places = jnp.arange(row_total_count, dtype=jnp.int32)
    member = (
        (seq_owner[None, :] == device)
        & (starts[None, :] <= places[:, None])
        & (places[:, None] < (starts + seq_lengths)[None, :])
    )
    seq_id = jnp.sum(jnp.where(member, seq_index[None, :], 0), axis=1)
    token_position = jnp.sum(jnp.where(member, places[:, None] - starts[None, :], 0), axis=1)
    return (seq_id, token_position)


def rotation_table(values, token_position, direction):
    half_width = HEAD_SIZE // 2
    frequency = jnp.exp(
        jnp.arange(half_width, dtype=jnp.float32) * (-2.0 * math.log(rope_base) / HEAD_SIZE)
    )
    angles = token_position.astype(jnp.float32)[:, None] * frequency[None, :]
    cosine = jnp.cos(angles)[:, None, :]
    sine_part = jnp.sin(angles)[:, None, :] * direction
    first_half = values[..., :half_width]
    second = values[..., half_width:]
    return jnp.concatenate(
        [first_half * cosine - second * sine_part, second * cosine + first_half * sine_part],
        axis=-1,
    )


def norm_forward(values, gain):
    inverse = lax.rsqrt(jnp.mean(values * values, axis=-1, keepdims=True) + epsilon)
    unit_rows = values * inverse
    return (unit_rows * gain, unit_rows, inverse)


def norm_backward(grad_out, unit_rows, inverse, gain, axes):
    grad_gain = jnp.sum(grad_out * unit_rows, axis=axes)
    scaled = grad_out * gain
    grad_in = inverse * (scaled - unit_rows * jnp.mean(scaled * unit_rows, axis=-1, keepdims=True))
    return (grad_in, grad_gain)


def exchange(values, count, mask):
    return lax.ppermute(values, "fsdp", [(source, source ^ mask) for source in range(count)])


def scatter_sum(grad, device, count, flip):
    bits = count.bit_length() - 1
    columns = grad.shape[1]
    held = grad.astype(jnp.bfloat16).reshape((4,) + (2,) * (bits - 2) + (grad.shape[0] // count, columns))
    middle = list(range(1, bits - 2))
    if flip:
        middle = middle[::-1]
    left = list(range(bits - 3, -1, -1))
    for bit in [0] + middle:
        axis = 1 + left.index(bit)
        left.remove(bit)
        mine = (device >> bit) & 1
        sent = lax.dynamic_index_in_dim(held, 1 - mine, axis, keepdims=False)
        kept = lax.dynamic_index_in_dim(held, mine, axis, keepdims=False)
        came = exchange(sent, count, 1 << bit)
        held = (kept.astype(jnp.float32) + came.astype(jnp.float32)).astype(jnp.bfloat16)
    top = device >> (bits - 2)
    total = lax.dynamic_index_in_dim(held, top, 0, keepdims=False).astype(jnp.float32)
    for step in (1, 2, 3):
        sent = lax.dynamic_index_in_dim(held, top ^ step, 0, keepdims=False)
        total = total + exchange(sent, count, step << (bits - 2)).astype(jnp.float32)
    return total


def gain_columns(first, second, third, fourth, rows):
    columns = [jnp.pad(v, (0, rows - v.shape[0]))[:, None] for v in (first, second, third, fourth)]
    return jnp.pad(jnp.concatenate(columns, axis=1), ((0, 0), (0, 124)))


def head_scores(query_group, key_rows, allowed, score_scale):
    scores = (
        jnp.einsum("qgd,sd->gqs", query_group, key_rows, preferred_element_type=jnp.float32)
        * score_scale
    )
    return jnp.where(allowed[None], scores, -1e30)


def on_device(
    tokens,
    seq_lengths,
    seq_owner,
    g_attn,
    w_query,
    key_projection,
    value_projection,
    query_norm_gain,
    g_key,
    w_out,
    g_ffn,
    w_gate,
    w_up,
    w_down,
    cotangent,
):
    row_total_count = tokens.shape[0]
    query_group_count = QUERY_HEADS // KEY_VALUE_HEADS
    score_scale = 1.0 / math.sqrt(HEAD_SIZE)
    seq_id, token_position = layout(seq_lengths, seq_owner, lax.axis_index("fsdp"), row_total_count)
    places = jnp.arange(row_total_count, dtype=jnp.int32)
    allowed = (seq_id[:, None] == seq_id[None, :]) & (places[None, :] <= places[:, None])
    inputs = tokens.astype(jnp.float32)
    count = lax.axis_size("fsdp")
    device = lax.axis_index("fsdp")
    shard = g_attn.shape[0]
    head_shard = query_norm_gain.shape[0]
    gains = gain_columns(g_attn, g_ffn, query_norm_gain, g_key, shard)
    projections = lax.all_gather(
        jnp.concatenate([w_query, key_projection, value_projection, gains], axis=1), "fsdp", axis=0, tiled=True
    )
    back_rows = lax.all_gather(jnp.concatenate([w_out, w_down], axis=0), "fsdp", axis=0, tiled=False)
    gate_up = lax.all_gather(jnp.concatenate([w_gate, w_up], axis=1), "fsdp", axis=0, tiled=True)
    out_rows = w_out.shape[0]
    out_weight = back_rows[:, :out_rows].reshape(count * out_rows, -1)
    down_weight = back_rows[:, out_rows:].reshape(count * w_down.shape[0], -1)
    query_width = w_query.shape[1]
    key_width = key_projection.shape[1]
    qkv_width = query_width + 2 * key_width
    gain_block = projections[:, qkv_width:].astype(jnp.float32)
    gain_one = gain_block[:, 0]
    gain_two = gain_block[:, 1]
    head_gains = gain_block.reshape(count, shard, 128)[:, :head_shard, 2:4]
    gain_query = head_gains[..., 0].reshape(-1)
    gain_key = head_gains[..., 1].reshape(-1)
    normed_in, unit_one, inverse_one = norm_forward(inputs, gain_one)
    normed_low = normed_in.astype(jnp.bfloat16)
    raw = jnp.dot(normed_low, projections[:, :qkv_width], preferred_element_type=jnp.float32)
    query_unnormed = raw[:, :query_width].reshape(row_total_count, QUERY_HEADS, HEAD_SIZE)
    key_unnormed = raw[:, query_width : query_width + key_width].reshape(row_total_count, KEY_VALUE_HEADS, HEAD_SIZE)
    value_low = (
        raw[:, query_width + key_width :].astype(jnp.bfloat16).reshape(row_total_count, KEY_VALUE_HEADS, HEAD_SIZE)
    )
    query_normed, unit_query, inverse_query = norm_forward(query_unnormed, gain_query)
    query_matrix = rotation_table(query_normed, token_position, 1.0).astype(jnp.bfloat16)
    key_normed, unit_key, inverse_key = norm_forward(key_unnormed, gain_key)
    keys = rotation_table(key_normed, token_position, 1.0).astype(jnp.bfloat16)
    head_outputs = []
    log_totals = []
    for shared_key_head in range(KEY_VALUE_HEADS):
        query_group = query_matrix[
            :, shared_key_head * query_group_count : (shared_key_head + 1) * query_group_count, :
        ]
        scores = head_scores(query_group, keys[:, shared_key_head, :], allowed, score_scale)
        row_max = jnp.max(scores, axis=-1, keepdims=True)
        log_total = row_max + jnp.log(jnp.sum(jnp.exp(scores - row_max), axis=-1, keepdims=True))
        probs_low = jnp.exp(scores - log_total).astype(jnp.bfloat16)
        head_outputs.append(
            jnp.einsum(
                "gqs,sd->qgd",
                probs_low,
                value_low[:, shared_key_head, :],
                preferred_element_type=jnp.float32,
            )
        )
        log_totals.append(log_total)
    attended = (
        jnp.concatenate(head_outputs, axis=1)
        .reshape(row_total_count, QUERY_HEADS * HEAD_SIZE)
        .astype(jnp.bfloat16)
    )
    residual = inputs + jnp.dot(attended, out_weight, preferred_element_type=jnp.float32)
    normed_mid, unit_two, inverse_two = norm_forward(residual, gain_two)
    normed_two = normed_mid.astype(jnp.bfloat16)
    hidden_width = w_gate.shape[1]
    both_rows = jnp.dot(normed_two, gate_up, preferred_element_type=jnp.float32)
    gate_rows = both_rows[:, :hidden_width]
    up_rows = both_rows[:, hidden_width:]
    sigmoid_gate = jax.nn.sigmoid(gate_rows)
    silu_gate = gate_rows * sigmoid_gate
    hidden = (silu_gate * up_rows).astype(jnp.bfloat16)
    ffn_rows = jnp.dot(hidden, down_weight, preferred_element_type=jnp.float32)
    mixed = (residual + ffn_rows).astype(jnp.bfloat16)
    grad_out = cotangent.astype(jnp.float32)
    grad_w_down = jnp.einsum("rf,rd->fd", hidden, cotangent, preferred_element_type=jnp.float32)
    grad_hidden = jnp.einsum(
        "rd,fd->rf", cotangent, down_weight, preferred_element_type=jnp.float32
    )
    grad_gate = (
        grad_hidden * up_rows * sigmoid_gate * (1.0 + gate_rows * (1.0 - sigmoid_gate))
    ).astype(jnp.bfloat16)
    grad_up = (grad_hidden * silu_gate).astype(jnp.bfloat16)
    grad_both = jnp.concatenate([grad_gate, grad_up], axis=1)
    grad_gate_up = jnp.einsum("rd,rf->df", normed_two, grad_both, preferred_element_type=jnp.float32)
    grad_normed_two = jnp.einsum("rf,df->rd", grad_both, gate_up, preferred_element_type=jnp.float32)
    grad_mid, grad_gain_two = norm_backward(grad_normed_two, unit_two, inverse_two, gain_two, (0,))
    sum_down = scatter_sum(grad_w_down, device, count, False)
    sum_gate = scatter_sum(grad_gate_up[:, :hidden_width], device, count, True)
    sum_up = scatter_sum(grad_gate_up[:, hidden_width:], device, count, False)
    grad_residual = grad_out + grad_mid
    grad_res_low = grad_residual.astype(jnp.bfloat16)
    grad_w_out = jnp.einsum("ra,rd->ad", attended, grad_res_low, preferred_element_type=jnp.float32)
    grad_attended = jnp.einsum(
        "rd,ad->ra", grad_res_low, out_weight, preferred_element_type=jnp.float32
    )
    grad_attended = grad_attended.astype(jnp.bfloat16).reshape(
        row_total_count, QUERY_HEADS, HEAD_SIZE
    )
    grad_query_parts = []
    grad_key_parts = []
    value_gradient_pieces = []
    for shared_key_head in range(KEY_VALUE_HEADS):
        query_group = query_matrix[
            :, shared_key_head * query_group_count : (shared_key_head + 1) * query_group_count, :
        ]
        key_rows = keys[:, shared_key_head, :]
        scores = head_scores(query_group, key_rows, allowed, score_scale)
        probs = jnp.exp(scores - log_totals[shared_key_head])
        probs_low = probs.astype(jnp.bfloat16)
        grad_heads = grad_attended[
            :, shared_key_head * query_group_count : (shared_key_head + 1) * query_group_count, :
        ]
        grad_probs = jnp.einsum(
            "qgd,sd->gqs",
            grad_heads,
            value_low[:, shared_key_head, :],
            preferred_element_type=jnp.float32,
        )
        value_gradient_pieces.append(
            jnp.einsum("gqs,qgd->sd", probs_low, grad_heads, preferred_element_type=jnp.float32)
        )
        inner_sum = jnp.sum(probs * grad_probs, axis=-1, keepdims=True)
        grad_scores = (probs * (grad_probs - inner_sum)).astype(jnp.bfloat16)
        grad_query_parts.append(
            jnp.einsum("gqs,sd->qgd", grad_scores, key_rows, preferred_element_type=jnp.float32)
            * score_scale
        )
        grad_key_parts.append(
            jnp.einsum("gqs,qgd->sd", grad_scores, query_group, preferred_element_type=jnp.float32)
            * score_scale
        )
    grad_queries = jnp.concatenate(grad_query_parts, axis=1)
    grad_keys = jnp.stack(grad_key_parts, axis=1)
    grad_value_low = (
        jnp.stack(value_gradient_pieces, axis=1)
        .reshape(row_total_count, KEY_VALUE_HEADS * HEAD_SIZE)
        .astype(jnp.bfloat16)
    )
    grad_query_raw, grad_gain_query = norm_backward(
        rotation_table(grad_queries, token_position, -1.0),
        unit_query,
        inverse_query,
        gain_query,
        (0, 1),
    )
    key_gradient_unnormed, grad_gain_key = norm_backward(
        rotation_table(grad_keys, token_position, -1.0), unit_key, inverse_key, gain_key, (0, 1)
    )
    grad_query_low = grad_query_raw.reshape(row_total_count, QUERY_HEADS * HEAD_SIZE).astype(
        jnp.bfloat16
    )
    key_gradient_lowered = key_gradient_unnormed.reshape(
        row_total_count, KEY_VALUE_HEADS * HEAD_SIZE
    ).astype(jnp.bfloat16)
    grad_raw = jnp.concatenate([grad_query_low, key_gradient_lowered, grad_value_low], axis=1)
    grad_projections = jnp.einsum("rd,ra->da", normed_low, grad_raw, preferred_element_type=jnp.float32)
    grad_normed = jnp.einsum(
        "ra,da->rd", grad_raw, projections[:, :qkv_width], preferred_element_type=jnp.float32
    )
    grad_first, grad_gain_one = norm_backward(grad_normed, unit_one, inverse_one, gain_one, (0,))
    grad_tokens = (grad_residual + grad_first).astype(jnp.bfloat16)
    sum_out = scatter_sum(grad_w_out, device, count, True)
    sum_query = scatter_sum(grad_projections[:, :query_width], device, count, False)
    head_pad = ((0, 0), (0, shard - head_shard))
    gain_grads = gain_columns(
        grad_gain_one,
        grad_gain_two,
        jnp.pad(grad_gain_query.reshape(count, head_shard), head_pad).reshape(-1),
        jnp.pad(grad_gain_key.reshape(count, head_shard), head_pad).reshape(-1),
        count * shard,
    )
    sum_rest = scatter_sum(
        jnp.concatenate([grad_projections[:, query_width:], gain_grads], axis=1), device, count, True
    )
    sum_gains = sum_rest[:, 2 * key_width :]
    return (
        mixed,
        grad_tokens,
        sum_gains[:, 0],
        sum_query,
        sum_rest[:, :key_width],
        sum_rest[:, key_width : 2 * key_width],
        sum_gains[:head_shard, 2],
        sum_gains[:head_shard, 3],
        sum_out,
        sum_gains[:, 1],
        sum_gate,
        sum_up,
        sum_down,
    )


def solution(mesh):
    return jax.shard_map(
        on_device,
        mesh=mesh,
        in_specs=(
            P("fsdp", None),
            P(),
            P(),
            P("fsdp"),
            P("fsdp", None),
            P("fsdp", None),
            P("fsdp", None),
            P("fsdp"),
            P("fsdp"),
            P("fsdp", None),
            P("fsdp"),
            P("fsdp", None),
            P("fsdp", None),
            P("fsdp", None),
            P("fsdp", None),
        ),
        out_specs=(
            P("fsdp", None),
            P("fsdp", None),
            P("fsdp"),
            P("fsdp", None),
            P("fsdp", None),
            P("fsdp", None),
            P("fsdp"),
            P("fsdp"),
            P("fsdp", None),
            P("fsdp"),
            P("fsdp", None),
            P("fsdp", None),
            P("fsdp", None),
        ),
        check_vma=False,
    )
```

```python
import functools
import math

import jax
import jax.numpy as jnp
from jax import lax
from jax.experimental import pallas as pl
from jax.experimental.pallas import tpu as pltpu
from jax.sharding import PartitionSpec as P

QUERY_HEADS = 16
KEY_VALUE_HEADS = 8
HEAD_SIZE = 128


epsilon = 1e-06
rope_base = 1000000.0


def layout(seq_lengths, seq_owner, device, row_total_count):
    seq_index = jnp.arange(seq_lengths.shape[0], dtype=jnp.int32)
    same_owner = seq_owner[:, None] == seq_owner[None, :]
    before = seq_index[None, :] < seq_index[:, None]
    starts = jnp.sum(jnp.where(same_owner & before, seq_lengths[None, :], 0), axis=1)
    places = jnp.arange(row_total_count, dtype=jnp.int32)
    member = (
        (seq_owner[None, :] == device)
        & (starts[None, :] <= places[:, None])
        & (places[:, None] < (starts + seq_lengths)[None, :])
    )
    seq_id = jnp.sum(jnp.where(member, seq_index[None, :], 0), axis=1)
    token_position = jnp.sum(jnp.where(member, places[:, None] - starts[None, :], 0), axis=1)
    return (seq_id, token_position)


def rotation_factors(token_position):
    half_width = HEAD_SIZE // 2
    frequency = jnp.exp(
        jnp.arange(half_width, dtype=jnp.float32) * (-2.0 * math.log(rope_base) / HEAD_SIZE)
    )
    angles = token_position.astype(jnp.float32)[:, None] * frequency[None, :]
    cosine = jnp.cos(angles)
    sine = jnp.sin(angles)
    return jnp.concatenate([cosine, cosine], axis=1), jnp.concatenate([-sine, sine], axis=1)


def norm_forward(values, gain):
    inverse = lax.rsqrt(jnp.mean(values * values, axis=-1, keepdims=True) + epsilon)
    unit_rows = values * inverse
    return (unit_rows * gain, unit_rows, inverse)


def norm_backward(grad_out, unit_rows, inverse, gain, axes):
    grad_gain = jnp.sum(grad_out * unit_rows, axis=axes)
    scaled = grad_out * gain
    grad_in = inverse * (scaled - unit_rows * jnp.mean(scaled * unit_rows, axis=-1, keepdims=True))
    return (grad_in, grad_gain)


def exchange(values, count, mask):
    return lax.ppermute(values, "fsdp", [(source, source ^ mask) for source in range(count)])


def middle_bits(count, flip):
    bits = list(range(1, count.bit_length() - 3))
    return bits[::-1] if flip else bits


def row_order(count, flip):
    bits = count.bit_length() - 1
    sequence = [0] + middle_bits(count, flip)
    order = []
    for place_index in range(count):
        mask = (place_index & 3) << (bits - 2)
        for step, bit in enumerate(sequence):
            mask |= ((place_index >> (bits - 1 - step)) & 1) << bit
        order.append(mask)
    return order


def turn_body(device_ref, values_ref, out_ref, turned_ref, *, order):
    turned_ref[...] = values_ref[...].astype(turned_ref.dtype).T
    device = device_ref[0]
    rows = out_ref.shape[0] // len(order)
    group = max(1, 16 // rows)
    for first in range(0, len(order), group):
        blocks = [
            turned_ref[pl.ds(pl.multiple_of((device ^ mask) * rows, rows), rows), :]
            for mask in order[first : first + group]
        ]
        block = blocks[0] if group == 1 else jnp.concatenate(blocks, axis=0)
        out_ref[first * rows : (first + group) * rows, :] = block.astype(out_ref.dtype)


def turn(values, device, count, flip):
    rows, columns = values.shape
    held = jnp.bfloat16 if columns // count % 16 == 0 else jnp.float32
    return pl.pallas_call(
        functools.partial(turn_body, order=row_order(count, flip)),
        grid_spec=pltpu.PrefetchScalarGridSpec(
            num_scalar_prefetch=1,
            grid=(1,),
            in_specs=[pl.BlockSpec((rows, columns), lambda i, d: (0, 0))],
            out_specs=pl.BlockSpec((columns, rows), lambda i, d: (0, 0)),
            scratch_shapes=[pltpu.VMEM((columns, rows), held)],
        ),
        out_shape=jax.ShapeDtypeStruct((columns, rows), values.dtype),
        compiler_params=pltpu.CompilerParams(vmem_limit_bytes=40 * 1024 * 1024),
        name="turn",
    )(device.reshape(1), values)


def add_low(first, second):
    return (first.astype(jnp.float32) + second.astype(jnp.float32)).astype(jnp.bfloat16)


def product_low(left, right):
    return jnp.dot(left, right, preferred_element_type=jnp.float32).astype(jnp.bfloat16)


def sum_start(turned, right, count, extra=None):
    half = turned.shape[0] // 2
    sent = product_low(turned[half:], right)
    kept = product_low(turned[:half], right)
    if extra is not None:
        sent = jnp.concatenate([sent, extra[half:]], axis=1)
        kept = jnp.concatenate([kept, extra[:half]], axis=1)
    return (kept, exchange(sent, count, 1))


def sum_fold(pair, count, bits):
    for bit in bits:
        kept, came = pair
        half = kept.shape[0] // 2
        sent = add_low(kept[half:], came[half:])
        pair = (add_low(kept[:half], came[:half]), exchange(sent, count, 1 << bit))
    return pair


def sum_end(pair, count):
    kept, came = pair
    rows = kept.shape[0] // 4
    total = kept[:rows].astype(jnp.float32) + came[:rows].astype(jnp.float32)
    for step in (1, 2, 3):
        part = slice(step * rows, (step + 1) * rows)
        sent = add_low(kept[part], came[part])
        total = total + exchange(sent, count, step * (count // 4)).astype(jnp.float32)
    return total


def place_body(device_ref, *refs):
    parts = refs[:-2]
    out_ref, semaphores = refs[-2:]
    device = device_ref[0]
    copies = [
        pltpu.make_async_copy(part, out_ref.at[:, device ^ mask], semaphores.at[mask])
        for mask, part in enumerate(parts)
    ]
    for copy in copies:
        copy.start()
    for copy in copies:
        copy.wait()


def place(parts, inner):
    top, rows, columns = parts[0].shape
    return pl.pallas_call(
        place_body,
        grid_spec=pltpu.PrefetchScalarGridSpec(
            num_scalar_prefetch=1,
            grid=(1,),
            in_specs=[pl.BlockSpec(memory_space=pl.ANY)] * len(parts),
            out_specs=pl.BlockSpec((top, len(parts), rows, columns), lambda i, d: (0, 0, 0, 0)),
            scratch_shapes=[pltpu.SemaphoreType.DMA((len(parts),))],
        ),
        out_shape=jax.ShapeDtypeStruct((top, len(parts), rows, columns), parts[0].dtype),
        compiler_params=pltpu.CompilerParams(vmem_limit_bytes=40 * 1024 * 1024),
        name="place",
    )(inner.reshape(1), *parts).reshape(top * len(parts) * rows, columns)


def gather_rows(block, device, count, flip):
    quarter = count // 4
    tops = [block[None]] + [exchange(block, count, step * quarter)[None] for step in (1, 2, 3)]
    parts = {0: place(tops, device // quarter).reshape((4,) + block.shape)}
    for bit in middle_bits(count, flip) + [0]:
        for mask in list(parts):
            parts[mask | (1 << bit)] = exchange(parts[mask], count, 1 << bit)
    return place([parts[mask] for mask in range(quarter)], device & (quarter - 1))


def gain_columns(first, second, third, fourth, rows):
    columns = [jnp.pad(v, (0, rows - v.shape[0]))[:, None] for v in (first, second, third, fourth)]
    return jnp.pad(jnp.concatenate(columns, axis=1), ((0, 0), (0, 124)))


def swap_halves(head):
    return pltpu.roll(head, HEAD_SIZE // 2, 1)


def unit_head(raw):
    inverse = lax.rsqrt(jnp.mean(raw * raw, axis=-1, keepdims=True) + epsilon)
    return raw * inverse, inverse


def contract(left, right, left_axis, right_axis):
    return lax.dot_general(
        left, right, (((left_axis,), (right_axis,)), ((), ())), preferred_element_type=jnp.float32
    )


def block_scores(group, key_rows, first_row, row_start):
    scores = contract(group, key_rows, 1, 1) * (1.0 / math.sqrt(HEAD_SIZE))
    rows = lax.broadcasted_iota(jnp.int32, scores.shape, 0)
    half = scores.shape[0] // 2
    rows = jnp.where(rows >= half, rows - half, rows) + row_start
    columns = lax.broadcasted_iota(jnp.int32, scores.shape, 1)
    return jnp.where((columns <= rows) & (columns >= first_row), scores, -1e30)


def head_pair(ref, block):
    return jnp.concatenate([ref[block, :HEAD_SIZE], ref[block, HEAD_SIZE:]], axis=0)


def pair_rows(first_row_ref, block):
    rows = first_row_ref[block, :]
    return jnp.concatenate([rows, rows], axis=0)


def attend_body(
    normed_ref, wq_ref, wk_ref, wv_ref, gains_ref, cosine_ref, sine_ref, first_ref,
    attended_ref, query_ref, key_ref, value_ref, raw_query_ref, raw_key_ref, total_ref,
):
    normed = normed_ref[...]
    cosine = cosine_ref[...]
    sine = sine_ref[...]

    def turned(raw, gain):
        scaled = unit_head(raw)[0] * gain
        return (scaled * cosine + swap_halves(scaled) * sine).astype(jnp.bfloat16)

    raw_query = jnp.dot(normed, wq_ref[...], preferred_element_type=jnp.float32)
    raw_query_ref[...] = raw_query
    for head in range(2):
        part = slice(head * HEAD_SIZE, (head + 1) * HEAD_SIZE)
        query_ref[:, part] = turned(raw_query[:, part], gains_ref[0:1, :])
    raw_key = jnp.dot(normed, wk_ref[...], preferred_element_type=jnp.float32)
    raw_key_ref[...] = raw_key
    key_ref[...] = turned(raw_key, gains_ref[1:2, :])
    value_ref[...] = jnp.dot(normed, wv_ref[...], preferred_element_type=jnp.float32).astype(jnp.bfloat16)
    step = 128
    for start in range(0, normed.shape[0], step):
        block = slice(start, start + step)
        seen = slice(0, start + step)
        scores = block_scores(head_pair(query_ref, block), key_ref[seen, :], pair_rows(first_ref, block), start)
        top = jnp.max(scores, axis=-1, keepdims=True)
        log_total = top + jnp.log(jnp.sum(jnp.exp(scores - top), axis=-1, keepdims=True))
        probs_low = jnp.exp(scores - log_total).astype(jnp.bfloat16)
        out = jnp.dot(probs_low, value_ref[seen, :], preferred_element_type=jnp.float32).astype(jnp.bfloat16)
        attended_ref[block, :HEAD_SIZE] = out[:step]
        attended_ref[block, HEAD_SIZE:] = out[step:]
        total_ref[0, block, 0:1] = log_total[:step]
        total_ref[0, block, 1:2] = log_total[step:]


def attend(normed, query_weight, rest_weight, head_gains, cosine, sine, first_row):
    rows, width = normed.shape
    whole = lambda shape: pl.BlockSpec(shape, lambda h: (0, 0))
    columns = lambda size, shift: pl.BlockSpec((rows, size), lambda h: (0, h + shift))
    pair = 2 * HEAD_SIZE
    low = lambda size: jax.ShapeDtypeStruct((rows, size), jnp.bfloat16)
    full = lambda size: jax.ShapeDtypeStruct((rows, size), jnp.float32)
    return pl.pallas_call(
        attend_body,
        grid=(KEY_VALUE_HEADS,),
        in_specs=[
            whole((rows, width)),
            pl.BlockSpec((width, pair), lambda h: (0, h)),
            pl.BlockSpec((width, HEAD_SIZE), lambda h: (0, h)),
            pl.BlockSpec((width, HEAD_SIZE), lambda h: (0, h + KEY_VALUE_HEADS)),
            whole((2, HEAD_SIZE)),
            whole((rows, HEAD_SIZE)),
            whole((rows, HEAD_SIZE)),
            whole((rows, 1)),
        ],
        out_specs=[
            columns(pair, 0),
            columns(pair, 0),
            columns(HEAD_SIZE, 0),
            columns(HEAD_SIZE, 0),
            columns(pair, 0),
            columns(HEAD_SIZE, 0),
            pl.BlockSpec((1, rows, 2), lambda h: (h, 0, 0)),
        ],
        out_shape=[
            low(QUERY_HEADS * HEAD_SIZE),
            low(QUERY_HEADS * HEAD_SIZE),
            low(KEY_VALUE_HEADS * HEAD_SIZE),
            low(KEY_VALUE_HEADS * HEAD_SIZE),
            full(QUERY_HEADS * HEAD_SIZE),
            full(KEY_VALUE_HEADS * HEAD_SIZE),
            jax.ShapeDtypeStruct((KEY_VALUE_HEADS, rows, 2), jnp.float32),
        ],
        compiler_params=pltpu.CompilerParams(vmem_limit_bytes=40 * 1024 * 1024),
        cost_estimate=pl.CostEstimate(flops=10_000_000_000, bytes_accessed=20_000_000, transcendentals=4_000_000),
        name="attend",
    )(normed, query_weight, rest_weight, rest_weight, head_gains, cosine, sine, first_row)


def attend_back_body(
    residual_ref, wo_ref, query_ref, key_ref, value_ref, raw_query_ref, raw_key_ref, total_ref,
    gains_ref, cosine_ref, sine_ref, first_ref,
    grad_query_ref, grad_key_ref, grad_value_ref, grad_gains_ref,
    grad_out_ref, query_sum_ref, key_sum_ref, value_sum_ref,
):
    scale = 1.0 / math.sqrt(HEAD_SIZE)

    @pl.when(pl.program_id(0) == 0)
    def _():
        grad_gains_ref[...] = jnp.zeros_like(grad_gains_ref)

    grad_out_ref[...] = contract(residual_ref[...], wo_ref[...], 1, 1).astype(jnp.bfloat16)
    key_sum_ref[...] = jnp.zeros_like(key_sum_ref)
    value_sum_ref[...] = jnp.zeros_like(value_sum_ref)
    step = 128
    for start in range(0, residual_ref.shape[0], step):
        block = slice(start, start + step)
        seen = slice(0, start + step)
        group = head_pair(query_ref, block)
        grad_out = head_pair(grad_out_ref, block)
        key_rows = key_ref[seen, :]
        scores = block_scores(group, key_rows, pair_rows(first_ref, block), start)
        log_total = jnp.concatenate([total_ref[0, block, 0:1], total_ref[0, block, 1:2]], axis=0)
        probs = jnp.exp(scores - log_total)
        grad_probs = contract(grad_out, value_ref[seen, :], 1, 1)
        value_sum_ref[seen, :] += contract(probs.astype(jnp.bfloat16), grad_out, 0, 0)
        inner = jnp.sum(probs * grad_probs, axis=-1, keepdims=True)
        grad_scores = (probs * (grad_probs - inner)).astype(jnp.bfloat16)
        grad_group = jnp.dot(grad_scores, key_rows, preferred_element_type=jnp.float32) * scale
        query_sum_ref[block, :HEAD_SIZE] = grad_group[:step]
        query_sum_ref[block, HEAD_SIZE:] = grad_group[step:]
        key_sum_ref[seen, :] += contract(grad_scores, group, 0, 0)
    grad_value_ref[...] = value_sum_ref[...].astype(jnp.bfloat16)
    cosine = cosine_ref[...]
    sine = sine_ref[...]

    def back(grad, raw, gain):
        turned = grad * cosine - swap_halves(grad) * sine
        unit, inverse = unit_head(raw)
        product = turned * unit
        scaled = turned * gain
        grad_raw = inverse * (scaled - unit * jnp.mean(product * gain, axis=-1, keepdims=True))
        return grad_raw.astype(jnp.bfloat16), jnp.sum(product, axis=0, keepdims=True)

    for head in range(2):
        part = slice(head * HEAD_SIZE, (head + 1) * HEAD_SIZE)
        low, gain_sum = back(query_sum_ref[:, part], raw_query_ref[:, part], gains_ref[0:1, :])
        grad_query_ref[:, part] = low
        grad_gains_ref[0:1, :] += gain_sum
    low, gain_sum = back(key_sum_ref[...] * scale, raw_key_ref[...], gains_ref[1:2, :])
    grad_key_ref[...] = low
    grad_gains_ref[1:2, :] += gain_sum


def attend_back(residual_low, out_weight, saved, head_gains, cosine, sine, first_row):
    rows, width = residual_low.shape
    query, key, value, raw_query, raw_key, totals = saved
    whole = lambda shape: pl.BlockSpec(shape, lambda h: (0, 0))
    columns = lambda size: pl.BlockSpec((rows, size), lambda h: (0, h))
    pair = 2 * HEAD_SIZE
    low = lambda size: jax.ShapeDtypeStruct((rows, size), jnp.bfloat16)
    return pl.pallas_call(
        attend_back_body,
        grid=(KEY_VALUE_HEADS,),
        in_specs=[
            whole((rows, width)),
            pl.BlockSpec((pair, width), lambda h: (h, 0)),
            columns(pair),
            columns(HEAD_SIZE),
            columns(HEAD_SIZE),
            columns(pair),
            columns(HEAD_SIZE),
            pl.BlockSpec((1, rows, 2), lambda h: (h, 0, 0)),
            whole((2, HEAD_SIZE)),
            whole((rows, HEAD_SIZE)),
            whole((rows, HEAD_SIZE)),
            whole((rows, 1)),
        ],
        out_specs=[columns(pair), columns(HEAD_SIZE), columns(HEAD_SIZE), whole((2, HEAD_SIZE))],
        out_shape=[
            low(QUERY_HEADS * HEAD_SIZE),
            low(KEY_VALUE_HEADS * HEAD_SIZE),
            low(KEY_VALUE_HEADS * HEAD_SIZE),
            jax.ShapeDtypeStruct((2, HEAD_SIZE), jnp.float32),
        ],
        scratch_shapes=[
            pltpu.VMEM((rows, pair), jnp.bfloat16),
            pltpu.VMEM((rows, pair), jnp.float32),
            pltpu.VMEM((rows, HEAD_SIZE), jnp.float32),
            pltpu.VMEM((rows, HEAD_SIZE), jnp.float32),
        ],
        compiler_params=pltpu.CompilerParams(vmem_limit_bytes=40 * 1024 * 1024),
        cost_estimate=pl.CostEstimate(flops=16_000_000_000, bytes_accessed=20_000_000, transcendentals=4_000_000),
        name="attend_back",
    )(
        residual_low, out_weight, query, key, value, raw_query, raw_key, totals,
        head_gains, cosine, sine, first_row,
    )


def on_device(
    tokens,
    seq_lengths,
    seq_owner,
    g_attn,
    w_query,
    key_projection,
    value_projection,
    query_norm_gain,
    g_key,
    w_out,
    g_ffn,
    w_gate,
    w_up,
    w_down,
    cotangent,
):
    row_total_count = tokens.shape[0]
    seq_id, token_position = layout(seq_lengths, seq_owner, lax.axis_index("fsdp"), row_total_count)
    first_row = (jnp.arange(row_total_count, dtype=jnp.int32) - token_position)[:, None]
    cosine, sine = rotation_factors(token_position)
    inputs = tokens.astype(jnp.float32)
    count = lax.axis_size("fsdp")
    device = lax.axis_index("fsdp")
    shard = g_attn.shape[0]
    head_shard = query_norm_gain.shape[0]
    gains = gain_columns(g_attn, g_ffn, query_norm_gain, g_key, shard)
    query_weight = gather_rows(w_query, device, count, False)
    rest_weight = gather_rows(
        jnp.concatenate([key_projection, value_projection, gains], axis=1), device, count, True
    )
    out_weight = gather_rows(w_out, device, count, False)
    down_weight = gather_rows(w_down, device, count, True)
    gate_up = lax.all_gather(jnp.concatenate([w_gate, w_up], axis=1), "fsdp", axis=0, tiled=True)
    key_width = key_projection.shape[1]
    gain_block = rest_weight[:, 2 * key_width :].astype(jnp.float32)
    gain_one = gain_block[:, 0]
    gain_two = gain_block[:, 1]
    head_gains = gain_block.reshape(count, shard, 128)[:, :head_shard, 2:4].reshape(HEAD_SIZE, 2).T
    normed_in, unit_one, inverse_one = norm_forward(inputs, gain_one)
    normed_low = normed_in.astype(jnp.bfloat16)
    attended, *saved = attend(normed_low, query_weight, rest_weight, head_gains, cosine, sine, first_row)
    residual = inputs + jnp.dot(attended, out_weight, preferred_element_type=jnp.float32)
    normed_mid, unit_two, inverse_two = norm_forward(residual, gain_two)
    normed_two = normed_mid.astype(jnp.bfloat16)
    hidden_width = w_gate.shape[1]
    both_rows = jnp.dot(normed_two, gate_up, preferred_element_type=jnp.float32)
    gate_rows = both_rows[:, :hidden_width]
    up_rows = both_rows[:, hidden_width:]
    sigmoid_gate = jax.nn.sigmoid(gate_rows)
    silu_gate = gate_rows * sigmoid_gate
    hidden = (silu_gate * up_rows).astype(jnp.bfloat16)
    ffn_rows = jnp.dot(hidden, down_weight, preferred_element_type=jnp.float32)
    mixed = (residual + ffn_rows).astype(jnp.bfloat16)
    grad_out = cotangent.astype(jnp.float32)
    grad_hidden = jnp.einsum(
        "rd,fd->rf", cotangent, down_weight, preferred_element_type=jnp.float32
    )
    grad_gate = (
        grad_hidden * up_rows * sigmoid_gate * (1.0 + gate_rows * (1.0 - sigmoid_gate))
    ).astype(jnp.bfloat16)
    grad_up = (grad_hidden * silu_gate).astype(jnp.bfloat16)
    grad_both = jnp.concatenate([grad_gate, grad_up], axis=1)
    early = middle_bits(count, False)
    late = middle_bits(count, True)
    cut = len(early) // 2
    turned_two = turn(normed_two, device, count, False)
    sum_down = sum_start(turn(hidden, device, count, True), cotangent, count)
    sum_gate = sum_start(turned_two, grad_gate, count)
    grad_both, sum_down, sum_gate = lax.optimization_barrier((grad_both, sum_down, sum_gate))
    sum_up = sum_start(turned_two, grad_up, count)
    sum_down = sum_fold(sum_down, count, late[:cut])
    sum_gate = sum_fold(sum_gate, count, early[:cut])
    grad_normed_two = jnp.einsum("rf,df->rd", grad_both, gate_up, preferred_element_type=jnp.float32)
    grad_mid, grad_gain_two = norm_backward(grad_normed_two, unit_two, inverse_two, gain_two, (0,))
    grad_residual = grad_out + grad_mid
    grad_res_low = grad_residual.astype(jnp.bfloat16)
    sum_out = sum_start(turn(attended, device, count, True), grad_res_low, count)
    grad_res_tied, sum_down, sum_gate, sum_up, sum_out = lax.optimization_barrier(
        (grad_res_low, sum_down, sum_gate, sum_up, sum_out)
    )
    grad_query_low, grad_key_low, grad_value_low, grad_head_gains = attend_back(
        grad_res_tied, out_weight, saved, head_gains, cosine, sine, first_row
    )
    grad_gain_query = grad_head_gains[0]
    grad_gain_key = grad_head_gains[1]
    grad_rest_low = jnp.concatenate([grad_key_low, grad_value_low], axis=1)
    sum_down = sum_fold(sum_down, count, late[cut:])
    sum_gate = sum_fold(sum_gate, count, early[cut:])
    sum_up = sum_fold(sum_up, count, early[:cut])
    sum_out = sum_fold(sum_out, count, late[:cut])
    sum_down = sum_end(sum_down, count)
    sum_gate = sum_end(sum_gate, count)
    sum_up = sum_fold(sum_up, count, early[cut:])
    sum_out = sum_fold(sum_out, count, late[cut:])
    grad_query_low, grad_rest_low, sum_down, sum_gate, sum_up, sum_out = lax.optimization_barrier(
        (grad_query_low, grad_rest_low, sum_down, sum_gate, sum_up, sum_out)
    )
    sum_query = sum_start(turn(normed_low, device, count, False), grad_query_low, count)
    sum_up = sum_end(sum_up, count)
    sum_out = sum_end(sum_out, count)
    grad_normed = jnp.einsum("ra,da->rd", grad_query_low, query_weight, preferred_element_type=jnp.float32)
    grad_normed = grad_normed + jnp.einsum(
        "ra,da->rd", grad_rest_low, rest_weight[:, : 2 * key_width], preferred_element_type=jnp.float32
    )
    grad_first, grad_gain_one = norm_backward(grad_normed, unit_one, inverse_one, gain_one, (0,))
    grad_tokens = (grad_residual + grad_first).astype(jnp.bfloat16)
    head_pad = ((0, 0), (0, shard - head_shard))
    gain_grads = gain_columns(
        grad_gain_one,
        grad_gain_two,
        jnp.pad(grad_gain_query.reshape(count, head_shard), head_pad).reshape(-1),
        jnp.pad(grad_gain_key.reshape(count, head_shard), head_pad).reshape(-1),
        count * shard,
    )
    order = jnp.asarray(row_order(count, True), jnp.int32) ^ device
    gain_grads = gain_grads.astype(jnp.bfloat16).reshape(count, shard, 128)[order].reshape(count * shard, 128)
    sum_rest = sum_start(turn(normed_low, device, count, True), grad_rest_low, count, gain_grads)
    sum_query = sum_end(sum_fold(sum_query, count, early), count)
    sum_rest = sum_end(sum_fold(sum_rest, count, late), count)
    sum_gains = sum_rest[:, 2 * key_width :]
    return (
        mixed,
        grad_tokens,
        sum_gains[:, 0],
        sum_query,
        sum_rest[:, :key_width],
        sum_rest[:, key_width : 2 * key_width],
        sum_gains[:head_shard, 2],
        sum_gains[:head_shard, 3],
        sum_out,
        sum_gains[:, 1],
        sum_gate,
        sum_up,
        sum_down,
    )


def solution(mesh):
    return jax.shard_map(
        on_device,
        mesh=mesh,
        in_specs=(
            P("fsdp", None),
            P(),
            P(),
            P("fsdp"),
            P("fsdp", None),
            P("fsdp", None),
            P("fsdp", None),
            P("fsdp"),
            P("fsdp"),
            P("fsdp", None),
            P("fsdp"),
            P("fsdp", None),
            P("fsdp", None),
            P("fsdp", None),
            P("fsdp", None),
        ),
        out_specs=(
            P("fsdp", None),
            P("fsdp", None),
            P("fsdp"),
            P("fsdp", None),
            P("fsdp", None),
            P("fsdp", None),
            P("fsdp"),
            P("fsdp"),
            P("fsdp", None),
            P("fsdp"),
            P("fsdp", None),
            P("fsdp", None),
            P("fsdp", None),
        ),
        check_vma=False,
    )
```

```python
import functools
import math

import jax
import jax.numpy as jnp
from jax import lax
from jax.experimental import pallas as pl
from jax.experimental.pallas import tpu as pltpu
from jax.sharding import PartitionSpec as P

QUERY_HEADS = 16
KEY_VALUE_HEADS = 8
HEAD_SIZE = 128


SMALL = pl.CostEstimate(flops=1, bytes_accessed=1, transcendentals=0)

epsilon = 1e-06
rope_base = 1000000.0


def layout(seq_lengths, seq_owner, device, row_total_count):
    seq_index = jnp.arange(seq_lengths.shape[0], dtype=jnp.int32)
    same_owner = seq_owner[:, None] == seq_owner[None, :]
    before = seq_index[None, :] < seq_index[:, None]
    starts = jnp.sum(jnp.where(same_owner & before, seq_lengths[None, :], 0), axis=1)
    places = jnp.arange(row_total_count, dtype=jnp.int32)
    member = (
        (seq_owner[None, :] == device)
        & (starts[None, :] <= places[:, None])
        & (places[:, None] < (starts + seq_lengths)[None, :])
    )
    seq_id = jnp.sum(jnp.where(member, seq_index[None, :], 0), axis=1)
    token_position = jnp.sum(jnp.where(member, places[:, None] - starts[None, :], 0), axis=1)
    return (seq_id, token_position)


def rotation_factors(token_position):
    half_width = HEAD_SIZE // 2
    frequency = jnp.exp(
        jnp.arange(half_width, dtype=jnp.float32) * (-2.0 * math.log(rope_base) / HEAD_SIZE)
    )
    angles = token_position.astype(jnp.float32)[:, None] * frequency[None, :]
    cosine = jnp.cos(angles)
    sine = jnp.sin(angles)
    return jnp.concatenate([cosine, cosine], axis=1), jnp.concatenate([-sine, sine], axis=1)


def norm_forward(values, gain):
    inverse = lax.rsqrt(jnp.mean(values * values, axis=-1, keepdims=True) + epsilon)
    unit_rows = values * inverse
    return (unit_rows * gain, unit_rows, inverse)


def exchange(values, count, mask):
    return lax.ppermute(values, "fsdp", [(source, source ^ mask) for source in range(count)])


def middle_bits(count, flip):
    bits = list(range(1, count.bit_length() - 3))
    return bits[::-1] if flip else bits


def sum_bits(count, flip, top_early=False):
    bits = count.bit_length() - 1
    middle = middle_bits(count, flip)
    top = [bits - 2, bits - 1]
    return [0, middle[0]] + top + middle[1:] if top_early else [0] + middle + top


def row_order(count, sequence):
    bits = len(sequence)
    return [
        sum(((index >> (bits - 1 - step)) & 1) << bit for step, bit in enumerate(sequence)) for index in range(count)
    ]


def turn_body(device_ref, values_ref, out_ref, turned_ref, *, order):
    turned_ref[...] = values_ref[...].astype(turned_ref.dtype).T
    device = device_ref[0]
    rows = out_ref.shape[0] // len(order)
    group = max(1, 16 // rows)
    for first in range(0, len(order), group):
        blocks = [
            turned_ref[pl.ds(pl.multiple_of((device ^ mask) * rows, rows), rows), :]
            for mask in order[first : first + group]
        ]
        block = blocks[0] if group == 1 else jnp.concatenate(blocks, axis=0)
        out_ref[first * rows : (first + group) * rows, :] = block.astype(out_ref.dtype)


def turn(values, device, order):
    count = len(order)
    rows, columns = values.shape
    held = jnp.bfloat16 if columns // count % 16 == 0 else jnp.float32
    return pl.pallas_call(
        functools.partial(turn_body, order=order),
        grid_spec=pltpu.PrefetchScalarGridSpec(
            num_scalar_prefetch=1,
            grid=(1,),
            in_specs=[pl.BlockSpec((rows, columns), lambda i, d: (0, 0))],
            out_specs=pl.BlockSpec((columns, rows), lambda i, d: (0, 0)),
            scratch_shapes=[pltpu.VMEM((columns, rows), held)],
        ),
        out_shape=jax.ShapeDtypeStruct((columns, rows), values.dtype),
        compiler_params=pltpu.CompilerParams(vmem_limit_bytes=40 * 1024 * 1024),
        cost_estimate=SMALL,
        name="turn",
    )(device.reshape(1), values)


def add_body(first_ref, second_ref, out_ref):
    out_ref[...] = (first_ref[...].astype(jnp.float32) + second_ref[...].astype(jnp.float32)).astype(out_ref.dtype)


def add_half(first, second, half):
    rows, columns = first.shape[0] // 2, first.shape[1]
    steps = next(n for n in (4, 2, 1) if rows % (16 * n) == 0 or n == 1)
    spec = lambda shift: pl.BlockSpec((rows // steps, columns), lambda i: (i + shift, 0))
    return pl.pallas_call(
        add_body,
        grid=(steps,),
        in_specs=[spec(half * steps), spec(half * steps)],
        out_specs=spec(0),
        out_shape=jax.ShapeDtypeStruct((rows, columns), jnp.bfloat16),
        compiler_params=pltpu.CompilerParams(vmem_limit_bytes=40 * 1024 * 1024),
        cost_estimate=SMALL,
        name="add_half",
    )(first, second)


def product_body(left_ref, right_ref, out_ref):
    out_ref[...] = jnp.dot(left_ref[...], right_ref[...], preferred_element_type=jnp.float32).astype(jnp.bfloat16)


def product_half(left, right, half=None):
    rows, depth = left.shape
    if half is not None:
        rows //= 2
    columns = right.shape[1]
    row_tile, column_tile = min(rows, 512), min(columns, 512)
    shift = half * (rows // row_tile) if half else 0
    return pl.pallas_call(
        product_body,
        grid=(rows // row_tile, columns // column_tile),
        in_specs=[
            pl.BlockSpec((row_tile, depth), lambda i, j: (i + shift, 0)),
            pl.BlockSpec((depth, column_tile), lambda i, j: (0, j)),
        ],
        out_specs=pl.BlockSpec((row_tile, column_tile), lambda i, j: (i, j)),
        out_shape=jax.ShapeDtypeStruct((rows, columns), jnp.bfloat16),
        compiler_params=pltpu.CompilerParams(vmem_limit_bytes=40 * 1024 * 1024),
        cost_estimate=SMALL,
        name="product",
    )(left, right)


def sum_end(pair):
    return pair[0].astype(jnp.float32) + pair[1].astype(jnp.float32)


def place_body(device_ref, *refs):
    parts = refs[:-2]
    out_ref, semaphores = refs[-2:]
    device = device_ref[0]
    copies = [
        pltpu.make_async_copy(part, out_ref.at[:, device ^ mask], semaphores.at[mask])
        for mask, part in enumerate(parts)
    ]
    for copy in copies:
        copy.start()
    for copy in copies:
        copy.wait()


def place(parts, inner):
    top, rows, columns = parts[0].shape
    return pl.pallas_call(
        place_body,
        grid_spec=pltpu.PrefetchScalarGridSpec(
            num_scalar_prefetch=1,
            grid=(1,),
            in_specs=[pl.BlockSpec(memory_space=pl.ANY)] * len(parts),
            out_specs=pl.BlockSpec((top, len(parts), rows, columns), lambda i, d: (0, 0, 0, 0)),
            scratch_shapes=[pltpu.SemaphoreType.DMA((len(parts),))],
        ),
        out_shape=jax.ShapeDtypeStruct((top, len(parts), rows, columns), parts[0].dtype),
        compiler_params=pltpu.CompilerParams(vmem_limit_bytes=40 * 1024 * 1024),
        cost_estimate=SMALL,
        name="place",
    )(inner.reshape(1), *parts).reshape(top * len(parts) * rows, columns)


def gather_top(block, count):
    return [block[None]] + [exchange(block, count, step * (count // 4))[None] for step in (1, 2, 3)]


def lay_top(blocks, device, count):
    return {0: place(blocks, device // (count // 4)).reshape((4,) + blocks[0].shape[1:])}


def split_body(device_ref, *refs):
    parts = refs[:4]
    left_ref, right_ref, semaphores = refs[4:]
    width = left_ref.shape[-1]
    copies = []
    for mask, part in enumerate(parts):
        target = device_ref[0] ^ mask
        copies += [
            pltpu.make_async_copy(part.at[:, :width], left_ref.at[target], semaphores.at[2 * mask]),
            pltpu.make_async_copy(part.at[:, width:], right_ref.at[target], semaphores.at[2 * mask + 1]),
        ]
    for copy in copies:
        copy.start()
    for copy in copies:
        copy.wait()


def lay_top_split(blocks, device, count, width):
    rows, columns = blocks[0].shape[1:]
    shapes = [(4, rows, width), (4, rows, columns - width)]
    return pl.pallas_call(
        split_body,
        grid_spec=pltpu.PrefetchScalarGridSpec(
            num_scalar_prefetch=1,
            grid=(1,),
            in_specs=[pl.BlockSpec(memory_space=pl.ANY)] * 4,
            out_specs=[pl.BlockSpec(shape, lambda i, d: (0, 0, 0)) for shape in shapes],
            scratch_shapes=[pltpu.SemaphoreType.DMA((8,))],
        ),
        out_shape=[jax.ShapeDtypeStruct(shape, blocks[0].dtype) for shape in shapes],
        compiler_params=pltpu.CompilerParams(vmem_limit_bytes=40 * 1024 * 1024),
        cost_estimate=SMALL,
        name="lay_top_split",
    )((device // (count // 4)).reshape(1), *[block[0] for block in blocks])


def gather_bits(parts, count, bits):
    parts = dict(parts)
    for bit in bits:
        for mask in list(parts):
            parts[mask | (1 << bit)] = exchange(parts[mask], count, 1 << bit)
    return parts


def lay(parts, device, count):
    return place([parts[mask] for mask in range(count // 4)], device & (count // 4 - 1))


def gain_columns(first, second, third, fourth, rows):
    columns = [jnp.pad(v, (0, rows - v.shape[0]))[:, None] for v in (first, second, third, fourth)]
    return jnp.pad(jnp.concatenate(columns, axis=1), ((0, 0), (0, 124)))


def swap_halves(head):
    return pltpu.roll(head, HEAD_SIZE // 2, 1)


def unit_head(raw):
    inverse = lax.rsqrt(jnp.mean(raw * raw, axis=-1, keepdims=True) + epsilon)
    return raw * inverse, inverse


def contract(left, right, left_axis, right_axis):
    return lax.dot_general(
        left, right, (((left_axis,), (right_axis,)), ((), ())), preferred_element_type=jnp.float32
    )


def block_scores(group, key_rows, first_row, row_start):
    scores = contract(group, key_rows, 1, 1) * (1.0 / math.sqrt(HEAD_SIZE))
    rows = lax.broadcasted_iota(jnp.int32, scores.shape, 0)
    half = scores.shape[0] // 2
    rows = jnp.where(rows >= half, rows - half, rows) + row_start
    columns = lax.broadcasted_iota(jnp.int32, scores.shape, 1)
    return jnp.where((columns <= rows) & (columns >= first_row), scores, -1e30)


def head_pair(ref, block):
    return jnp.concatenate([ref[block, :HEAD_SIZE], ref[block, HEAD_SIZE:]], axis=0)


def pair_rows(first_row_ref, block):
    rows = first_row_ref[block, :]
    return jnp.concatenate([rows, rows], axis=0)


def attend_body(
    normed_ref, wq_ref, wk_ref, wv_ref, gains_ref, cosine_ref, sine_ref, first_ref,
    attended_ref, query_ref, key_ref, value_ref, raw_query_ref, raw_key_ref, total_ref,
):
    normed = normed_ref[...]
    cosine = cosine_ref[...]
    sine = sine_ref[...]

    def turned(raw, gain):
        scaled = unit_head(raw)[0] * gain
        return (scaled * cosine + swap_halves(scaled) * sine).astype(jnp.bfloat16)

    raw_query = jnp.dot(normed, wq_ref[...], preferred_element_type=jnp.float32)
    raw_query_ref[...] = raw_query
    for head in range(2):
        part = slice(head * HEAD_SIZE, (head + 1) * HEAD_SIZE)
        query_ref[:, part] = turned(raw_query[:, part], gains_ref[0:1, :])
    raw_key = jnp.dot(normed, wk_ref[...], preferred_element_type=jnp.float32)
    raw_key_ref[...] = raw_key
    key_ref[...] = turned(raw_key, gains_ref[1:2, :])
    value_ref[...] = jnp.dot(normed, wv_ref[...], preferred_element_type=jnp.float32).astype(jnp.bfloat16)
    step = 128
    for start in range(0, normed.shape[0], step):
        block = slice(start, start + step)
        seen = slice(0, start + step)
        scores = block_scores(head_pair(query_ref, block), key_ref[seen, :], pair_rows(first_ref, block), start)
        top = jnp.max(scores, axis=-1, keepdims=True)
        log_total = top + jnp.log(jnp.sum(jnp.exp(scores - top), axis=-1, keepdims=True))
        probs_low = jnp.exp(scores - log_total).astype(jnp.bfloat16)
        out = jnp.dot(probs_low, value_ref[seen, :], preferred_element_type=jnp.float32).astype(jnp.bfloat16)
        attended_ref[block, :HEAD_SIZE] = out[:step]
        attended_ref[block, HEAD_SIZE:] = out[step:]
        total_ref[0, block, 0:1] = log_total[:step]
        total_ref[0, block, 1:2] = log_total[step:]


def attend(normed, query_weight, rest_weight, head_gains, cosine, sine, first_row):
    rows, width = normed.shape
    whole = lambda shape: pl.BlockSpec(shape, lambda h: (0, 0))
    columns = lambda size, shift: pl.BlockSpec((rows, size), lambda h: (0, h + shift))
    pair = 2 * HEAD_SIZE
    low = lambda size: jax.ShapeDtypeStruct((rows, size), jnp.bfloat16)
    full = lambda size: jax.ShapeDtypeStruct((rows, size), jnp.float32)
    return pl.pallas_call(
        attend_body,
        grid=(KEY_VALUE_HEADS,),
        in_specs=[
            whole((rows, width)),
            pl.BlockSpec((width, pair), lambda h: (0, h)),
            pl.BlockSpec((width, HEAD_SIZE), lambda h: (0, h)),
            pl.BlockSpec((width, HEAD_SIZE), lambda h: (0, h + KEY_VALUE_HEADS)),
            whole((2, HEAD_SIZE)),
            whole((rows, HEAD_SIZE)),
            whole((rows, HEAD_SIZE)),
            whole((rows, 1)),
        ],
        out_specs=[
            columns(pair, 0),
            columns(pair, 0),
            columns(HEAD_SIZE, 0),
            columns(HEAD_SIZE, 0),
            columns(pair, 0),
            columns(HEAD_SIZE, 0),
            pl.BlockSpec((1, rows, 2), lambda h: (h, 0, 0)),
        ],
        out_shape=[
            low(QUERY_HEADS * HEAD_SIZE),
            low(QUERY_HEADS * HEAD_SIZE),
            low(KEY_VALUE_HEADS * HEAD_SIZE),
            low(KEY_VALUE_HEADS * HEAD_SIZE),
            full(QUERY_HEADS * HEAD_SIZE),
            full(KEY_VALUE_HEADS * HEAD_SIZE),
            jax.ShapeDtypeStruct((KEY_VALUE_HEADS, rows, 2), jnp.float32),
        ],
        compiler_params=pltpu.CompilerParams(vmem_limit_bytes=40 * 1024 * 1024),
        cost_estimate=SMALL,
        name="attend",
    )(normed, query_weight, rest_weight, rest_weight, head_gains, cosine, sine, first_row)


def attend_back_body(
    device_ref, residual_ref, wo_ref, query_ref, key_ref, value_ref, raw_query_ref, raw_key_ref, total_ref,
    gains_ref, cosine_ref, sine_ref, first_ref, turned_query_ref, turned_rest_ref, wq_ref, wk_ref, wv_ref,
    tokens_ref, gain_ref, grad_residual_ref, gain_two_ref,
    query_kept_ref, query_sent_ref, rest_kept_ref, rest_sent_ref, tokens_out_ref,
    grad_out_ref, query_sum_ref, key_sum_ref, value_sum_ref, grad_query_ref, head_gains_ref, normed_sum_ref, lines_ref,
    *, order, shard, head_shard,
):
    scale = 1.0 / math.sqrt(HEAD_SIZE)
    head = pl.program_id(0)

    @pl.when(head == 0)
    def _():
        head_gains_ref[...] = jnp.zeros_like(head_gains_ref)
        normed_sum_ref[...] = jnp.zeros_like(normed_sum_ref)

    grad_out_ref[...] = contract(residual_ref[...], wo_ref[...], 1, 1).astype(jnp.bfloat16)
    key_sum_ref[...] = jnp.zeros_like(key_sum_ref)
    value_sum_ref[...] = jnp.zeros_like(value_sum_ref)
    step = 128
    for start in range(0, residual_ref.shape[0], step):
        block = slice(start, start + step)
        seen = slice(0, start + step)
        group = head_pair(query_ref, block)
        grad_out = head_pair(grad_out_ref, block)
        key_rows = key_ref[seen, :]
        scores = block_scores(group, key_rows, pair_rows(first_ref, block), start)
        log_total = jnp.concatenate([total_ref[0, block, 0:1], total_ref[0, block, 1:2]], axis=0)
        probs = jnp.exp(scores - log_total)
        grad_probs = contract(grad_out, value_ref[seen, :], 1, 1)
        value_sum_ref[seen, :] += contract(probs.astype(jnp.bfloat16), grad_out, 0, 0)
        inner = jnp.sum(probs * grad_probs, axis=-1, keepdims=True)
        grad_scores = (probs * (grad_probs - inner)).astype(jnp.bfloat16)
        grad_group = jnp.dot(grad_scores, key_rows, preferred_element_type=jnp.float32) * scale
        query_sum_ref[block, :HEAD_SIZE] = grad_group[:step]
        query_sum_ref[block, HEAD_SIZE:] = grad_group[step:]
        key_sum_ref[seen, :] += contract(grad_scores, group, 0, 0)
    grad_value = value_sum_ref[...].astype(jnp.bfloat16)
    cosine = cosine_ref[...]
    sine = sine_ref[...]

    def back(grad, raw, gain):
        turned = grad * cosine - swap_halves(grad) * sine
        unit, inverse = unit_head(raw)
        product = turned * unit
        scaled = turned * gain
        grad_raw = inverse * (scaled - unit * jnp.mean(product * gain, axis=-1, keepdims=True))
        return grad_raw.astype(jnp.bfloat16), jnp.sum(product, axis=0, keepdims=True)

    for index in range(2):
        part = slice(index * HEAD_SIZE, (index + 1) * HEAD_SIZE)
        low, gain_sum = back(query_sum_ref[:, part], raw_query_ref[:, part], gains_ref[0:1, :])
        grad_query_ref[:, part] = low
        head_gains_ref[0:1, :] += gain_sum
    grad_key, gain_sum = back(key_sum_ref[...] * scale, raw_key_ref[...], gains_ref[1:2, :])
    head_gains_ref[1:2, :] += gain_sum
    grad_query = grad_query_ref[...]

    half = turned_query_ref.shape[0] // 2
    product = jnp.dot(turned_query_ref[...], grad_query, preferred_element_type=jnp.float32).astype(jnp.bfloat16)
    query_kept_ref[...] = product[:half]
    query_sent_ref[...] = product[half:]
    turned_rest = turned_rest_ref[...]
    for grad, shift in ((grad_key, 0), (grad_value, KEY_VALUE_HEADS)):
        product = jnp.dot(turned_rest, grad, preferred_element_type=jnp.float32).astype(jnp.bfloat16)
        columns = pl.ds(pl.multiple_of((head + shift) * HEAD_SIZE, HEAD_SIZE), HEAD_SIZE)
        rest_kept_ref[:, columns] = product[:half]
        rest_sent_ref[:, columns] = product[half:]
    normed_sum_ref[...] += (
        contract(grad_query, wq_ref[...], 1, 1)
        + contract(grad_key, wk_ref[...], 1, 1)
        + contract(grad_value, wv_ref[...], 1, 1)
    )

    @pl.when(head == pl.num_programs(0) - 1)
    def _():
        unit, inverse = unit_head(tokens_ref[...].astype(jnp.float32))
        grad = normed_sum_ref[...]
        scaled = grad * gain_ref[...]
        grad_first = inverse * (scaled - unit * jnp.mean(scaled * unit, axis=-1, keepdims=True))
        tokens_out_ref[...] = (grad_residual_ref[...] + grad_first).astype(jnp.bfloat16)
        width = grad.shape[1]
        source = lax.broadcasted_iota(jnp.int32, (HEAD_SIZE, width), 0)
        target = lax.broadcasted_iota(jnp.int32, (HEAD_SIZE, width), 1)
        spread = jnp.where(source // head_shard * shard + source % head_shard == target, 1.0, 0.0)
        heads = jnp.dot(
            head_gains_ref[...], spread, precision=lax.Precision.HIGHEST, preferred_element_type=jnp.float32
        )
        lines = jnp.concatenate(
            [
                jnp.sum(grad * unit, axis=0, keepdims=True),
                gain_two_ref[...],
                heads,
                jnp.zeros((124, width), jnp.float32),
            ],
            axis=0,
        )
        lines_ref[...] = lines.T
        device = device_ref[0]
        group = max(1, 16 // shard)
        last = slice(2 * KEY_VALUE_HEADS * HEAD_SIZE, None)
        for first in range(0, len(order), group):
            blocks = [
                lines_ref[pl.ds(pl.multiple_of((device ^ mask) * shard, shard), shard), :]
                for mask in order[first : first + group]
            ]
            block = (blocks[0] if group == 1 else jnp.concatenate(blocks, axis=0)).astype(jnp.bfloat16)
            row = first * shard
            target_ref = rest_kept_ref if row < half else rest_sent_ref
            target_ref[row % half : row % half + group * shard, last] = block


def attend_back(
    device, residual_low, out_weight, saved, head_gains, cosine, sine, first_row, turned_query, turned_rest,
    query_weight, rest_weight, tokens, gain, grad_residual, grad_gain_two, order, shard, head_shard,
):
    rows, width = residual_low.shape
    query, key, value, raw_query, raw_key, totals = saved
    whole = lambda shape: pl.BlockSpec(shape, lambda h, d: (0, 0))
    columns = lambda height, size, shift=0: pl.BlockSpec((height, size), lambda h, d: (0, h + shift))
    pair = 2 * HEAD_SIZE
    low = lambda height, size: jax.ShapeDtypeStruct((height, size), jnp.bfloat16)
    half = width // 2
    rest_width = rest_weight.shape[1]
    return pl.pallas_call(
        functools.partial(attend_back_body, order=order, shard=shard, head_shard=head_shard),
        grid_spec=pltpu.PrefetchScalarGridSpec(
            num_scalar_prefetch=1,
            grid=(KEY_VALUE_HEADS,),
            in_specs=[
                whole((rows, width)),
                pl.BlockSpec((pair, width), lambda h, d: (h, 0)),
                columns(rows, pair),
                columns(rows, HEAD_SIZE),
                columns(rows, HEAD_SIZE),
                columns(rows, pair),
                columns(rows, HEAD_SIZE),
                pl.BlockSpec((1, rows, 2), lambda h, d: (h, 0, 0)),
                whole((2, HEAD_SIZE)),
                whole((rows, HEAD_SIZE)),
                whole((rows, HEAD_SIZE)),
                whole((rows, 1)),
                whole((width, rows)),
                whole((width, rows)),
                columns(width, pair),
                columns(width, HEAD_SIZE),
                columns(width, HEAD_SIZE, KEY_VALUE_HEADS),
                whole((rows, width)),
                whole((1, width)),
                whole((rows, width)),
                whole((1, width)),
            ],
            out_specs=[
                columns(half, pair),
                columns(half, pair),
                whole((half, rest_width)),
                whole((half, rest_width)),
                whole((rows, width)),
            ],
            scratch_shapes=[
                pltpu.VMEM((rows, pair), jnp.bfloat16),
                pltpu.VMEM((rows, pair), jnp.float32),
                pltpu.VMEM((rows, HEAD_SIZE), jnp.float32),
                pltpu.VMEM((rows, HEAD_SIZE), jnp.float32),
                pltpu.VMEM((rows, pair), jnp.bfloat16),
                pltpu.VMEM((2, HEAD_SIZE), jnp.float32),
                pltpu.VMEM((rows, width), jnp.float32),
                pltpu.VMEM((width, 128), jnp.float32),
            ],
        ),
        out_shape=[
            low(half, QUERY_HEADS * HEAD_SIZE),
            low(half, QUERY_HEADS * HEAD_SIZE),
            low(half, rest_width),
            low(half, rest_width),
            low(rows, width),
        ],
        compiler_params=pltpu.CompilerParams(vmem_limit_bytes=48 * 1024 * 1024),
        cost_estimate=SMALL,
        name="attend_back",
    )(
        device.reshape(1), residual_low, out_weight, query, key, value, raw_query, raw_key, totals, head_gains, cosine,
        sine, first_row, turned_query, turned_rest, query_weight, rest_weight, rest_weight, tokens, gain,
        grad_residual, grad_gain_two,
    )


def feed_forward_body(
    residual_ref, gain_ref, cotangent_ref, gate_ref, up_ref, down_ref,
    mixed_ref, normed_ref, hidden_ref, grad_gate_ref, grad_up_ref, grad_residual_ref, grad_low_ref, grad_gain_ref,
    out_ref, back_ref, down_weight_ref,
):
    step = pl.program_id(0)

    @pl.when(step == 0)
    def _():
        unit, _ = unit_head(residual_ref[...])
        normed_ref[...] = (unit * gain_ref[...]).astype(jnp.bfloat16)
        out_ref[...] = jnp.zeros_like(out_ref)
        back_ref[...] = jnp.zeros_like(back_ref)

    normed = normed_ref[...]
    width = normed.shape[1]
    gate_weight = gate_ref[...].reshape(width, gate_ref.shape[-1])
    up_weight = up_ref[...].reshape(width, up_ref.shape[-1])
    devices, rows, _ = down_ref.shape
    pieces = down_ref.shape[2] // width
    for device in range(devices):
        for piece in range(pieces):
            first = (device * pieces + piece) * rows
            down_weight_ref[first : first + rows, :] = down_ref[device, :, piece * width : (piece + 1) * width]
    down_weight = down_weight_ref[...]
    gate = jnp.dot(normed, gate_weight, preferred_element_type=jnp.float32)
    up = jnp.dot(normed, up_weight, preferred_element_type=jnp.float32)
    grad_hidden = contract(cotangent_ref[...], down_weight, 1, 1)
    sigmoid = jax.nn.sigmoid(gate)
    silu = gate * sigmoid
    hidden = (silu * up).astype(jnp.bfloat16)
    grad_gate = (grad_hidden * up * sigmoid * (1.0 + gate * (1.0 - sigmoid))).astype(jnp.bfloat16)
    grad_up = (grad_hidden * silu).astype(jnp.bfloat16)
    hidden_ref[...] = hidden
    grad_gate_ref[...] = grad_gate
    grad_up_ref[...] = grad_up
    out_ref[...] += jnp.dot(hidden, down_weight, preferred_element_type=jnp.float32)
    back_ref[...] += contract(grad_gate, gate_weight, 1, 1) + contract(grad_up, up_weight, 1, 1)

    @pl.when(step == pl.num_programs(0) - 1)
    def _():
        residual = residual_ref[...]
        mixed_ref[...] = (residual + out_ref[...]).astype(jnp.bfloat16)
        unit, inverse = unit_head(residual)
        grad = back_ref[...]
        grad_gain_ref[...] = jnp.sum(grad * unit, axis=0, keepdims=True)
        scaled = grad * gain_ref[...]
        grad_mid = inverse * (scaled - unit * jnp.mean(scaled * unit, axis=-1, keepdims=True))
        grad_residual = cotangent_ref[...].astype(jnp.float32) + grad_mid
        grad_residual_ref[...] = grad_residual
        grad_low_ref[...] = grad_residual.astype(jnp.bfloat16)


def feed_forward(residual, gain, cotangent, weights, shard):
    rows, width = residual.shape
    count, _, hidden_width = weights.shape
    tile = 4 * hidden_width // 32
    tiles = hidden_width // tile
    whole = pl.BlockSpec((rows, width), lambda j: (0, 0))
    row = pl.BlockSpec((1, width), lambda j: (0, 0))
    columns = pl.BlockSpec((rows, tile), lambda j: (0, j))
    low = lambda size: jax.ShapeDtypeStruct((rows, size), jnp.bfloat16)
    if shard % 16 == 0:
        weight_args = [weights, weights, weights]
        weight_specs = [
            pl.BlockSpec((count, shard, tile), lambda j: (0, 0, j)),
            pl.BlockSpec((count, shard, tile), lambda j: (0, 1, j)),
            pl.BlockSpec((count // tiles, shard, hidden_width), lambda j: (j, 2, 0)),
        ]
    else:
        gate, up, down = (weights[:, part * shard : (part + 1) * shard] for part in range(3))
        down = down.reshape(count, shard, -1, width).transpose(0, 2, 1, 3).reshape(tiles, tile, width)
        weight_args = [gate.reshape(width, hidden_width), up.reshape(width, hidden_width), down]
        weight_specs = [
            pl.BlockSpec((width, tile), lambda j: (0, j)),
            pl.BlockSpec((width, tile), lambda j: (0, j)),
            pl.BlockSpec((1, tile, width), lambda j: (j, 0, 0)),
        ]
    return pl.pallas_call(
        feed_forward_body,
        grid=(tiles,),
        in_specs=[whole, row, whole] + weight_specs,
        out_specs=[whole, whole, columns, columns, columns, whole, whole, row],
        out_shape=[
            low(width),
            low(width),
            low(hidden_width),
            low(hidden_width),
            low(hidden_width),
            jax.ShapeDtypeStruct((rows, width), jnp.float32),
            low(width),
            jax.ShapeDtypeStruct((1, width), jnp.float32),
        ],
        scratch_shapes=[
            pltpu.VMEM((rows, width), jnp.float32),
            pltpu.VMEM((rows, width), jnp.float32),
            pltpu.VMEM((tile, width), jnp.bfloat16),
        ],
        compiler_params=pltpu.CompilerParams(vmem_limit_bytes=48 * 1024 * 1024),
        cost_estimate=SMALL,
        name="feed_forward",
    )(residual, gain, cotangent, *weight_args)


def on_device(
    tokens,
    seq_lengths,
    seq_owner,
    g_attn,
    w_query,
    key_projection,
    value_projection,
    query_norm_gain,
    g_key,
    w_out,
    g_ffn,
    w_gate,
    w_up,
    w_down,
    cotangent,
):
    row_total_count = tokens.shape[0]
    fence = lax.optimization_barrier
    count = lax.axis_size("fsdp")
    device = lax.axis_index("fsdp")
    early = middle_bits(count, False)
    late = middle_bits(count, True)
    cut_bits = len(early) // 2
    shard = g_attn.shape[0]
    head_shard = query_norm_gain.shape[0]
    key_width = key_projection.shape[1]

    pieces = w_down.shape[0] // shard
    down_pieces = w_down.reshape(pieces, shard, -1).transpose(1, 0, 2).reshape(shard, -1)
    ffn_weights = lax.all_gather(jnp.concatenate([w_gate, w_up, down_pieces], axis=0), "fsdp", axis=0, tiled=False)
    gains = gain_columns(g_attn, g_ffn, query_norm_gain, g_key, shard)
    projections = jnp.concatenate([w_query, key_projection, value_projection, gains], axis=1)
    top = gather_top(projections, count)
    top, w_out = fence((top, w_out))
    query_part, rest_part = lay_top_split(top, device, count, w_query.shape[1])
    query_parts = gather_bits({0: query_part}, count, early[:cut_bits])
    rest_parts = gather_bits({0: rest_part}, count, late[:cut_bits])
    out_top = gather_top(w_out, count)
    query_parts, rest_parts, out_top = fence((query_parts, rest_parts, out_top))
    query_parts = gather_bits(query_parts, count, early[cut_bits:])
    rest_parts = gather_bits(rest_parts, count, late[cut_bits:])
    out_parts = lay_top(out_top, device, count)
    query_parts, rest_parts, out_parts = fence((query_parts, rest_parts, out_parts))
    out_parts = gather_bits(out_parts, count, early[:cut_bits])
    query_parts = gather_bits(query_parts, count, [0])
    rest_parts = gather_bits(rest_parts, count, [0])
    query_parts, rest_parts = fence((query_parts, rest_parts))
    query_weight = lay(query_parts, device, count)
    rest_weight = lay(rest_parts, device, count)

    seq_id, token_position = layout(seq_lengths, seq_owner, device, row_total_count)
    first_row = (jnp.arange(row_total_count, dtype=jnp.int32) - token_position)[:, None]
    cosine, sine = rotation_factors(token_position)
    inputs = tokens.astype(jnp.float32)
    gain_block = rest_weight[:, 2 * key_width :].astype(jnp.float32)
    head_gains = gain_block.reshape(count, shard, 128)[:, :head_shard, 2:4].reshape(HEAD_SIZE, 2).T
    gain_one = gain_block[:, 0]
    gain_two = gain_block[:, 1]
    normed_low = norm_forward(inputs, gain_one)[0].astype(jnp.bfloat16)
    normed_low, out_parts = fence((normed_low, out_parts))
    out_parts = gather_bits(out_parts, count, early[cut_bits:])
    attended, *saved = attend(normed_low, query_weight, rest_weight, head_gains, cosine, sine, first_row)
    attended, out_parts = fence((attended, out_parts))
    out_parts = gather_bits(out_parts, count, [0])
    out_weight = lay(out_parts, device, count)
    residual = inputs + jnp.dot(attended, out_weight, preferred_element_type=jnp.float32)
    mixed, normed_two, hidden, grad_gate, grad_up, grad_residual, grad_res_low, grad_gain_two = feed_forward(
        residual, gain_two[None], cotangent, ffn_weights, shard
    )

    live = dict(
        hidden=hidden, two=normed_two, grad_gate=grad_gate, grad_up=grad_up, attended=attended, low=grad_res_low,
        one=normed_low,
    )
    flying = {}
    stages = dict(
        down=sum_bits(count, True, True),
        gate=sum_bits(count, False),
        out=sum_bits(count, False),
        query=sum_bits(count, False),
        rest=sum_bits(count, True),
    )
    orders = {name: row_order(count, bits) for name, bits in stages.items()}
    stages = {name: list(bits) for name, bits in stages.items()}

    def cut():
        live.update(fence(dict(live)))

    def fly(**sent):
        live.update({name + "_sent": value for name, value in sent.items()})
        cut()
        for name in sent:
            flying[name] = exchange(live.pop(name + "_sent"), count, 1 << stages[name].pop(0))

    def land(*names):
        live.update({name + "_came": flying.pop(name) for name in names})
        cut()

    def pass_on(*names):
        land(*names)
        fly(**{name: add_half(live[name], live[name + "_came"], 1) for name in names})

    def keep(name):
        live[name] = add_half(live[name], live.pop(name + "_came"), 0)

    live["up"] = product_half(turn(live["two"], jnp.zeros_like(device), list(range(count))), live["grad_up"])
    cut()
    sum_up = lax.psum_scatter(live.pop("up"), "fsdp", scatter_dimension=0, tiled=True)
    turned_down = turn(live["hidden"], device, orders["down"])
    fly(down=product_half(turned_down, cotangent, 1))
    turned_gate = turn(live["two"], device, orders["gate"])
    fly(gate=product_half(turned_gate, live["grad_gate"], 1))
    live["down"] = product_half(turned_down, cotangent, 0)
    pass_on("down")
    live["gate"] = product_half(turned_gate, live["grad_gate"], 0)
    pass_on("gate")
    keep("down")
    keep("gate")
    turned_query = turn(live["one"], device, orders["query"])
    turned_rest = turn(live["one"], device, orders["rest"])
    live["query"], query_sent, live["rest"], rest_sent, live["grad_tokens"] = attend_back(
        device, live["low"], out_weight, saved, head_gains, cosine, sine, first_row, turned_query, turned_rest,
        query_weight, rest_weight, tokens, gain_one[None], grad_residual, grad_gain_two, orders["rest"], shard,
        head_shard,
    )
    live["query_sent"], live["rest_sent"] = query_sent, rest_sent
    land("down", "gate")
    fly(
        down=add_half(live["down"], live["down_came"], 1),
        gate=add_half(live["gate"], live["gate_came"], 1),
        query=live["query_sent"],
        rest=live["rest_sent"],
    )
    pass_on("query", "rest")
    turned_out = turn(live["attended"], device, orders["out"])
    fly(out=product_half(turned_out, live["low"], 1))
    keep("down")
    keep("gate")
    keep("query")
    keep("rest")
    live["out"] = product_half(turned_out, live["low"], 0)
    pass_on("out")
    keep("out")
    grad_tokens = live.pop("grad_tokens")
    for name in ("hidden", "two", "grad_gate", "grad_up", "attended", "low", "one"):
        del live[name]
    sequence = [
        "down", "gate", "query", "gate", "down", "rest", "out", "query", "rest", "query", "out", "rest", "out",
    ]
    while any(stages.values()):
        name = sequence.pop(0) if sequence else max(stages, key=lambda n: len(stages[n]))
        if stages[name]:
            pass_on(name)
            keep(name)
    ends = {}
    for name in ("gate", "down", "out", "query", "rest"):
        land(name)
        ends[name] = sum_end((live.pop(name), live.pop(name + "_came")))
    sum_down, sum_gate, sum_out, sum_query, sum_rest = (
        ends[name] for name in ("down", "gate", "out", "query", "rest")
    )
    sum_gains = sum_rest[:, 2 * key_width :]
    return (
        mixed,
        grad_tokens,
        sum_gains[:, 0],
        sum_query,
        sum_rest[:, :key_width],
        sum_rest[:, key_width : 2 * key_width],
        sum_gains[:head_shard, 2],
        sum_gains[:head_shard, 3],
        sum_out,
        sum_gains[:, 1],
        sum_gate,
        sum_up.astype(jnp.float32),
        sum_down,
    )


def solution(mesh):
    return jax.shard_map(
        on_device,
        mesh=mesh,
        in_specs=(
            P("fsdp", None),
            P(),
            P(),
            P("fsdp"),
            P("fsdp", None),
            P("fsdp", None),
            P("fsdp", None),
            P("fsdp"),
            P("fsdp"),
            P("fsdp", None),
            P("fsdp"),
            P("fsdp", None),
            P("fsdp", None),
            P("fsdp", None),
            P("fsdp", None),
        ),
        out_specs=(
            P("fsdp", None),
            P("fsdp", None),
            P("fsdp"),
            P("fsdp", None),
            P("fsdp", None),
            P("fsdp", None),
            P("fsdp"),
            P("fsdp"),
            P("fsdp", None),
            P("fsdp"),
            P("fsdp", None),
            P("fsdp", None),
            P("fsdp", None),
        ),
        check_vma=False,
    )
```

```python
import functools
import math

import jax
import jax.numpy as jnp
from jax import lax
from jax.experimental import pallas as pl
from jax.experimental.pallas import tpu as pltpu
from jax.sharding import PartitionSpec as P

QUERY_HEADS = 16
KEY_VALUE_HEADS = 8
HEAD_SIZE = 128


SMALL = pl.CostEstimate(flops=1, bytes_accessed=1, transcendentals=0)


def far(shape, dtype):
    return pltpu.HBM(tuple(shape), dtype)


epsilon = 1e-06
rope_base = 1000000.0


def layout(seq_lengths, seq_owner, device, row_total_count):
    seq_index = jnp.arange(seq_lengths.shape[0], dtype=jnp.int32)
    same_owner = seq_owner[:, None] == seq_owner[None, :]
    before = seq_index[None, :] < seq_index[:, None]
    starts = jnp.sum(jnp.where(same_owner & before, seq_lengths[None, :], 0), axis=1)
    places = jnp.arange(row_total_count, dtype=jnp.int32)
    member = (
        (seq_owner[None, :] == device)
        & (starts[None, :] <= places[:, None])
        & (places[:, None] < (starts + seq_lengths)[None, :])
    )
    seq_id = jnp.sum(jnp.where(member, seq_index[None, :], 0), axis=1)
    token_position = jnp.sum(jnp.where(member, places[:, None] - starts[None, :], 0), axis=1)
    return (seq_id, token_position)


def rotation_factors(token_position):
    half_width = HEAD_SIZE // 2
    frequency = jnp.exp(
        jnp.arange(half_width, dtype=jnp.float32) * (-2.0 * math.log(rope_base) / HEAD_SIZE)
    )
    angles = token_position.astype(jnp.float32)[:, None] * frequency[None, :]
    cosine = jnp.cos(angles)
    sine = jnp.sin(angles)
    return jnp.concatenate([cosine, cosine], axis=1), jnp.concatenate([-sine, sine], axis=1)


def norm_forward(values, gain):
    inverse = lax.rsqrt(jnp.mean(values * values, axis=-1, keepdims=True) + epsilon)
    unit_rows = values * inverse
    return (unit_rows * gain, unit_rows, inverse)


def exchange(values, count, mask):
    return lax.ppermute(values, "fsdp", [(source, source ^ mask) for source in range(count)])


def middle_bits(count, flip):
    bits = list(range(1, count.bit_length() - 3))
    return bits[::-1] if flip else bits


def sum_bits(count):
    bits = count.bit_length() - 1
    middle = list(range(1, bits - 2))
    low, high = bits - 2, bits - 1
    return dict(
        down=[0, middle[-1], high, low] + middle[-2::-1],
        gate=[0] + middle + [low, high],
        up=[0, low, middle[-1], high] + middle[-2::-1],
        out=[0] + middle + [low, high],
        first=[0, low] + middle[::-1] + [high],
        second=[0] + middle + [low, high],
    )


def row_order(count, sequence):
    bits = len(sequence)
    return [
        sum(((index >> (bits - 1 - step)) & 1) << bit for step, bit in enumerate(sequence)) for index in range(count)
    ]


def turn_body(device_ref, *refs, order):
    values, (out_ref, turned_ref) = refs[:-2], refs[-2:]
    start = 0
    for ref in values:
        turned_ref[start : start + ref.shape[1], :] = ref[...].astype(turned_ref.dtype).T
        start += ref.shape[1]
    device = device_ref[0]
    rows = out_ref.shape[0] // len(order)
    group = max(1, 16 // rows)
    for first in range(0, len(order), group):
        blocks = [
            turned_ref[pl.ds(pl.multiple_of((device ^ mask) * rows, rows), rows), :]
            for mask in order[first : first + group]
        ]
        block = blocks[0] if group == 1 else jnp.concatenate(blocks, axis=0)
        out_ref[first * rows : (first + group) * rows, :] = block.astype(out_ref.dtype)


def turn(values, device, order):
    count = len(order)
    rows = values[0].shape[0]
    columns = sum(value.shape[1] for value in values)
    held = jnp.bfloat16 if columns // count % 16 == 0 else jnp.float32
    return pl.pallas_call(
        functools.partial(turn_body, order=order),
        grid_spec=pltpu.PrefetchScalarGridSpec(
            num_scalar_prefetch=1,
            grid=(1,),
            in_specs=[pl.BlockSpec(value.shape, lambda i, d: (0, 0)) for value in values],
            out_specs=pl.BlockSpec((columns, rows), lambda i, d: (0, 0)),
            scratch_shapes=[pltpu.VMEM((columns, rows), held)],
        ),
        out_shape=jax.ShapeDtypeStruct((columns, rows), values[0].dtype),
        compiler_params=pltpu.CompilerParams(vmem_limit_bytes=16 * 1024 * 1024),
        cost_estimate=SMALL,
        name="turn",
    )(device.reshape(1), *values)


def fold_body(*refs):
    pairs = len(refs) // 6

    def add(first, second):
        return (first[...].astype(jnp.float32) + second[...].astype(jnp.float32)).astype(jnp.bfloat16)

    for index in range(pairs):
        kept_first, kept_second, came_first, came_second = refs[4 * index : 4 * index + 4]
        kept_ref, sent_ref = refs[4 * pairs + 2 * index : 4 * pairs + 2 * index + 2]
        sent_ref[...] = add(kept_second, came_second)
        kept_ref[...] = add(kept_first, came_first)


def fold(*pairs):
    halves = [kept.shape[0] // 2 for kept, _ in pairs]
    steps = next(n for n in (4, 2, 1) if n == 1 or all(rows % (16 * n) == 0 for rows in halves))
    in_specs, out_specs, out_shape, operands = [], [], [], []
    for rows, (kept, came) in zip(halves, pairs):
        columns = kept.shape[1]
        first = pl.BlockSpec((rows // steps, columns), lambda i: (i, 0))
        second = pl.BlockSpec((rows // steps, columns), lambda i: (i + steps, 0))
        in_specs += [first, second, first, second]
        operands += [kept, kept, came, came]
        out_specs += [first, first]
        out_shape += [jax.ShapeDtypeStruct((rows, columns), jnp.bfloat16)] * 2
    block_bytes = sum(6 * 2 * (rows // steps) * kept.shape[1] for rows, (kept, _) in zip(halves, pairs))
    out = pl.pallas_call(
        fold_body,
        grid=(steps,),
        in_specs=in_specs,
        out_specs=out_specs,
        out_shape=out_shape,
        compiler_params=pltpu.CompilerParams(vmem_limit_bytes=2 * block_bytes + 6 * 1024 * 1024),
        cost_estimate=SMALL,
        name="fold",
    )(*operands)
    return [out[2 * index : 2 * index + 2] for index in range(len(pairs))]


def sum_end(pair):
    return pair[0].astype(jnp.float32) + pair[1].astype(jnp.float32)


def place_body(device_ref, *refs):
    parts = refs[:-2]
    out_ref, semaphores = refs[-2:]
    device = device_ref[0]
    copies = [
        pltpu.make_async_copy(part, out_ref.at[:, device ^ mask], semaphores.at[mask])
        for mask, part in enumerate(parts)
    ]
    for copy in copies:
        copy.start()
    for copy in copies:
        copy.wait()


def place(parts, inner):
    top, rows, columns = parts[0].shape
    return pl.pallas_call(
        place_body,
        grid_spec=pltpu.PrefetchScalarGridSpec(
            num_scalar_prefetch=1,
            grid=(1,),
            in_specs=[pl.BlockSpec(memory_space=pl.ANY)] * len(parts),
            out_specs=pl.BlockSpec((top, len(parts), rows, columns), lambda i, d: (0, 0, 0, 0)),
            scratch_shapes=[pltpu.SemaphoreType.DMA((len(parts),))],
        ),
        out_shape=far((top, len(parts), rows, columns), parts[0].dtype)
        if top > 1
        else jax.ShapeDtypeStruct((top, len(parts), rows, columns), parts[0].dtype),
        compiler_params=pltpu.CompilerParams(vmem_limit_bytes=14 * 1024 * 1024),
        cost_estimate=SMALL,
        name="place",
    )(inner.reshape(1), *parts).reshape(top * len(parts) * rows, columns)


def gather_top(block, count):
    return [block, exchange(block, count, count // 4), exchange(block, count, count // 2)]


def gather_top_rest(blocks, count):
    return [block[None] for block in blocks + [exchange(blocks[2], count, count // 4)]]


def join_body(query_ref, key_ref, value_ref, gains_ref, out_ref):
    groups = KEY_VALUE_HEADS
    pair = query_ref.shape[1] // groups
    one = key_ref.shape[1] // groups
    shift = 0
    for group in range(groups):
        for ref, size in ((query_ref, pair), (key_ref, one), (value_ref, one)):
            out_ref[:, shift : shift + size] = ref[:, group * size : (group + 1) * size]
            shift += size
        if group == groups // 2 - 1:
            out_ref[:, shift : shift + 128] = gains_ref[...]
            shift += 128


def join(w_query, key_projection, value_projection, gains):
    rows = w_query.shape[0]
    columns = w_query.shape[1] + 2 * key_projection.shape[1] + 128
    return pl.pallas_call(
        join_body,
        out_shape=jax.ShapeDtypeStruct((rows, columns), w_query.dtype),
        cost_estimate=SMALL,
        name="join",
    )(w_query, key_projection, value_projection, gains)


def lay_top(blocks, device, count):
    return {0: place(blocks, device // (count // 4)).reshape((4,) + blocks[0].shape[1:])}


def split_body(device_ref, *refs):
    parts = refs[:4]
    left_ref, right_ref, semaphores = refs[4:]
    width = left_ref.shape[-1]
    copies = []
    for mask, part in enumerate(parts):
        target = device_ref[0] ^ mask
        copies += [
            pltpu.make_async_copy(part.at[:, :width], left_ref.at[target], semaphores.at[2 * mask]),
            pltpu.make_async_copy(part.at[:, width:], right_ref.at[target], semaphores.at[2 * mask + 1]),
        ]
    for copy in copies:
        copy.start()
    for copy in copies:
        copy.wait()


def lay_top_split(blocks, device, count, width):
    rows, columns = blocks[0].shape[1:]
    shapes = [(4, rows, width), (4, rows, columns - width)]
    return pl.pallas_call(
        split_body,
        grid_spec=pltpu.PrefetchScalarGridSpec(
            num_scalar_prefetch=1,
            grid=(1,),
            in_specs=[pl.BlockSpec(memory_space=pl.ANY)] * 4,
            out_specs=[pl.BlockSpec(shape, lambda i, d: (0, 0, 0)) for shape in shapes],
            scratch_shapes=[pltpu.SemaphoreType.DMA((8,))],
        ),
        out_shape=[jax.ShapeDtypeStruct(shape, blocks[0].dtype) for shape in shapes],
        compiler_params=pltpu.CompilerParams(vmem_limit_bytes=10 * 1024 * 1024),
        cost_estimate=SMALL,
        name="lay_top_split",
    )((device // (count // 4)).reshape(1), *[block[0] for block in blocks])


def gather_bits(parts, count, bits):
    parts = dict(parts)
    for bit in bits:
        for mask in list(parts):
            parts[mask | (1 << bit)] = exchange(parts[mask], count, 1 << bit)
    return parts


def lay(parts, device, count):
    return place([parts[mask] for mask in range(count // 4)], device & (count // 4 - 1))


def gain_columns(first, second, third, fourth, rows):
    columns = [jnp.pad(v, (0, rows - v.shape[0]))[:, None] for v in (first, second, third, fourth)]
    return jnp.pad(jnp.concatenate(columns, axis=1), ((0, 0), (0, 124)))


def swap_halves(head):
    return pltpu.roll(head, HEAD_SIZE // 2, 1)


def unit_head(raw):
    inverse = lax.rsqrt(jnp.mean(raw * raw, axis=-1, keepdims=True) + epsilon)
    return raw * inverse, inverse


def contract(left, right, left_axis, right_axis):
    return lax.dot_general(
        left, right, (((left_axis,), (right_axis,)), ((), ())), preferred_element_type=jnp.float32
    )


def block_scores(group, key_rows, first_row, row_start):
    scores = contract(group, key_rows, 1, 1) * (1.0 / math.sqrt(HEAD_SIZE))
    rows = lax.broadcasted_iota(jnp.int32, scores.shape, 0)
    half = scores.shape[0] // 2
    rows = jnp.where(rows >= half, rows - half, rows) + row_start
    columns = lax.broadcasted_iota(jnp.int32, scores.shape, 1)
    return jnp.where((columns <= rows) & (columns >= first_row), scores, -1e30)


def head_pair(ref, block):
    return jnp.concatenate([ref[block, :HEAD_SIZE], ref[block, HEAD_SIZE:]], axis=0)


def pair_rows(first_row_ref, block):
    rows = first_row_ref[block, :]
    return jnp.concatenate([rows, rows], axis=0)


GROUP = 4 * HEAD_SIZE


def attend_body(
    normed_ref, weight_ref, gains_ref, cosine_ref, sine_ref, first_ref,
    attended_ref, query_ref, key_ref, value_ref, raw_ref, total_ref,
):
    cosine = cosine_ref[...]
    sine = sine_ref[...]

    def turned(raw, gain):
        scaled = unit_head(raw)[0] * gain
        return (scaled * cosine + swap_halves(scaled) * sine).astype(jnp.bfloat16)

    raw = jnp.dot(normed_ref[...], weight_ref[...], preferred_element_type=jnp.float32)
    raw_ref[...] = raw[:, : 3 * HEAD_SIZE]
    for head in range(2):
        part = slice(head * HEAD_SIZE, (head + 1) * HEAD_SIZE)
        query_ref[:, part] = turned(raw[:, part], gains_ref[0:1, :])
    key_ref[...] = turned(raw[:, 2 * HEAD_SIZE : 3 * HEAD_SIZE], gains_ref[1:2, :])
    value_ref[...] = raw[:, 3 * HEAD_SIZE :].astype(jnp.bfloat16)
    step = 128
    for start in range(0, raw.shape[0], step):
        block = slice(start, start + step)
        seen = slice(0, start + step)
        scores = block_scores(head_pair(query_ref, block), key_ref[seen, :], pair_rows(first_ref, block), start)
        top = jnp.max(scores, axis=-1, keepdims=True)
        log_total = top + jnp.log(jnp.sum(jnp.exp(scores - top), axis=-1, keepdims=True))
        probs_low = jnp.exp(scores - log_total).astype(jnp.bfloat16)
        out = jnp.dot(probs_low, value_ref[seen, :], preferred_element_type=jnp.float32).astype(jnp.bfloat16)
        attended_ref[block, :HEAD_SIZE] = out[:step]
        attended_ref[block, HEAD_SIZE:] = out[step:]
        total_ref[0, block, 0:1] = log_total[:step]
        total_ref[0, block, 1:2] = log_total[step:]


def attend(normed, weight, head_gains, cosine, sine, first_row):
    rows, width = normed.shape
    groups = KEY_VALUE_HEADS // 2
    whole = lambda *shape: pl.BlockSpec(shape, lambda h: (0, 0))
    columns = lambda size: pl.BlockSpec((rows, size), lambda h: (0, h))
    low = lambda size: jax.ShapeDtypeStruct((rows, groups * size), jnp.bfloat16)
    pair = 2 * HEAD_SIZE
    return pl.pallas_call(
        attend_body,
        grid=(groups,),
        in_specs=[
            whole(rows, width),
            pl.BlockSpec((width, GROUP), lambda h: (0, h)),
            whole(2, HEAD_SIZE),
            whole(rows, HEAD_SIZE),
            whole(rows, HEAD_SIZE),
            whole(rows, 1),
        ],
        out_specs=[
            columns(pair),
            columns(pair),
            columns(HEAD_SIZE),
            columns(HEAD_SIZE),
            columns(3 * HEAD_SIZE),
            pl.BlockSpec((1, rows, 2), lambda h: (h, 0, 0)),
        ],
        out_shape=[
            low(pair),
            low(pair),
            low(HEAD_SIZE),
            low(HEAD_SIZE),
            jax.ShapeDtypeStruct((rows, groups * 3 * HEAD_SIZE), jnp.float32),
            jax.ShapeDtypeStruct((groups, rows, 2), jnp.float32),
        ],
        compiler_params=pltpu.CompilerParams(vmem_limit_bytes=26 * 1024 * 1024),
        cost_estimate=SMALL,
        name="attend",
    )(normed, weight, head_gains, cosine, sine, first_row)


def attend_back_body(
    device_ref, residual_ref, wo_ref, query_ref, key_ref, value_ref, raw_ref, total_ref,
    gains_ref, cosine_ref, sine_ref, first_ref, turned_ref, weight_ref, *refs,
    order, shard, head_shard, last, head=None,
):
    if last:
        head_gains_in_ref, normed_in_ref = refs[:2]
        refs = refs[2:]
        tokens_ref, gain_ref, grad_residual_ref, gain_two_ref, kept_ref, sent_ref, tokens_out_ref = refs[:7]
        head_gains_ref, normed_sum_ref, lines_ref = refs[7:10]
        scratch = refs[10:]
    else:
        kept_ref, sent_ref, head_gains_ref, normed_sum_ref = refs[:4]
        scratch = refs[4:]
    grad_out_ref, query_sum_ref, key_sum_ref, value_sum_ref, grads_ref = scratch
    scale = 1.0 / math.sqrt(HEAD_SIZE)
    heads = KEY_VALUE_HEADS // 2
    if head is None:
        head = pl.program_id(0)

    @pl.when(head == 0)
    def _():
        head_gains_ref[...] = head_gains_in_ref[...] if last else jnp.zeros_like(head_gains_ref)
        normed_sum_ref[...] = normed_in_ref[...] if last else jnp.zeros_like(normed_sum_ref)

    grad_out_ref[...] = contract(residual_ref[...], wo_ref[...], 1, 1).astype(jnp.bfloat16)
    key_sum_ref[...] = jnp.zeros_like(key_sum_ref)
    value_sum_ref[...] = jnp.zeros_like(value_sum_ref)
    step = 128
    for start in range(0, residual_ref.shape[0], step):
        block = slice(start, start + step)
        seen = slice(0, start + step)
        group = head_pair(query_ref, block)
        grad_out = head_pair(grad_out_ref, block)
        key_rows = key_ref[seen, :]
        scores = block_scores(group, key_rows, pair_rows(first_ref, block), start)
        log_total = jnp.concatenate([total_ref[0, block, 0:1], total_ref[0, block, 1:2]], axis=0)
        probs = jnp.exp(scores - log_total)
        grad_probs = contract(grad_out, value_ref[seen, :], 1, 1)
        value_sum_ref[seen, :] += contract(probs.astype(jnp.bfloat16), grad_out, 0, 0)
        inner = jnp.sum(probs * grad_probs, axis=-1, keepdims=True)
        grad_scores = (probs * (grad_probs - inner)).astype(jnp.bfloat16)
        grad_group = jnp.dot(grad_scores, key_rows, preferred_element_type=jnp.float32) * scale
        query_sum_ref[block, :HEAD_SIZE] = grad_group[:step]
        query_sum_ref[block, HEAD_SIZE:] = grad_group[step:]
        key_sum_ref[seen, :] += contract(grad_scores, group, 0, 0)
    grads_ref[:, 3 * HEAD_SIZE :] = value_sum_ref[...].astype(jnp.bfloat16)
    cosine = cosine_ref[...]
    sine = sine_ref[...]

    def back(grad, part, gain):
        turned = grad * cosine - swap_halves(grad) * sine
        unit, inverse = unit_head(raw_ref[:, part])
        product = turned * unit
        scaled = turned * gain
        grad_raw = inverse * (scaled - unit * jnp.mean(product * gain, axis=-1, keepdims=True))
        grads_ref[:, part] = grad_raw.astype(jnp.bfloat16)
        return jnp.sum(product, axis=0, keepdims=True)

    for index in range(2):
        part = slice(index * HEAD_SIZE, (index + 1) * HEAD_SIZE)
        head_gains_ref[0:1, :] += back(query_sum_ref[:, part], part, gains_ref[0:1, :])
    part = slice(2 * HEAD_SIZE, 3 * HEAD_SIZE)
    head_gains_ref[1:2, :] += back(key_sum_ref[...] * scale, part, gains_ref[1:2, :])

    grads = grads_ref[...]
    half = turned_ref.shape[0] // 2
    product = jnp.dot(turned_ref[...], grads, preferred_element_type=jnp.float32).astype(jnp.bfloat16)
    columns = pl.ds(pl.multiple_of(head * GROUP, GROUP), GROUP)
    kept_ref[:, columns] = product[:half]
    sent_ref[:, columns] = product[half:]
    normed_sum_ref[...] += contract(grads, weight_ref[...], 1, 1)

    if not last:
        return

    @pl.when(head == heads - 1)
    def _():
        unit, inverse = unit_head(tokens_ref[...].astype(jnp.float32))
        grad = normed_sum_ref[...]
        scaled = grad * gain_ref[...]
        grad_first = inverse * (scaled - unit * jnp.mean(scaled * unit, axis=-1, keepdims=True))
        tokens_out_ref[...] = (grad_residual_ref[...] + grad_first).astype(jnp.bfloat16)
        width = grad.shape[1]
        source = lax.broadcasted_iota(jnp.int32, (HEAD_SIZE, width), 0)
        target = lax.broadcasted_iota(jnp.int32, (HEAD_SIZE, width), 1)
        spread = jnp.where(source // head_shard * shard + source % head_shard == target, 1.0, 0.0)
        heads = jnp.dot(
            head_gains_ref[...], spread, precision=lax.Precision.HIGHEST, preferred_element_type=jnp.float32
        )
        lines = jnp.concatenate(
            [
                jnp.sum(grad * unit, axis=0, keepdims=True),
                gain_two_ref[...],
                heads,
                jnp.zeros((124, width), jnp.float32),
            ],
            axis=0,
        )
        lines_ref[...] = lines.T
        device = device_ref[0]
        group = max(1, 16 // shard)
        end = slice(kept_ref.shape[1] - 128, None)
        for first in range(0, len(order), group):
            blocks = [
                lines_ref[pl.ds(pl.multiple_of((device ^ mask) * shard, shard), shard), :]
                for mask in order[first : first + group]
            ]
            block = (blocks[0] if group == 1 else jnp.concatenate(blocks, axis=0)).astype(jnp.bfloat16)
            row = first * shard
            target_ref = kept_ref if row < half else sent_ref
            target_ref[row % half : row % half + group * shard, end] = block


def attend_back_specs(rows, width, part, head):
    first = part * KEY_VALUE_HEADS // 2
    whole = lambda *shape: pl.BlockSpec(shape, lambda *j: (0, 0))
    columns = lambda height, size: pl.BlockSpec((height, size), lambda *j: (0, head(*j)))
    pair = 2 * HEAD_SIZE
    return [
        pl.BlockSpec((pair, width), lambda *j: (head(*j) + first, 0)),
        columns(rows, pair),
        columns(rows, HEAD_SIZE),
        columns(rows, HEAD_SIZE),
        columns(rows, 3 * HEAD_SIZE),
        pl.BlockSpec((1, rows, 2), lambda *j: (head(*j), 0, 0)),
        whole(2, HEAD_SIZE),
        whole(rows, HEAD_SIZE),
        whole(rows, HEAD_SIZE),
        whole(rows, 1),
        whole(width, rows),
        columns(width, GROUP),
    ]


def attend_back_scratch(rows):
    pair = 2 * HEAD_SIZE
    return [
        pltpu.VMEM((rows, pair), jnp.bfloat16),
        pltpu.VMEM((rows, pair), jnp.float32),
        pltpu.VMEM((rows, HEAD_SIZE), jnp.float32),
        pltpu.VMEM((rows, HEAD_SIZE), jnp.float32),
        pltpu.VMEM((rows, GROUP), jnp.bfloat16),
    ]


def attend_back_last(
    device, residual_low, operands, sums, tokens, gain, grad_residual, grad_gain_two, order, shard, head_shard
):
    rows, width = residual_low.shape
    whole = lambda *shape: pl.BlockSpec(shape, lambda *j: (0, 0))
    own_width = KEY_VALUE_HEADS * 2 * HEAD_SIZE + 128
    half = jax.ShapeDtypeStruct((width // 2, own_width), jnp.bfloat16)
    return pl.pallas_call(
        functools.partial(attend_back_body, order=order, shard=shard, head_shard=head_shard, last=True),
        grid_spec=pltpu.PrefetchScalarGridSpec(
            num_scalar_prefetch=1,
            grid=(KEY_VALUE_HEADS // 2,),
            in_specs=[whole(rows, width)]
            + attend_back_specs(rows, width, 1, lambda h, d: h)
            + [whole(2, HEAD_SIZE), whole(rows, width)]
            + [whole(rows, width), whole(1, width), whole(rows, width), whole(1, width)],
            out_specs=[whole(width // 2, own_width), whole(width // 2, own_width), whole(rows, width)],
            scratch_shapes=[
                pltpu.VMEM((2, HEAD_SIZE), jnp.float32),
                pltpu.VMEM((rows, width), jnp.float32),
                pltpu.VMEM((width, 128), jnp.float32),
            ]
            + attend_back_scratch(rows),
        ),
        out_shape=[half, half, jax.ShapeDtypeStruct((rows, width), jnp.bfloat16)],
        compiler_params=pltpu.CompilerParams(vmem_limit_bytes=38 * 1024 * 1024),
        cost_estimate=SMALL,
        name="attend_back_last",
    )(device.reshape(1), residual_low, *operands, *sums, tokens, gain, grad_residual, grad_gain_two)


def gather_down(down_ref, down_weight_ref, width):
    devices, rows, _ = down_ref.shape
    pieces = down_ref.shape[2] // width
    for index in range(devices):
        for piece in range(pieces):
            first = (index * pieces + piece) * rows
            down_weight_ref[first : first + rows, :] = down_ref[index, :, piece * width : (piece + 1) * width]


def feed_forward_body(
    device_ref, residual_ref, gain_ref, cotangent_ref, gate_ref, up_ref, down_ref,
    hidden_ref, grad_gate_ref, grad_up_ref, gate_kept_ref, gate_sent_ref, up_kept_ref, up_sent_ref,
    down_kept_ref, down_sent_ref, normed_ref, down_weight_ref, turned_ref, for_gate_ref, for_up_ref, product_ref,
    *, gate_order, up_order,
):
    device = device_ref[0]
    width = residual_ref.shape[1]

    @pl.when(pl.program_id(0) == 0)
    def _():
        unit, _ = unit_head(residual_ref[...])
        normed = (unit * gain_ref[...]).astype(jnp.bfloat16)
        normed_ref[...] = normed
        turned_ref[...] = normed.astype(turned_ref.dtype).T
        rows = width // len(gate_order)
        group = max(1, 16 // rows)
        for order, ref in ((gate_order, for_gate_ref), (up_order, for_up_ref)):
            for first in range(0, len(order), group):
                blocks = [
                    turned_ref[pl.ds(pl.multiple_of((device ^ mask) * rows, rows), rows), :]
                    for mask in order[first : first + group]
                ]
                block = blocks[0] if group == 1 else jnp.concatenate(blocks, axis=0)
                ref[first * rows : (first + group) * rows, :] = block.astype(jnp.bfloat16)

    normed = normed_ref[...]
    gather_down(down_ref, down_weight_ref, width)
    cotangent = cotangent_ref[...]
    gate = jnp.dot(normed, gate_ref[...].reshape(width, gate_ref.shape[-1]), preferred_element_type=jnp.float32)
    up = jnp.dot(normed, up_ref[...].reshape(width, up_ref.shape[-1]), preferred_element_type=jnp.float32)
    grad_hidden = contract(cotangent, down_weight_ref[...], 1, 1)
    sigmoid = jax.nn.sigmoid(gate)
    silu = gate * sigmoid
    hidden = (silu * up).astype(jnp.bfloat16)
    grad_gate = (grad_hidden * up * sigmoid * (1.0 + gate * (1.0 - sigmoid))).astype(jnp.bfloat16)
    hidden_ref[...] = hidden
    grad_gate_ref[...] = grad_gate
    grad_up = (grad_hidden * silu).astype(jnp.bfloat16)
    grad_up_ref[...] = grad_up

    for ordered_ref, grad, kept_ref, sent_ref in (
        (for_gate_ref, grad_gate, gate_kept_ref, gate_sent_ref),
        (for_up_ref, grad_up, up_kept_ref, up_sent_ref),
    ):
        product = jnp.dot(ordered_ref[...], grad, preferred_element_type=jnp.float32).astype(jnp.bfloat16)
        half = product.shape[0] // 2
        kept_ref[...] = product[:half]
        sent_ref[...] = product[half:]
    product_ref[...] = contract(hidden, cotangent, 0, 0).reshape(product_ref.shape)
    owners = product_ref.shape[0]
    low = device & (owners - 1)
    for target, core in ((down_kept_ref, 0), (down_sent_ref, 1)):
        blocks = [product_ref[low ^ (index | core)] for index in range(0, owners, 2)]
        target[...] = jnp.concatenate(blocks, axis=0).astype(jnp.bfloat16)


def ffn_operands(weights, shard, width, tiles, at):
    count, _, hidden_width = weights.shape
    tile = hidden_width // tiles
    if shard % 16 == 0:
        return [weights, weights, weights], [
            pl.BlockSpec((count, shard, tile), lambda *j: (0, 0, at(*j))),
            pl.BlockSpec((count, shard, tile), lambda *j: (0, 1, at(*j))),
            pl.BlockSpec((count // tiles, shard, hidden_width), lambda *j: (at(*j), 2, 0)),
        ]
    gate, up, down = (weights[:, part * shard : (part + 1) * shard] for part in range(3))
    down = down.reshape(count, shard, -1, width).transpose(0, 2, 1, 3).reshape(tiles, tile, width)
    return [gate.reshape(width, hidden_width), up.reshape(width, hidden_width), down], [
        pl.BlockSpec((width, tile), lambda *j: (0, at(*j))),
        pl.BlockSpec((width, tile), lambda *j: (0, at(*j))),
        pl.BlockSpec((1, tile, width), lambda *j: (at(*j), 0, 0)),
    ]


def feed_forward(device, residual, gain, cotangent, weights, shard, gate_order, up_order):
    rows, width = residual.shape
    count, _, hidden_width = weights.shape
    tiles = 8
    tile = hidden_width // tiles
    owners = count // tiles
    at = lambda j, d: j ^ (d[0] // owners)
    back = lambda j: (j & 1) * 4 + j // 2
    whole = pl.BlockSpec((rows, width), lambda j, d: (0, 0))
    row = pl.BlockSpec((1, width), lambda j, d: (0, 0))
    low = lambda height, size: jax.ShapeDtypeStruct((height, size), jnp.bfloat16)
    weight_args, weight_specs = ffn_operands(weights, shard, width, tiles, at)
    columns = lambda height: pl.BlockSpec((height, tile), lambda j, d: (0, at(j, d)))
    down_half = pl.BlockSpec((tile // 2, width), lambda j, d: (back(j), 0))
    return pl.pallas_call(
        functools.partial(feed_forward_body, gate_order=gate_order, up_order=up_order),
        grid_spec=pltpu.PrefetchScalarGridSpec(
            num_scalar_prefetch=1,
            grid=(tiles,),
            in_specs=[whole, row, whole] + weight_specs,
            out_specs=[
                columns(rows),
                columns(rows),
                columns(rows),
                columns(width // 2),
                columns(width // 2),
                columns(width // 2),
                columns(width // 2),
                down_half,
                down_half,
            ],
            scratch_shapes=[
                pltpu.VMEM((rows, width), jnp.bfloat16),
                pltpu.VMEM((tile, width), jnp.bfloat16),
                pltpu.VMEM((width, rows), jnp.bfloat16 if shard % 16 == 0 else jnp.float32),
                pltpu.VMEM((width, rows), jnp.bfloat16),
                pltpu.VMEM((width, rows), jnp.bfloat16),
                pltpu.VMEM((owners, tile // owners, width), jnp.float32),
            ],
        ),
        out_shape=[
            low(rows, hidden_width),
            low(rows, hidden_width),
            low(rows, hidden_width),
            low(width // 2, hidden_width),
            low(width // 2, hidden_width),
            low(width // 2, hidden_width),
            low(width // 2, hidden_width),
            low(hidden_width // 2, width),
            low(hidden_width // 2, width),
        ],
        compiler_params=pltpu.CompilerParams(vmem_limit_bytes=40 * 1024 * 1024),
        cost_estimate=SMALL,
        name="feed_forward",
    )(device.reshape(1), residual, gain, cotangent, *weight_args)


FFN_STEPS = 8


def back_body(device_ref, *refs):
    (
        residual_ref, gain_ref, cotangent_ref, grad_gate_ref, grad_up_ref, gate_ref, up_ref, turned_out_ref
    ), refs = refs[:8], refs[8:]
    operands, refs = refs[:12], refs[12:]
    (
        grad_residual_ref, grad_low_ref, grad_gain_ref, out_kept_ref, out_sent_ref, kept_ref, sent_ref, head_gains_ref,
        normed_sum_ref, back_ref,
    ), scratch = refs[:10], refs[10:]
    step = pl.program_id(0)
    width = residual_ref.shape[1]

    @pl.when(step == 0)
    def _():
        back_ref[...] = jnp.zeros_like(back_ref)

    @pl.when(step < FFN_STEPS)
    def _():
        back_ref[...] += contract(
            grad_gate_ref[...], gate_ref[...].reshape(width, gate_ref.shape[-1]), 1, 1
        ) + contract(grad_up_ref[...], up_ref[...].reshape(width, up_ref.shape[-1]), 1, 1)

    @pl.when(step == FFN_STEPS - 1)
    def _():
        unit, inverse = unit_head(residual_ref[...])
        grad = back_ref[...]
        grad_gain_ref[...] = jnp.sum(grad * unit, axis=0, keepdims=True)
        scaled = grad * gain_ref[...]
        grad_mid = inverse * (scaled - unit * jnp.mean(scaled * unit, axis=-1, keepdims=True))
        grad_residual = cotangent_ref[...].astype(jnp.float32) + grad_mid
        grad_residual_ref[...] = grad_residual
        grad_low = grad_residual.astype(jnp.bfloat16)
        grad_low_ref[...] = grad_low
        half = out_kept_ref.shape[0]
        for start in range(0, half, 512):
            for ref, shift in ((out_kept_ref, 0), (out_sent_ref, half)):
                rows = slice(start + shift, start + shift + 512)
                ref[start : start + 512, :] = jnp.dot(
                    turned_out_ref[rows, :], grad_low, preferred_element_type=jnp.float32
                ).astype(jnp.bfloat16)

    @pl.when(step >= FFN_STEPS)
    def _():
        attend_back_body(
            device_ref, grad_low_ref, *operands, kept_ref, sent_ref, head_gains_ref, normed_sum_ref, *scratch,
            order=None, shard=None, head_shard=None, last=False, head=step - FFN_STEPS,
        )


def back(device, residual, gain, cotangent, grad_gate, grad_up, weights, shard, turned_out, operands):
    rows, width = residual.shape
    tile = weights.shape[2] // FFN_STEPS
    at = lambda j, d: jnp.minimum(j, FFN_STEPS - 1)
    head = lambda j, d: jnp.maximum(j - FFN_STEPS, 0)
    whole = lambda *shape: pl.BlockSpec(shape, lambda *j: (0, 0))
    columns = pl.BlockSpec((rows, tile), lambda *j: (0, at(*j)))
    weight_args, weight_specs = ffn_operands(weights, shard, width, FFN_STEPS, at)
    out_rows = turned_out.shape[0]
    own_width = KEY_VALUE_HEADS * 2 * HEAD_SIZE
    low = lambda height, size: jax.ShapeDtypeStruct((height, size), jnp.bfloat16)
    wide = jax.ShapeDtypeStruct((rows, width), jnp.float32)
    return pl.pallas_call(
        back_body,
        grid_spec=pltpu.PrefetchScalarGridSpec(
            num_scalar_prefetch=1,
            grid=(FFN_STEPS + KEY_VALUE_HEADS // 2,),
            in_specs=[whole(rows, width), whole(1, width), whole(rows, width), columns, columns]
            + weight_specs[:2]
            + [whole(out_rows, rows)]
            + attend_back_specs(rows, width, 0, head),
            out_specs=[
                whole(rows, width),
                whole(rows, width),
                whole(1, width),
                whole(out_rows // 2, width),
                whole(out_rows // 2, width),
                whole(width // 2, own_width),
                whole(width // 2, own_width),
                whole(2, HEAD_SIZE),
                whole(rows, width),
            ],
            scratch_shapes=[pltpu.VMEM((rows, width), jnp.float32)] + attend_back_scratch(rows),
        ),
        out_shape=[
            wide,
            low(rows, width),
            jax.ShapeDtypeStruct((1, width), jnp.float32),
            low(out_rows // 2, width),
            low(out_rows // 2, width),
            low(width // 2, own_width),
            low(width // 2, own_width),
            jax.ShapeDtypeStruct((2, HEAD_SIZE), jnp.float32),
            wide,
        ],
        compiler_params=pltpu.CompilerParams(vmem_limit_bytes=46 * 1024 * 1024),
        cost_estimate=SMALL,
        name="back",
    )(device.reshape(1), residual, gain, cotangent, grad_gate, grad_up, *weight_args[:2], turned_out, *operands)


def ffn_out_body(residual_ref, hidden_ref, down_ref, mixed_ref, sum_ref, down_weight_ref):
    @pl.when(pl.program_id(0) == 0)
    def _():
        sum_ref[...] = residual_ref[...]

    gather_down(down_ref, down_weight_ref, residual_ref.shape[1])
    sum_ref[...] += jnp.dot(hidden_ref[...], down_weight_ref[...], preferred_element_type=jnp.float32)

    @pl.when(pl.program_id(0) == pl.num_programs(0) - 1)
    def _():
        mixed_ref[...] = sum_ref[...].astype(jnp.bfloat16)


def ffn_out(residual, hidden, weights, shard):
    rows, width = residual.shape
    tiles = 8
    tile = weights.shape[2] // tiles
    whole = pl.BlockSpec((rows, width), lambda j: (0, 0))
    weight_args, weight_specs = ffn_operands(weights, shard, width, tiles, lambda j: j)
    return pl.pallas_call(
        ffn_out_body,
        grid=(tiles,),
        in_specs=[whole, pl.BlockSpec((rows, tile), lambda j: (0, j)), weight_specs[2]],
        out_specs=whole,
        out_shape=jax.ShapeDtypeStruct((rows, width), jnp.bfloat16),
        scratch_shapes=[pltpu.VMEM((rows, width), jnp.float32), pltpu.VMEM((tile, width), jnp.bfloat16)],
        compiler_params=pltpu.CompilerParams(vmem_limit_bytes=16 * 1024 * 1024),
        cost_estimate=SMALL,
        name="ffn_out",
    )(residual, hidden, weight_args[2])


def end_body(first_kept, first_came, second_kept, second_came, query_ref, key_ref, value_ref, *gain_refs):
    def part(kept, came, start, size):
        columns = slice(start, start + size)
        return kept[:, columns].astype(jnp.float32) + came[:, columns].astype(jnp.float32)

    group = 0
    for kept, came in ((first_kept, first_came), (second_kept, second_came)):
        for start in range(0, KEY_VALUE_HEADS // 2 * GROUP, GROUP):
            for ref, size in ((query_ref, 2 * HEAD_SIZE), (key_ref, HEAD_SIZE), (value_ref, HEAD_SIZE)):
                ref[:, group * size : (group + 1) * size] = part(kept, came, start, size)
                start += size
            group += 1
    gains = part(second_kept, second_came, KEY_VALUE_HEADS // 2 * GROUP, 128).T
    for index, ref in enumerate(gain_refs):
        ref[...] = gains[index : index + 1, : ref.shape[1]]


def end_projections(first, second, head_shard):
    rows = first[0].shape[0]
    query_width, key_width = QUERY_HEADS * HEAD_SIZE, KEY_VALUE_HEADS * HEAD_SIZE
    return pl.pallas_call(
        end_body,
        out_shape=[
            jax.ShapeDtypeStruct(shape, jnp.float32)
            for shape in (
                (rows, query_width), (rows, key_width), (rows, key_width), (1, rows), (1, rows), (1, head_shard),
                (1, head_shard),
            )
        ],
        cost_estimate=SMALL,
        name="end_projections",
    )(*first, *second)


def on_device(
    tokens,
    seq_lengths,
    seq_owner,
    g_attn,
    w_query,
    key_projection,
    value_projection,
    query_norm_gain,
    g_key,
    w_out,
    g_ffn,
    w_gate,
    w_up,
    w_down,
    cotangent,
):
    row_total_count = tokens.shape[0]
    fence = lax.optimization_barrier
    count = lax.axis_size("fsdp")
    device = lax.axis_index("fsdp")
    early = middle_bits(count, False)
    late = middle_bits(count, True)
    cut_bits = len(early) // 2
    shard = g_attn.shape[0]
    head_shard = query_norm_gain.shape[0]

    pieces = w_down.shape[0] // shard
    down_pieces = w_down.reshape(pieces, shard, -1).transpose(1, 0, 2).reshape(shard, -1)
    ffn_weights = lax.all_gather(jnp.concatenate([w_gate, w_up, down_pieces], axis=0), "fsdp", axis=0, tiled=False)
    projections = join(
        w_query, key_projection, value_projection, gain_columns(g_attn, g_ffn, query_norm_gain, g_key, shard)
    )
    top = gather_top(projections, count)
    top, w_out = fence((top, w_out))
    top = gather_top_rest(top, count)
    top, w_out = fence((top, w_out))
    first_part, second_part = lay_top_split(top, device, count, KEY_VALUE_HEADS // 2 * GROUP + 128)
    first_parts = gather_bits({0: first_part}, count, early[:cut_bits])
    second_parts = gather_bits({0: second_part}, count, late[:cut_bits])
    out_top = gather_top(w_out, count)
    first_parts, second_parts, out_top = fence((first_parts, second_parts, out_top))
    first_parts = gather_bits(first_parts, count, early[cut_bits:])
    second_parts = gather_bits(second_parts, count, late[cut_bits:])
    out_top = gather_top_rest(out_top, count)
    first_parts, second_parts, out_top = fence((first_parts, second_parts, out_top))
    first_parts = gather_bits(first_parts, count, [0])
    out_parts = gather_bits(lay_top(out_top, device, count), count, early[:cut_bits])
    first_parts, second_parts = fence((first_parts, second_parts))
    second_parts = gather_bits(second_parts, count, [0])
    first_weight = lay(first_parts, device, count)

    seq_id, token_position = layout(seq_lengths, seq_owner, device, row_total_count)
    first_row = (jnp.arange(row_total_count, dtype=jnp.int32) - token_position)[:, None]
    cosine, sine = rotation_factors(token_position)
    inputs = tokens.astype(jnp.float32)
    gain_block = first_weight[:, KEY_VALUE_HEADS // 2 * GROUP :].astype(jnp.float32)
    head_gains = gain_block.reshape(count, shard, 128)[:, :head_shard, 2:4].reshape(HEAD_SIZE, 2).T
    gain_one = gain_block[:, 0]
    gain_two = gain_block[:, 1]
    normed_low = norm_forward(inputs, gain_one)[0].astype(jnp.bfloat16)
    attended_first, *saved_first = attend(normed_low, first_weight, head_gains, cosine, sine, first_row)
    attended_first, second_parts, out_parts = fence((attended_first, second_parts, out_parts))
    out_parts = gather_bits(out_parts, count, early[cut_bits:])
    second_weight = lay(second_parts, device, count)
    attended_second, *saved_second = attend(normed_low, second_weight, head_gains, cosine, sine, first_row)
    stages = sum_bits(count)
    orders = {name: row_order(count, bits) for name, bits in stages.items()}
    turned = {
        name: turn(values, device, orders[name])
        for name, values in (
            ("out", (attended_first, attended_second)), ("first", (normed_low,)), ("second", (normed_low,))
        )
    }
    attended_first, attended_second, turned, out_parts = fence((attended_first, attended_second, turned, out_parts))
    out_parts = gather_bits(out_parts, count, [0])
    out_weight = lay(out_parts, device, count)
    half_width = out_weight.shape[0] // 2
    residual = (
        inputs
        + jnp.dot(attended_first, out_weight[:half_width], preferred_element_type=jnp.float32)
        + jnp.dot(attended_second, out_weight[half_width:], preferred_element_type=jnp.float32)
    )
    (
        hidden, grad_gate, grad_up, gate_kept, gate_sent, up_kept, up_sent, down_kept, down_sent
    ) = feed_forward(
        device, residual, gain_two[None], cotangent, ffn_weights, shard, orders["gate"], orders["up"]
    )

    live = dict(
        hidden=hidden, grad_gate=grad_gate, grad_up=grad_up, gate=gate_kept, up=up_kept, down=down_kept,
    )
    flying = {}

    def cut():
        live.update(fence(dict(live)))

    def fly(**sent):
        live.update({name + "_sent": value for name, value in sent.items()})
        cut()
        for name in sent:
            flying[name] = exchange(live.pop(name + "_sent"), count, 1 << stages[name].pop(0))

    def land(*names):
        live.update({name + "_came": flying.pop(name) for name in names})
        cut()

    def halve(*names):
        halves = fold(*[(live[name], live.pop(name + "_came")) for name in names])
        live.update({name: kept for name, (kept, _) in zip(names, halves)})
        fly(**{name: sent for name, (_, sent) in zip(names, halves)})

    def pass_on(*names):
        land(*names)
        halve(*names)

    def end(*names):
        land(*names)
        return [(live.pop(name), live.pop(name + "_came")) for name in names]

    def operands(name, saved, weight):
        return out_weight, *saved, head_gains, cosine, sine, first_row, turned[name], weight

    fly(down=down_sent, gate=gate_sent, up=up_sent)
    pass_on("down")
    pass_on("gate")
    pass_on("up")
    (
        live["grad_residual"], live["low"], live["grad_gain_two"], live["out"], live["out_sent"], live["first"],
        live["first_sent"], live["head_sums"], live["normed_sum"],
    ) = back(
        device, residual, gain_two[None], cotangent, live.pop("grad_gate"), live.pop("grad_up"), ffn_weights, shard,
        turned["out"], operands("first", saved_first, first_weight),
    )
    land("down", "gate", "up")
    fly(first=live["first_sent"], out=live["out_sent"])
    halve("down", "gate", "up")
    pass_on("first", "out")
    live["second"], live["second_sent"], live["grad_tokens"] = attend_back_last(
        device, live.pop("low"), operands("second", saved_second, second_weight), (live.pop("head_sums"), live.pop("normed_sum")), tokens,
        gain_one[None], live.pop("grad_residual"), live.pop("grad_gain_two"), orders["second"], shard, head_shard,
    )
    land("down", "gate", "up", "first", "out")
    fly(second=live["second_sent"])
    halve("down", "gate", "up")
    land("second")
    halve("first", "out", "second")
    live["mixed"] = ffn_out(residual, live.pop("hidden"), ffn_weights, shard)
    cut()
    mixed, grad_tokens = live.pop("mixed"), live.pop("grad_tokens")
    while stages["down"]:
        pass_on("down", "gate", "up")
        pass_on("first", "out", "second")
    sums = {name: sum_end(pair) for name, pair in zip(("down", "gate", "up"), end("down", "gate", "up"))}
    live.update(sums)
    while stages["out"]:
        pass_on("first", "out", "second")
    sum_down, sum_gate, sum_up = live.pop("down"), live.pop("gate"), live.pop("up")
    first, out = end("first", "out")
    pass_on_last = stages["second"]
    while pass_on_last:
        pass_on("second")
    (second,) = end("second")
    sum_out = sum_end(out)
    sum_query, sum_key, sum_value, *sum_gains = end_projections(first, second, head_shard)
    return (
        mixed,
        grad_tokens,
        sum_gains[0].reshape(-1),
        sum_query,
        sum_key,
        sum_value,
        sum_gains[2].reshape(-1),
        sum_gains[3].reshape(-1),
        sum_out,
        sum_gains[1].reshape(-1),
        sum_gate,
        sum_up,
        sum_down,
    )


def solution(mesh):
    return jax.shard_map(
        on_device,
        mesh=mesh,
        in_specs=(
            P("fsdp", None),
            P(),
            P(),
            P("fsdp"),
            P("fsdp", None),
            P("fsdp", None),
            P("fsdp", None),
            P("fsdp"),
            P("fsdp"),
            P("fsdp", None),
            P("fsdp"),
            P("fsdp", None),
            P("fsdp", None),
            P("fsdp", None),
            P("fsdp", None),
        ),
        out_specs=(
            P("fsdp", None),
            P("fsdp", None),
            P("fsdp"),
            P("fsdp", None),
            P("fsdp", None),
            P("fsdp", None),
            P("fsdp"),
            P("fsdp"),
            P("fsdp", None),
            P("fsdp"),
            P("fsdp", None),
            P("fsdp", None),
            P("fsdp", None),
        ),
        check_vma=False,
    )
```

```python
import functools
import math

import jax
import jax.numpy as jnp
from jax import lax
from jax.experimental import pallas as pl
from jax.experimental.pallas import tpu as pltpu
from jax.sharding import PartitionSpec as P

QUERY_HEADS = 16
KEY_VALUE_HEADS = 8
HEAD_SIZE = 128


SMALL = pl.CostEstimate(flops=1, bytes_accessed=1, transcendentals=0)


def far(shape, dtype):
    return pltpu.HBM(tuple(shape), dtype)


def from_far(*values):
    return [pltpu.with_memory_space_constraint(value, pltpu.HBM) for value in values]


epsilon = 1e-06
rope_base = 1000000.0


def layout(seq_lengths, seq_owner, device, row_total_count):
    seq_index = jnp.arange(seq_lengths.shape[0], dtype=jnp.int32)
    same_owner = seq_owner[:, None] == seq_owner[None, :]
    before = seq_index[None, :] < seq_index[:, None]
    starts = jnp.sum(jnp.where(same_owner & before, seq_lengths[None, :], 0), axis=1)
    places = jnp.arange(row_total_count, dtype=jnp.int32)
    member = (
        (seq_owner[None, :] == device)
        & (starts[None, :] <= places[:, None])
        & (places[:, None] < (starts + seq_lengths)[None, :])
    )
    seq_id = jnp.sum(jnp.where(member, seq_index[None, :], 0), axis=1)
    token_position = jnp.sum(jnp.where(member, places[:, None] - starts[None, :], 0), axis=1)
    return (seq_id, token_position)


def rotation_factors(token_position):
    half_width = HEAD_SIZE // 2
    frequency = jnp.exp(
        jnp.arange(half_width, dtype=jnp.float32) * (-2.0 * math.log(rope_base) / HEAD_SIZE)
    )
    angles = token_position.astype(jnp.float32)[:, None] * frequency[None, :]
    cosine = jnp.cos(angles)
    sine = jnp.sin(angles)
    return jnp.concatenate([cosine, cosine], axis=1), jnp.concatenate([-sine, sine], axis=1)


def norm_forward(values, gain):
    inverse = lax.rsqrt(jnp.mean(values * values, axis=-1, keepdims=True) + epsilon)
    unit_rows = values * inverse
    return (unit_rows * gain, unit_rows, inverse)


def exchange(values, count, mask):
    return lax.ppermute(values, "fsdp", [(source, source ^ mask) for source in range(count)])


def middle_bits(count, flip):
    bits = list(range(1, count.bit_length() - 3))
    return bits[::-1] if flip else bits


def sum_bits(count):
    bits = count.bit_length() - 1
    middle = list(range(1, bits - 2))
    low, high = bits - 2, bits - 1
    return dict(
        down=[0, middle[-1], high, low] + middle[-2::-1],
        gate=[0] + middle + [low, high],
        up=[0, low, middle[-1], high] + middle[-2::-1],
        out=[0] + middle + [low, high],
        first=[0, low] + middle[::-1] + [high],
        second=[0] + middle + [low, high],
    )


def row_order(count, sequence):
    bits = len(sequence)
    return [
        sum(((index >> (bits - 1 - step)) & 1) << bit for step, bit in enumerate(sequence)) for index in range(count)
    ]


def turn_body(device_ref, *refs, order):
    values, (out_ref, turned_ref) = refs[:-2], refs[-2:]
    start = 0
    for ref in values:
        turned_ref[start : start + ref.shape[1], :] = ref[...].astype(turned_ref.dtype).T
        start += ref.shape[1]
    device = device_ref[0]
    rows = out_ref.shape[0] // len(order)
    group = max(1, 16 // rows)
    for first in range(0, len(order), group):
        blocks = [
            turned_ref[pl.ds(pl.multiple_of((device ^ mask) * rows, rows), rows), :]
            for mask in order[first : first + group]
        ]
        block = blocks[0] if group == 1 else jnp.concatenate(blocks, axis=0)
        out_ref[first * rows : (first + group) * rows, :] = block.astype(out_ref.dtype)


def turn(values, device, order):
    count = len(order)
    rows = values[0].shape[0]
    columns = sum(value.shape[1] for value in values)
    held = jnp.bfloat16 if columns // count % 16 == 0 else jnp.float32
    return pl.pallas_call(
        functools.partial(turn_body, order=order),
        grid_spec=pltpu.PrefetchScalarGridSpec(
            num_scalar_prefetch=1,
            grid=(1,),
            in_specs=[pl.BlockSpec(value.shape, lambda i, d: (0, 0)) for value in values],
            out_specs=pl.BlockSpec((columns, rows), lambda i, d: (0, 0)),
            scratch_shapes=[pltpu.VMEM((columns, rows), held)],
        ),
        out_shape=far((columns, rows), values[0].dtype),
        compiler_params=pltpu.CompilerParams(vmem_limit_bytes=16 * 1024 * 1024),
        cost_estimate=SMALL,
        name="turn",
    )(device.reshape(1), *values)


def fold_body(*refs):
    pairs = len(refs) // 6

    def add(first, second):
        return (first[...].astype(jnp.float32) + second[...].astype(jnp.float32)).astype(jnp.bfloat16)

    for index in range(pairs):
        kept_first, kept_second, came_first, came_second = refs[4 * index : 4 * index + 4]
        kept_ref, sent_ref = refs[4 * pairs + 2 * index : 4 * pairs + 2 * index + 2]
        sent_ref[...] = add(kept_second, came_second)
        kept_ref[...] = add(kept_first, came_first)


def fold(*pairs):
    halves = [kept.shape[0] // 2 for kept, _ in pairs]
    steps = next(n for n in (4, 2, 1) if n == 1 or all(rows % (16 * n) == 0 for rows in halves))
    in_specs, out_specs, out_shape, operands = [], [], [], []
    for rows, (kept, came) in zip(halves, pairs):
        columns = kept.shape[1]
        first = pl.BlockSpec((rows // steps, columns), lambda i: (i, 0))
        second = pl.BlockSpec((rows // steps, columns), lambda i: (i + steps, 0))
        in_specs += [first, second, first, second]
        operands += [kept, kept, came, came]
        out_specs += [first, first]
        out_shape += [jax.ShapeDtypeStruct((rows, columns), jnp.bfloat16)] * 2
    block_bytes = sum(6 * 2 * (rows // steps) * kept.shape[1] for rows, (kept, _) in zip(halves, pairs))
    out = pl.pallas_call(
        fold_body,
        grid=(steps,),
        in_specs=in_specs,
        out_specs=out_specs,
        out_shape=out_shape,
        compiler_params=pltpu.CompilerParams(vmem_limit_bytes=2 * block_bytes + 6 * 1024 * 1024),
        cost_estimate=SMALL,
        name="fold",
    )(*operands)
    return [out[2 * index : 2 * index + 2] for index in range(len(pairs))]


def sum_end(pair):
    return pair[0].astype(jnp.float32) + pair[1].astype(jnp.float32)


def place_body(device_ref, *refs):
    parts = refs[:-2]
    out_ref, semaphores = refs[-2:]
    device = device_ref[0]
    copies = [
        pltpu.make_async_copy(part, out_ref.at[:, device ^ mask], semaphores.at[mask])
        for mask, part in enumerate(parts)
    ]
    for copy in copies:
        copy.start()
    for copy in copies:
        copy.wait()


def place(parts, inner):
    top, rows, columns = parts[0].shape
    return pl.pallas_call(
        place_body,
        grid_spec=pltpu.PrefetchScalarGridSpec(
            num_scalar_prefetch=1,
            grid=(1,),
            in_specs=[pl.BlockSpec(memory_space=pl.ANY)] * len(parts),
            out_specs=pl.BlockSpec((top, len(parts), rows, columns), lambda i, d: (0, 0, 0, 0)),
            scratch_shapes=[pltpu.SemaphoreType.DMA((len(parts),))],
        ),
        out_shape=far((top, len(parts), rows, columns), parts[0].dtype)
        if top > 1
        else jax.ShapeDtypeStruct((top, len(parts), rows, columns), parts[0].dtype),
        compiler_params=pltpu.CompilerParams(vmem_limit_bytes=14 * 1024 * 1024),
        cost_estimate=SMALL,
        name="place",
    )(inner.reshape(1), *parts).reshape(top * len(parts) * rows, columns)


def gather_top(block, count):
    return [block, exchange(block, count, count // 4), exchange(block, count, count // 2)]


def gather_top_rest(blocks, count):
    return [block[None] for block in blocks + [exchange(blocks[2], count, count // 4)]]


def join_body(query_ref, key_ref, value_ref, gains_ref, out_ref):
    groups = KEY_VALUE_HEADS
    pair = query_ref.shape[1] // groups
    one = key_ref.shape[1] // groups
    shift = 0
    for group in range(groups):
        for ref, size in ((query_ref, pair), (key_ref, one), (value_ref, one)):
            out_ref[:, shift : shift + size] = ref[:, group * size : (group + 1) * size]
            shift += size
        if group == groups // 2 - 1:
            out_ref[:, shift : shift + 128] = gains_ref[...]
            shift += 128


def join(w_query, key_projection, value_projection, gains):
    rows = w_query.shape[0]
    columns = w_query.shape[1] + 2 * key_projection.shape[1] + 128
    return pl.pallas_call(
        join_body,
        out_shape=jax.ShapeDtypeStruct((rows, columns), w_query.dtype),
        cost_estimate=SMALL,
        name="join",
    )(w_query, key_projection, value_projection, gains)


def lay_top(blocks, device, count):
    return {0: place(from_far(*blocks), device // (count // 4)).reshape((4,) + blocks[0].shape[1:])}


def split_body(device_ref, *refs):
    parts = refs[:4]
    left_ref, right_ref, semaphores = refs[4:]
    width = left_ref.shape[-1]
    copies = []
    for mask, part in enumerate(parts):
        target = device_ref[0] ^ mask
        copies += [
            pltpu.make_async_copy(part.at[:, :width], left_ref.at[target], semaphores.at[2 * mask]),
            pltpu.make_async_copy(part.at[:, width:], right_ref.at[target], semaphores.at[2 * mask + 1]),
        ]
    for copy in copies:
        copy.start()
    for copy in copies:
        copy.wait()


def lay_top_split(blocks, device, count, width):
    rows, columns = blocks[0].shape[1:]
    shapes = [(4, rows, width), (4, rows, columns - width)]
    return pl.pallas_call(
        split_body,
        grid_spec=pltpu.PrefetchScalarGridSpec(
            num_scalar_prefetch=1,
            grid=(1,),
            in_specs=[pl.BlockSpec(memory_space=pl.ANY)] * 4,
            out_specs=[pl.BlockSpec(shape, lambda i, d: (0, 0, 0)) for shape in shapes],
            scratch_shapes=[pltpu.SemaphoreType.DMA((8,))],
        ),
        out_shape=[jax.ShapeDtypeStruct(shape, blocks[0].dtype) for shape in shapes],
        compiler_params=pltpu.CompilerParams(vmem_limit_bytes=10 * 1024 * 1024),
        cost_estimate=SMALL,
        name="lay_top_split",
    )((device // (count // 4)).reshape(1), *from_far(*[block[0] for block in blocks]))


def gather_bits(parts, count, bits):
    parts = dict(parts)
    for bit in bits:
        for mask in list(parts):
            parts[mask | (1 << bit)] = exchange(parts[mask], count, 1 << bit)
    return parts


def lay(parts, device, count):
    return place([parts[mask] for mask in range(count // 4)], device & (count // 4 - 1))


def gain_columns(first, second, third, fourth, rows):
    columns = [jnp.pad(v, (0, rows - v.shape[0]))[:, None] for v in (first, second, third, fourth)]
    return jnp.pad(jnp.concatenate(columns, axis=1), ((0, 0), (0, 124)))


def swap_halves(head):
    return pltpu.roll(head, HEAD_SIZE // 2, 1)


def unit_head(raw):
    inverse = lax.rsqrt(jnp.mean(raw * raw, axis=-1, keepdims=True) + epsilon)
    return raw * inverse, inverse


def contract(left, right, left_axis, right_axis):
    return lax.dot_general(
        left, right, (((left_axis,), (right_axis,)), ((), ())), preferred_element_type=jnp.float32
    )


def block_scores(group, key_rows, first_row, row_start):
    scores = contract(group, key_rows, 1, 1) * (1.0 / math.sqrt(HEAD_SIZE))
    rows = lax.broadcasted_iota(jnp.int32, scores.shape, 0)
    half = scores.shape[0] // 2
    rows = jnp.where(rows >= half, rows - half, rows) + row_start
    columns = lax.broadcasted_iota(jnp.int32, scores.shape, 1)
    return jnp.where((columns <= rows) & (columns >= first_row), scores, -1e30)


def head_pair(ref, block):
    return jnp.concatenate([ref[block, :HEAD_SIZE], ref[block, HEAD_SIZE:]], axis=0)


def pair_rows(first_row_ref, block):
    rows = first_row_ref[block, :]
    return jnp.concatenate([rows, rows], axis=0)


GROUP = 4 * HEAD_SIZE


def weight_parts(parts, device, count):
    if parts[0].shape[1] % 16 == 0:
        return [parts[mask] for mask in range(count // 4)]
    weight = lay(parts, device, count)
    return [weight[None]]


def part_specs(parts, index):
    top, rows, _ = parts[0].shape
    return [pl.BlockSpec((top, rows, GROUP), lambda *j: (0, 0, index(*j))) for _ in parts]


def join_parts(device_ref, part_refs, weight_ref):
    inner = device_ref[0] & (len(part_refs) - 1)
    for mask, ref in enumerate(part_refs):
        weight_ref[:, inner ^ mask] = ref[...]
    top, count, rows, columns = weight_ref.shape
    return weight_ref[...].reshape(top * count * rows, columns)


def attend_body(device_ref, *refs):
    (*part_refs, normed_ref, gains_ref, cosine_ref, sine_ref, first_ref), out_refs = refs[:-7], refs[-7:]
    attended_ref, query_ref, key_ref, value_ref, raw_ref, total_ref, weight_ref = out_refs
    cosine = cosine_ref[...]
    sine = sine_ref[...]

    def turned(raw, gain):
        scaled = unit_head(raw)[0] * gain
        return (scaled * cosine + swap_halves(scaled) * sine).astype(jnp.bfloat16)

    weight = join_parts(device_ref, part_refs, weight_ref)
    raw = jnp.dot(normed_ref[...], weight, preferred_element_type=jnp.float32)
    raw_ref[...] = raw[:, : 3 * HEAD_SIZE]
    for head in range(2):
        part = slice(head * HEAD_SIZE, (head + 1) * HEAD_SIZE)
        query_ref[:, part] = turned(raw[:, part], gains_ref[0:1, :])
    key_ref[...] = turned(raw[:, 2 * HEAD_SIZE : 3 * HEAD_SIZE], gains_ref[1:2, :])
    value_ref[...] = raw[:, 3 * HEAD_SIZE :].astype(jnp.bfloat16)
    step = 128
    for start in range(0, raw.shape[0], step):
        block = slice(start, start + step)
        seen = slice(0, start + step)
        scores = block_scores(head_pair(query_ref, block), key_ref[seen, :], pair_rows(first_ref, block), start)
        top = jnp.max(scores, axis=-1, keepdims=True)
        log_total = top + jnp.log(jnp.sum(jnp.exp(scores - top), axis=-1, keepdims=True))
        probs_low = jnp.exp(scores - log_total).astype(jnp.bfloat16)
        out = jnp.dot(probs_low, value_ref[seen, :], preferred_element_type=jnp.float32).astype(jnp.bfloat16)
        attended_ref[block, :HEAD_SIZE] = out[:step]
        attended_ref[block, HEAD_SIZE:] = out[step:]
        total_ref[0, block, 0:1] = log_total[:step]
        total_ref[0, block, 1:2] = log_total[step:]


def attend(device, normed, parts, head_gains, cosine, sine, first_row):
    rows, width = normed.shape
    groups = KEY_VALUE_HEADS // 2
    whole = lambda *shape: pl.BlockSpec(shape, lambda h, d: (0, 0))
    columns = lambda size: pl.BlockSpec((rows, size), lambda h, d: (0, h))
    low = lambda size: far((rows, groups * size), jnp.bfloat16)
    pair = 2 * HEAD_SIZE
    return pl.pallas_call(
        attend_body,
        grid_spec=pltpu.PrefetchScalarGridSpec(
            num_scalar_prefetch=1,
            grid=(groups,),
            in_specs=part_specs(parts, lambda h, d: h)
            + [
                whole(rows, width),
                whole(2, HEAD_SIZE),
                whole(rows, HEAD_SIZE),
                whole(rows, HEAD_SIZE),
                whole(rows, 1),
            ],
            out_specs=[
                columns(pair),
                columns(pair),
                columns(HEAD_SIZE),
                columns(HEAD_SIZE),
                columns(3 * HEAD_SIZE),
                pl.BlockSpec((1, rows, 2), lambda h, d: (h, 0, 0)),
            ],
            scratch_shapes=[pltpu.VMEM((parts[0].shape[0], len(parts), parts[0].shape[1], GROUP), jnp.bfloat16)],
        ),
        out_shape=[
            jax.ShapeDtypeStruct((rows, groups * pair), jnp.bfloat16),
            low(pair),
            low(HEAD_SIZE),
            low(HEAD_SIZE),
            far((rows, groups * 3 * HEAD_SIZE), jnp.float32),
            far((groups, rows, 2), jnp.float32),
        ],
        compiler_params=pltpu.CompilerParams(vmem_limit_bytes=26 * 1024 * 1024),
        cost_estimate=SMALL,
        name="attend",
    )(device.reshape(1), *parts, normed, head_gains, cosine, sine, first_row)


def attend_back_body(
    device_ref, residual_ref, wo_ref, query_ref, key_ref, value_ref, raw_ref, total_ref,
    gains_ref, cosine_ref, sine_ref, first_ref, turned_ref, *refs,
    order, shard, head_shard, last, parts, head=None,
):
    part_refs, refs = refs[:parts], refs[parts:]
    if last:
        head_gains_in_ref, normed_in_ref = refs[:2]
        refs = refs[2:]
        tokens_ref, gain_ref, grad_residual_ref, gain_two_ref, kept_ref, sent_ref, tokens_out_ref = refs[:7]
        head_gains_ref, normed_sum_ref, lines_ref = refs[7:10]
        scratch = refs[10:]
    else:
        kept_ref, sent_ref, head_gains_ref, normed_sum_ref = refs[:4]
        scratch = refs[4:]
    grad_out_ref, query_sum_ref, key_sum_ref, value_sum_ref, grads_ref, weight_ref = scratch
    scale = 1.0 / math.sqrt(HEAD_SIZE)
    heads = KEY_VALUE_HEADS // 2
    if head is None:
        head = pl.program_id(0)

    @pl.when(head == 0)
    def _():
        head_gains_ref[...] = head_gains_in_ref[...] if last else jnp.zeros_like(head_gains_ref)
        normed_sum_ref[...] = normed_in_ref[...] if last else jnp.zeros_like(normed_sum_ref)

    grad_out_ref[...] = contract(residual_ref[...], wo_ref[...], 1, 1).astype(jnp.bfloat16)
    key_sum_ref[...] = jnp.zeros_like(key_sum_ref)
    value_sum_ref[...] = jnp.zeros_like(value_sum_ref)
    step = 128
    for start in range(0, residual_ref.shape[0], step):
        block = slice(start, start + step)
        seen = slice(0, start + step)
        group = head_pair(query_ref, block)
        grad_out = head_pair(grad_out_ref, block)
        key_rows = key_ref[seen, :]
        scores = block_scores(group, key_rows, pair_rows(first_ref, block), start)
        log_total = jnp.concatenate([total_ref[0, block, 0:1], total_ref[0, block, 1:2]], axis=0)
        probs = jnp.exp(scores - log_total)
        grad_probs = contract(grad_out, value_ref[seen, :], 1, 1)
        value_sum_ref[seen, :] += contract(probs.astype(jnp.bfloat16), grad_out, 0, 0)
        inner = jnp.sum(probs * grad_probs, axis=-1, keepdims=True)
        grad_scores = (probs * (grad_probs - inner)).astype(jnp.bfloat16)
        grad_group = jnp.dot(grad_scores, key_rows, preferred_element_type=jnp.float32) * scale
        query_sum_ref[block, :HEAD_SIZE] = grad_group[:step]
        query_sum_ref[block, HEAD_SIZE:] = grad_group[step:]
        key_sum_ref[seen, :] += contract(grad_scores, group, 0, 0)
    grads_ref[:, 3 * HEAD_SIZE :] = value_sum_ref[...].astype(jnp.bfloat16)
    cosine = cosine_ref[...]
    sine = sine_ref[...]

    def back(grad, part, gain):
        turned = grad * cosine - swap_halves(grad) * sine
        unit, inverse = unit_head(raw_ref[:, part])
        product = turned * unit
        scaled = turned * gain
        grad_raw = inverse * (scaled - unit * jnp.mean(product * gain, axis=-1, keepdims=True))
        grads_ref[:, part] = grad_raw.astype(jnp.bfloat16)
        return jnp.sum(product, axis=0, keepdims=True)

    for index in range(2):
        part = slice(index * HEAD_SIZE, (index + 1) * HEAD_SIZE)
        head_gains_ref[0:1, :] += back(query_sum_ref[:, part], part, gains_ref[0:1, :])
    part = slice(2 * HEAD_SIZE, 3 * HEAD_SIZE)
    head_gains_ref[1:2, :] += back(key_sum_ref[...] * scale, part, gains_ref[1:2, :])

    grads = grads_ref[...]
    half = turned_ref.shape[0] // 2
    product = jnp.dot(turned_ref[...], grads, preferred_element_type=jnp.float32).astype(jnp.bfloat16)
    columns = pl.ds(pl.multiple_of(head * GROUP, GROUP), GROUP)
    kept_ref[:, columns] = product[:half]
    sent_ref[:, columns] = product[half:]
    normed_sum_ref[...] += contract(grads, join_parts(device_ref, part_refs, weight_ref), 1, 1)

    if not last:
        return

    @pl.when(head == heads - 1)
    def _():
        unit, inverse = unit_head(tokens_ref[...].astype(jnp.float32))
        grad = normed_sum_ref[...]
        scaled = grad * gain_ref[...]
        grad_first = inverse * (scaled - unit * jnp.mean(scaled * unit, axis=-1, keepdims=True))
        tokens_out_ref[...] = (grad_residual_ref[...] + grad_first).astype(jnp.bfloat16)
        width = grad.shape[1]
        source = lax.broadcasted_iota(jnp.int32, (HEAD_SIZE, width), 0)
        target = lax.broadcasted_iota(jnp.int32, (HEAD_SIZE, width), 1)
        spread = jnp.where(source // head_shard * shard + source % head_shard == target, 1.0, 0.0)
        heads = jnp.dot(
            head_gains_ref[...], spread, precision=lax.Precision.HIGHEST, preferred_element_type=jnp.float32
        )
        lines = jnp.concatenate(
            [
                jnp.sum(grad * unit, axis=0, keepdims=True),
                gain_two_ref[...],
                heads,
                jnp.zeros((124, width), jnp.float32),
            ],
            axis=0,
        )
        lines_ref[...] = lines.T
        device = device_ref[0]
        group = max(1, 16 // shard)
        end = slice(kept_ref.shape[1] - 128, None)
        for first in range(0, len(order), group):
            blocks = [
                lines_ref[pl.ds(pl.multiple_of((device ^ mask) * shard, shard), shard), :]
                for mask in order[first : first + group]
            ]
            block = (blocks[0] if group == 1 else jnp.concatenate(blocks, axis=0)).astype(jnp.bfloat16)
            row = first * shard
            target_ref = kept_ref if row < half else sent_ref
            target_ref[row % half : row % half + group * shard, end] = block


def attend_back_specs(rows, width, part, head, parts):
    first = part * KEY_VALUE_HEADS // 2
    whole = lambda *shape: pl.BlockSpec(shape, lambda *j: (0, 0))
    columns = lambda height, size: pl.BlockSpec((height, size), lambda *j: (0, head(*j)))
    pair = 2 * HEAD_SIZE
    return [
        pl.BlockSpec((pair, width), lambda *j: (head(*j) + first, 0)),
        columns(rows, pair),
        columns(rows, HEAD_SIZE),
        columns(rows, HEAD_SIZE),
        columns(rows, 3 * HEAD_SIZE),
        pl.BlockSpec((1, rows, 2), lambda *j: (head(*j), 0, 0)),
        whole(2, HEAD_SIZE),
        whole(rows, HEAD_SIZE),
        whole(rows, HEAD_SIZE),
        whole(rows, 1),
        whole(width, rows),
    ] + part_specs(parts, head)


def attend_back_scratch(rows, parts):
    pair = 2 * HEAD_SIZE
    return [
        pltpu.VMEM((rows, pair), jnp.bfloat16),
        pltpu.VMEM((rows, pair), jnp.float32),
        pltpu.VMEM((rows, HEAD_SIZE), jnp.float32),
        pltpu.VMEM((rows, HEAD_SIZE), jnp.float32),
        pltpu.VMEM((rows, GROUP), jnp.bfloat16),
        pltpu.VMEM((parts[0].shape[0], len(parts), parts[0].shape[1], GROUP), jnp.bfloat16),
    ]


def attend_back_last(
    device, residual_low, operands, parts, sums, tokens, gain, grad_residual, grad_gain_two, order, shard, head_shard
):
    rows, width = residual_low.shape
    whole = lambda *shape: pl.BlockSpec(shape, lambda *j: (0, 0))
    own_width = KEY_VALUE_HEADS * 2 * HEAD_SIZE + 128
    half = jax.ShapeDtypeStruct((width // 2, own_width), jnp.bfloat16)
    return pl.pallas_call(
        functools.partial(
            attend_back_body, order=order, shard=shard, head_shard=head_shard, last=True, parts=len(parts)
        ),
        grid_spec=pltpu.PrefetchScalarGridSpec(
            num_scalar_prefetch=1,
            grid=(KEY_VALUE_HEADS // 2,),
            in_specs=[whole(rows, width)]
            + attend_back_specs(rows, width, 1, lambda h, d: h, parts)
            + [whole(2, HEAD_SIZE), whole(rows, width)]
            + [whole(rows, width), whole(1, width), whole(rows, width), whole(1, width)],
            out_specs=[whole(width // 2, own_width), whole(width // 2, own_width), whole(rows, width)],
            scratch_shapes=[
                pltpu.VMEM((2, HEAD_SIZE), jnp.float32),
                pltpu.VMEM((rows, width), jnp.float32),
                pltpu.VMEM((width, 128), jnp.float32),
            ]
            + attend_back_scratch(rows, parts),
        ),
        out_shape=[half, half, jax.ShapeDtypeStruct((rows, width), jnp.bfloat16)],
        compiler_params=pltpu.CompilerParams(vmem_limit_bytes=38 * 1024 * 1024),
        cost_estimate=SMALL,
        name="attend_back_last",
    )(
        device.reshape(1), residual_low, *operands, *parts, sums[0], *from_far(sums[1], tokens), gain, *from_far(grad_residual),
        grad_gain_two,
    )


def project_body(device_ref, *refs):
    (*part_refs, tokens_ref, attended_ref), (residual_ref, weight_out_ref) = refs[:-2], refs[-2:]
    inner = device_ref[0] & (len(part_refs) - 1)

    @pl.when(pl.program_id(0) == 0)
    def _():
        residual_ref[...] = tokens_ref[...].astype(jnp.float32)

    for mask, ref in enumerate(part_refs):
        weight_out_ref[:, inner ^ mask] = ref[...]
    top, count, rows, columns = weight_out_ref.shape
    weight = weight_out_ref[...].reshape(top * count * rows, columns)
    residual_ref[...] += jnp.dot(attended_ref[...], weight, preferred_element_type=jnp.float32)


def project(device, parts, tokens, attended):
    rows, width = tokens.shape
    top, part_rows, _ = parts[0].shape
    step_rows = len(parts) * part_rows
    whole = pl.BlockSpec((rows, width), lambda j, d: (0, 0))
    residual, weight = pl.pallas_call(
        project_body,
        grid_spec=pltpu.PrefetchScalarGridSpec(
            num_scalar_prefetch=1,
            grid=(top,),
            in_specs=[pl.BlockSpec((1, part_rows, width), lambda j, d: (j, 0, 0)) for _ in parts]
            + [whole, pl.BlockSpec((rows, step_rows), lambda j, d: (0, j))],
            out_specs=[whole, pl.BlockSpec((1, len(parts), part_rows, width), lambda j, d: (j, 0, 0, 0))],
        ),
        out_shape=[
            jax.ShapeDtypeStruct((rows, width), jnp.float32),
            far((top, len(parts), part_rows, width), jnp.bfloat16),
        ],
        compiler_params=pltpu.CompilerParams(vmem_limit_bytes=20 * 1024 * 1024),
        cost_estimate=SMALL,
        name="project",
    )(device.reshape(1), *parts, tokens, attended)
    return residual, weight.reshape(top * step_rows, width)


def gather_down(down_ref, down_weight_ref, width):
    devices, rows, _ = down_ref.shape
    pieces = down_ref.shape[2] // width
    for index in range(devices):
        for piece in range(pieces):
            first = (index * pieces + piece) * rows
            down_weight_ref[first : first + rows, :] = down_ref[index, :, piece * width : (piece + 1) * width]


def feed_forward_body(
    device_ref, residual_ref, gain_ref, cotangent_ref, gate_ref, up_ref, down_ref,
    hidden_ref, grad_gate_ref, grad_up_ref, gate_kept_ref, gate_sent_ref, up_kept_ref, up_sent_ref,
    down_kept_ref, down_sent_ref, normed_ref, down_weight_ref, turned_ref, for_gate_ref, for_up_ref, product_ref,
    *, gate_order, up_order,
):
    device = device_ref[0]
    width = residual_ref.shape[1]

    @pl.when(pl.program_id(0) == 0)
    def _():
        unit, _ = unit_head(residual_ref[...])
        normed = (unit * gain_ref[...]).astype(jnp.bfloat16)
        normed_ref[...] = normed
        turned_ref[...] = normed.astype(turned_ref.dtype).T
        rows = width // len(gate_order)
        group = max(1, 16 // rows)
        for order, ref in ((gate_order, for_gate_ref), (up_order, for_up_ref)):
            for first in range(0, len(order), group):
                blocks = [
                    turned_ref[pl.ds(pl.multiple_of((device ^ mask) * rows, rows), rows), :]
                    for mask in order[first : first + group]
                ]
                block = blocks[0] if group == 1 else jnp.concatenate(blocks, axis=0)
                ref[first * rows : (first + group) * rows, :] = block.astype(jnp.bfloat16)

    normed = normed_ref[...]
    gather_down(down_ref, down_weight_ref, width)
    cotangent = cotangent_ref[...]
    gate = jnp.dot(normed, gate_ref[...].reshape(width, gate_ref.shape[-1]), preferred_element_type=jnp.float32)
    up = jnp.dot(normed, up_ref[...].reshape(width, up_ref.shape[-1]), preferred_element_type=jnp.float32)
    grad_hidden = contract(cotangent, down_weight_ref[...], 1, 1)
    sigmoid = jax.nn.sigmoid(gate)
    silu = gate * sigmoid
    hidden = (silu * up).astype(jnp.bfloat16)
    grad_gate = (grad_hidden * up * sigmoid * (1.0 + gate * (1.0 - sigmoid))).astype(jnp.bfloat16)
    hidden_ref[...] = hidden
    grad_gate_ref[...] = grad_gate
    grad_up = (grad_hidden * silu).astype(jnp.bfloat16)
    grad_up_ref[...] = grad_up

    for ordered_ref, grad, kept_ref, sent_ref in (
        (for_gate_ref, grad_gate, gate_kept_ref, gate_sent_ref),
        (for_up_ref, grad_up, up_kept_ref, up_sent_ref),
    ):
        product = jnp.dot(ordered_ref[...], grad, preferred_element_type=jnp.float32).astype(jnp.bfloat16)
        half = product.shape[0] // 2
        kept_ref[...] = product[:half]
        sent_ref[...] = product[half:]
    product_ref[...] = contract(hidden, cotangent, 0, 0).reshape(product_ref.shape)
    owners = product_ref.shape[0]
    low = device & (owners - 1)
    for target, core in ((down_kept_ref, 0), (down_sent_ref, 1)):
        blocks = [product_ref[low ^ (index | core)] for index in range(0, owners, 2)]
        target[...] = jnp.concatenate(blocks, axis=0).astype(jnp.bfloat16).reshape(target.shape)


def ffn_operands(weights, shard, width, tiles, at):
    count, _, hidden_width = weights.shape
    tile = hidden_width // tiles
    if shard % 16 == 0:
        return [weights, weights, weights], [
            pl.BlockSpec((count, shard, tile), lambda *j: (0, 0, at(*j))),
            pl.BlockSpec((count, shard, tile), lambda *j: (0, 1, at(*j))),
            pl.BlockSpec((count // tiles, shard, hidden_width), lambda *j: (at(*j), 2, 0)),
        ]
    gate, up, down = (weights[:, part * shard : (part + 1) * shard] for part in range(3))
    down = down.reshape(count, shard, -1, width).transpose(0, 2, 1, 3).reshape(tiles, tile, width)
    return [gate.reshape(width, hidden_width), up.reshape(width, hidden_width), down], [
        pl.BlockSpec((width, tile), lambda *j: (0, at(*j))),
        pl.BlockSpec((width, tile), lambda *j: (0, at(*j))),
        pl.BlockSpec((1, tile, width), lambda *j: (at(*j), 0, 0)),
    ]


def feed_forward(device, residual, gain, cotangent, weights, shard, gate_order, up_order):
    rows, width = residual.shape
    count, _, hidden_width = weights.shape
    tiles = 4
    tile = hidden_width // tiles
    owners = count // tiles
    at = lambda j, d: j ^ (d[0] // owners)
    whole = pl.BlockSpec((rows, width), lambda j, d: (0, 0))
    row = pl.BlockSpec((1, width), lambda j, d: (0, 0))
    low = lambda height, size: jax.ShapeDtypeStruct((height, size), jnp.bfloat16)
    low4 = jax.ShapeDtypeStruct((2, tiles, tile // 4, width), jnp.bfloat16)
    weight_args, weight_specs = ffn_operands(weights, shard, width, tiles, at)
    columns = lambda height: pl.BlockSpec((height, tile), lambda j, d: (0, at(j, d)))
    down_half = pl.BlockSpec((2, 1, tile // 4, width), lambda j, d: (0, j, 0, 0))
    *out, down_kept, down_sent = pl.pallas_call(
        functools.partial(feed_forward_body, gate_order=gate_order, up_order=up_order),
        grid_spec=pltpu.PrefetchScalarGridSpec(
            num_scalar_prefetch=1,
            grid=(tiles,),
            in_specs=[whole, row, whole] + weight_specs,
            out_specs=[
                columns(rows),
                columns(rows),
                columns(rows),
                columns(width // 2),
                columns(width // 2),
                columns(width // 2),
                columns(width // 2),
                down_half,
                down_half,
            ],
            scratch_shapes=[
                pltpu.VMEM((rows, width), jnp.bfloat16),
                pltpu.VMEM((tile, width), jnp.bfloat16),
                pltpu.VMEM((width, rows), jnp.bfloat16 if shard % 16 == 0 else jnp.float32),
                pltpu.VMEM((width, rows), jnp.bfloat16),
                pltpu.VMEM((width, rows), jnp.bfloat16),
                pltpu.VMEM((owners, tile // owners, width), jnp.float32),
            ],
        ),
        out_shape=[
            far((rows, hidden_width), jnp.bfloat16),
            far((rows, hidden_width), jnp.bfloat16),
            far((rows, hidden_width), jnp.bfloat16),
            low(width // 2, hidden_width),
            low(width // 2, hidden_width),
            low(width // 2, hidden_width),
            low(width // 2, hidden_width),
            low4,
            low4,
        ],
        compiler_params=pltpu.CompilerParams(vmem_limit_bytes=56 * 1024 * 1024),
        cost_estimate=SMALL,
        name="feed_forward",
    )(device.reshape(1), residual, gain, *from_far(cotangent, *weight_args))
    return *out, down_kept.reshape(-1, width), down_sent.reshape(-1, width)


FFN_STEPS = 4


def back_body(device_ref, *refs, parts):
    (
        residual_ref, gain_ref, cotangent_ref, grad_gate_ref, grad_up_ref, gate_ref, up_ref, turned_out_ref
    ), refs = refs[:8], refs[8:]
    operands, refs = refs[: 11 + parts], refs[11 + parts :]
    (
        grad_residual_ref, grad_low_ref, grad_gain_ref, out_kept_ref, out_sent_ref, kept_ref, sent_ref, head_gains_ref,
        normed_sum_ref, back_ref,
    ), scratch = refs[:10], refs[10:]
    step = pl.program_id(0)
    width = residual_ref.shape[1]

    @pl.when(step == 0)
    def _():
        back_ref[...] = jnp.zeros_like(back_ref)

    @pl.when(step < FFN_STEPS)
    def _():
        back_ref[...] += contract(
            grad_gate_ref[...], gate_ref[...].reshape(width, gate_ref.shape[-1]), 1, 1
        ) + contract(grad_up_ref[...], up_ref[...].reshape(width, up_ref.shape[-1]), 1, 1)

    @pl.when(step == FFN_STEPS - 1)
    def _():
        unit, inverse = unit_head(residual_ref[...])
        grad = back_ref[...]
        grad_gain_ref[...] = jnp.sum(grad * unit, axis=0, keepdims=True)
        scaled = grad * gain_ref[...]
        grad_mid = inverse * (scaled - unit * jnp.mean(scaled * unit, axis=-1, keepdims=True))
        grad_residual = cotangent_ref[...].astype(jnp.float32) + grad_mid
        grad_residual_ref[...] = grad_residual
        grad_low = grad_residual.astype(jnp.bfloat16)
        grad_low_ref[...] = grad_low
        half = out_kept_ref.shape[0]
        for start in range(0, half, 512):
            for ref, shift in ((out_kept_ref, 0), (out_sent_ref, half)):
                rows = slice(start + shift, start + shift + 512)
                ref[start : start + 512, :] = jnp.dot(
                    turned_out_ref[rows, :], grad_low, preferred_element_type=jnp.float32
                ).astype(jnp.bfloat16)

    @pl.when(step >= FFN_STEPS)
    def _():
        attend_back_body(
            device_ref, grad_low_ref, *operands, kept_ref, sent_ref, head_gains_ref, normed_sum_ref, *scratch,
            order=None, shard=None, head_shard=None, last=False, parts=parts, head=step - FFN_STEPS,
        )


def back(device, residual, gain, cotangent, grad_gate, grad_up, weights, shard, turned_out, operands, parts):
    rows, width = residual.shape
    tile = weights.shape[2] // FFN_STEPS
    at = lambda j, d: jnp.minimum(j, FFN_STEPS - 1)
    head = lambda j, d: jnp.maximum(j - FFN_STEPS, 0)
    whole = lambda *shape: pl.BlockSpec(shape, lambda *j: (0, 0))
    columns = pl.BlockSpec((rows, tile), lambda *j: (0, at(*j)))
    weight_args, weight_specs = ffn_operands(weights, shard, width, FFN_STEPS, at)
    out_rows = turned_out.shape[0]
    own_width = KEY_VALUE_HEADS * 2 * HEAD_SIZE
    low = lambda height, size: jax.ShapeDtypeStruct((height, size), jnp.bfloat16)
    wide = far((rows, width), jnp.float32)
    return pl.pallas_call(
        functools.partial(back_body, parts=len(parts)),
        grid_spec=pltpu.PrefetchScalarGridSpec(
            num_scalar_prefetch=1,
            grid=(FFN_STEPS + KEY_VALUE_HEADS // 2,),
            in_specs=[whole(rows, width), whole(1, width), whole(rows, width), columns, columns]
            + weight_specs[:2]
            + [whole(out_rows, rows)]
            + attend_back_specs(rows, width, 0, head, parts),
            out_specs=[
                whole(rows, width),
                whole(rows, width),
                whole(1, width),
                whole(out_rows // 2, width),
                whole(out_rows // 2, width),
                whole(width // 2, own_width),
                whole(width // 2, own_width),
                whole(2, HEAD_SIZE),
                whole(rows, width),
            ],
            scratch_shapes=[pltpu.VMEM((rows, width), jnp.float32)] + attend_back_scratch(rows, parts),
        ),
        out_shape=[
            wide,
            low(rows, width),
            jax.ShapeDtypeStruct((1, width), jnp.float32),
            low(out_rows // 2, width),
            low(out_rows // 2, width),
            low(width // 2, own_width),
            low(width // 2, own_width),
            jax.ShapeDtypeStruct((2, HEAD_SIZE), jnp.float32),
            wide,
        ],
        compiler_params=pltpu.CompilerParams(vmem_limit_bytes=50 * 1024 * 1024),
        cost_estimate=SMALL,
        name="back",
    )(
        device.reshape(1), residual, gain, *from_far(cotangent, grad_gate, grad_up, *weight_args[:2], turned_out), *operands, *parts
    )


def ffn_out_body(residual_ref, hidden_ref, down_ref, mixed_ref, sum_ref, down_weight_ref):
    @pl.when(pl.program_id(0) == 0)
    def _():
        sum_ref[...] = residual_ref[...]

    gather_down(down_ref, down_weight_ref, residual_ref.shape[1])
    sum_ref[...] += jnp.dot(hidden_ref[...], down_weight_ref[...], preferred_element_type=jnp.float32)

    @pl.when(pl.program_id(0) == pl.num_programs(0) - 1)
    def _():
        mixed_ref[...] = sum_ref[...].astype(jnp.bfloat16)


def ffn_out(residual, hidden, weights, shard):
    rows, width = residual.shape
    tiles = 8
    tile = weights.shape[2] // tiles
    whole = pl.BlockSpec((rows, width), lambda j: (0, 0))
    weight_args, weight_specs = ffn_operands(weights, shard, width, tiles, lambda j: j)
    return pl.pallas_call(
        ffn_out_body,
        grid=(tiles,),
        in_specs=[whole, pl.BlockSpec((rows, tile), lambda j: (0, j)), weight_specs[2]],
        out_specs=whole,
        out_shape=jax.ShapeDtypeStruct((rows, width), jnp.bfloat16),
        scratch_shapes=[pltpu.VMEM((rows, width), jnp.float32), pltpu.VMEM((tile, width), jnp.bfloat16)],
        compiler_params=pltpu.CompilerParams(vmem_limit_bytes=16 * 1024 * 1024),
        cost_estimate=SMALL,
        name="ffn_out",
    )(*from_far(residual, hidden, weight_args[2]))


def end_body(first_kept, first_came, second_kept, second_came, query_ref, key_ref, value_ref, *gain_refs):
    def part(kept, came, start, size):
        columns = slice(start, start + size)
        return kept[:, columns].astype(jnp.float32) + came[:, columns].astype(jnp.float32)

    group = 0
    for kept, came in ((first_kept, first_came), (second_kept, second_came)):
        for start in range(0, KEY_VALUE_HEADS // 2 * GROUP, GROUP):
            for ref, size in ((query_ref, 2 * HEAD_SIZE), (key_ref, HEAD_SIZE), (value_ref, HEAD_SIZE)):
                ref[:, group * size : (group + 1) * size] = part(kept, came, start, size)
                start += size
            group += 1
    gains = part(second_kept, second_came, KEY_VALUE_HEADS // 2 * GROUP, 128).T
    for index, ref in enumerate(gain_refs):
        ref[...] = gains[index : index + 1, : ref.shape[1]]


def end_projections(first, second, head_shard):
    rows = first[0].shape[0]
    query_width, key_width = QUERY_HEADS * HEAD_SIZE, KEY_VALUE_HEADS * HEAD_SIZE
    return pl.pallas_call(
        end_body,
        out_shape=[
            jax.ShapeDtypeStruct(shape, jnp.float32)
            for shape in (
                (rows, query_width), (rows, key_width), (rows, key_width), (1, rows), (1, rows), (1, head_shard),
                (1, head_shard),
            )
        ],
        cost_estimate=SMALL,
        name="end_projections",
    )(*first, *second)


def on_device(
    tokens,
    seq_lengths,
    seq_owner,
    g_attn,
    w_query,
    key_projection,
    value_projection,
    query_norm_gain,
    g_key,
    w_out,
    g_ffn,
    w_gate,
    w_up,
    w_down,
    cotangent,
):
    row_total_count = tokens.shape[0]
    fence = lax.optimization_barrier
    count = lax.axis_size("fsdp")
    device = lax.axis_index("fsdp")
    early = middle_bits(count, False)
    late = middle_bits(count, True)
    cut_bits = len(early) // 2
    shard = g_attn.shape[0]
    head_shard = query_norm_gain.shape[0]

    pieces = w_down.shape[0] // shard
    down_pieces = w_down.reshape(pieces, shard, -1).transpose(1, 0, 2).reshape(shard, -1)
    ffn_weights = lax.all_gather(jnp.concatenate([w_gate, w_up, down_pieces], axis=0), "fsdp", axis=0, tiled=False)
    projections = join(
        w_query, key_projection, value_projection, gain_columns(g_attn, g_ffn, query_norm_gain, g_key, shard)
    )
    top = gather_top(projections, count)
    top, w_out = fence((top, w_out))
    top = gather_top_rest(top, count)
    top, w_out = fence((top, w_out))
    first_part, second_part = lay_top_split(top, device, count, KEY_VALUE_HEADS // 2 * GROUP + 128)
    first_parts = gather_bits({0: first_part}, count, early[:cut_bits])
    second_parts = gather_bits({0: second_part}, count, late[:cut_bits])
    out_top = gather_top(w_out, count)
    first_parts, second_parts, out_top = fence((first_parts, second_parts, out_top))
    first_parts = gather_bits(first_parts, count, early[cut_bits:])
    second_parts = gather_bits(second_parts, count, late[cut_bits:])
    out_top = gather_top_rest(out_top, count)
    first_parts, second_parts, out_top = fence((first_parts, second_parts, out_top))
    first_parts = gather_bits(first_parts, count, [0])
    out_parts = gather_bits(lay_top(out_top, device, count), count, early[:cut_bits])
    first_parts, second_parts = fence((first_parts, second_parts))
    second_parts = gather_bits(second_parts, count, [0])
    first_gains = lay({mask: part[..., -128:] for mask, part in first_parts.items()}, device, count)
    first_weight = weight_parts(first_parts, device, count)

    seq_id, token_position = layout(seq_lengths, seq_owner, device, row_total_count)
    first_row = (jnp.arange(row_total_count, dtype=jnp.int32) - token_position)[:, None]
    cosine, sine = rotation_factors(token_position)
    inputs = tokens.astype(jnp.float32)
    gain_block = first_gains.astype(jnp.float32)
    head_gains = gain_block.reshape(count, shard, 128)[:, :head_shard, 2:4].reshape(HEAD_SIZE, 2).T
    gain_one = gain_block[:, 0]
    gain_two = gain_block[:, 1]
    normed_low = norm_forward(inputs, gain_one)[0].astype(jnp.bfloat16)
    attended_first, *saved_first = attend(device, normed_low, first_weight, head_gains, cosine, sine, first_row)
    attended_first, second_parts, out_parts = fence((attended_first, second_parts, out_parts))
    out_parts = gather_bits(out_parts, count, early[cut_bits:])
    second_weight = weight_parts(second_parts, device, count)
    attended_second, *saved_second = attend(device, normed_low, second_weight, head_gains, cosine, sine, first_row)
    stages = sum_bits(count)
    orders = {name: row_order(count, bits) for name, bits in stages.items()}
    attended_first, attended_second, out_parts = fence((attended_first, attended_second, out_parts))
    out_parts = gather_bits(out_parts, count, [0])
    residual, out_weight = project(
        device,
        [out_parts[mask] for mask in range(count // 4)],
        tokens,
        jnp.concatenate([attended_first, attended_second], axis=1),
    )
    (
        hidden, grad_gate, grad_up, gate_kept, gate_sent, up_kept, up_sent, down_kept, down_sent
    ) = feed_forward(
        device, residual, gain_two[None], cotangent, ffn_weights, shard, orders["gate"], orders["up"]
    )

    live = dict(
        hidden=hidden, grad_gate=grad_gate, grad_up=grad_up, gate=gate_kept, up=up_kept, down=down_kept,
    )
    flying = {}

    def cut():
        live.update(fence(dict(live)))

    def fly(**sent):
        live.update({name + "_sent": value for name, value in sent.items()})
        cut()
        for name in sent:
            flying[name] = exchange(live.pop(name + "_sent"), count, 1 << stages[name].pop(0))

    def land(*names):
        live.update({name + "_came": flying.pop(name) for name in names})
        cut()

    def halve(*names):
        halves = fold(*[(live[name], live.pop(name + "_came")) for name in names])
        live.update({name: kept for name, (kept, _) in zip(names, halves)})
        fly(**{name: sent for name, (_, sent) in zip(names, halves)})

    def pass_on(*names):
        land(*names)
        halve(*names)

    def end(*names):
        land(*names)
        return [(live.pop(name), live.pop(name + "_came")) for name in names]

    def operands(name, saved):
        return *from_far(out_weight, *saved), head_gains, cosine, sine, first_row, *from_far(turned[name])

    live.update(attended_first=attended_first, attended_second=attended_second, normed=normed_low)
    fly(down=down_sent, gate=gate_sent, up=up_sent)
    live["turned"] = dict(
        out=turn((live.pop("attended_first"), live.pop("attended_second")), device, orders["out"]),
        first=turn((live["normed"],), device, orders["first"]),
        second=turn((live.pop("normed"),), device, orders["second"]),
    )
    pass_on("down")
    pass_on("gate")
    pass_on("up")
    turned = live.pop("turned")
    (
        live["grad_residual"], live["low"], live["grad_gain_two"], live["out"], live["out_sent"], live["first"],
        live["first_sent"], live["head_sums"], live["normed_sum"],
    ) = back(
        device, residual, gain_two[None], cotangent, live.pop("grad_gate"), live.pop("grad_up"), ffn_weights, shard,
        turned["out"], operands("first", saved_first), first_weight,
    )
    land("down", "gate", "up")
    fly(first=live["first_sent"], out=live["out_sent"])
    halve("down", "gate", "up")
    pass_on("first", "out")
    live["second"], live["second_sent"], live["grad_tokens"] = attend_back_last(
        device, live.pop("low"), operands("second", saved_second), second_weight, (live.pop("head_sums"), live.pop("normed_sum")), tokens,
        gain_one[None], live.pop("grad_residual"), live.pop("grad_gain_two"), orders["second"], shard, head_shard,
    )
    land("down", "gate", "up")
    land("first", "out")
    fly(second=live["second_sent"])
    halve("down", "gate", "up")
    pass_on("second")
    halve("first", "out")
    live["mixed"] = ffn_out(residual, live.pop("hidden"), ffn_weights, shard)
    cut()
    mixed, grad_tokens = live.pop("mixed"), live.pop("grad_tokens")
    while stages["down"]:
        pass_on("down", "gate", "up")
        pass_on("first", "out")
        pass_on("second")
    sums = {name: sum_end(pair) for name, pair in zip(("down", "gate", "up"), end("down", "gate", "up"))}
    live.update(sums)
    while stages["out"]:
        pass_on("first", "out", "second")
    sum_down, sum_gate, sum_up = live.pop("down"), live.pop("gate"), live.pop("up")
    first, out = end("first", "out")
    pass_on_last = stages["second"]
    while pass_on_last:
        pass_on("second")
    (second,) = end("second")
    sum_out = sum_end(out)
    sum_query, sum_key, sum_value, *sum_gains = end_projections(first, second, head_shard)
    return (
        mixed,
        grad_tokens,
        sum_gains[0].reshape(-1),
        sum_query,
        sum_key,
        sum_value,
        sum_gains[2].reshape(-1),
        sum_gains[3].reshape(-1),
        sum_out,
        sum_gains[1].reshape(-1),
        sum_gate,
        sum_up,
        sum_down,
    )


def solution(mesh):
    return jax.shard_map(
        on_device,
        mesh=mesh,
        in_specs=(
            P("fsdp", None),
            P(),
            P(),
            P("fsdp"),
            P("fsdp", None),
            P("fsdp", None),
            P("fsdp", None),
            P("fsdp"),
            P("fsdp"),
            P("fsdp", None),
            P("fsdp"),
            P("fsdp", None),
            P("fsdp", None),
            P("fsdp", None),
            P("fsdp", None),
        ),
        out_specs=(
            P("fsdp", None),
            P("fsdp", None),
            P("fsdp"),
            P("fsdp", None),
            P("fsdp", None),
            P("fsdp", None),
            P("fsdp"),
            P("fsdp"),
            P("fsdp", None),
            P("fsdp"),
            P("fsdp", None),
            P("fsdp", None),
            P("fsdp", None),
        ),
        check_vma=False,
    )
```

```python
import functools
import math

import jax
import jax.numpy as jnp
from jax import lax
from jax.experimental import pallas as pl
from jax.experimental.pallas import tpu as pltpu
from jax.sharding import PartitionSpec as P

QUERY_HEADS = 16
KEY_VALUE_HEADS = 8
HEAD_SIZE = 128


SMALL = pl.CostEstimate(flops=1, bytes_accessed=1, transcendentals=0)


def far(shape, dtype):
    return pltpu.HBM(tuple(shape), dtype)


def from_far(*values):
    return [pltpu.with_memory_space_constraint(value, pltpu.HBM) for value in values]


epsilon = 1e-06
rope_base = 1000000.0


def layout(seq_lengths, seq_owner, device, row_total_count):
    seq_index = jnp.arange(seq_lengths.shape[0], dtype=jnp.int32)
    same_owner = seq_owner[:, None] == seq_owner[None, :]
    before = seq_index[None, :] < seq_index[:, None]
    starts = jnp.sum(jnp.where(same_owner & before, seq_lengths[None, :], 0), axis=1)
    places = jnp.arange(row_total_count, dtype=jnp.int32)
    member = (
        (seq_owner[None, :] == device)
        & (starts[None, :] <= places[:, None])
        & (places[:, None] < (starts + seq_lengths)[None, :])
    )
    seq_id = jnp.sum(jnp.where(member, seq_index[None, :], 0), axis=1)
    token_position = jnp.sum(jnp.where(member, places[:, None] - starts[None, :], 0), axis=1)
    return (seq_id, token_position)


def rotation_factors(token_position):
    half_width = HEAD_SIZE // 2
    frequency = jnp.exp(
        jnp.arange(half_width, dtype=jnp.float32) * (-2.0 * math.log(rope_base) / HEAD_SIZE)
    )
    angles = token_position.astype(jnp.float32)[:, None] * frequency[None, :]
    cosine = jnp.cos(angles)
    sine = jnp.sin(angles)
    return jnp.concatenate([cosine, cosine], axis=1), jnp.concatenate([-sine, sine], axis=1)


def norm_forward(values, gain):
    inverse = lax.rsqrt(jnp.mean(values * values, axis=-1, keepdims=True) + epsilon)
    unit_rows = values * inverse
    return (unit_rows * gain, unit_rows, inverse)


def exchange(values, count, mask):
    return lax.ppermute(values, "fsdp", [(source, source ^ mask) for source in range(count)])


def middle_bits(count, flip):
    bits = list(range(1, count.bit_length() - 3))
    return bits[::-1] if flip else bits


def sum_bits(count):
    bits = count.bit_length() - 1
    middle = list(range(1, bits - 2))
    low, high = bits - 2, bits - 1
    return dict(
        down=[0, middle[-1], high, low] + middle[-2::-1],
        gate=[0] + middle + [low, high],
        up=[0, low, middle[-1], high] + middle[-2::-1],
        out=[0] + middle + [low, high],
        first=[0, low] + middle[::-1] + [high],
        second=[0] + middle + [low, high],
    )


def row_order(count, sequence):
    bits = len(sequence)
    return [
        sum(((index >> (bits - 1 - step)) & 1) << bit for step, bit in enumerate(sequence)) for index in range(count)
    ]


def turn_body(device_ref, *refs, order):
    values, (out_ref, turned_ref) = refs[:-2], refs[-2:]
    start = 0
    for ref in values:
        turned_ref[start : start + ref.shape[1], :] = ref[...].astype(turned_ref.dtype).T
        start += ref.shape[1]
    device = device_ref[0]
    rows = out_ref.shape[0] // len(order)
    group = max(1, 16 // rows)
    for first in range(0, len(order), group):
        blocks = [
            turned_ref[pl.ds(pl.multiple_of((device ^ mask) * rows, rows), rows), :]
            for mask in order[first : first + group]
        ]
        block = blocks[0] if group == 1 else jnp.concatenate(blocks, axis=0)
        out_ref[first * rows : (first + group) * rows, :] = block.astype(out_ref.dtype)


def turn(values, device, order):
    count = len(order)
    rows = values[0].shape[0]
    columns = sum(value.shape[1] for value in values)
    held = jnp.bfloat16 if columns // count % 16 == 0 else jnp.float32
    return pl.pallas_call(
        functools.partial(turn_body, order=order),
        grid_spec=pltpu.PrefetchScalarGridSpec(
            num_scalar_prefetch=1,
            grid=(1,),
            in_specs=[pl.BlockSpec(value.shape, lambda i, d: (0, 0)) for value in values],
            out_specs=pl.BlockSpec((columns, rows), lambda i, d: (0, 0)),
            scratch_shapes=[pltpu.VMEM((columns, rows), held)],
        ),
        out_shape=far((columns, rows), values[0].dtype),
        compiler_params=pltpu.CompilerParams(vmem_limit_bytes=16 * 1024 * 1024),
        cost_estimate=SMALL,
        name="turn",
    )(device.reshape(1), *values)


def fold_body(*refs, pairs, merged):
    def add(first, second):
        return (first[...].astype(jnp.float32) + second[...].astype(jnp.float32)).astype(jnp.bfloat16)

    out_refs = refs[4 * pairs :]
    start = 0
    for index in range(pairs):
        kept_first, kept_second, came_first, came_second = refs[4 * index : 4 * index + 4]
        sent = add(kept_second, came_second)
        if merged:
            out_refs[pairs][:, start : start + sent.shape[1]] = sent
            start += sent.shape[1]
        else:
            out_refs[pairs + index][...] = sent
        out_refs[index][...] = add(kept_first, came_first)


def fold(*pairs, merged=False):
    halves = [kept.shape[0] // 2 for kept, *_ in pairs]
    steps = next(n for n in (4, 2, 1) if n == 1 or all(rows % (16 * n) == 0 for rows in halves))
    in_specs, out_specs, out_shape, operands = [], [], [], []
    for rows, (kept, came, place) in zip(halves, pairs):
        columns = kept.shape[1]
        spec = lambda shift, place=0, rows=rows, columns=columns: pl.BlockSpec(
            (rows // steps, columns), lambda i: (i + shift, place)
        )
        in_specs += [spec(0), spec(steps), spec(0, place), spec(steps, place)]
        operands += [kept, kept, came, came]
        out_specs += [spec(0)]
        out_shape += [jax.ShapeDtypeStruct((rows, columns), jnp.bfloat16)]
    if merged:
        columns = sum(kept.shape[1] for kept, *_ in pairs)
        sent_specs = [pl.BlockSpec((halves[0] // steps, columns), lambda i: (i, 0))]
        sent_shape = [jax.ShapeDtypeStruct((halves[0], columns), jnp.bfloat16)]
    else:
        sent_specs, sent_shape = list(out_specs), list(out_shape)
    block_bytes = sum(6 * 2 * (rows // steps) * kept.shape[1] for rows, (kept, *_) in zip(halves, pairs))
    return pl.pallas_call(
        functools.partial(fold_body, pairs=len(pairs), merged=merged),
        grid=(steps,),
        in_specs=in_specs,
        out_specs=out_specs + sent_specs,
        out_shape=out_shape + sent_shape,
        compiler_params=pltpu.CompilerParams(vmem_limit_bytes=2 * block_bytes + 6 * 1024 * 1024),
        cost_estimate=SMALL,
        name="fold",
    )(*operands)


def sum_end(pair):
    return pair[0].astype(jnp.float32) + pair[1].astype(jnp.float32)


def place_body(device_ref, *refs):
    parts = refs[:-2]
    out_ref, semaphores = refs[-2:]
    device = device_ref[0]
    copies = [
        pltpu.make_async_copy(part, out_ref.at[:, device ^ mask], semaphores.at[mask])
        for mask, part in enumerate(parts)
    ]
    for copy in copies:
        copy.start()
    for copy in copies:
        copy.wait()


def place(parts, inner):
    top, rows, columns = parts[0].shape
    return pl.pallas_call(
        place_body,
        grid_spec=pltpu.PrefetchScalarGridSpec(
            num_scalar_prefetch=1,
            grid=(1,),
            in_specs=[pl.BlockSpec(memory_space=pl.ANY)] * len(parts),
            out_specs=pl.BlockSpec((top, len(parts), rows, columns), lambda i, d: (0, 0, 0, 0)),
            scratch_shapes=[pltpu.SemaphoreType.DMA((len(parts),))],
        ),
        out_shape=far((top, len(parts), rows, columns), parts[0].dtype)
        if top > 1
        else jax.ShapeDtypeStruct((top, len(parts), rows, columns), parts[0].dtype),
        compiler_params=pltpu.CompilerParams(vmem_limit_bytes=14 * 1024 * 1024),
        cost_estimate=SMALL,
        name="place",
    )(inner.reshape(1), *parts).reshape(top * len(parts) * rows, columns)


def gather_top(block, count):
    return [block, exchange(block, count, count // 4), exchange(block, count, count // 2)]


def gather_top_rest(blocks, count):
    return [block[None] for block in blocks + [exchange(blocks[2], count, count // 4)]]


def stack_body(gate_ref, up_ref, down_ref, out_ref):
    rows = gate_ref.shape[0]
    width = down_ref.shape[1]
    out_ref[:rows, :] = gate_ref[...]
    out_ref[rows : 2 * rows, :] = up_ref[...]
    for piece in range(down_ref.shape[0] // rows):
        columns = slice(piece * width, (piece + 1) * width)
        out_ref[2 * rows :, columns] = down_ref[piece * rows : (piece + 1) * rows, :]


def stack(w_gate, w_up, w_down):
    rows, columns = w_gate.shape
    pieces = w_down.shape[0] // rows
    if rows % 16:
        down = w_down.reshape(pieces, rows, -1).transpose(1, 0, 2).reshape(rows, -1)
        return jnp.concatenate([w_gate, w_up, down], axis=0)
    return pl.pallas_call(
        stack_body,
        out_shape=jax.ShapeDtypeStruct((3 * rows, columns), w_gate.dtype),
        cost_estimate=SMALL,
        name="stack",
    )(w_gate, w_up, w_down)


def join_body(query_ref, key_ref, value_ref, gains_ref, out_ref):
    groups = KEY_VALUE_HEADS
    pair = query_ref.shape[1] // groups
    one = key_ref.shape[1] // groups
    shift = 0
    for group in range(groups):
        for ref, size in ((query_ref, pair), (key_ref, one), (value_ref, one)):
            out_ref[:, shift : shift + size] = ref[:, group * size : (group + 1) * size]
            shift += size
        if group == groups // 2 - 1:
            out_ref[:, shift : shift + 128] = gains_ref[...]
            shift += 128


def join(w_query, key_projection, value_projection, gains):
    rows = w_query.shape[0]
    columns = w_query.shape[1] + 2 * key_projection.shape[1] + 128
    return pl.pallas_call(
        join_body,
        out_shape=jax.ShapeDtypeStruct((rows, columns), w_query.dtype),
        cost_estimate=SMALL,
        name="join",
    )(w_query, key_projection, value_projection, gains)


def lay_top(blocks, device, count):
    return {0: place(from_far(*blocks), device // (count // 4)).reshape((4,) + blocks[0].shape[1:])}


def split_body(device_ref, *refs):
    parts = refs[:4]
    left_ref, right_ref, semaphores = refs[4:]
    width = left_ref.shape[-1]
    copies = []
    for mask, part in enumerate(parts):
        target = device_ref[0] ^ mask
        copies += [
            pltpu.make_async_copy(part.at[:, :width], left_ref.at[target], semaphores.at[2 * mask]),
            pltpu.make_async_copy(part.at[:, width:], right_ref.at[target], semaphores.at[2 * mask + 1]),
        ]
    for copy in copies:
        copy.start()
    for copy in copies:
        copy.wait()


def lay_top_split(blocks, device, count, width):
    rows, columns = blocks[0].shape[1:]
    shapes = [(4, rows, width), (4, rows, columns - width)]
    return pl.pallas_call(
        split_body,
        grid_spec=pltpu.PrefetchScalarGridSpec(
            num_scalar_prefetch=1,
            grid=(1,),
            in_specs=[pl.BlockSpec(memory_space=pl.ANY)] * 4,
            out_specs=[pl.BlockSpec(shape, lambda i, d: (0, 0, 0)) for shape in shapes],
            scratch_shapes=[pltpu.SemaphoreType.DMA((8,))],
        ),
        out_shape=[jax.ShapeDtypeStruct(shape, blocks[0].dtype) for shape in shapes],
        compiler_params=pltpu.CompilerParams(vmem_limit_bytes=10 * 1024 * 1024),
        cost_estimate=SMALL,
        name="lay_top_split",
    )((device // (count // 4)).reshape(1), *from_far(*[block[0] for block in blocks]))


def gather_bits(parts, count, bits):
    parts = dict(parts)
    for bit in bits:
        for mask in list(parts):
            parts[mask | (1 << bit)] = exchange(parts[mask], count, 1 << bit)
    return parts


def lay(parts, device, count):
    return place([parts[mask] for mask in range(count // 4)], device & (count // 4 - 1))


def gain_columns(first, second, third, fourth, rows):
    columns = [jnp.pad(v, (0, rows - v.shape[0]))[:, None] for v in (first, second, third, fourth)]
    return jnp.pad(jnp.concatenate(columns, axis=1), ((0, 0), (0, 124)))


def swap_halves(head):
    return pltpu.roll(head, HEAD_SIZE // 2, 1)


def unit_head(raw):
    inverse = lax.rsqrt(jnp.mean(raw * raw, axis=-1, keepdims=True) + epsilon)
    return raw * inverse, inverse


def contract(left, right, left_axis, right_axis):
    return lax.dot_general(
        left, right, (((left_axis,), (right_axis,)), ((), ())), preferred_element_type=jnp.float32
    )


def block_scores(group, key_rows, first_row, row_start):
    scores = contract(group, key_rows, 1, 1) * (1.0 / math.sqrt(HEAD_SIZE))
    rows = lax.broadcasted_iota(jnp.int32, scores.shape, 0)
    half = scores.shape[0] // 2
    rows = jnp.where(rows >= half, rows - half, rows) + row_start
    columns = lax.broadcasted_iota(jnp.int32, scores.shape, 1)
    return jnp.where((columns <= rows) & (columns >= first_row), scores, -1e30)


def head_pair(ref, block):
    return jnp.concatenate([ref[block, :HEAD_SIZE], ref[block, HEAD_SIZE:]], axis=0)


def pair_rows(first_row_ref, block):
    rows = first_row_ref[block, :]
    return jnp.concatenate([rows, rows], axis=0)


GROUP = 4 * HEAD_SIZE


def weight_parts(parts, device, count):
    if parts[0].shape[1] % 16 == 0:
        return [parts[mask] for mask in range(count // 4)]
    weight = lay(parts, device, count)
    return [weight[None]]


def part_specs(parts, index):
    top, rows, _ = parts[0].shape
    return [pl.BlockSpec((top, rows, GROUP), lambda *j: (0, 0, index(*j))) for _ in parts]


def join_parts(device_ref, part_refs, weight_ref):
    inner = device_ref[0] & (len(part_refs) - 1)
    for mask, ref in enumerate(part_refs):
        weight_ref[:, inner ^ mask] = ref[...]
    top, count, rows, columns = weight_ref.shape
    return weight_ref[...].reshape(top * count * rows, columns)


def attend_body(device_ref, *refs):
    (*part_refs, normed_ref, gains_ref, cosine_ref, sine_ref, first_ref), out_refs = refs[:-7], refs[-7:]
    attended_ref, query_ref, key_ref, value_ref, raw_ref, total_ref, weight_ref = out_refs
    cosine = cosine_ref[...]
    sine = sine_ref[...]

    def turned(raw, gain):
        scaled = unit_head(raw)[0] * gain
        return (scaled * cosine + swap_halves(scaled) * sine).astype(jnp.bfloat16)

    weight = join_parts(device_ref, part_refs, weight_ref)
    raw = jnp.dot(normed_ref[...], weight, preferred_element_type=jnp.float32)
    raw_ref[...] = raw[:, : 3 * HEAD_SIZE]
    for head in range(2):
        part = slice(head * HEAD_SIZE, (head + 1) * HEAD_SIZE)
        query_ref[:, part] = turned(raw[:, part], gains_ref[0:1, :])
    key_ref[...] = turned(raw[:, 2 * HEAD_SIZE : 3 * HEAD_SIZE], gains_ref[1:2, :])
    value_ref[...] = raw[:, 3 * HEAD_SIZE :].astype(jnp.bfloat16)
    step = 128
    for start in range(0, raw.shape[0], step):
        block = slice(start, start + step)
        seen = slice(0, start + step)
        scores = block_scores(head_pair(query_ref, block), key_ref[seen, :], pair_rows(first_ref, block), start)
        top = jnp.max(scores, axis=-1, keepdims=True)
        log_total = top + jnp.log(jnp.sum(jnp.exp(scores - top), axis=-1, keepdims=True))
        probs_low = jnp.exp(scores - log_total).astype(jnp.bfloat16)
        out = jnp.dot(probs_low, value_ref[seen, :], preferred_element_type=jnp.float32).astype(jnp.bfloat16)
        attended_ref[block, :HEAD_SIZE] = out[:step]
        attended_ref[block, HEAD_SIZE:] = out[step:]
        total_ref[0, block, 0:1] = log_total[:step]
        total_ref[0, block, 1:2] = log_total[step:]


def attend(device, normed, parts, head_gains, cosine, sine, first_row):
    rows, width = normed.shape
    groups = KEY_VALUE_HEADS // 2
    whole = lambda *shape: pl.BlockSpec(shape, lambda h, d: (0, 0))
    columns = lambda size: pl.BlockSpec((rows, size), lambda h, d: (0, h))
    low = lambda size: far((rows, groups * size), jnp.bfloat16)
    pair = 2 * HEAD_SIZE
    return pl.pallas_call(
        attend_body,
        grid_spec=pltpu.PrefetchScalarGridSpec(
            num_scalar_prefetch=1,
            grid=(groups,),
            in_specs=part_specs(parts, lambda h, d: h)
            + [
                whole(rows, width),
                whole(2, HEAD_SIZE),
                whole(rows, HEAD_SIZE),
                whole(rows, HEAD_SIZE),
                whole(rows, 1),
            ],
            out_specs=[
                columns(pair),
                columns(pair),
                columns(HEAD_SIZE),
                columns(HEAD_SIZE),
                columns(3 * HEAD_SIZE),
                pl.BlockSpec((1, rows, 2), lambda h, d: (h, 0, 0)),
            ],
            scratch_shapes=[pltpu.VMEM((parts[0].shape[0], len(parts), parts[0].shape[1], GROUP), jnp.bfloat16)],
        ),
        out_shape=[
            jax.ShapeDtypeStruct((rows, groups * pair), jnp.bfloat16),
            low(pair),
            low(HEAD_SIZE),
            low(HEAD_SIZE),
            far((rows, groups * 3 * HEAD_SIZE), jnp.float32),
            far((groups, rows, 2), jnp.float32),
        ],
        compiler_params=pltpu.CompilerParams(vmem_limit_bytes=26 * 1024 * 1024),
        cost_estimate=SMALL,
        name="attend",
    )(device.reshape(1), *parts, normed, head_gains, cosine, sine, first_row)


def attend_back_body(
    device_ref, residual_ref, wo_ref, query_ref, key_ref, value_ref, raw_ref, total_ref,
    gains_ref, cosine_ref, sine_ref, first_ref, turned_ref, *refs,
    order, shard, head_shard, last, parts, head=None,
):
    part_refs, refs = refs[:parts], refs[parts:]
    if last:
        head_gains_in_ref, normed_in_ref = refs[:2]
        refs = refs[2:]
        tokens_ref, gain_ref, grad_residual_ref, gain_two_ref, hidden_ref, down_ref, ffn_in_ref = refs[:7]
        kept_ref, sent_ref, tokens_out_ref, mixed_ref = refs[7:11]
        head_gains_ref, normed_sum_ref, lines_ref, mixed_sum_ref, down_weight_ref = refs[11:16]
        scratch = refs[16:]
    else:
        kept_ref, sent_ref, head_gains_ref, normed_sum_ref = refs[:4]
        scratch = refs[4:]
    grad_out_ref, query_sum_ref, key_sum_ref, value_sum_ref, grads_ref, weight_ref = scratch
    scale = 1.0 / math.sqrt(HEAD_SIZE)
    heads = KEY_VALUE_HEADS // 2
    if head is None:
        head = pl.program_id(0)

    @pl.when(head == 0)
    def _():
        head_gains_ref[...] = head_gains_in_ref[...] if last else jnp.zeros_like(head_gains_ref)
        normed_sum_ref[...] = normed_in_ref[...] if last else jnp.zeros_like(normed_sum_ref)

    if last:
        gather_down(down_ref, down_weight_ref, down_weight_ref.shape[1])

        @pl.when(head == 0)
        def _():
            mixed_sum_ref[...] = ffn_in_ref[...]

        mixed_sum_ref[...] += jnp.dot(hidden_ref[...], down_weight_ref[...], preferred_element_type=jnp.float32)

        @pl.when(head == heads - 1)
        def _():
            mixed_ref[...] = mixed_sum_ref[...].astype(jnp.bfloat16)

    grad_out_ref[...] = contract(residual_ref[...], wo_ref[...], 1, 1).astype(jnp.bfloat16)
    key_sum_ref[...] = jnp.zeros_like(key_sum_ref)
    value_sum_ref[...] = jnp.zeros_like(value_sum_ref)
    step = 128
    for start in range(0, residual_ref.shape[0], step):
        block = slice(start, start + step)
        seen = slice(0, start + step)
        group = head_pair(query_ref, block)
        grad_out = head_pair(grad_out_ref, block)
        key_rows = key_ref[seen, :]
        scores = block_scores(group, key_rows, pair_rows(first_ref, block), start)
        log_total = jnp.concatenate([total_ref[0, block, 0:1], total_ref[0, block, 1:2]], axis=0)
        probs = jnp.exp(scores - log_total)
        grad_probs = contract(grad_out, value_ref[seen, :], 1, 1)
        value_sum_ref[seen, :] += contract(probs.astype(jnp.bfloat16), grad_out, 0, 0)
        inner = jnp.sum(probs * grad_probs, axis=-1, keepdims=True)
        grad_scores = (probs * (grad_probs - inner)).astype(jnp.bfloat16)
        grad_group = jnp.dot(grad_scores, key_rows, preferred_element_type=jnp.float32) * scale
        query_sum_ref[block, :HEAD_SIZE] = grad_group[:step]
        query_sum_ref[block, HEAD_SIZE:] = grad_group[step:]
        key_sum_ref[seen, :] += contract(grad_scores, group, 0, 0)
    grads_ref[:, 3 * HEAD_SIZE :] = value_sum_ref[...].astype(jnp.bfloat16)
    cosine = cosine_ref[...]
    sine = sine_ref[...]

    def back(grad, part, gain):
        turned = grad * cosine - swap_halves(grad) * sine
        unit, inverse = unit_head(raw_ref[:, part])
        product = turned * unit
        scaled = turned * gain
        grad_raw = inverse * (scaled - unit * jnp.mean(product * gain, axis=-1, keepdims=True))
        grads_ref[:, part] = grad_raw.astype(jnp.bfloat16)
        return jnp.sum(product, axis=0, keepdims=True)

    for index in range(2):
        part = slice(index * HEAD_SIZE, (index + 1) * HEAD_SIZE)
        head_gains_ref[0:1, :] += back(query_sum_ref[:, part], part, gains_ref[0:1, :])
    part = slice(2 * HEAD_SIZE, 3 * HEAD_SIZE)
    head_gains_ref[1:2, :] += back(key_sum_ref[...] * scale, part, gains_ref[1:2, :])

    grads = grads_ref[...]
    half = turned_ref.shape[0] // 2
    product = jnp.dot(turned_ref[...], grads, preferred_element_type=jnp.float32).astype(jnp.bfloat16)
    columns = pl.ds(pl.multiple_of(head * GROUP, GROUP), GROUP)
    kept_ref[:, columns] = product[:half]
    sent_ref[:, columns] = product[half:]
    normed_sum_ref[...] += contract(grads, join_parts(device_ref, part_refs, weight_ref), 1, 1)

    if not last:
        return

    @pl.when(head == heads - 1)
    def _():
        unit, inverse = unit_head(tokens_ref[...].astype(jnp.float32))
        grad = normed_sum_ref[...]
        scaled = grad * gain_ref[...]
        grad_first = inverse * (scaled - unit * jnp.mean(scaled * unit, axis=-1, keepdims=True))
        tokens_out_ref[...] = (grad_residual_ref[...] + grad_first).astype(jnp.bfloat16)
        width = grad.shape[1]
        source = lax.broadcasted_iota(jnp.int32, (HEAD_SIZE, width), 0)
        target = lax.broadcasted_iota(jnp.int32, (HEAD_SIZE, width), 1)
        spread = jnp.where(source // head_shard * shard + source % head_shard == target, 1.0, 0.0)
        heads = jnp.dot(
            head_gains_ref[...], spread, precision=lax.Precision.HIGHEST, preferred_element_type=jnp.float32
        )
        lines = jnp.concatenate(
            [
                jnp.sum(grad * unit, axis=0, keepdims=True),
                gain_two_ref[...],
                heads,
                jnp.zeros((124, width), jnp.float32),
            ],
            axis=0,
        )
        lines_ref[...] = lines.T
        device = device_ref[0]
        group = max(1, 16 // shard)
        end = slice(kept_ref.shape[1] - 128, None)
        for first in range(0, len(order), group):
            blocks = [
                lines_ref[pl.ds(pl.multiple_of((device ^ mask) * shard, shard), shard), :]
                for mask in order[first : first + group]
            ]
            block = (blocks[0] if group == 1 else jnp.concatenate(blocks, axis=0)).astype(jnp.bfloat16)
            row = first * shard
            target_ref = kept_ref if row < half else sent_ref
            target_ref[row % half : row % half + group * shard, end] = block


def attend_back_specs(rows, width, part, head, parts):
    first = part * KEY_VALUE_HEADS // 2
    whole = lambda *shape: pl.BlockSpec(shape, lambda *j: (0, 0))
    columns = lambda height, size: pl.BlockSpec((height, size), lambda *j: (0, head(*j)))
    pair = 2 * HEAD_SIZE
    return [
        pl.BlockSpec((pair, width), lambda *j: (head(*j) + first, 0)),
        columns(rows, pair),
        columns(rows, HEAD_SIZE),
        columns(rows, HEAD_SIZE),
        columns(rows, 3 * HEAD_SIZE),
        pl.BlockSpec((1, rows, 2), lambda *j: (head(*j), 0, 0)),
        whole(2, HEAD_SIZE),
        whole(rows, HEAD_SIZE),
        whole(rows, HEAD_SIZE),
        whole(rows, 1),
        whole(width, rows),
    ] + part_specs(parts, head)


def attend_back_scratch(rows, parts):
    pair = 2 * HEAD_SIZE
    return [
        pltpu.VMEM((rows, pair), jnp.bfloat16),
        pltpu.VMEM((rows, pair), jnp.float32),
        pltpu.VMEM((rows, HEAD_SIZE), jnp.float32),
        pltpu.VMEM((rows, HEAD_SIZE), jnp.float32),
        pltpu.VMEM((rows, GROUP), jnp.bfloat16),
        pltpu.VMEM((parts[0].shape[0], len(parts), parts[0].shape[1], GROUP), jnp.bfloat16),
    ]


def attend_back_last(
    device, residual_low, operands, parts, sums, tokens, gain, grad_residual, grad_gain_two, ffn_in, hidden, weights,
    order, shard, head_shard,
):
    rows, width = residual_low.shape
    whole = lambda *shape: pl.BlockSpec(shape, lambda *j: (0, 0))
    own_width = KEY_VALUE_HEADS * 2 * HEAD_SIZE + 128
    half = jax.ShapeDtypeStruct((width // 2, own_width), jnp.bfloat16)
    low = jax.ShapeDtypeStruct((rows, width), jnp.bfloat16)
    tiles = KEY_VALUE_HEADS // 2
    tile = weights.shape[2] // tiles
    weight_args, weight_specs = ffn_operands(weights, shard, width, tiles, lambda h, d: h)
    return pl.pallas_call(
        functools.partial(
            attend_back_body, order=order, shard=shard, head_shard=head_shard, last=True, parts=len(parts)
        ),
        grid_spec=pltpu.PrefetchScalarGridSpec(
            num_scalar_prefetch=1,
            grid=(KEY_VALUE_HEADS // 2,),
            in_specs=[whole(rows, width)]
            + attend_back_specs(rows, width, 1, lambda h, d: h, parts)
            + [whole(2, HEAD_SIZE), whole(rows, width)]
            + [whole(rows, width), whole(1, width), whole(rows, width), whole(1, width)]
            + [pl.BlockSpec((rows, tile), lambda h, d: (0, h)), weight_specs[2], whole(rows, width)],
            out_specs=[
                whole(width // 2, own_width), whole(width // 2, own_width), whole(rows, width), whole(rows, width)
            ],
            scratch_shapes=[
                pltpu.VMEM((2, HEAD_SIZE), jnp.float32),
                pltpu.VMEM((rows, width), jnp.float32),
                pltpu.VMEM((width, 128), jnp.float32),
                pltpu.VMEM((rows, width), jnp.float32),
                pltpu.VMEM((tile, width), jnp.bfloat16),
            ]
            + attend_back_scratch(rows, parts),
        ),
        out_shape=[half, half, low, low],
        compiler_params=pltpu.CompilerParams(vmem_limit_bytes=46 * 1024 * 1024),
        cost_estimate=SMALL,
        name="attend_back_last",
    )(
        device.reshape(1), residual_low, *operands, *parts, sums[0], *from_far(sums[1], tokens), gain, *from_far(grad_residual),
        grad_gain_two, *from_far(hidden, weight_args[2], ffn_in),
    )


def project_body(device_ref, *refs):
    (*part_refs, tokens_ref, attended_ref), (residual_ref, weight_out_ref) = refs[:-2], refs[-2:]
    inner = device_ref[0] & (len(part_refs) - 1)

    @pl.when(pl.program_id(0) == 0)
    def _():
        residual_ref[...] = tokens_ref[...].astype(jnp.float32)

    for mask, ref in enumerate(part_refs):
        weight_out_ref[:, inner ^ mask] = ref[...]
    top, count, rows, columns = weight_out_ref.shape
    weight = weight_out_ref[...].reshape(top * count * rows, columns)
    residual_ref[...] += jnp.dot(attended_ref[...], weight, preferred_element_type=jnp.float32)


def project(device, parts, tokens, attended):
    rows, width = tokens.shape
    top, part_rows, _ = parts[0].shape
    step_rows = len(parts) * part_rows
    whole = pl.BlockSpec((rows, width), lambda j, d: (0, 0))
    residual, weight = pl.pallas_call(
        project_body,
        grid_spec=pltpu.PrefetchScalarGridSpec(
            num_scalar_prefetch=1,
            grid=(top,),
            in_specs=[pl.BlockSpec((1, part_rows, width), lambda j, d: (j, 0, 0)) for _ in parts]
            + [whole, pl.BlockSpec((rows, step_rows), lambda j, d: (0, j))],
            out_specs=[whole, pl.BlockSpec((1, len(parts), part_rows, width), lambda j, d: (j, 0, 0, 0))],
        ),
        out_shape=[
            jax.ShapeDtypeStruct((rows, width), jnp.float32),
            far((top, len(parts), part_rows, width), jnp.bfloat16),
        ],
        compiler_params=pltpu.CompilerParams(vmem_limit_bytes=20 * 1024 * 1024),
        cost_estimate=SMALL,
        name="project",
    )(device.reshape(1), *parts, tokens, attended)
    return residual, weight.reshape(top * step_rows, width)


def gather_down(down_ref, down_weight_ref, width):
    devices, rows, _ = down_ref.shape
    pieces = down_ref.shape[2] // width
    for index in range(devices):
        for piece in range(pieces):
            first = (index * pieces + piece) * rows
            down_weight_ref[first : first + rows, :] = down_ref[index, :, piece * width : (piece + 1) * width]


def feed_forward_body(
    device_ref, residual_ref, gain_ref, cotangent_ref, gate_ref, up_ref, down_ref,
    hidden_ref, grad_gate_ref, grad_up_ref, gate_kept_ref, gate_sent_ref, up_kept_ref, up_sent_ref,
    down_kept_ref, down_sent_ref, normed_ref, down_weight_ref, turned_ref, for_gate_ref, for_up_ref, product_ref,
    *, gate_order, up_order,
):
    device = device_ref[0]
    width = residual_ref.shape[1]

    @pl.when(pl.program_id(0) == 0)
    def _():
        unit, _ = unit_head(residual_ref[...])
        normed = (unit * gain_ref[...]).astype(jnp.bfloat16)
        normed_ref[...] = normed
        turned_ref[...] = normed.astype(turned_ref.dtype).T
        rows = width // len(gate_order)
        group = max(1, 16 // rows)
        for order, ref in ((gate_order, for_gate_ref), (up_order, for_up_ref)):
            for first in range(0, len(order), group):
                blocks = [
                    turned_ref[pl.ds(pl.multiple_of((device ^ mask) * rows, rows), rows), :]
                    for mask in order[first : first + group]
                ]
                block = blocks[0] if group == 1 else jnp.concatenate(blocks, axis=0)
                ref[first * rows : (first + group) * rows, :] = block.astype(jnp.bfloat16)

    normed = normed_ref[...]
    gather_down(down_ref, down_weight_ref, width)
    cotangent = cotangent_ref[...]
    gate = jnp.dot(normed, gate_ref[...].reshape(width, gate_ref.shape[-1]), preferred_element_type=jnp.float32)
    up = jnp.dot(normed, up_ref[...].reshape(width, up_ref.shape[-1]), preferred_element_type=jnp.float32)
    grad_hidden = contract(cotangent, down_weight_ref[...], 1, 1)
    sigmoid = jax.nn.sigmoid(gate)
    silu = gate * sigmoid
    hidden = (silu * up).astype(jnp.bfloat16)
    grad_gate = (grad_hidden * up * sigmoid * (1.0 + gate * (1.0 - sigmoid))).astype(jnp.bfloat16)
    hidden_ref[...] = hidden
    grad_gate_ref[...] = grad_gate
    grad_up = (grad_hidden * silu).astype(jnp.bfloat16)
    grad_up_ref[...] = grad_up

    for ordered_ref, grad, kept_ref, sent_ref in (
        (for_gate_ref, grad_gate, gate_kept_ref, gate_sent_ref),
        (for_up_ref, grad_up, up_kept_ref, up_sent_ref),
    ):
        product = jnp.dot(ordered_ref[...], grad, preferred_element_type=jnp.float32).astype(jnp.bfloat16)
        half = product.shape[0] // 2
        kept_ref[...] = product[:half]
        sent_ref[...] = product[half:]
    product_ref[...] = contract(hidden, cotangent, 0, 0).reshape(product_ref.shape)
    owners = product_ref.shape[0]
    low = device & (owners - 1)
    for target, core in ((down_kept_ref, 0), (down_sent_ref, 1)):
        blocks = [product_ref[low ^ (index | core)] for index in range(0, owners, 2)]
        target[...] = jnp.concatenate(blocks, axis=0).astype(jnp.bfloat16).reshape(target.shape)


def ffn_operands(weights, shard, width, tiles, at):
    count, _, hidden_width = weights.shape
    tile = hidden_width // tiles
    if shard % 16 == 0:
        return [weights, weights, weights], [
            pl.BlockSpec((count, shard, tile), lambda *j: (0, 0, at(*j))),
            pl.BlockSpec((count, shard, tile), lambda *j: (0, 1, at(*j))),
            pl.BlockSpec((count // tiles, shard, hidden_width), lambda *j: (at(*j), 2, 0)),
        ]
    gate, up, down = (weights[:, part * shard : (part + 1) * shard] for part in range(3))
    down = down.reshape(count, shard, -1, width).transpose(0, 2, 1, 3).reshape(tiles, tile, width)
    return [gate.reshape(width, hidden_width), up.reshape(width, hidden_width), down], [
        pl.BlockSpec((width, tile), lambda *j: (0, at(*j))),
        pl.BlockSpec((width, tile), lambda *j: (0, at(*j))),
        pl.BlockSpec((1, tile, width), lambda *j: (at(*j), 0, 0)),
    ]


def feed_forward(device, residual, gain, cotangent, weights, shard, gate_order, up_order):
    rows, width = residual.shape
    count, _, hidden_width = weights.shape
    tiles = 4
    tile = hidden_width // tiles
    owners = count // tiles
    at = lambda j, d: j ^ (d[0] // owners)
    whole = pl.BlockSpec((rows, width), lambda j, d: (0, 0))
    row = pl.BlockSpec((1, width), lambda j, d: (0, 0))
    low = lambda height, size: jax.ShapeDtypeStruct((height, size), jnp.bfloat16)
    low4 = jax.ShapeDtypeStruct((2, tiles, tile // 4, width), jnp.bfloat16)
    weight_args, weight_specs = ffn_operands(weights, shard, width, tiles, at)
    columns = lambda height: pl.BlockSpec((height, tile), lambda j, d: (0, at(j, d)))
    down_half = pl.BlockSpec((2, 1, tile // 4, width), lambda j, d: (0, j, 0, 0))
    *out, down_kept, down_sent = pl.pallas_call(
        functools.partial(feed_forward_body, gate_order=gate_order, up_order=up_order),
        grid_spec=pltpu.PrefetchScalarGridSpec(
            num_scalar_prefetch=1,
            grid=(tiles,),
            in_specs=[whole, row, whole] + weight_specs,
            out_specs=[
                columns(rows),
                columns(rows),
                columns(rows),
                columns(width // 2),
                columns(width // 2),
                columns(width // 2),
                columns(width // 2),
                down_half,
                down_half,
            ],
            scratch_shapes=[
                pltpu.VMEM((rows, width), jnp.bfloat16),
                pltpu.VMEM((tile, width), jnp.bfloat16),
                pltpu.VMEM((width, rows), jnp.bfloat16 if shard % 16 == 0 else jnp.float32),
                pltpu.VMEM((width, rows), jnp.bfloat16),
                pltpu.VMEM((width, rows), jnp.bfloat16),
                pltpu.VMEM((owners, tile // owners, width), jnp.float32),
            ],
        ),
        out_shape=[
            far((rows, hidden_width), jnp.bfloat16),
            far((rows, hidden_width), jnp.bfloat16),
            far((rows, hidden_width), jnp.bfloat16),
            low(width // 2, hidden_width),
            low(width // 2, hidden_width),
            low(width // 2, hidden_width),
            low(width // 2, hidden_width),
            low4,
            low4,
        ],
        compiler_params=pltpu.CompilerParams(vmem_limit_bytes=56 * 1024 * 1024),
        cost_estimate=SMALL,
        name="feed_forward",
    )(device.reshape(1), residual, gain, *from_far(cotangent, *weight_args))
    return *out, down_kept.reshape(-1, width), down_sent.reshape(-1, width)


FFN_STEPS = 4


def back_body(device_ref, *refs, parts):
    (
        residual_ref, gain_ref, cotangent_ref, grad_gate_ref, grad_up_ref, gate_ref, up_ref, turned_out_ref
    ), refs = refs[:8], refs[8:]
    operands, refs = refs[: 11 + parts], refs[11 + parts :]
    (
        grad_residual_ref, grad_low_ref, grad_gain_ref, out_kept_ref, out_sent_ref, kept_ref, sent_ref, head_gains_ref,
        normed_sum_ref, back_ref,
    ), scratch = refs[:10], refs[10:]
    step = pl.program_id(0)
    width = residual_ref.shape[1]

    @pl.when(step == 0)
    def _():
        back_ref[...] = jnp.zeros_like(back_ref)

    @pl.when(step < FFN_STEPS)
    def _():
        back_ref[...] += contract(
            grad_gate_ref[...], gate_ref[...].reshape(width, gate_ref.shape[-1]), 1, 1
        ) + contract(grad_up_ref[...], up_ref[...].reshape(width, up_ref.shape[-1]), 1, 1)

    @pl.when(step == FFN_STEPS - 1)
    def _():
        unit, inverse = unit_head(residual_ref[...])
        grad = back_ref[...]
        grad_gain_ref[...] = jnp.sum(grad * unit, axis=0, keepdims=True)
        scaled = grad * gain_ref[...]
        grad_mid = inverse * (scaled - unit * jnp.mean(scaled * unit, axis=-1, keepdims=True))
        grad_residual = cotangent_ref[...].astype(jnp.float32) + grad_mid
        grad_residual_ref[...] = grad_residual
        grad_low = grad_residual.astype(jnp.bfloat16)
        grad_low_ref[...] = grad_low
        half = out_kept_ref.shape[0]
        for start in range(0, half, 512):
            for ref, shift in ((out_kept_ref, 0), (out_sent_ref, half)):
                rows = slice(start + shift, start + shift + 512)
                ref[start : start + 512, :] = jnp.dot(
                    turned_out_ref[rows, :], grad_low, preferred_element_type=jnp.float32
                ).astype(jnp.bfloat16)

    @pl.when(step >= FFN_STEPS)
    def _():
        attend_back_body(
            device_ref, grad_low_ref, *operands, kept_ref, sent_ref, head_gains_ref, normed_sum_ref, *scratch,
            order=None, shard=None, head_shard=None, last=False, parts=parts, head=step - FFN_STEPS,
        )


def back(device, residual, gain, cotangent, grad_gate, grad_up, weights, shard, turned_out, operands, parts):
    rows, width = residual.shape
    tile = weights.shape[2] // FFN_STEPS
    at = lambda j, d: jnp.minimum(j, FFN_STEPS - 1)
    head = lambda j, d: jnp.maximum(j - FFN_STEPS, 0)
    whole = lambda *shape: pl.BlockSpec(shape, lambda *j: (0, 0))
    columns = pl.BlockSpec((rows, tile), lambda *j: (0, at(*j)))
    weight_args, weight_specs = ffn_operands(weights, shard, width, FFN_STEPS, at)
    out_rows = turned_out.shape[0]
    own_width = KEY_VALUE_HEADS * 2 * HEAD_SIZE
    low = lambda height, size: jax.ShapeDtypeStruct((height, size), jnp.bfloat16)
    wide = far((rows, width), jnp.float32)
    return pl.pallas_call(
        functools.partial(back_body, parts=len(parts)),
        grid_spec=pltpu.PrefetchScalarGridSpec(
            num_scalar_prefetch=1,
            grid=(FFN_STEPS + KEY_VALUE_HEADS // 2,),
            in_specs=[whole(rows, width), whole(1, width), whole(rows, width), columns, columns]
            + weight_specs[:2]
            + [whole(out_rows, rows)]
            + attend_back_specs(rows, width, 0, head, parts),
            out_specs=[
                whole(rows, width),
                whole(rows, width),
                whole(1, width),
                whole(out_rows // 2, width),
                whole(out_rows // 2, width),
                whole(width // 2, own_width),
                whole(width // 2, own_width),
                whole(2, HEAD_SIZE),
                whole(rows, width),
            ],
            scratch_shapes=[pltpu.VMEM((rows, width), jnp.float32)] + attend_back_scratch(rows, parts),
        ),
        out_shape=[
            wide,
            low(rows, width),
            jax.ShapeDtypeStruct((1, width), jnp.float32),
            low(out_rows // 2, width),
            low(out_rows // 2, width),
            low(width // 2, own_width),
            low(width // 2, own_width),
            jax.ShapeDtypeStruct((2, HEAD_SIZE), jnp.float32),
            wide,
        ],
        compiler_params=pltpu.CompilerParams(vmem_limit_bytes=50 * 1024 * 1024),
        cost_estimate=SMALL,
        name="back",
    )(
        device.reshape(1), residual, gain, *from_far(cotangent, grad_gate, grad_up, *weight_args[:2], turned_out), *operands, *parts
    )


def end_body(first_kept, first_came, second_kept, second_came, query_ref, key_ref, value_ref, *gain_refs):
    def part(kept, came, start, size):
        columns = slice(start, start + size)
        return kept[:, columns].astype(jnp.float32) + came[:, columns].astype(jnp.float32)

    group = 0
    for kept, came in ((first_kept, first_came), (second_kept, second_came)):
        for start in range(0, KEY_VALUE_HEADS // 2 * GROUP, GROUP):
            for ref, size in ((query_ref, 2 * HEAD_SIZE), (key_ref, HEAD_SIZE), (value_ref, HEAD_SIZE)):
                ref[:, group * size : (group + 1) * size] = part(kept, came, start, size)
                start += size
            group += 1
    gains = part(second_kept, second_came, KEY_VALUE_HEADS // 2 * GROUP, 128).T
    for index, ref in enumerate(gain_refs):
        ref[...] = gains[index : index + 1, : ref.shape[1]]


def end_projections(first, second, head_shard):
    rows = first[0].shape[0]
    query_width, key_width = QUERY_HEADS * HEAD_SIZE, KEY_VALUE_HEADS * HEAD_SIZE
    return pl.pallas_call(
        end_body,
        out_shape=[
            jax.ShapeDtypeStruct(shape, jnp.float32)
            for shape in (
                (rows, query_width), (rows, key_width), (rows, key_width), (1, rows), (1, rows), (1, head_shard),
                (1, head_shard),
            )
        ],
        cost_estimate=SMALL,
        name="end_projections",
    )(*first, *second)


def on_device(
    tokens,
    seq_lengths,
    seq_owner,
    g_attn,
    w_query,
    key_projection,
    value_projection,
    query_norm_gain,
    g_key,
    w_out,
    g_ffn,
    w_gate,
    w_up,
    w_down,
    cotangent,
):
    row_total_count = tokens.shape[0]
    fence = lax.optimization_barrier
    count = lax.axis_size("fsdp")
    device = lax.axis_index("fsdp")
    early = middle_bits(count, False)
    late = middle_bits(count, True)
    cut_bits = len(early) // 2
    shard = g_attn.shape[0]
    head_shard = query_norm_gain.shape[0]

    ffn_weights = lax.all_gather(stack(w_gate, w_up, w_down), "fsdp", axis=0, tiled=False)
    projections = join(
        w_query, key_projection, value_projection, gain_columns(g_attn, g_ffn, query_norm_gain, g_key, shard)
    )
    top = gather_top(projections, count)
    top, w_out = fence((top, w_out))
    top = gather_top_rest(top, count)
    top, w_out = fence((top, w_out))
    first_part, second_part = lay_top_split(top, device, count, KEY_VALUE_HEADS // 2 * GROUP + 128)
    first_parts = gather_bits({0: first_part}, count, early[:cut_bits])
    second_parts = gather_bits({0: second_part}, count, late[:cut_bits])
    out_top = gather_top(w_out, count)
    first_parts, second_parts, out_top = fence((first_parts, second_parts, out_top))
    first_parts = gather_bits(first_parts, count, early[cut_bits:])
    second_parts = gather_bits(second_parts, count, late[cut_bits:])
    out_top = gather_top_rest(out_top, count)
    first_parts, second_parts, out_top = fence((first_parts, second_parts, out_top))
    first_parts = gather_bits(first_parts, count, [0])
    out_parts = gather_bits(lay_top(out_top, device, count), count, early[:cut_bits])
    first_parts, second_parts = fence((first_parts, second_parts))
    second_parts = gather_bits(second_parts, count, [0])
    first_gains = lay({mask: part[..., -128:] for mask, part in first_parts.items()}, device, count)
    first_weight = weight_parts(first_parts, device, count)

    seq_id, token_position = layout(seq_lengths, seq_owner, device, row_total_count)
    first_row = (jnp.arange(row_total_count, dtype=jnp.int32) - token_position)[:, None]
    cosine, sine = rotation_factors(token_position)
    inputs = tokens.astype(jnp.float32)
    gain_block = first_gains.astype(jnp.float32)
    head_gains = gain_block.reshape(count, shard, 128)[:, :head_shard, 2:4].reshape(HEAD_SIZE, 2).T
    gain_one = gain_block[:, 0]
    gain_two = gain_block[:, 1]
    normed_low = norm_forward(inputs, gain_one)[0].astype(jnp.bfloat16)
    attended_first, *saved_first = attend(device, normed_low, first_weight, head_gains, cosine, sine, first_row)
    attended_first, second_parts, out_parts = fence((attended_first, second_parts, out_parts))
    out_parts = gather_bits(out_parts, count, early[cut_bits:])
    second_weight = weight_parts(second_parts, device, count)
    attended_second, *saved_second = attend(device, normed_low, second_weight, head_gains, cosine, sine, first_row)
    stages = sum_bits(count)
    orders = {name: row_order(count, bits) for name, bits in stages.items()}
    attended_first, attended_second, out_parts = fence((attended_first, attended_second, out_parts))
    out_parts = gather_bits(out_parts, count, [0])
    residual, out_weight = project(
        device,
        [out_parts[mask] for mask in range(count // 4)],
        tokens,
        jnp.concatenate([attended_first, attended_second], axis=1),
    )
    (
        hidden, grad_gate, grad_up, gate_kept, gate_sent, up_kept, up_sent, down_kept, down_sent
    ) = feed_forward(
        device, residual, gain_two[None], cotangent, ffn_weights, shard, orders["gate"], orders["up"]
    )

    live = dict(
        hidden=hidden, grad_gate=grad_gate, grad_up=grad_up, gate=gate_kept, up=up_kept, down=down_kept,
    )
    flying = {}

    def cut():
        live.update(fence(dict(live)))

    def fly(**sent):
        live.update({name + "_sent": value for name, value in sent.items()})
        cut()
        for name in sent:
            flying[name] = exchange(live.pop(name + "_sent"), count, 1 << stages[name].pop(0))

    def land(*names):
        live.update({name + "_came": flying.pop(name) for name in names})
        cut()
        flying.update({name: live.pop(name + "_came") for name in names})

    def relay(*names, places=(0, 0, 0, 0, 0, 0)):
        for name, place in zip(names, places):
            live[name], sent = fold((live[name], flying[name], place))
            flying[name] = exchange(sent, count, 1 << stages[name].pop(0))

    def operands(name, saved):
        return *from_far(out_weight, *saved), head_gains, cosine, sine, first_row, *from_far(turned[name])

    live.update(attended_first=attended_first, attended_second=attended_second, normed=normed_low)
    fly(down=down_sent, gate=gate_sent, up=up_sent)
    live["turned"] = dict(
        out=turn((live.pop("attended_first"), live.pop("attended_second")), device, orders["out"]),
        first=turn((live["normed"],), device, orders["first"]),
        second=turn((live.pop("normed"),), device, orders["second"]),
    )
    cut()
    relay("down", "gate", "up")
    cut()
    turned = live.pop("turned")
    (
        live["grad_residual"], live["low"], live["grad_gain_two"], live["out"], live["out_sent"], live["first"],
        live["first_sent"], live["head_sums"], live["normed_sum"],
    ) = back(
        device, residual, gain_two[None], cotangent, live.pop("grad_gate"), live.pop("grad_up"), ffn_weights, shard,
        turned["out"], operands("first", saved_first), first_weight,
    )
    land("down", "gate", "up")
    fly(first=live["first_sent"], out=live["out_sent"])
    relay("down")
    live["gate"], live["up"], sent = fold(
        (live["gate"], flying["gate"], 0), (live["up"], flying["up"], 0), merged=True
    )
    stages["gate"].pop(0)
    flying["both"] = exchange(sent, count, 1 << stages["up"].pop(0))
    relay("first", "out")
    cut()
    live["second"], live["second_sent"], live["grad_tokens"], live["mixed"] = attend_back_last(
        device, live.pop("low"), operands("second", saved_second), second_weight,
        (live.pop("head_sums"), live.pop("normed_sum")), tokens, gain_one[None], live.pop("grad_residual"),
        live.pop("grad_gain_two"), residual, live.pop("hidden"), ffn_weights, orders["second"], shard, head_shard,
    )
    land("down", "both")
    land("first", "out")
    fly(second=live["second_sent"])
    relay("second")
    both = flying.pop("both")
    flying.update(gate=both, up=both)
    mixed, grad_tokens = live.pop("mixed"), live.pop("grad_tokens")
    relay("down", "gate", "up", places=(0, 0, 1))
    relay("first", "out")
    relay("down", "gate", "up")
    relay("second")
    cut()
    relay("first", "out", "second")
    cut()
    while any(stages.values()):
        for name in ("second", "first", "out", "down", "gate", "up"):
            if stages[name]:
                relay(name)
    pairs = {name: (live.pop(name), flying.pop(name)) for name in stages}
    sum_down, sum_gate, sum_up, sum_out = (sum_end(pairs[name]) for name in ("down", "gate", "up", "out"))
    first, second = pairs["first"], pairs["second"]
    sum_query, sum_key, sum_value, *sum_gains = end_projections(first, second, head_shard)
    return (
        mixed,
        grad_tokens,
        sum_gains[0].reshape(-1),
        sum_query,
        sum_key,
        sum_value,
        sum_gains[2].reshape(-1),
        sum_gains[3].reshape(-1),
        sum_out,
        sum_gains[1].reshape(-1),
        sum_gate,
        sum_up,
        sum_down,
    )


def solution(mesh):
    return jax.shard_map(
        on_device,
        mesh=mesh,
        in_specs=(
            P("fsdp", None),
            P(),
            P(),
            P("fsdp"),
            P("fsdp", None),
            P("fsdp", None),
            P("fsdp", None),
            P("fsdp"),
            P("fsdp"),
            P("fsdp", None),
            P("fsdp"),
            P("fsdp", None),
            P("fsdp", None),
            P("fsdp", None),
            P("fsdp", None),
        ),
        out_specs=(
            P("fsdp", None),
            P("fsdp", None),
            P("fsdp"),
            P("fsdp", None),
            P("fsdp", None),
            P("fsdp", None),
            P("fsdp"),
            P("fsdp"),
            P("fsdp", None),
            P("fsdp"),
            P("fsdp", None),
            P("fsdp", None),
            P("fsdp", None),
        ),
        check_vma=False,
    )
```

```python
import functools
import math

import jax
import jax.numpy as jnp
from jax import lax
from jax.experimental import pallas as pl
from jax.experimental.pallas import tpu as pltpu
from jax.sharding import PartitionSpec as P

QUERY_HEADS = 16
KEY_VALUE_HEADS = 8
HEAD_SIZE = 128


SMALL = pl.CostEstimate(flops=1, bytes_accessed=1, transcendentals=0)


def far(shape, dtype):
    return pltpu.HBM(tuple(shape), dtype)


def from_far(*values):
    return [pltpu.with_memory_space_constraint(value, pltpu.HBM) for value in values]


epsilon = 1e-06
rope_base = 1000000.0


def layout(seq_lengths, seq_owner, device, row_total_count):
    seq_index = jnp.arange(seq_lengths.shape[0], dtype=jnp.int32)
    same_owner = seq_owner[:, None] == seq_owner[None, :]
    before = seq_index[None, :] < seq_index[:, None]
    starts = jnp.sum(jnp.where(same_owner & before, seq_lengths[None, :], 0), axis=1)
    places = jnp.arange(row_total_count, dtype=jnp.int32)
    member = (
        (seq_owner[None, :] == device)
        & (starts[None, :] <= places[:, None])
        & (places[:, None] < (starts + seq_lengths)[None, :])
    )
    seq_id = jnp.sum(jnp.where(member, seq_index[None, :], 0), axis=1)
    token_position = jnp.sum(jnp.where(member, places[:, None] - starts[None, :], 0), axis=1)
    return (seq_id, token_position)


def rotation_factors(token_position):
    half_width = HEAD_SIZE // 2
    frequency = jnp.exp(
        jnp.arange(half_width, dtype=jnp.float32) * (-2.0 * math.log(rope_base) / HEAD_SIZE)
    )
    angles = token_position.astype(jnp.float32)[:, None] * frequency[None, :]
    cosine = jnp.cos(angles)
    sine = jnp.sin(angles)
    return jnp.concatenate([cosine, cosine], axis=1), jnp.concatenate([-sine, sine], axis=1)


def norm_forward(values, gain):
    inverse = lax.rsqrt(jnp.mean(values * values, axis=-1, keepdims=True) + epsilon)
    unit_rows = values * inverse
    return (unit_rows * gain, unit_rows, inverse)


def exchange(values, count, mask):
    return lax.ppermute(values, "fsdp", [(source, source ^ mask) for source in range(count)])


def middle_bits(count, flip):
    bits = list(range(1, count.bit_length() - 3))
    return bits[::-1] if flip else bits


def sum_bits(count):
    bits = count.bit_length() - 1
    middle = list(range(1, bits - 2))
    low, high = bits - 2, bits - 1
    return dict(
        down=[0, middle[-1], high, low] + middle[-2::-1],
        gate=[0] + middle + [low, high],
        up=[0, low, middle[-1], high] + middle[-2::-1],
        out=[0] + middle + [low, high],
        first=[0, low] + middle[::-1] + [high],
        second=[0] + middle + [low, high],
    )


def row_order(count, sequence):
    bits = len(sequence)
    return [
        sum(((index >> (bits - 1 - step)) & 1) << bit for step, bit in enumerate(sequence)) for index in range(count)
    ]


def turn_body(device_ref, *refs, order):
    values, (out_ref, turned_ref) = refs[:-2], refs[-2:]
    start = 0
    for ref in values:
        turned_ref[start : start + ref.shape[1], :] = ref[...].astype(turned_ref.dtype).T
        start += ref.shape[1]
    device = device_ref[0]
    rows = out_ref.shape[0] // len(order)
    group = max(1, 16 // rows)
    for first in range(0, len(order), group):
        blocks = [
            turned_ref[pl.ds(pl.multiple_of((device ^ mask) * rows, rows), rows), :]
            for mask in order[first : first + group]
        ]
        block = blocks[0] if group == 1 else jnp.concatenate(blocks, axis=0)
        out_ref[first * rows : (first + group) * rows, :] = block.astype(out_ref.dtype)


def turn(values, device, order):
    count = len(order)
    rows = values[0].shape[0]
    columns = sum(value.shape[1] for value in values)
    held = jnp.bfloat16 if columns // count % 16 == 0 else jnp.float32
    return pl.pallas_call(
        functools.partial(turn_body, order=order),
        grid_spec=pltpu.PrefetchScalarGridSpec(
            num_scalar_prefetch=1,
            grid=(1,),
            in_specs=[pl.BlockSpec(value.shape, lambda i, d: (0, 0)) for value in values],
            out_specs=pl.BlockSpec((columns, rows), lambda i, d: (0, 0)),
            scratch_shapes=[pltpu.VMEM((columns, rows), held)],
        ),
        out_shape=far((columns, rows), values[0].dtype),
        compiler_params=pltpu.CompilerParams(vmem_limit_bytes=16 * 1024 * 1024),
        cost_estimate=SMALL,
        name="turn",
    )(device.reshape(1), *values)


def fold_body(*refs, pairs, merged):
    def add(first, second):
        return (first[...].astype(jnp.float32) + second[...].astype(jnp.float32)).astype(jnp.bfloat16)

    out_refs = refs[4 * pairs :]
    start = 0
    for index in range(pairs):
        kept_first, kept_second, came_first, came_second = refs[4 * index : 4 * index + 4]
        sent = add(kept_second, came_second)
        if merged:
            out_refs[pairs][:, start : start + sent.shape[1]] = sent
            start += sent.shape[1]
        else:
            out_refs[pairs + index][...] = sent
        out_refs[index][...] = add(kept_first, came_first)


def fold(*pairs, merged=False):
    halves = [kept.shape[0] // 2 for kept, *_ in pairs]
    steps = next(n for n in (2, 1) if n == 1 or all(rows % (16 * n) == 0 for rows in halves))
    in_specs, out_specs, out_shape, operands = [], [], [], []
    for rows, (kept, came, place) in zip(halves, pairs):
        columns = kept.shape[1]
        spec = lambda shift, place=0, rows=rows, columns=columns: pl.BlockSpec(
            (rows // steps, columns), lambda i: (i + shift, place)
        )
        in_specs += [spec(0), spec(steps), spec(0, place), spec(steps, place)]
        operands += [kept, kept, came, came]
        out_specs += [spec(0)]
        out_shape += [jax.ShapeDtypeStruct((rows, columns), jnp.bfloat16)]
    if merged:
        columns = sum(kept.shape[1] for kept, *_ in pairs)
        sent_specs = [pl.BlockSpec((halves[0] // steps, columns), lambda i: (i, 0))]
        sent_shape = [jax.ShapeDtypeStruct((halves[0], columns), jnp.bfloat16)]
    else:
        sent_specs, sent_shape = list(out_specs), list(out_shape)
    block_bytes = sum(6 * 2 * (rows // steps) * kept.shape[1] for rows, (kept, *_) in zip(halves, pairs))
    return pl.pallas_call(
        functools.partial(fold_body, pairs=len(pairs), merged=merged),
        grid=(steps,),
        in_specs=in_specs,
        out_specs=out_specs + sent_specs,
        out_shape=out_shape + sent_shape,
        compiler_params=pltpu.CompilerParams(vmem_limit_bytes=2 * block_bytes + 6 * 1024 * 1024),
        cost_estimate=SMALL,
        name="fold",
    )(*operands)


def sum_end(pair):
    return pair[0].astype(jnp.float32) + pair[1].astype(jnp.float32)


def place_body(device_ref, *refs):
    parts = refs[:-2]
    out_ref, semaphores = refs[-2:]
    device = device_ref[0]
    copies = [
        pltpu.make_async_copy(part, out_ref.at[:, device ^ mask], semaphores.at[mask])
        for mask, part in enumerate(parts)
    ]
    for copy in copies:
        copy.start()
    for copy in copies:
        copy.wait()


def place(parts, inner):
    top, rows, columns = parts[0].shape
    return pl.pallas_call(
        place_body,
        grid_spec=pltpu.PrefetchScalarGridSpec(
            num_scalar_prefetch=1,
            grid=(1,),
            in_specs=[pl.BlockSpec(memory_space=pl.ANY)] * len(parts),
            out_specs=pl.BlockSpec((top, len(parts), rows, columns), lambda i, d: (0, 0, 0, 0)),
            scratch_shapes=[pltpu.SemaphoreType.DMA((len(parts),))],
        ),
        out_shape=far((top, len(parts), rows, columns), parts[0].dtype)
        if top > 1
        else jax.ShapeDtypeStruct((top, len(parts), rows, columns), parts[0].dtype),
        compiler_params=pltpu.CompilerParams(vmem_limit_bytes=14 * 1024 * 1024),
        cost_estimate=SMALL,
        name="place",
    )(inner.reshape(1), *parts).reshape(top * len(parts) * rows, columns)


def gather_top(block, count):
    return [block, exchange(block, count, count // 4), exchange(block, count, count // 2)]


def gather_top_rest(blocks, count):
    return [block[None] for block in blocks + [exchange(blocks[2], count, count // 4)]]


def stack_body(gate_ref, up_ref, down_ref, out_ref):
    rows = gate_ref.shape[0]
    width = down_ref.shape[1]
    out_ref[:rows, :] = gate_ref[...]
    out_ref[rows : 2 * rows, :] = up_ref[...]
    for piece in range(down_ref.shape[0] // rows):
        columns = slice(piece * width, (piece + 1) * width)
        out_ref[2 * rows :, columns] = down_ref[piece * rows : (piece + 1) * rows, :]


def stack(w_gate, w_up, w_down):
    rows, columns = w_gate.shape
    pieces = w_down.shape[0] // rows
    if rows % 16:
        down = w_down.reshape(pieces, rows, -1).transpose(1, 0, 2).reshape(rows, -1)
        return jnp.concatenate([w_gate, w_up, down], axis=0)
    return pl.pallas_call(
        stack_body,
        out_shape=jax.ShapeDtypeStruct((3 * rows, columns), w_gate.dtype),
        cost_estimate=SMALL,
        name="stack",
    )(w_gate, w_up, w_down)


def join_body(query_ref, key_ref, value_ref, gains_ref, out_ref):
    groups = KEY_VALUE_HEADS
    pair = query_ref.shape[1] // groups
    one = key_ref.shape[1] // groups
    shift = 0
    for group in range(groups):
        for ref, size in ((query_ref, pair), (key_ref, one), (value_ref, one)):
            out_ref[:, shift : shift + size] = ref[:, group * size : (group + 1) * size]
            shift += size
        if group == groups // 2 - 1:
            out_ref[:, shift : shift + 128] = gains_ref[...]
            shift += 128


def join(w_query, key_projection, value_projection, gains):
    rows = w_query.shape[0]
    columns = w_query.shape[1] + 2 * key_projection.shape[1] + 128
    return pl.pallas_call(
        join_body,
        out_shape=jax.ShapeDtypeStruct((rows, columns), w_query.dtype),
        cost_estimate=SMALL,
        name="join",
    )(w_query, key_projection, value_projection, gains)


def lay_top(blocks, device, count):
    return {0: place(from_far(*blocks), device // (count // 4)).reshape((4,) + blocks[0].shape[1:])}


def split_body(device_ref, *refs):
    parts = refs[:4]
    left_ref, right_ref, semaphores = refs[4:]
    width = left_ref.shape[-1]
    copies = []
    for mask, part in enumerate(parts):
        target = device_ref[0] ^ mask
        copies += [
            pltpu.make_async_copy(part.at[:, :width], left_ref.at[target], semaphores.at[2 * mask]),
            pltpu.make_async_copy(part.at[:, width:], right_ref.at[target], semaphores.at[2 * mask + 1]),
        ]
    for copy in copies:
        copy.start()
    for copy in copies:
        copy.wait()


def lay_top_split(blocks, device, count, width):
    rows, columns = blocks[0].shape[1:]
    shapes = [(4, rows, width), (4, rows, columns - width)]
    return pl.pallas_call(
        split_body,
        grid_spec=pltpu.PrefetchScalarGridSpec(
            num_scalar_prefetch=1,
            grid=(1,),
            in_specs=[pl.BlockSpec(memory_space=pl.ANY)] * 4,
            out_specs=[pl.BlockSpec(shape, lambda i, d: (0, 0, 0)) for shape in shapes],
            scratch_shapes=[pltpu.SemaphoreType.DMA((8,))],
        ),
        out_shape=[jax.ShapeDtypeStruct(shape, blocks[0].dtype) for shape in shapes],
        compiler_params=pltpu.CompilerParams(vmem_limit_bytes=10 * 1024 * 1024),
        cost_estimate=SMALL,
        name="lay_top_split",
    )((device // (count // 4)).reshape(1), *from_far(*[block[0] for block in blocks]))


def gather_bits(parts, count, bits):
    parts = dict(parts)
    for bit in bits:
        for mask in list(parts):
            parts[mask | (1 << bit)] = exchange(parts[mask], count, 1 << bit)
    return parts


def lay(parts, device, count):
    return place([parts[mask] for mask in range(count // 4)], device & (count // 4 - 1))


def gain_columns(first, second, third, fourth, rows):
    columns = [jnp.pad(v, (0, rows - v.shape[0]))[:, None] for v in (first, second, third, fourth)]
    return jnp.pad(jnp.concatenate(columns, axis=1), ((0, 0), (0, 124)))


def swap_halves(head):
    return pltpu.roll(head, HEAD_SIZE // 2, 1)


def unit_head(raw):
    inverse = lax.rsqrt(jnp.mean(raw * raw, axis=-1, keepdims=True) + epsilon)
    return raw * inverse, inverse


def contract(left, right, left_axis, right_axis):
    return lax.dot_general(
        left, right, (((left_axis,), (right_axis,)), ((), ())), preferred_element_type=jnp.float32
    )


def block_scores(group, key_rows, first_row, row_start):
    scores = contract(group, key_rows, 1, 1) * (1.0 / math.sqrt(HEAD_SIZE))
    rows = lax.broadcasted_iota(jnp.int32, scores.shape, 0)
    half = scores.shape[0] // 2
    rows = jnp.where(rows >= half, rows - half, rows) + row_start
    columns = lax.broadcasted_iota(jnp.int32, scores.shape, 1)
    return jnp.where((columns <= rows) & (columns >= first_row), scores, -1e30)


def head_pair(ref, block):
    return jnp.concatenate([ref[block, :HEAD_SIZE], ref[block, HEAD_SIZE:]], axis=0)


def pair_rows(first_row_ref, block):
    rows = first_row_ref[block, :]
    return jnp.concatenate([rows, rows], axis=0)


GROUP = 4 * HEAD_SIZE


def weight_parts(parts, device, count):
    if parts[0].shape[1] % 16 == 0:
        return [parts[mask] for mask in range(count // 4)]
    weight = lay(parts, device, count)
    return [weight[None]]


def part_specs(parts, index):
    top, rows, _ = parts[0].shape
    return [pl.BlockSpec((top, rows, GROUP), lambda *j: (0, 0, index(*j))) for _ in parts]


def join_parts(device_ref, part_refs, weight_ref):
    inner = device_ref[0] & (len(part_refs) - 1)
    for mask, ref in enumerate(part_refs):
        weight_ref[:, inner ^ mask] = ref[...]
    top, count, rows, columns = weight_ref.shape
    return weight_ref[...].reshape(top * count * rows, columns)


def prepare_body(device_ref, *refs, shard, head_shard):
    (*part_refs, tokens_ref), (normed_ref, first_gain_ref, second_gain_ref, head_gains_ref, gains_ref) = refs[:-5], refs[-5:]
    lines = join_parts(device_ref, part_refs, gains_ref).astype(jnp.float32).T
    gain = lines[0:1, :]
    first_gain_ref[...] = gain
    second_gain_ref[...] = lines[1:2, :]
    width = lines.shape[1]
    source = lax.broadcasted_iota(jnp.int32, (width, HEAD_SIZE), 0)
    target = lax.broadcasted_iota(jnp.int32, (width, HEAD_SIZE), 1)
    pick = jnp.where(target // head_shard * shard + target % head_shard == source, 1.0, 0.0)
    head_gains_ref[...] = jnp.dot(
        lines[2:4, :], pick, precision=lax.Precision.HIGHEST, preferred_element_type=jnp.float32
    )
    unit, _ = unit_head(tokens_ref[...].astype(jnp.float32))
    normed_ref[...] = (unit * gain).astype(jnp.bfloat16)


def prepare(device, parts, tokens, shard, head_shard):
    rows, width = tokens.shape
    top, part_rows, columns = parts[0].shape
    whole = lambda *shape: pl.BlockSpec(shape, lambda i, d: (0, 0))
    line = jax.ShapeDtypeStruct((1, width), jnp.float32)
    return pl.pallas_call(
        functools.partial(prepare_body, shard=shard, head_shard=head_shard),
        grid_spec=pltpu.PrefetchScalarGridSpec(
            num_scalar_prefetch=1,
            grid=(1,),
            in_specs=[pl.BlockSpec((top, part_rows, 128), lambda i, d: (0, 0, columns // 128 - 1)) for _ in parts]
            + [whole(rows, width)],
            out_specs=[whole(rows, width), whole(1, width), whole(1, width), whole(2, HEAD_SIZE)],
            scratch_shapes=[pltpu.VMEM((top, len(parts), part_rows, 128), jnp.bfloat16)],
        ),
        out_shape=[
            jax.ShapeDtypeStruct((rows, width), jnp.bfloat16),
            line,
            line,
            jax.ShapeDtypeStruct((2, HEAD_SIZE), jnp.float32),
        ],
        compiler_params=pltpu.CompilerParams(vmem_limit_bytes=16 * 1024 * 1024),
        cost_estimate=SMALL,
        name="prepare",
    )(device.reshape(1), *parts, tokens)


def attend_body(device_ref, *refs):
    (*part_refs, normed_ref, gains_ref, cosine_ref, sine_ref, first_ref), out_refs = refs[:-7], refs[-7:]
    attended_ref, query_ref, key_ref, value_ref, raw_ref, total_ref, weight_ref = out_refs
    cosine = cosine_ref[...]
    sine = sine_ref[...]

    def turned(raw, gain):
        scaled = unit_head(raw)[0] * gain
        return (scaled * cosine + swap_halves(scaled) * sine).astype(jnp.bfloat16)

    weight = join_parts(device_ref, part_refs, weight_ref)
    raw = jnp.dot(normed_ref[...], weight, preferred_element_type=jnp.float32)
    raw_ref[...] = raw[:, : 3 * HEAD_SIZE]
    for head in range(2):
        part = slice(head * HEAD_SIZE, (head + 1) * HEAD_SIZE)
        query_ref[:, part] = turned(raw[:, part], gains_ref[0:1, :])
    key_ref[...] = turned(raw[:, 2 * HEAD_SIZE : 3 * HEAD_SIZE], gains_ref[1:2, :])
    value_ref[...] = raw[:, 3 * HEAD_SIZE :].astype(jnp.bfloat16)
    step = 128
    for start in range(0, raw.shape[0], step):
        block = slice(start, start + step)
        seen = slice(0, start + step)
        scores = block_scores(head_pair(query_ref, block), key_ref[seen, :], pair_rows(first_ref, block), start)
        top = jnp.max(scores, axis=-1, keepdims=True)
        log_total = top + jnp.log(jnp.sum(jnp.exp(scores - top), axis=-1, keepdims=True))
        probs_low = jnp.exp(scores - log_total).astype(jnp.bfloat16)
        out = jnp.dot(probs_low, value_ref[seen, :], preferred_element_type=jnp.float32).astype(jnp.bfloat16)
        attended_ref[block, :HEAD_SIZE] = out[:step]
        attended_ref[block, HEAD_SIZE:] = out[step:]
        total_ref[0, block, 0:1] = log_total[:step]
        total_ref[0, block, 1:2] = log_total[step:]


def attend(device, normed, parts, head_gains, cosine, sine, first_row):
    rows, width = normed.shape
    groups = KEY_VALUE_HEADS // 2
    whole = lambda *shape: pl.BlockSpec(shape, lambda h, d: (0, 0))
    columns = lambda size: pl.BlockSpec((rows, size), lambda h, d: (0, h))
    low = lambda size: far((rows, groups * size), jnp.bfloat16)
    pair = 2 * HEAD_SIZE
    return pl.pallas_call(
        attend_body,
        grid_spec=pltpu.PrefetchScalarGridSpec(
            num_scalar_prefetch=1,
            grid=(groups,),
            in_specs=part_specs(parts, lambda h, d: h)
            + [
                whole(rows, width),
                whole(2, HEAD_SIZE),
                whole(rows, HEAD_SIZE),
                whole(rows, HEAD_SIZE),
                whole(rows, 1),
            ],
            out_specs=[
                columns(pair),
                columns(pair),
                columns(HEAD_SIZE),
                columns(HEAD_SIZE),
                columns(3 * HEAD_SIZE),
                pl.BlockSpec((1, rows, 2), lambda h, d: (h, 0, 0)),
            ],
            scratch_shapes=[pltpu.VMEM((parts[0].shape[0], len(parts), parts[0].shape[1], GROUP), jnp.bfloat16)],
        ),
        out_shape=[
            jax.ShapeDtypeStruct((rows, groups * pair), jnp.bfloat16),
            low(pair),
            low(HEAD_SIZE),
            low(HEAD_SIZE),
            far((rows, groups * 3 * HEAD_SIZE), jnp.float32),
            far((groups, rows, 2), jnp.float32),
        ],
        compiler_params=pltpu.CompilerParams(vmem_limit_bytes=26 * 1024 * 1024),
        cost_estimate=SMALL,
        name="attend",
    )(device.reshape(1), *parts, normed, head_gains, cosine, sine, first_row)


def attend_back_body(
    device_ref, residual_ref, wo_ref, query_ref, key_ref, value_ref, raw_ref, total_ref,
    gains_ref, cosine_ref, sine_ref, first_ref, turned_ref, *refs,
    order, shard, head_shard, last, parts, head=None,
):
    part_refs, refs = refs[:parts], refs[parts:]
    if last:
        head_gains_in_ref, normed_in_ref = refs[:2]
        refs = refs[2:]
        tokens_ref, gain_ref, grad_residual_ref, gain_two_ref, hidden_ref, down_ref, ffn_in_ref = refs[:7]
        kept_ref, sent_ref, tokens_out_ref, mixed_ref = refs[7:11]
        head_gains_ref, normed_sum_ref, lines_ref, mixed_sum_ref, down_weight_ref = refs[11:16]
        scratch = refs[16:]
    else:
        kept_ref, sent_ref, head_gains_ref, normed_sum_ref = refs[:4]
        scratch = refs[4:]
    grad_out_ref, query_sum_ref, key_sum_ref, value_sum_ref, grads_ref, weight_ref = scratch
    scale = 1.0 / math.sqrt(HEAD_SIZE)
    heads = KEY_VALUE_HEADS // 2
    if head is None:
        head = pl.program_id(0)

    @pl.when(head == 0)
    def _():
        head_gains_ref[...] = head_gains_in_ref[...] if last else jnp.zeros_like(head_gains_ref)
        normed_sum_ref[...] = normed_in_ref[...] if last else jnp.zeros_like(normed_sum_ref)

    if last:
        gather_down(down_ref, down_weight_ref, down_weight_ref.shape[1])

        @pl.when(head == 0)
        def _():
            mixed_sum_ref[...] = ffn_in_ref[...]

        mixed_sum_ref[...] += jnp.dot(hidden_ref[...], down_weight_ref[...], preferred_element_type=jnp.float32)

        @pl.when(head == heads - 1)
        def _():
            mixed_ref[...] = mixed_sum_ref[...].astype(jnp.bfloat16)

    grad_out_ref[...] = contract(residual_ref[...], wo_ref[...], 1, 1).astype(jnp.bfloat16)
    key_sum_ref[...] = jnp.zeros_like(key_sum_ref)
    value_sum_ref[...] = jnp.zeros_like(value_sum_ref)
    step = 128
    for start in range(0, residual_ref.shape[0], step):
        block = slice(start, start + step)
        seen = slice(0, start + step)
        group = head_pair(query_ref, block)
        grad_out = head_pair(grad_out_ref, block)
        key_rows = key_ref[seen, :]
        scores = block_scores(group, key_rows, pair_rows(first_ref, block), start)
        log_total = jnp.concatenate([total_ref[0, block, 0:1], total_ref[0, block, 1:2]], axis=0)
        probs = jnp.exp(scores - log_total)
        grad_probs = contract(grad_out, value_ref[seen, :], 1, 1)
        value_sum_ref[seen, :] += contract(probs.astype(jnp.bfloat16), grad_out, 0, 0)
        inner = jnp.sum(probs * grad_probs, axis=-1, keepdims=True)
        grad_scores = (probs * (grad_probs - inner)).astype(jnp.bfloat16)
        grad_group = jnp.dot(grad_scores, key_rows, preferred_element_type=jnp.float32) * scale
        query_sum_ref[block, :HEAD_SIZE] = grad_group[:step]
        query_sum_ref[block, HEAD_SIZE:] = grad_group[step:]
        key_sum_ref[seen, :] += contract(grad_scores, group, 0, 0)
    grads_ref[:, 3 * HEAD_SIZE :] = value_sum_ref[...].astype(jnp.bfloat16)
    cosine = cosine_ref[...]
    sine = sine_ref[...]

    def back(grad, part, gain):
        turned = grad * cosine - swap_halves(grad) * sine
        unit, inverse = unit_head(raw_ref[:, part])
        product = turned * unit
        scaled = turned * gain
        grad_raw = inverse * (scaled - unit * jnp.mean(product * gain, axis=-1, keepdims=True))
        grads_ref[:, part] = grad_raw.astype(jnp.bfloat16)
        return jnp.sum(product, axis=0, keepdims=True)

    for index in range(2):
        part = slice(index * HEAD_SIZE, (index + 1) * HEAD_SIZE)
        head_gains_ref[0:1, :] += back(query_sum_ref[:, part], part, gains_ref[0:1, :])
    part = slice(2 * HEAD_SIZE, 3 * HEAD_SIZE)
    head_gains_ref[1:2, :] += back(key_sum_ref[...] * scale, part, gains_ref[1:2, :])

    grads = grads_ref[...]
    half = turned_ref.shape[0] // 2
    product = jnp.dot(turned_ref[...], grads, preferred_element_type=jnp.float32).astype(jnp.bfloat16)
    columns = pl.ds(pl.multiple_of(head * GROUP, GROUP), GROUP)
    kept_ref[:, columns] = product[:half]
    sent_ref[:, columns] = product[half:]
    normed_sum_ref[...] += contract(grads, join_parts(device_ref, part_refs, weight_ref), 1, 1)

    if not last:
        return

    @pl.when(head == heads - 1)
    def _():
        unit, inverse = unit_head(tokens_ref[...].astype(jnp.float32))
        grad = normed_sum_ref[...]
        scaled = grad * gain_ref[...]
        grad_first = inverse * (scaled - unit * jnp.mean(scaled * unit, axis=-1, keepdims=True))
        tokens_out_ref[...] = (grad_residual_ref[...] + grad_first).astype(jnp.bfloat16)
        width = grad.shape[1]
        source = lax.broadcasted_iota(jnp.int32, (HEAD_SIZE, width), 0)
        target = lax.broadcasted_iota(jnp.int32, (HEAD_SIZE, width), 1)
        spread = jnp.where(source // head_shard * shard + source % head_shard == target, 1.0, 0.0)
        heads = jnp.dot(
            head_gains_ref[...], spread, precision=lax.Precision.HIGHEST, preferred_element_type=jnp.float32
        )
        lines = jnp.concatenate(
            [
                jnp.sum(grad * unit, axis=0, keepdims=True),
                gain_two_ref[...],
                heads,
                jnp.zeros((124, width), jnp.float32),
            ],
            axis=0,
        )
        lines_ref[...] = lines.T
        device = device_ref[0]
        group = max(1, 16 // shard)
        end = slice(kept_ref.shape[1] - 128, None)
        for first in range(0, len(order), group):
            blocks = [
                lines_ref[pl.ds(pl.multiple_of((device ^ mask) * shard, shard), shard), :]
                for mask in order[first : first + group]
            ]
            block = (blocks[0] if group == 1 else jnp.concatenate(blocks, axis=0)).astype(jnp.bfloat16)
            row = first * shard
            target_ref = kept_ref if row < half else sent_ref
            target_ref[row % half : row % half + group * shard, end] = block


def attend_back_specs(rows, width, part, head, parts):
    first = part * KEY_VALUE_HEADS // 2
    whole = lambda *shape: pl.BlockSpec(shape, lambda *j: (0, 0))
    columns = lambda height, size: pl.BlockSpec((height, size), lambda *j: (0, head(*j)))
    pair = 2 * HEAD_SIZE
    return [
        pl.BlockSpec((pair, width), lambda *j: (head(*j) + first, 0)),
        columns(rows, pair),
        columns(rows, HEAD_SIZE),
        columns(rows, HEAD_SIZE),
        columns(rows, 3 * HEAD_SIZE),
        pl.BlockSpec((1, rows, 2), lambda *j: (head(*j), 0, 0)),
        whole(2, HEAD_SIZE),
        whole(rows, HEAD_SIZE),
        whole(rows, HEAD_SIZE),
        whole(rows, 1),
        whole(width, rows),
    ] + part_specs(parts, head)


def attend_back_scratch(rows, parts):
    pair = 2 * HEAD_SIZE
    return [
        pltpu.VMEM((rows, pair), jnp.bfloat16),
        pltpu.VMEM((rows, pair), jnp.float32),
        pltpu.VMEM((rows, HEAD_SIZE), jnp.float32),
        pltpu.VMEM((rows, HEAD_SIZE), jnp.float32),
        pltpu.VMEM((rows, GROUP), jnp.bfloat16),
        pltpu.VMEM((parts[0].shape[0], len(parts), parts[0].shape[1], GROUP), jnp.bfloat16),
    ]


def attend_back_last(
    device, residual_low, operands, parts, sums, tokens, gain, grad_residual, grad_gain_two, ffn_in, hidden, weights,
    order, shard, head_shard,
):
    rows, width = residual_low.shape
    whole = lambda *shape: pl.BlockSpec(shape, lambda *j: (0, 0))
    own_width = KEY_VALUE_HEADS * 2 * HEAD_SIZE + 128
    half = jax.ShapeDtypeStruct((width // 2, own_width), jnp.bfloat16)
    low = jax.ShapeDtypeStruct((rows, width), jnp.bfloat16)
    tiles = KEY_VALUE_HEADS // 2
    tile = weights.shape[2] // tiles
    weight_args, weight_specs = ffn_operands(weights, shard, width, tiles, lambda h, d: h)
    return pl.pallas_call(
        functools.partial(
            attend_back_body, order=order, shard=shard, head_shard=head_shard, last=True, parts=len(parts)
        ),
        grid_spec=pltpu.PrefetchScalarGridSpec(
            num_scalar_prefetch=1,
            grid=(KEY_VALUE_HEADS // 2,),
            in_specs=[whole(rows, width)]
            + attend_back_specs(rows, width, 1, lambda h, d: h, parts)
            + [whole(2, HEAD_SIZE), whole(rows, width)]
            + [whole(rows, width), whole(1, width), whole(rows, width), whole(1, width)]
            + [pl.BlockSpec((rows, tile), lambda h, d: (0, h)), weight_specs[2], whole(rows, width)],
            out_specs=[
                whole(width // 2, own_width), whole(width // 2, own_width), whole(rows, width), whole(rows, width)
            ],
            scratch_shapes=[
                pltpu.VMEM((2, HEAD_SIZE), jnp.float32),
                pltpu.VMEM((rows, width), jnp.float32),
                pltpu.VMEM((width, 128), jnp.float32),
                pltpu.VMEM((rows, width), jnp.float32),
                pltpu.VMEM((tile, width), jnp.bfloat16),
            ]
            + attend_back_scratch(rows, parts),
        ),
        out_shape=[half, half, low, low],
        compiler_params=pltpu.CompilerParams(vmem_limit_bytes=46 * 1024 * 1024),
        cost_estimate=SMALL,
        name="attend_back_last",
    )(
        device.reshape(1), residual_low, *operands, *parts, sums[0], *from_far(sums[1], tokens), gain, *from_far(grad_residual),
        grad_gain_two, *from_far(hidden, weight_args[2], ffn_in),
    )


def project_body(device_ref, *refs, top_steps):
    (*part_refs, tokens_ref, first_ref, second_ref), (residual_ref, weight_out_ref) = refs[:-2], refs[-2:]
    inner = device_ref[0] & (len(part_refs) - 1)

    @pl.when(pl.program_id(0) == 0)
    def _():
        residual_ref[...] = tokens_ref[...].astype(jnp.float32)

    for mask, ref in enumerate(part_refs):
        weight_out_ref[:, inner ^ mask] = ref[...]
    top, count, rows, columns = weight_out_ref.shape
    weight = weight_out_ref[...].reshape(top * count * rows, columns)
    for ref, part in ((first_ref, 0), (second_ref, 1)):

        @pl.when(pl.program_id(0) // (top_steps // 2) == part)
        def _():
            residual_ref[...] += jnp.dot(ref[...], weight, preferred_element_type=jnp.float32)


def project(device, parts, tokens, first, second):
    rows, width = tokens.shape
    top, part_rows, _ = parts[0].shape
    step_rows = len(parts) * part_rows
    whole = pl.BlockSpec((rows, width), lambda j, d: (0, 0))
    residual, weight = pl.pallas_call(
        functools.partial(project_body, top_steps=top),
        grid_spec=pltpu.PrefetchScalarGridSpec(
            num_scalar_prefetch=1,
            grid=(top,),
            in_specs=[pl.BlockSpec((1, part_rows, width), lambda j, d: (j, 0, 0)) for _ in parts]
            + [
                whole,
                pl.BlockSpec((rows, step_rows), lambda j, d: (0, jnp.minimum(j, top // 2 - 1))),
                pl.BlockSpec((rows, step_rows), lambda j, d: (0, jnp.maximum(j - top // 2, 0))),
            ],
            out_specs=[whole, pl.BlockSpec((1, len(parts), part_rows, width), lambda j, d: (j, 0, 0, 0))],
        ),
        out_shape=[
            far((rows, width), jnp.float32),
            far((top, len(parts), part_rows, width), jnp.bfloat16),
        ],
        compiler_params=pltpu.CompilerParams(vmem_limit_bytes=20 * 1024 * 1024),
        cost_estimate=SMALL,
        name="project",
    )(device.reshape(1), *parts, tokens, first, second)
    return residual, weight.reshape(top * step_rows, width)


def gather_down(down_ref, down_weight_ref, width):
    devices, rows, _ = down_ref.shape
    pieces = down_ref.shape[2] // width
    for index in range(devices):
        for piece in range(pieces):
            first = (index * pieces + piece) * rows
            down_weight_ref[first : first + rows, :] = down_ref[index, :, piece * width : (piece + 1) * width]


def feed_forward_body(
    device_ref, residual_ref, gain_ref, cotangent_ref, gate_ref, up_ref, down_ref,
    hidden_ref, grad_gate_ref, grad_up_ref, gate_kept_ref, gate_sent_ref, up_kept_ref, up_sent_ref,
    down_kept_ref, down_sent_ref, normed_ref, down_weight_ref, turned_ref, for_gate_ref, for_up_ref, product_ref,
    *, gate_order, up_order,
):
    device = device_ref[0]
    width = residual_ref.shape[1]

    @pl.when(pl.program_id(0) == 0)
    def _():
        unit, _ = unit_head(residual_ref[...])
        normed = (unit * gain_ref[...]).astype(jnp.bfloat16)
        normed_ref[...] = normed
        turned_ref[...] = normed.astype(turned_ref.dtype).T
        rows = width // len(gate_order)
        group = max(1, 16 // rows)
        for order, ref in ((gate_order, for_gate_ref), (up_order, for_up_ref)):
            for first in range(0, len(order), group):
                blocks = [
                    turned_ref[pl.ds(pl.multiple_of((device ^ mask) * rows, rows), rows), :]
                    for mask in order[first : first + group]
                ]
                block = blocks[0] if group == 1 else jnp.concatenate(blocks, axis=0)
                ref[first * rows : (first + group) * rows, :] = block.astype(jnp.bfloat16)

    normed = normed_ref[...]
    gather_down(down_ref, down_weight_ref, width)
    cotangent = cotangent_ref[...]
    gate = jnp.dot(normed, gate_ref[...].reshape(width, gate_ref.shape[-1]), preferred_element_type=jnp.float32)
    up = jnp.dot(normed, up_ref[...].reshape(width, up_ref.shape[-1]), preferred_element_type=jnp.float32)
    grad_hidden = contract(cotangent, down_weight_ref[...], 1, 1)
    sigmoid = jax.nn.sigmoid(gate)
    silu = gate * sigmoid
    hidden = (silu * up).astype(jnp.bfloat16)
    grad_gate = (grad_hidden * up * sigmoid * (1.0 + gate * (1.0 - sigmoid))).astype(jnp.bfloat16)
    hidden_ref[...] = hidden
    grad_gate_ref[...] = grad_gate
    grad_up = (grad_hidden * silu).astype(jnp.bfloat16)
    grad_up_ref[...] = grad_up

    for ordered_ref, grad, kept_ref, sent_ref in (
        (for_gate_ref, grad_gate, gate_kept_ref, gate_sent_ref),
        (for_up_ref, grad_up, up_kept_ref, up_sent_ref),
    ):
        product = jnp.dot(ordered_ref[...], grad, preferred_element_type=jnp.float32).astype(jnp.bfloat16)
        half = product.shape[0] // 2
        kept_ref[...] = product[:half]
        sent_ref[...] = product[half:]
    product_ref[...] = contract(hidden, cotangent, 0, 0).reshape(product_ref.shape)
    owners = product_ref.shape[0]
    low = device & (owners - 1)
    for target, core in ((down_kept_ref, 0), (down_sent_ref, 1)):
        blocks = [product_ref[low ^ (index | core)] for index in range(0, owners, 2)]
        target[...] = jnp.concatenate(blocks, axis=0).astype(jnp.bfloat16).reshape(target.shape)


def ffn_operands(weights, shard, width, tiles, at):
    count, _, hidden_width = weights.shape
    tile = hidden_width // tiles
    if shard % 16 == 0:
        return [weights, weights, weights], [
            pl.BlockSpec((count, shard, tile), lambda *j: (0, 0, at(*j))),
            pl.BlockSpec((count, shard, tile), lambda *j: (0, 1, at(*j))),
            pl.BlockSpec((count // tiles, shard, hidden_width), lambda *j: (at(*j), 2, 0)),
        ]
    gate, up, down = (weights[:, part * shard : (part + 1) * shard] for part in range(3))
    down = down.reshape(count, shard, -1, width).transpose(0, 2, 1, 3).reshape(tiles, tile, width)
    return [gate.reshape(width, hidden_width), up.reshape(width, hidden_width), down], [
        pl.BlockSpec((width, tile), lambda *j: (0, at(*j))),
        pl.BlockSpec((width, tile), lambda *j: (0, at(*j))),
        pl.BlockSpec((1, tile, width), lambda *j: (at(*j), 0, 0)),
    ]


def feed_forward(device, residual, gain, cotangent, weights, shard, gate_order, up_order):
    rows, width = residual.shape
    count, _, hidden_width = weights.shape
    tiles = 4
    tile = hidden_width // tiles
    owners = count // tiles
    at = lambda j, d: j ^ (d[0] // owners)
    whole = pl.BlockSpec((rows, width), lambda j, d: (0, 0))
    row = pl.BlockSpec((1, width), lambda j, d: (0, 0))
    low = lambda height, size: jax.ShapeDtypeStruct((height, size), jnp.bfloat16)
    low4 = jax.ShapeDtypeStruct((2, tiles, tile // 4, width), jnp.bfloat16)
    weight_args, weight_specs = ffn_operands(weights, shard, width, tiles, at)
    columns = lambda height: pl.BlockSpec((height, tile), lambda j, d: (0, at(j, d)))
    down_half = pl.BlockSpec((2, 1, tile // 4, width), lambda j, d: (0, j, 0, 0))
    *out, down_kept, down_sent = pl.pallas_call(
        functools.partial(feed_forward_body, gate_order=gate_order, up_order=up_order),
        grid_spec=pltpu.PrefetchScalarGridSpec(
            num_scalar_prefetch=1,
            grid=(tiles,),
            in_specs=[whole, row, whole] + weight_specs,
            out_specs=[
                columns(rows),
                columns(rows),
                columns(rows),
                columns(width // 2),
                columns(width // 2),
                columns(width // 2),
                columns(width // 2),
                down_half,
                down_half,
            ],
            scratch_shapes=[
                pltpu.VMEM((rows, width), jnp.bfloat16),
                pltpu.VMEM((tile, width), jnp.bfloat16),
                pltpu.VMEM((width, rows), jnp.bfloat16 if shard % 16 == 0 else jnp.float32),
                pltpu.VMEM((width, rows), jnp.bfloat16),
                pltpu.VMEM((width, rows), jnp.bfloat16),
                pltpu.VMEM((owners, tile // owners, width), jnp.float32),
            ],
        ),
        out_shape=[
            far((rows, hidden_width), jnp.bfloat16),
            far((rows, hidden_width), jnp.bfloat16),
            far((rows, hidden_width), jnp.bfloat16),
            low(width // 2, hidden_width),
            low(width // 2, hidden_width),
            low(width // 2, hidden_width),
            low(width // 2, hidden_width),
            low4,
            low4,
        ],
        compiler_params=pltpu.CompilerParams(vmem_limit_bytes=56 * 1024 * 1024),
        cost_estimate=SMALL,
        name="feed_forward",
    )(device.reshape(1), residual, gain, *from_far(cotangent, *weight_args))
    return *out, down_kept.reshape(-1, width), down_sent.reshape(-1, width)


FFN_STEPS = 4


def back_body(device_ref, *refs, parts):
    (
        residual_ref, gain_ref, cotangent_ref, grad_gate_ref, grad_up_ref, gate_ref, up_ref, turned_out_ref
    ), refs = refs[:8], refs[8:]
    operands, refs = refs[: 11 + parts], refs[11 + parts :]
    (
        grad_residual_ref, grad_low_ref, grad_gain_ref, out_kept_ref, out_sent_ref, kept_ref, sent_ref, head_gains_ref,
        normed_sum_ref, back_ref,
    ), scratch = refs[:10], refs[10:]
    step = pl.program_id(0)
    width = residual_ref.shape[1]

    @pl.when(step == 0)
    def _():
        back_ref[...] = jnp.zeros_like(back_ref)

    @pl.when(step < FFN_STEPS)
    def _():
        back_ref[...] += contract(
            grad_gate_ref[...], gate_ref[...].reshape(width, gate_ref.shape[-1]), 1, 1
        ) + contract(grad_up_ref[...], up_ref[...].reshape(width, up_ref.shape[-1]), 1, 1)

    @pl.when(step == FFN_STEPS - 1)
    def _():
        unit, inverse = unit_head(residual_ref[...])
        grad = back_ref[...]
        grad_gain_ref[...] = jnp.sum(grad * unit, axis=0, keepdims=True)
        scaled = grad * gain_ref[...]
        grad_mid = inverse * (scaled - unit * jnp.mean(scaled * unit, axis=-1, keepdims=True))
        grad_residual = cotangent_ref[...].astype(jnp.float32) + grad_mid
        grad_residual_ref[...] = grad_residual
        grad_low = grad_residual.astype(jnp.bfloat16)
        grad_low_ref[...] = grad_low
        half = out_kept_ref.shape[0]
        for start in range(0, half, 512):
            for ref, shift in ((out_kept_ref, 0), (out_sent_ref, half)):
                rows = slice(start + shift, start + shift + 512)
                ref[start : start + 512, :] = jnp.dot(
                    turned_out_ref[rows, :], grad_low, preferred_element_type=jnp.float32
                ).astype(jnp.bfloat16)

    @pl.when(step >= FFN_STEPS)
    def _():
        attend_back_body(
            device_ref, grad_low_ref, *operands, kept_ref, sent_ref, head_gains_ref, normed_sum_ref, *scratch,
            order=None, shard=None, head_shard=None, last=False, parts=parts, head=step - FFN_STEPS,
        )


def back(device, residual, gain, cotangent, grad_gate, grad_up, weights, shard, turned_out, operands, parts):
    rows, width = residual.shape
    tile = weights.shape[2] // FFN_STEPS
    at = lambda j, d: jnp.minimum(j, FFN_STEPS - 1)
    head = lambda j, d: jnp.maximum(j - FFN_STEPS, 0)
    whole = lambda *shape: pl.BlockSpec(shape, lambda *j: (0, 0))
    columns = pl.BlockSpec((rows, tile), lambda *j: (0, at(*j)))
    weight_args, weight_specs = ffn_operands(weights, shard, width, FFN_STEPS, at)
    out_rows = turned_out.shape[0]
    own_width = KEY_VALUE_HEADS * 2 * HEAD_SIZE
    low = lambda height, size: jax.ShapeDtypeStruct((height, size), jnp.bfloat16)
    wide = far((rows, width), jnp.float32)
    return pl.pallas_call(
        functools.partial(back_body, parts=len(parts)),
        grid_spec=pltpu.PrefetchScalarGridSpec(
            num_scalar_prefetch=1,
            grid=(FFN_STEPS + KEY_VALUE_HEADS // 2,),
            in_specs=[whole(rows, width), whole(1, width), whole(rows, width), columns, columns]
            + weight_specs[:2]
            + [whole(out_rows, rows)]
            + attend_back_specs(rows, width, 0, head, parts),
            out_specs=[
                whole(rows, width),
                whole(rows, width),
                whole(1, width),
                whole(out_rows // 2, width),
                whole(out_rows // 2, width),
                whole(width // 2, own_width),
                whole(width // 2, own_width),
                whole(2, HEAD_SIZE),
                whole(rows, width),
            ],
            scratch_shapes=[pltpu.VMEM((rows, width), jnp.float32)] + attend_back_scratch(rows, parts),
        ),
        out_shape=[
            wide,
            low(rows, width),
            jax.ShapeDtypeStruct((1, width), jnp.float32),
            low(out_rows // 2, width),
            low(out_rows // 2, width),
            low(width // 2, own_width),
            low(width // 2, own_width),
            jax.ShapeDtypeStruct((2, HEAD_SIZE), jnp.float32),
            wide,
        ],
        compiler_params=pltpu.CompilerParams(vmem_limit_bytes=50 * 1024 * 1024),
        cost_estimate=SMALL,
        name="back",
    )(
        device.reshape(1), residual, gain, *from_far(cotangent, grad_gate, grad_up, *weight_args[:2], turned_out), *operands, *parts
    )


def end_body(first_kept, first_came, second_kept, second_came, query_ref, key_ref, value_ref, *gain_refs):
    def part(kept, came, start, size):
        columns = slice(start, start + size)
        return kept[:, columns].astype(jnp.float32) + came[:, columns].astype(jnp.float32)

    group = 0
    for kept, came in ((first_kept, first_came), (second_kept, second_came)):
        for start in range(0, KEY_VALUE_HEADS // 2 * GROUP, GROUP):
            for ref, size in ((query_ref, 2 * HEAD_SIZE), (key_ref, HEAD_SIZE), (value_ref, HEAD_SIZE)):
                ref[:, group * size : (group + 1) * size] = part(kept, came, start, size)
                start += size
            group += 1
    gains = part(second_kept, second_came, KEY_VALUE_HEADS // 2 * GROUP, 128).T
    for index, ref in enumerate(gain_refs):
        ref[...] = gains[index : index + 1, : ref.shape[1]]


def end_projections(first, second, head_shard):
    rows = first[0].shape[0]
    query_width, key_width = QUERY_HEADS * HEAD_SIZE, KEY_VALUE_HEADS * HEAD_SIZE
    return pl.pallas_call(
        end_body,
        out_shape=[
            jax.ShapeDtypeStruct(shape, jnp.float32)
            for shape in (
                (rows, query_width), (rows, key_width), (rows, key_width), (1, rows), (1, rows), (1, head_shard),
                (1, head_shard),
            )
        ],
        cost_estimate=SMALL,
        name="end_projections",
    )(*first, *second)


def on_device(
    tokens,
    seq_lengths,
    seq_owner,
    g_attn,
    w_query,
    key_projection,
    value_projection,
    query_norm_gain,
    g_key,
    w_out,
    g_ffn,
    w_gate,
    w_up,
    w_down,
    cotangent,
):
    row_total_count = tokens.shape[0]
    fence = lax.optimization_barrier
    count = lax.axis_size("fsdp")
    device = lax.axis_index("fsdp")
    early = middle_bits(count, False)
    late = middle_bits(count, True)
    cut_bits = len(early) // 2
    shard = g_attn.shape[0]
    head_shard = query_norm_gain.shape[0]

    ffn_weights = lax.all_gather(stack(w_gate, w_up, w_down), "fsdp", axis=0, tiled=False)
    projections = join(
        w_query, key_projection, value_projection, gain_columns(g_attn, g_ffn, query_norm_gain, g_key, shard)
    )
    top = gather_top(projections, count)
    top, w_out = fence((top, w_out))
    top = gather_top_rest(top, count)
    top, w_out = fence((top, w_out))
    first_part, second_part = lay_top_split(top, device, count, KEY_VALUE_HEADS // 2 * GROUP + 128)
    first_parts = gather_bits({0: first_part}, count, early[:cut_bits])
    second_parts = gather_bits({0: second_part}, count, late[:cut_bits])
    out_top = gather_top(w_out, count)
    seq_id, token_position = layout(seq_lengths, seq_owner, device, row_total_count)
    first_row = (jnp.arange(row_total_count, dtype=jnp.int32) - token_position)[:, None]
    cosine, sine = rotation_factors(token_position)
    first_parts, second_parts, out_top, first_row, cosine, sine = fence(
        (first_parts, second_parts, out_top, first_row, cosine, sine)
    )
    first_parts = gather_bits(first_parts, count, early[cut_bits:])
    second_parts = gather_bits(second_parts, count, late[cut_bits:])
    out_top = gather_top_rest(out_top, count)
    first_parts, second_parts, out_top = fence((first_parts, second_parts, out_top))
    first_parts = gather_bits(first_parts, count, [0])
    out_parts = gather_bits(lay_top(out_top, device, count), count, early[:cut_bits])
    first_parts, second_parts = fence((first_parts, second_parts))
    second_parts = gather_bits(second_parts, count, [0])
    first_weight = weight_parts(first_parts, device, count)

    normed_low, gain_one, gain_two, head_gains = prepare(device, first_weight, tokens, shard, head_shard)
    attended_first, *saved_first = attend(device, normed_low, first_weight, head_gains, cosine, sine, first_row)
    attended_first, second_parts, out_parts = fence((attended_first, second_parts, out_parts))
    out_parts = gather_bits(out_parts, count, early[cut_bits:])
    second_weight = weight_parts(second_parts, device, count)
    attended_second, *saved_second = attend(device, normed_low, second_weight, head_gains, cosine, sine, first_row)
    stages = sum_bits(count)
    orders = {name: row_order(count, bits) for name, bits in stages.items()}
    attended_first, attended_second, out_parts = fence((attended_first, attended_second, out_parts))
    out_parts = gather_bits(out_parts, count, [0])
    residual, out_weight = project(
        device,
        [out_parts[mask] for mask in range(count // 4)],
        tokens,
        attended_first,
        attended_second,
    )
    (
        hidden, grad_gate, grad_up, gate_kept, gate_sent, up_kept, up_sent, down_kept, down_sent
    ) = feed_forward(
        device, residual, gain_two, cotangent, ffn_weights, shard, orders["gate"], orders["up"]
    )

    live = dict(
        hidden=hidden, grad_gate=grad_gate, grad_up=grad_up, gate=gate_kept, up=up_kept, down=down_kept,
    )
    flying = {}

    def cut():
        live.update(fence(dict(live)))

    def fly(**sent):
        live.update({name + "_sent": value for name, value in sent.items()})
        cut()
        for name in sent:
            flying[name] = exchange(live.pop(name + "_sent"), count, 1 << stages[name].pop(0))

    def land(*names):
        live.update({name + "_came": flying.pop(name) for name in names})
        cut()
        flying.update({name: live.pop(name + "_came") for name in names})

    def relay(*names, places=(0, 0, 0, 0, 0, 0)):
        for name, place in zip(names, places):
            live[name], sent = fold((live[name], flying[name], place))
            flying[name] = exchange(sent, count, 1 << stages[name].pop(0))

    def operands(name, saved):
        return *from_far(out_weight, *saved), head_gains, cosine, sine, first_row, *from_far(turned[name])

    live.update(attended_first=attended_first, attended_second=attended_second, normed=normed_low)
    fly(down=down_sent, gate=gate_sent, up=up_sent)
    live["turned"] = dict(
        out=turn((live.pop("attended_first"), live.pop("attended_second")), device, orders["out"]),
        first=turn((live["normed"],), device, orders["first"]),
        second=turn((live.pop("normed"),), device, orders["second"]),
    )
    cut()
    relay("up", "gate", "down")
    cut()
    turned = live.pop("turned")
    (
        live["grad_residual"], live["low"], live["grad_gain_two"], live["out"], live["out_sent"], live["first"],
        live["first_sent"], live["head_sums"], live["normed_sum"],
    ) = back(
        device, residual, gain_two, cotangent, live.pop("grad_gate"), live.pop("grad_up"), ffn_weights, shard,
        turned["out"], operands("first", saved_first), first_weight,
    )
    land("down", "gate", "up")
    fly(first=live["first_sent"], out=live["out_sent"])
    relay("down")
    live["gate"], live["up"], sent = fold(
        (live["gate"], flying["gate"], 0), (live["up"], flying["up"], 0), merged=True
    )
    stages["gate"].pop(0)
    flying["both"] = exchange(sent, count, 1 << stages["up"].pop(0))
    relay("first", "out")
    cut()
    live["second"], live["second_sent"], live["grad_tokens"], live["mixed"] = attend_back_last(
        device, live.pop("low"), operands("second", saved_second), second_weight,
        (live.pop("head_sums"), live.pop("normed_sum")), tokens, gain_one, live.pop("grad_residual"),
        live.pop("grad_gain_two"), residual, live.pop("hidden"), ffn_weights, orders["second"], shard, head_shard,
    )
    land("down", "both")
    land("first", "out")
    fly(second=live["second_sent"])
    relay("second")
    both = flying.pop("both")
    flying.update(gate=both, up=both)
    mixed, grad_tokens = live.pop("mixed"), live.pop("grad_tokens")
    relay("down", "gate", "up", places=(0, 0, 1))
    relay("first", "out")
    relay("down", "gate", "up")
    relay("second")
    cut()
    relay("first", "out", "second")
    cut()
    while any(stages.values()):
        for name in ("second", "first", "out", "down", "gate", "up"):
            if stages[name]:
                relay(name)
    pairs = {name: (live.pop(name), flying.pop(name)) for name in stages}
    sum_down, sum_gate, sum_up, sum_out = (sum_end(pairs[name]) for name in ("down", "gate", "up", "out"))
    first, second = pairs["first"], pairs["second"]
    sum_query, sum_key, sum_value, *sum_gains = end_projections(first, second, head_shard)
    return (
        mixed,
        grad_tokens,
        sum_gains[0].reshape(-1),
        sum_query,
        sum_key,
        sum_value,
        sum_gains[2].reshape(-1),
        sum_gains[3].reshape(-1),
        sum_out,
        sum_gains[1].reshape(-1),
        sum_gate,
        sum_up,
        sum_down,
    )


def solution(mesh):
    return jax.shard_map(
        on_device,
        mesh=mesh,
        in_specs=(
            P("fsdp", None),
            P(),
            P(),
            P("fsdp"),
            P("fsdp", None),
            P("fsdp", None),
            P("fsdp", None),
            P("fsdp"),
            P("fsdp"),
            P("fsdp", None),
            P("fsdp"),
            P("fsdp", None),
            P("fsdp", None),
            P("fsdp", None),
            P("fsdp", None),
        ),
        out_specs=(
            P("fsdp", None),
            P("fsdp", None),
            P("fsdp"),
            P("fsdp", None),
            P("fsdp", None),
            P("fsdp", None),
            P("fsdp"),
            P("fsdp"),
            P("fsdp", None),
            P("fsdp"),
            P("fsdp", None),
            P("fsdp", None),
            P("fsdp", None),
        ),
        check_vma=False,
    )
```

```python
import functools
import math

import jax
import jax.numpy as jnp
from jax import lax
from jax.experimental import pallas as pl
from jax.experimental.pallas import tpu as pltpu
from jax.sharding import PartitionSpec as P

QUERY_HEADS = 16
KEY_VALUE_HEADS = 8
HEAD_SIZE = 128


SMALL = pl.CostEstimate(flops=1, bytes_accessed=1, transcendentals=0)


def far(shape, dtype):
    return pltpu.HBM(tuple(shape), dtype)


def from_far(*values):
    return [pltpu.with_memory_space_constraint(value, pltpu.HBM) for value in values]


epsilon = 1e-06
rope_base = 1000000.0


def layout(seq_lengths, seq_owner, device, row_total_count):
    seq_index = jnp.arange(seq_lengths.shape[0], dtype=jnp.int32)
    same_owner = seq_owner[:, None] == seq_owner[None, :]
    before = seq_index[None, :] < seq_index[:, None]
    starts = jnp.sum(jnp.where(same_owner & before, seq_lengths[None, :], 0), axis=1)
    places = jnp.arange(row_total_count, dtype=jnp.int32)
    member = (
        (seq_owner[None, :] == device)
        & (starts[None, :] <= places[:, None])
        & (places[:, None] < (starts + seq_lengths)[None, :])
    )
    seq_id = jnp.sum(jnp.where(member, seq_index[None, :], 0), axis=1)
    token_position = jnp.sum(jnp.where(member, places[:, None] - starts[None, :], 0), axis=1)
    return (seq_id, token_position)


def rotation_factors(token_position):
    half_width = HEAD_SIZE // 2
    frequency = jnp.exp(
        jnp.arange(half_width, dtype=jnp.float32) * (-2.0 * math.log(rope_base) / HEAD_SIZE)
    )
    angles = token_position.astype(jnp.float32)[:, None] * frequency[None, :]
    cosine = jnp.cos(angles)
    sine = jnp.sin(angles)
    return jnp.concatenate([cosine, cosine], axis=1), jnp.concatenate([-sine, sine], axis=1)


def norm_forward(values, gain):
    inverse = lax.rsqrt(jnp.mean(values * values, axis=-1, keepdims=True) + epsilon)
    unit_rows = values * inverse
    return (unit_rows * gain, unit_rows, inverse)


def exchange(values, count, mask):
    return lax.ppermute(values, "fsdp", [(source, source ^ mask) for source in range(count)])


def middle_bits(count, flip):
    bits = list(range(1, count.bit_length() - 3))
    return bits[::-1] if flip else bits


def sum_bits(count):
    bits = count.bit_length() - 1
    middle = list(range(1, bits - 2))
    low, high = bits - 2, bits - 1
    return dict(
        down=[0, middle[-1], high, low] + middle[-2::-1],
        gate=[0] + middle + [low, high],
        up=[0, low, middle[-1], high] + middle[-2::-1],
        out=[0] + middle + [low, high],
        first=[0, low] + middle[::-1] + [high],
        second=[0] + middle + [low, high],
    )


def row_order(count, sequence):
    bits = len(sequence)
    return [
        sum(((index >> (bits - 1 - step)) & 1) << bit for step, bit in enumerate(sequence)) for index in range(count)
    ]


def turn_body(device_ref, *refs, order):
    values, (out_ref, turned_ref) = refs[:-2], refs[-2:]
    start = 0
    for ref in values:
        turned_ref[start : start + ref.shape[1], :] = ref[...].astype(turned_ref.dtype).T
        start += ref.shape[1]
    device = device_ref[0]
    rows = out_ref.shape[0] // len(order)
    group = max(1, 16 // rows)
    for first in range(0, len(order), group):
        blocks = [
            turned_ref[pl.ds(pl.multiple_of((device ^ mask) * rows, rows), rows), :]
            for mask in order[first : first + group]
        ]
        block = blocks[0] if group == 1 else jnp.concatenate(blocks, axis=0)
        out_ref[first * rows : (first + group) * rows, :] = block.astype(out_ref.dtype)


def turn(values, device, order):
    count = len(order)
    rows = values[0].shape[0]
    columns = sum(value.shape[1] for value in values)
    held = jnp.bfloat16 if columns // count % 16 == 0 else jnp.float32
    return pl.pallas_call(
        functools.partial(turn_body, order=order),
        grid_spec=pltpu.PrefetchScalarGridSpec(
            num_scalar_prefetch=1,
            grid=(1,),
            in_specs=[pl.BlockSpec(value.shape, lambda i, d: (0, 0)) for value in values],
            out_specs=pl.BlockSpec((columns, rows), lambda i, d: (0, 0)),
            scratch_shapes=[pltpu.VMEM((columns, rows), held)],
        ),
        out_shape=far((columns, rows), values[0].dtype),
        compiler_params=pltpu.CompilerParams(vmem_limit_bytes=16 * 1024 * 1024),
        cost_estimate=SMALL,
        name="turn",
    )(device.reshape(1), *values)


def fold_body(*refs, pairs, merged):
    def add(first, second):
        return (first[...].astype(jnp.float32) + second[...].astype(jnp.float32)).astype(jnp.bfloat16)

    out_refs = refs[4 * pairs :]
    start = 0
    for index in range(pairs):
        kept_first, kept_second, came_first, came_second = refs[4 * index : 4 * index + 4]
        sent = add(kept_second, came_second)
        if merged:
            out_refs[pairs][:, start : start + sent.shape[1]] = sent
            start += sent.shape[1]
        else:
            out_refs[pairs + index][...] = sent
        out_refs[index][...] = add(kept_first, came_first)


def fold(*pairs, merged=False):
    halves = [kept.shape[0] // 2 for kept, *_ in pairs]
    steps = next(n for n in (2, 1) if n == 1 or all(rows % (16 * n) == 0 for rows in halves))
    in_specs, out_specs, out_shape, operands = [], [], [], []
    for rows, (kept, came, place) in zip(halves, pairs):
        columns = kept.shape[1]
        spec = lambda shift, place=0, rows=rows, columns=columns: pl.BlockSpec(
            (rows // steps, columns), lambda i: (i + shift, place)
        )
        in_specs += [spec(0), spec(steps), spec(0, place), spec(steps, place)]
        operands += [kept, kept, came, came]
        out_specs += [spec(0)]
        out_shape += [jax.ShapeDtypeStruct((rows, columns), jnp.bfloat16)]
    if merged:
        columns = sum(kept.shape[1] for kept, *_ in pairs)
        sent_specs = [pl.BlockSpec((halves[0] // steps, columns), lambda i: (i, 0))]
        sent_shape = [jax.ShapeDtypeStruct((halves[0], columns), jnp.bfloat16)]
    else:
        sent_specs, sent_shape = list(out_specs), list(out_shape)
    block_bytes = sum(6 * 2 * (rows // steps) * kept.shape[1] for rows, (kept, *_) in zip(halves, pairs))
    return pl.pallas_call(
        functools.partial(fold_body, pairs=len(pairs), merged=merged),
        grid=(steps,),
        in_specs=in_specs,
        out_specs=out_specs + sent_specs,
        out_shape=out_shape + sent_shape,
        compiler_params=pltpu.CompilerParams(vmem_limit_bytes=2 * block_bytes + 6 * 1024 * 1024),
        cost_estimate=SMALL,
        name="fold",
    )(*operands)


def sum_end(pair):
    return pair[0].astype(jnp.float32) + pair[1].astype(jnp.float32)


def place_body(device_ref, *refs):
    parts = refs[:-2]
    out_ref, semaphores = refs[-2:]
    device = device_ref[0]
    copies = [
        pltpu.make_async_copy(part, out_ref.at[:, device ^ mask], semaphores.at[mask])
        for mask, part in enumerate(parts)
    ]
    for copy in copies:
        copy.start()
    for copy in copies:
        copy.wait()


def place(parts, inner):
    top, rows, columns = parts[0].shape
    return pl.pallas_call(
        place_body,
        grid_spec=pltpu.PrefetchScalarGridSpec(
            num_scalar_prefetch=1,
            grid=(1,),
            in_specs=[pl.BlockSpec(memory_space=pl.ANY)] * len(parts),
            out_specs=pl.BlockSpec((top, len(parts), rows, columns), lambda i, d: (0, 0, 0, 0)),
            scratch_shapes=[pltpu.SemaphoreType.DMA((len(parts),))],
        ),
        out_shape=far((top, len(parts), rows, columns), parts[0].dtype)
        if top > 1
        else jax.ShapeDtypeStruct((top, len(parts), rows, columns), parts[0].dtype),
        compiler_params=pltpu.CompilerParams(vmem_limit_bytes=14 * 1024 * 1024),
        cost_estimate=SMALL,
        name="place",
    )(inner.reshape(1), *parts).reshape(top * len(parts) * rows, columns)


def gather_top(block, count):
    return [block, exchange(block, count, count // 4), exchange(block, count, count // 2)]


def gather_top_rest(blocks, count):
    return [block[None] for block in blocks + [exchange(blocks[2], count, count // 4)]]


def stack_body(gate_ref, up_ref, down_ref, out_ref):
    rows = gate_ref.shape[0]
    width = down_ref.shape[1]
    out_ref[:rows, :] = gate_ref[...]
    out_ref[rows : 2 * rows, :] = up_ref[...]
    for piece in range(down_ref.shape[0] // rows):
        columns = slice(piece * width, (piece + 1) * width)
        out_ref[2 * rows :, columns] = down_ref[piece * rows : (piece + 1) * rows, :]


def stack(w_gate, w_up, w_down):
    rows, columns = w_gate.shape
    pieces = w_down.shape[0] // rows
    if rows % 16:
        down = w_down.reshape(pieces, rows, -1).transpose(1, 0, 2).reshape(rows, -1)
        return jnp.concatenate([w_gate, w_up, down], axis=0)
    return pl.pallas_call(
        stack_body,
        out_shape=jax.ShapeDtypeStruct((3 * rows, columns), w_gate.dtype),
        cost_estimate=SMALL,
        name="stack",
    )(w_gate, w_up, w_down)


def join_body(query_ref, key_ref, value_ref, gains_ref, out_ref):
    groups = KEY_VALUE_HEADS
    pair = query_ref.shape[1] // groups
    one = key_ref.shape[1] // groups
    shift = 0
    for group in range(groups):
        for ref, size in ((query_ref, pair), (key_ref, one), (value_ref, one)):
            out_ref[:, shift : shift + size] = ref[:, group * size : (group + 1) * size]
            shift += size
        if group == groups // 2 - 1:
            out_ref[:, shift : shift + 128] = gains_ref[...]
            shift += 128


def join(w_query, key_projection, value_projection, gains):
    rows = w_query.shape[0]
    columns = w_query.shape[1] + 2 * key_projection.shape[1] + 128
    return pl.pallas_call(
        join_body,
        out_shape=jax.ShapeDtypeStruct((rows, columns), w_query.dtype),
        cost_estimate=SMALL,
        name="join",
    )(w_query, key_projection, value_projection, gains)


def lay_top(blocks, device, count):
    return {0: place(from_far(*blocks), device // (count // 4)).reshape((4,) + blocks[0].shape[1:])}


def split_body(device_ref, *refs):
    parts = refs[:4]
    left_ref, right_ref, semaphores = refs[4:]
    width = left_ref.shape[-1]
    copies = []
    for mask, part in enumerate(parts):
        target = device_ref[0] ^ mask
        copies += [
            pltpu.make_async_copy(part.at[:, :width], left_ref.at[target], semaphores.at[2 * mask]),
            pltpu.make_async_copy(part.at[:, width:], right_ref.at[target], semaphores.at[2 * mask + 1]),
        ]
    for copy in copies:
        copy.start()
    for copy in copies:
        copy.wait()


def lay_top_split(blocks, device, count, width):
    rows, columns = blocks[0].shape[1:]
    shapes = [(4, rows, width), (4, rows, columns - width)]
    return pl.pallas_call(
        split_body,
        grid_spec=pltpu.PrefetchScalarGridSpec(
            num_scalar_prefetch=1,
            grid=(1,),
            in_specs=[pl.BlockSpec(memory_space=pl.ANY)] * 4,
            out_specs=[pl.BlockSpec(shape, lambda i, d: (0, 0, 0)) for shape in shapes],
            scratch_shapes=[pltpu.SemaphoreType.DMA((8,))],
        ),
        out_shape=[jax.ShapeDtypeStruct(shape, blocks[0].dtype) for shape in shapes],
        compiler_params=pltpu.CompilerParams(vmem_limit_bytes=10 * 1024 * 1024),
        cost_estimate=SMALL,
        name="lay_top_split",
    )((device // (count // 4)).reshape(1), *from_far(*[block[0] for block in blocks]))


def gather_bits(parts, count, bits):
    parts = dict(parts)
    for bit in bits:
        for mask in list(parts):
            parts[mask | (1 << bit)] = exchange(parts[mask], count, 1 << bit)
    return parts


def lay(parts, device, count):
    return place([parts[mask] for mask in range(count // 4)], device & (count // 4 - 1))


def gain_columns(first, second, third, fourth, rows):
    columns = [jnp.pad(v, (0, rows - v.shape[0]))[:, None] for v in (first, second, third, fourth)]
    return jnp.pad(jnp.concatenate(columns, axis=1), ((0, 0), (0, 124)))


def swap_halves(head):
    return pltpu.roll(head, HEAD_SIZE // 2, 1)


def unit_head(raw):
    inverse = lax.rsqrt(jnp.mean(raw * raw, axis=-1, keepdims=True) + epsilon)
    return raw * inverse, inverse


def contract(left, right, left_axis, right_axis):
    return lax.dot_general(
        left, right, (((left_axis,), (right_axis,)), ((), ())), preferred_element_type=jnp.float32
    )


def block_scores(group, key_rows, first_row, row_start):
    scores = contract(group, key_rows, 1, 1) * (1.0 / math.sqrt(HEAD_SIZE))
    rows = lax.broadcasted_iota(jnp.int32, scores.shape, 0)
    half = scores.shape[0] // 2
    rows = jnp.where(rows >= half, rows - half, rows) + row_start
    columns = lax.broadcasted_iota(jnp.int32, scores.shape, 1)
    return jnp.where((columns <= rows) & (columns >= first_row), scores, -1e30)


def head_pair(ref, block):
    return jnp.concatenate([ref[block, :HEAD_SIZE], ref[block, HEAD_SIZE:]], axis=0)


def pair_rows(first_row_ref, block):
    rows = first_row_ref[block, :]
    return jnp.concatenate([rows, rows], axis=0)


GROUP = 4 * HEAD_SIZE


def weight_parts(parts, device, count):
    if parts[0].shape[1] % 16 == 0:
        return [parts[mask] for mask in range(count // 4)]
    weight = lay(parts, device, count)
    return [weight[None]]


def part_specs(parts, index):
    top, rows, _ = parts[0].shape
    return [pl.BlockSpec((top, rows, GROUP), lambda *j: (0, 0, index(*j))) for _ in parts]


def join_parts(device_ref, part_refs, weight_ref):
    inner = device_ref[0] & (len(part_refs) - 1)
    for mask, ref in enumerate(part_refs):
        weight_ref[:, inner ^ mask] = ref[...]
    top, count, rows, columns = weight_ref.shape
    return weight_ref[...].reshape(top * count * rows, columns)


def prepare_body(device_ref, *refs, shard, head_shard):
    (*part_refs, tokens_ref), (normed_ref, first_gain_ref, second_gain_ref, head_gains_ref, gains_ref) = refs[:-5], refs[-5:]
    lines = join_parts(device_ref, part_refs, gains_ref).astype(jnp.float32).T
    gain = lines[0:1, :]
    first_gain_ref[...] = gain
    second_gain_ref[...] = lines[1:2, :]
    width = lines.shape[1]
    source = lax.broadcasted_iota(jnp.int32, (width, HEAD_SIZE), 0)
    target = lax.broadcasted_iota(jnp.int32, (width, HEAD_SIZE), 1)
    pick = jnp.where(target // head_shard * shard + target % head_shard == source, 1.0, 0.0)
    head_gains_ref[...] = jnp.dot(
        lines[2:4, :], pick, precision=lax.Precision.HIGHEST, preferred_element_type=jnp.float32
    )
    unit, _ = unit_head(tokens_ref[...].astype(jnp.float32))
    normed_ref[...] = (unit * gain).astype(jnp.bfloat16)


def prepare(device, parts, tokens, shard, head_shard):
    rows, width = tokens.shape
    top, part_rows, columns = parts[0].shape
    whole = lambda *shape: pl.BlockSpec(shape, lambda i, d: (0, 0))
    line = jax.ShapeDtypeStruct((1, width), jnp.float32)
    return pl.pallas_call(
        functools.partial(prepare_body, shard=shard, head_shard=head_shard),
        grid_spec=pltpu.PrefetchScalarGridSpec(
            num_scalar_prefetch=1,
            grid=(1,),
            in_specs=[pl.BlockSpec((top, part_rows, 128), lambda i, d: (0, 0, columns // 128 - 1)) for _ in parts]
            + [whole(rows, width)],
            out_specs=[whole(rows, width), whole(1, width), whole(1, width), whole(2, HEAD_SIZE)],
            scratch_shapes=[pltpu.VMEM((top, len(parts), part_rows, 128), jnp.bfloat16)],
        ),
        out_shape=[
            jax.ShapeDtypeStruct((rows, width), jnp.bfloat16),
            line,
            line,
            jax.ShapeDtypeStruct((2, HEAD_SIZE), jnp.float32),
        ],
        compiler_params=pltpu.CompilerParams(vmem_limit_bytes=16 * 1024 * 1024),
        cost_estimate=SMALL,
        name="prepare",
    )(device.reshape(1), *parts, tokens)


def attend_body(device_ref, *refs):
    (*part_refs, normed_ref, gains_ref, cosine_ref, sine_ref, first_ref), out_refs = refs[:-7], refs[-7:]
    attended_ref, query_ref, key_ref, value_ref, raw_ref, total_ref, weight_ref = out_refs
    cosine = cosine_ref[...]
    sine = sine_ref[...]

    def turned(raw, gain):
        scaled = unit_head(raw)[0] * gain
        return (scaled * cosine + swap_halves(scaled) * sine).astype(jnp.bfloat16)

    weight = join_parts(device_ref, part_refs, weight_ref)
    raw = jnp.dot(normed_ref[...], weight, preferred_element_type=jnp.float32)
    raw_ref[...] = raw[:, : 3 * HEAD_SIZE]
    for head in range(2):
        part = slice(head * HEAD_SIZE, (head + 1) * HEAD_SIZE)
        query_ref[:, part] = turned(raw[:, part], gains_ref[0:1, :])
    key_ref[...] = turned(raw[:, 2 * HEAD_SIZE : 3 * HEAD_SIZE], gains_ref[1:2, :])
    value_ref[...] = raw[:, 3 * HEAD_SIZE :].astype(jnp.bfloat16)
    step = 128
    for start in range(0, raw.shape[0], step):
        block = slice(start, start + step)
        seen = slice(0, start + step)
        scores = block_scores(head_pair(query_ref, block), key_ref[seen, :], pair_rows(first_ref, block), start)
        top = jnp.max(scores, axis=-1, keepdims=True)
        log_total = top + jnp.log(jnp.sum(jnp.exp(scores - top), axis=-1, keepdims=True))
        probs_low = jnp.exp(scores - log_total).astype(jnp.bfloat16)
        out = jnp.dot(probs_low, value_ref[seen, :], preferred_element_type=jnp.float32).astype(jnp.bfloat16)
        attended_ref[block, :HEAD_SIZE] = out[:step]
        attended_ref[block, HEAD_SIZE:] = out[step:]
        total_ref[0, block, 0:1] = log_total[:step]
        total_ref[0, block, 1:2] = log_total[step:]


def attend(device, normed, parts, head_gains, cosine, sine, first_row):
    rows, width = normed.shape
    groups = KEY_VALUE_HEADS // 2
    whole = lambda *shape: pl.BlockSpec(shape, lambda h, d: (0, 0))
    columns = lambda size: pl.BlockSpec((rows, size), lambda h, d: (0, h))
    low = lambda size: far((rows, groups * size), jnp.bfloat16)
    pair = 2 * HEAD_SIZE
    return pl.pallas_call(
        attend_body,
        grid_spec=pltpu.PrefetchScalarGridSpec(
            num_scalar_prefetch=1,
            grid=(groups,),
            in_specs=part_specs(parts, lambda h, d: h)
            + [
                whole(rows, width),
                whole(2, HEAD_SIZE),
                whole(rows, HEAD_SIZE),
                whole(rows, HEAD_SIZE),
                whole(rows, 1),
            ],
            out_specs=[
                columns(pair),
                columns(pair),
                columns(HEAD_SIZE),
                columns(HEAD_SIZE),
                columns(3 * HEAD_SIZE),
                pl.BlockSpec((1, rows, 2), lambda h, d: (h, 0, 0)),
            ],
            scratch_shapes=[pltpu.VMEM((parts[0].shape[0], len(parts), parts[0].shape[1], GROUP), jnp.bfloat16)],
        ),
        out_shape=[
            jax.ShapeDtypeStruct((rows, groups * pair), jnp.bfloat16),
            low(pair),
            low(HEAD_SIZE),
            low(HEAD_SIZE),
            far((rows, groups * 3 * HEAD_SIZE), jnp.float32),
            far((groups, rows, 2), jnp.float32),
        ],
        compiler_params=pltpu.CompilerParams(vmem_limit_bytes=26 * 1024 * 1024),
        cost_estimate=SMALL,
        name="attend",
    )(device.reshape(1), *parts, normed, head_gains, cosine, sine, first_row)


def attend_back_body(
    device_ref, residual_ref, wo_ref, query_ref, key_ref, value_ref, raw_ref, total_ref,
    gains_ref, cosine_ref, sine_ref, first_ref, turned_ref, *refs,
    order, shard, head_shard, last, parts, head=None,
):
    part_refs, refs = refs[:parts], refs[parts:]
    if last:
        head_gains_in_ref, normed_in_ref = refs[:2]
        refs = refs[2:]
        tokens_ref, gain_ref, grad_residual_ref, gain_two_ref, hidden_ref, down_ref, ffn_in_ref = refs[:7]
        kept_ref, sent_ref, tokens_out_ref, mixed_ref = refs[7:11]
        head_gains_ref, normed_sum_ref, lines_ref, mixed_sum_ref, down_weight_ref = refs[11:16]
        scratch = refs[16:]
    else:
        kept_ref, sent_ref, head_gains_ref, normed_sum_ref = refs[:4]
        scratch = refs[4:]
    grad_out_ref, query_sum_ref, key_sum_ref, value_sum_ref, grads_ref, weight_ref = scratch
    scale = 1.0 / math.sqrt(HEAD_SIZE)
    heads = KEY_VALUE_HEADS // 2
    if head is None:
        head = pl.program_id(0)

    @pl.when(head == 0)
    def _():
        head_gains_ref[...] = head_gains_in_ref[...] if last else jnp.zeros_like(head_gains_ref)
        normed_sum_ref[...] = normed_in_ref[...] if last else jnp.zeros_like(normed_sum_ref)

    if last:
        gather_down(down_ref, down_weight_ref, down_weight_ref.shape[1])

        @pl.when(head == 0)
        def _():
            mixed_sum_ref[...] = ffn_in_ref[...]

        mixed_sum_ref[...] += jnp.dot(hidden_ref[...], down_weight_ref[...], preferred_element_type=jnp.float32)

        @pl.when(head == heads - 1)
        def _():
            mixed_ref[...] = mixed_sum_ref[...].astype(jnp.bfloat16)

    grad_out_ref[...] = contract(residual_ref[...], wo_ref[...], 1, 1).astype(jnp.bfloat16)
    key_sum_ref[...] = jnp.zeros_like(key_sum_ref)
    value_sum_ref[...] = jnp.zeros_like(value_sum_ref)
    step = 128
    for start in range(0, residual_ref.shape[0], step):
        block = slice(start, start + step)
        seen = slice(0, start + step)
        group = head_pair(query_ref, block)
        grad_out = head_pair(grad_out_ref, block)
        key_rows = key_ref[seen, :]
        scores = block_scores(group, key_rows, pair_rows(first_ref, block), start)
        log_total = jnp.concatenate([total_ref[0, block, 0:1], total_ref[0, block, 1:2]], axis=0)
        probs = jnp.exp(scores - log_total)
        grad_probs = contract(grad_out, value_ref[seen, :], 1, 1)
        value_sum_ref[seen, :] += contract(probs.astype(jnp.bfloat16), grad_out, 0, 0)
        inner = jnp.sum(probs * grad_probs, axis=-1, keepdims=True)
        grad_scores = (probs * (grad_probs - inner)).astype(jnp.bfloat16)
        grad_group = jnp.dot(grad_scores, key_rows, preferred_element_type=jnp.float32) * scale
        query_sum_ref[block, :HEAD_SIZE] = grad_group[:step]
        query_sum_ref[block, HEAD_SIZE:] = grad_group[step:]
        key_sum_ref[seen, :] += contract(grad_scores, group, 0, 0)
    grads_ref[:, 3 * HEAD_SIZE :] = value_sum_ref[...].astype(jnp.bfloat16)
    cosine = cosine_ref[...]
    sine = sine_ref[...]

    def back(grad, part, gain):
        turned = grad * cosine - swap_halves(grad) * sine
        unit, inverse = unit_head(raw_ref[:, part])
        product = turned * unit
        scaled = turned * gain
        grad_raw = inverse * (scaled - unit * jnp.mean(product * gain, axis=-1, keepdims=True))
        grads_ref[:, part] = grad_raw.astype(jnp.bfloat16)
        return jnp.sum(product, axis=0, keepdims=True)

    for index in range(2):
        part = slice(index * HEAD_SIZE, (index + 1) * HEAD_SIZE)
        head_gains_ref[0:1, :] += back(query_sum_ref[:, part], part, gains_ref[0:1, :])
    part = slice(2 * HEAD_SIZE, 3 * HEAD_SIZE)
    head_gains_ref[1:2, :] += back(key_sum_ref[...] * scale, part, gains_ref[1:2, :])

    grads = grads_ref[...]
    half = turned_ref.shape[0] // 2
    product = jnp.dot(turned_ref[...], grads, preferred_element_type=jnp.float32).astype(jnp.bfloat16)
    columns = pl.ds(pl.multiple_of(head * GROUP, GROUP), GROUP)
    kept_ref[:, columns] = product[:half]
    sent_ref[:, columns] = product[half:]
    normed_sum_ref[...] += contract(grads, join_parts(device_ref, part_refs, weight_ref), 1, 1)

    if not last:
        return

    @pl.when(head == heads - 1)
    def _():
        unit, inverse = unit_head(tokens_ref[...].astype(jnp.float32))
        grad = normed_sum_ref[...]
        scaled = grad * gain_ref[...]
        grad_first = inverse * (scaled - unit * jnp.mean(scaled * unit, axis=-1, keepdims=True))
        tokens_out_ref[...] = (grad_residual_ref[...] + grad_first).astype(jnp.bfloat16)
        width = grad.shape[1]
        source = lax.broadcasted_iota(jnp.int32, (HEAD_SIZE, width), 0)
        target = lax.broadcasted_iota(jnp.int32, (HEAD_SIZE, width), 1)
        spread = jnp.where(source // head_shard * shard + source % head_shard == target, 1.0, 0.0)
        heads = jnp.dot(
            head_gains_ref[...], spread, precision=lax.Precision.HIGHEST, preferred_element_type=jnp.float32
        )
        lines = jnp.concatenate(
            [
                jnp.sum(grad * unit, axis=0, keepdims=True),
                gain_two_ref[...],
                heads,
                jnp.zeros((124, width), jnp.float32),
            ],
            axis=0,
        )
        lines_ref[...] = lines.T
        device = device_ref[0]
        group = max(1, 16 // shard)
        end = slice(kept_ref.shape[1] - 128, None)
        for first in range(0, len(order), group):
            blocks = [
                lines_ref[pl.ds(pl.multiple_of((device ^ mask) * shard, shard), shard), :]
                for mask in order[first : first + group]
            ]
            block = (blocks[0] if group == 1 else jnp.concatenate(blocks, axis=0)).astype(jnp.bfloat16)
            row = first * shard
            target_ref = kept_ref if row < half else sent_ref
            target_ref[row % half : row % half + group * shard, end] = block


def attend_back_specs(rows, width, part, head, parts):
    first = part * KEY_VALUE_HEADS // 2
    whole = lambda *shape: pl.BlockSpec(shape, lambda *j: (0, 0))
    columns = lambda height, size: pl.BlockSpec((height, size), lambda *j: (0, head(*j)))
    pair = 2 * HEAD_SIZE
    return [
        pl.BlockSpec((pair, width), lambda *j: (head(*j) + first, 0)),
        columns(rows, pair),
        columns(rows, HEAD_SIZE),
        columns(rows, HEAD_SIZE),
        columns(rows, 3 * HEAD_SIZE),
        pl.BlockSpec((1, rows, 2), lambda *j: (head(*j), 0, 0)),
        whole(2, HEAD_SIZE),
        whole(rows, HEAD_SIZE),
        whole(rows, HEAD_SIZE),
        whole(rows, 1),
        whole(width, rows),
    ] + part_specs(parts, head)


def attend_back_scratch(rows, parts):
    pair = 2 * HEAD_SIZE
    return [
        pltpu.VMEM((rows, pair), jnp.bfloat16),
        pltpu.VMEM((rows, pair), jnp.float32),
        pltpu.VMEM((rows, HEAD_SIZE), jnp.float32),
        pltpu.VMEM((rows, HEAD_SIZE), jnp.float32),
        pltpu.VMEM((rows, GROUP), jnp.bfloat16),
        pltpu.VMEM((parts[0].shape[0], len(parts), parts[0].shape[1], GROUP), jnp.bfloat16),
    ]


def attend_back_last(
    device, residual_low, operands, parts, sums, tokens, gain, grad_residual, grad_gain_two, ffn_in, hidden, weights,
    order, shard, head_shard,
):
    rows, width = residual_low.shape
    whole = lambda *shape: pl.BlockSpec(shape, lambda *j: (0, 0))
    own_width = KEY_VALUE_HEADS * 2 * HEAD_SIZE + 128
    half = jax.ShapeDtypeStruct((width // 2, own_width), jnp.bfloat16)
    low = jax.ShapeDtypeStruct((rows, width), jnp.bfloat16)
    tiles = KEY_VALUE_HEADS // 2
    tile = weights.shape[2] // tiles
    weight_args, weight_specs = ffn_operands(weights, shard, width, tiles, lambda h, d: h)
    return pl.pallas_call(
        functools.partial(
            attend_back_body, order=order, shard=shard, head_shard=head_shard, last=True, parts=len(parts)
        ),
        grid_spec=pltpu.PrefetchScalarGridSpec(
            num_scalar_prefetch=1,
            grid=(KEY_VALUE_HEADS // 2,),
            in_specs=[whole(rows, width)]
            + attend_back_specs(rows, width, 1, lambda h, d: h, parts)
            + [whole(2, HEAD_SIZE), whole(rows, width)]
            + [whole(rows, width), whole(1, width), whole(rows, width), whole(1, width)]
            + [pl.BlockSpec((rows, tile), lambda h, d: (0, h)), weight_specs[2], whole(rows, width)],
            out_specs=[
                whole(width // 2, own_width), whole(width // 2, own_width), whole(rows, width), whole(rows, width)
            ],
            scratch_shapes=[
                pltpu.VMEM((2, HEAD_SIZE), jnp.float32),
                pltpu.VMEM((rows, width), jnp.float32),
                pltpu.VMEM((width, 128), jnp.float32),
                pltpu.VMEM((rows, width), jnp.float32),
                pltpu.VMEM((tile, width), jnp.bfloat16),
            ]
            + attend_back_scratch(rows, parts),
        ),
        out_shape=[half, half, low, low],
        compiler_params=pltpu.CompilerParams(vmem_limit_bytes=46 * 1024 * 1024),
        cost_estimate=SMALL,
        name="attend_back_last",
    )(
        device.reshape(1), residual_low, *operands, *parts, sums[0], *from_far(sums[1], tokens), gain, *from_far(grad_residual),
        grad_gain_two, *from_far(hidden, weight_args[2], ffn_in),
    )


def project_body(device_ref, *refs, top_steps):
    (*part_refs, tokens_ref, first_ref, second_ref), (residual_ref, weight_out_ref) = refs[:-2], refs[-2:]
    inner = device_ref[0] & (len(part_refs) - 1)

    @pl.when(pl.program_id(0) == 0)
    def _():
        residual_ref[...] = tokens_ref[...].astype(jnp.float32)

    for mask, ref in enumerate(part_refs):
        weight_out_ref[:, inner ^ mask] = ref[...]
    top, count, rows, columns = weight_out_ref.shape
    weight = weight_out_ref[...].reshape(top * count * rows, columns)
    for ref, part in ((first_ref, 0), (second_ref, 1)):

        @pl.when(pl.program_id(0) // (top_steps // 2) == part)
        def _():
            residual_ref[...] += jnp.dot(ref[...], weight, preferred_element_type=jnp.float32)


def project(device, parts, tokens, first, second):
    rows, width = tokens.shape
    top, part_rows, _ = parts[0].shape
    step_rows = len(parts) * part_rows
    whole = pl.BlockSpec((rows, width), lambda j, d: (0, 0))
    residual, weight = pl.pallas_call(
        functools.partial(project_body, top_steps=top),
        grid_spec=pltpu.PrefetchScalarGridSpec(
            num_scalar_prefetch=1,
            grid=(top,),
            in_specs=[pl.BlockSpec((1, part_rows, width), lambda j, d: (j, 0, 0)) for _ in parts]
            + [
                whole,
                pl.BlockSpec((rows, step_rows), lambda j, d: (0, jnp.minimum(j, top // 2 - 1))),
                pl.BlockSpec((rows, step_rows), lambda j, d: (0, jnp.maximum(j - top // 2, 0))),
            ],
            out_specs=[whole, pl.BlockSpec((1, len(parts), part_rows, width), lambda j, d: (j, 0, 0, 0))],
        ),
        out_shape=[
            far((rows, width), jnp.float32),
            far((top, len(parts), part_rows, width), jnp.bfloat16),
        ],
        compiler_params=pltpu.CompilerParams(vmem_limit_bytes=20 * 1024 * 1024),
        cost_estimate=SMALL,
        name="project",
    )(device.reshape(1), *parts, tokens, first, second)
    return residual, weight.reshape(top * step_rows, width)


def gather_down(down_ref, down_weight_ref, width):
    devices, rows, _ = down_ref.shape
    pieces = down_ref.shape[2] // width
    for index in range(devices):
        for piece in range(pieces):
            first = (index * pieces + piece) * rows
            down_weight_ref[first : first + rows, :] = down_ref[index, :, piece * width : (piece + 1) * width]


def feed_forward_body(
    device_ref, residual_ref, gain_ref, cotangent_ref, gate_ref, up_ref, down_ref,
    hidden_ref, grad_gate_ref, grad_up_ref, gate_kept_ref, gate_sent_ref, for_up_ref,
    down_kept_ref, down_sent_ref, normed_ref, down_weight_ref, turned_ref, for_gate_ref, product_ref,
    *, gate_order, up_order,
):
    device = device_ref[0]
    width = residual_ref.shape[1]

    @pl.when(pl.program_id(0) == 0)
    def _():
        unit, _ = unit_head(residual_ref[...])
        normed = (unit * gain_ref[...]).astype(jnp.bfloat16)
        normed_ref[...] = normed
        turned_ref[...] = normed.astype(turned_ref.dtype).T
        rows = width // len(gate_order)
        group = max(1, 16 // rows)
        for order, ref in ((gate_order, for_gate_ref), (up_order, for_up_ref)):
            for first in range(0, len(order), group):
                blocks = [
                    turned_ref[pl.ds(pl.multiple_of((device ^ mask) * rows, rows), rows), :]
                    for mask in order[first : first + group]
                ]
                block = blocks[0] if group == 1 else jnp.concatenate(blocks, axis=0)
                ref[first * rows : (first + group) * rows, :] = block.astype(jnp.bfloat16)

    normed = normed_ref[...]
    gather_down(down_ref, down_weight_ref, width)
    cotangent = cotangent_ref[...]
    gate = jnp.dot(normed, gate_ref[...].reshape(width, gate_ref.shape[-1]), preferred_element_type=jnp.float32)
    up = jnp.dot(normed, up_ref[...].reshape(width, up_ref.shape[-1]), preferred_element_type=jnp.float32)
    grad_hidden = contract(cotangent, down_weight_ref[...], 1, 1)
    sigmoid = jax.nn.sigmoid(gate)
    silu = gate * sigmoid
    hidden = (silu * up).astype(jnp.bfloat16)
    grad_gate = (grad_hidden * up * sigmoid * (1.0 + gate * (1.0 - sigmoid))).astype(jnp.bfloat16)
    hidden_ref[...] = hidden
    grad_gate_ref[...] = grad_gate
    grad_up = (grad_hidden * silu).astype(jnp.bfloat16)
    grad_up_ref[...] = grad_up

    product = jnp.dot(for_gate_ref[...], grad_gate, preferred_element_type=jnp.float32).astype(jnp.bfloat16)
    half = product.shape[0] // 2
    gate_kept_ref[...] = product[:half]
    gate_sent_ref[...] = product[half:]
    product_ref[...] = contract(hidden, cotangent, 0, 0).reshape(product_ref.shape)
    owners = product_ref.shape[0]
    low = device & (owners - 1)
    for target, core in ((down_kept_ref, 0), (down_sent_ref, 1)):
        blocks = [product_ref[low ^ (index | core)] for index in range(0, owners, 2)]
        target[...] = jnp.concatenate(blocks, axis=0).astype(jnp.bfloat16).reshape(target.shape)


def ffn_operands(weights, shard, width, tiles, at):
    count, _, hidden_width = weights.shape
    tile = hidden_width // tiles
    if shard % 16 == 0:
        return [weights, weights, weights], [
            pl.BlockSpec((count, shard, tile), lambda *j: (0, 0, at(*j))),
            pl.BlockSpec((count, shard, tile), lambda *j: (0, 1, at(*j))),
            pl.BlockSpec((count // tiles, shard, hidden_width), lambda *j: (at(*j), 2, 0)),
        ]
    gate, up, down = (weights[:, part * shard : (part + 1) * shard] for part in range(3))
    down = down.reshape(count, shard, -1, width).transpose(0, 2, 1, 3).reshape(tiles, tile, width)
    return [gate.reshape(width, hidden_width), up.reshape(width, hidden_width), down], [
        pl.BlockSpec((width, tile), lambda *j: (0, at(*j))),
        pl.BlockSpec((width, tile), lambda *j: (0, at(*j))),
        pl.BlockSpec((1, tile, width), lambda *j: (at(*j), 0, 0)),
    ]


def feed_forward(device, residual, gain, cotangent, weights, shard, gate_order, up_order):
    rows, width = residual.shape
    count, _, hidden_width = weights.shape
    tiles = 4
    tile = hidden_width // tiles
    owners = count // tiles
    at = lambda j, d: j ^ (d[0] // owners)
    whole = pl.BlockSpec((rows, width), lambda j, d: (0, 0))
    row = pl.BlockSpec((1, width), lambda j, d: (0, 0))
    low = lambda height, size: jax.ShapeDtypeStruct((height, size), jnp.bfloat16)
    low4 = jax.ShapeDtypeStruct((2, tiles, tile // 4, width), jnp.bfloat16)
    weight_args, weight_specs = ffn_operands(weights, shard, width, tiles, at)
    columns = lambda height: pl.BlockSpec((height, tile), lambda j, d: (0, at(j, d)))
    down_half = pl.BlockSpec((2, 1, tile // 4, width), lambda j, d: (0, j, 0, 0))
    *out, down_kept, down_sent = pl.pallas_call(
        functools.partial(feed_forward_body, gate_order=gate_order, up_order=up_order),
        grid_spec=pltpu.PrefetchScalarGridSpec(
            num_scalar_prefetch=1,
            grid=(tiles,),
            in_specs=[whole, row, whole] + weight_specs,
            out_specs=[
                columns(rows),
                columns(rows),
                columns(rows),
                columns(width // 2),
                columns(width // 2),
                pl.BlockSpec((width, rows), lambda j, d: (0, 0)),
                down_half,
                down_half,
            ],
            scratch_shapes=[
                pltpu.VMEM((rows, width), jnp.bfloat16),
                pltpu.VMEM((tile, width), jnp.bfloat16),
                pltpu.VMEM((width, rows), jnp.bfloat16 if shard % 16 == 0 else jnp.float32),
                pltpu.VMEM((width, rows), jnp.bfloat16),
                pltpu.VMEM((owners, tile // owners, width), jnp.float32),
            ],
        ),
        out_shape=[
            far((rows, hidden_width), jnp.bfloat16),
            far((rows, hidden_width), jnp.bfloat16),
            far((rows, hidden_width), jnp.bfloat16),
            low(width // 2, hidden_width),
            low(width // 2, hidden_width),
            low(width, rows),
            low4,
            low4,
        ],
        compiler_params=pltpu.CompilerParams(vmem_limit_bytes=56 * 1024 * 1024),
        cost_estimate=SMALL,
        name="feed_forward",
    )(device.reshape(1), residual, gain, *from_far(cotangent, *weight_args))
    return *out, down_kept.reshape(-1, width), down_sent.reshape(-1, width)


def product_body(left_ref, right_ref, kept_ref, sent_ref):
    product = jnp.dot(left_ref[...], right_ref[...], preferred_element_type=jnp.float32).astype(jnp.bfloat16)
    half = product.shape[0] // 2
    kept_ref[...] = product[:half]
    sent_ref[...] = product[half:]


def product_halves(left, right):
    rows, depth = left.shape
    columns = right.shape[1]
    tile = min(columns, 768)
    half = jax.ShapeDtypeStruct((rows // 2, columns), jnp.bfloat16)
    return pl.pallas_call(
        product_body,
        grid=(columns // tile,),
        in_specs=[pl.BlockSpec((rows, depth), lambda j: (0, 0)), pl.BlockSpec((depth, tile), lambda j: (0, j))],
        out_specs=[pl.BlockSpec((rows // 2, tile), lambda j: (0, j))] * 2,
        out_shape=[half, half],
        compiler_params=pltpu.CompilerParams(vmem_limit_bytes=20 * 1024 * 1024),
        cost_estimate=SMALL,
        name="product_halves",
    )(left, right)


FFN_STEPS = 4


def back_body(device_ref, *refs, parts):
    (
        residual_ref, gain_ref, cotangent_ref, grad_gate_ref, grad_up_ref, gate_ref, up_ref, turned_out_ref
    ), refs = refs[:8], refs[8:]
    operands, refs = refs[: 11 + parts], refs[11 + parts :]
    (
        grad_residual_ref, grad_low_ref, grad_gain_ref, out_kept_ref, out_sent_ref, kept_ref, sent_ref, head_gains_ref,
        normed_sum_ref, back_ref,
    ), scratch = refs[:10], refs[10:]
    step = pl.program_id(0)
    width = residual_ref.shape[1]

    @pl.when(step == 0)
    def _():
        back_ref[...] = jnp.zeros_like(back_ref)

    @pl.when(step < FFN_STEPS)
    def _():
        back_ref[...] += contract(
            grad_gate_ref[...], gate_ref[...].reshape(width, gate_ref.shape[-1]), 1, 1
        ) + contract(grad_up_ref[...], up_ref[...].reshape(width, up_ref.shape[-1]), 1, 1)

    @pl.when(step == FFN_STEPS - 1)
    def _():
        unit, inverse = unit_head(residual_ref[...])
        grad = back_ref[...]
        grad_gain_ref[...] = jnp.sum(grad * unit, axis=0, keepdims=True)
        scaled = grad * gain_ref[...]
        grad_mid = inverse * (scaled - unit * jnp.mean(scaled * unit, axis=-1, keepdims=True))
        grad_residual = cotangent_ref[...].astype(jnp.float32) + grad_mid
        grad_residual_ref[...] = grad_residual
        grad_low = grad_residual.astype(jnp.bfloat16)
        grad_low_ref[...] = grad_low
        half = out_kept_ref.shape[0]
        for start in range(0, half, 512):
            for ref, shift in ((out_kept_ref, 0), (out_sent_ref, half)):
                rows = slice(start + shift, start + shift + 512)
                ref[start : start + 512, :] = jnp.dot(
                    turned_out_ref[rows, :], grad_low, preferred_element_type=jnp.float32
                ).astype(jnp.bfloat16)

    @pl.when(step >= FFN_STEPS)
    def _():
        attend_back_body(
            device_ref, grad_low_ref, *operands, kept_ref, sent_ref, head_gains_ref, normed_sum_ref, *scratch,
            order=None, shard=None, head_shard=None, last=False, parts=parts, head=step - FFN_STEPS,
        )


def back(device, residual, gain, cotangent, grad_gate, grad_up, weights, shard, turned_out, operands, parts):
    rows, width = residual.shape
    tile = weights.shape[2] // FFN_STEPS
    at = lambda j, d: jnp.minimum(j, FFN_STEPS - 1)
    head = lambda j, d: jnp.maximum(j - FFN_STEPS, 0)
    whole = lambda *shape: pl.BlockSpec(shape, lambda *j: (0, 0))
    columns = pl.BlockSpec((rows, tile), lambda *j: (0, at(*j)))
    weight_args, weight_specs = ffn_operands(weights, shard, width, FFN_STEPS, at)
    out_rows = turned_out.shape[0]
    own_width = KEY_VALUE_HEADS * 2 * HEAD_SIZE
    low = lambda height, size: jax.ShapeDtypeStruct((height, size), jnp.bfloat16)
    wide = far((rows, width), jnp.float32)
    return pl.pallas_call(
        functools.partial(back_body, parts=len(parts)),
        grid_spec=pltpu.PrefetchScalarGridSpec(
            num_scalar_prefetch=1,
            grid=(FFN_STEPS + KEY_VALUE_HEADS // 2,),
            in_specs=[whole(rows, width), whole(1, width), whole(rows, width), columns, columns]
            + weight_specs[:2]
            + [whole(out_rows, rows)]
            + attend_back_specs(rows, width, 0, head, parts),
            out_specs=[
                whole(rows, width),
                whole(rows, width),
                whole(1, width),
                whole(out_rows // 2, width),
                whole(out_rows // 2, width),
                whole(width // 2, own_width),
                whole(width // 2, own_width),
                whole(2, HEAD_SIZE),
                whole(rows, width),
            ],
            scratch_shapes=[pltpu.VMEM((rows, width), jnp.float32)] + attend_back_scratch(rows, parts),
        ),
        out_shape=[
            wide,
            low(rows, width),
            jax.ShapeDtypeStruct((1, width), jnp.float32),
            low(out_rows // 2, width),
            low(out_rows // 2, width),
            low(width // 2, own_width),
            low(width // 2, own_width),
            jax.ShapeDtypeStruct((2, HEAD_SIZE), jnp.float32),
            wide,
        ],
        compiler_params=pltpu.CompilerParams(vmem_limit_bytes=50 * 1024 * 1024),
        cost_estimate=SMALL,
        name="back",
    )(
        device.reshape(1), residual, gain, *from_far(cotangent, grad_gate, grad_up, *weight_args[:2], turned_out), *operands, *parts
    )


def end_body(first_kept, first_came, second_kept, second_came, query_ref, key_ref, value_ref, *gain_refs):
    def part(kept, came, start, size):
        columns = slice(start, start + size)
        return kept[:, columns].astype(jnp.float32) + came[:, columns].astype(jnp.float32)

    group = 0
    for kept, came in ((first_kept, first_came), (second_kept, second_came)):
        for start in range(0, KEY_VALUE_HEADS // 2 * GROUP, GROUP):
            for ref, size in ((query_ref, 2 * HEAD_SIZE), (key_ref, HEAD_SIZE), (value_ref, HEAD_SIZE)):
                ref[:, group * size : (group + 1) * size] = part(kept, came, start, size)
                start += size
            group += 1
    gains = part(second_kept, second_came, KEY_VALUE_HEADS // 2 * GROUP, 128).T
    for index, ref in enumerate(gain_refs):
        ref[...] = gains[index : index + 1, : ref.shape[1]]


def end_projections(first, second, head_shard):
    rows = first[0].shape[0]
    query_width, key_width = QUERY_HEADS * HEAD_SIZE, KEY_VALUE_HEADS * HEAD_SIZE
    return pl.pallas_call(
        end_body,
        out_shape=[
            jax.ShapeDtypeStruct(shape, jnp.float32)
            for shape in (
                (rows, query_width), (rows, key_width), (rows, key_width), (1, rows), (1, rows), (1, head_shard),
                (1, head_shard),
            )
        ],
        cost_estimate=SMALL,
        name="end_projections",
    )(*first, *second)


def on_device(
    tokens,
    seq_lengths,
    seq_owner,
    g_attn,
    w_query,
    key_projection,
    value_projection,
    query_norm_gain,
    g_key,
    w_out,
    g_ffn,
    w_gate,
    w_up,
    w_down,
    cotangent,
):
    row_total_count = tokens.shape[0]
    fence = lax.optimization_barrier
    count = lax.axis_size("fsdp")
    device = lax.axis_index("fsdp")
    early = middle_bits(count, False)
    late = middle_bits(count, True)
    cut_bits = len(early) // 2
    shard = g_attn.shape[0]
    head_shard = query_norm_gain.shape[0]

    ffn_weights = lax.all_gather(stack(w_gate, w_up, w_down), "fsdp", axis=0, tiled=False)
    projections = join(
        w_query, key_projection, value_projection, gain_columns(g_attn, g_ffn, query_norm_gain, g_key, shard)
    )
    top = gather_top(projections, count)
    top, w_out = fence((top, w_out))
    top = gather_top_rest(top, count)
    top, w_out = fence((top, w_out))
    first_part, second_part = lay_top_split(top, device, count, KEY_VALUE_HEADS // 2 * GROUP + 128)
    first_parts = gather_bits({0: first_part}, count, early[:cut_bits])
    second_parts = gather_bits({0: second_part}, count, late[:cut_bits])
    out_top = gather_top(w_out, count)
    seq_id, token_position = layout(seq_lengths, seq_owner, device, row_total_count)
    first_row = (jnp.arange(row_total_count, dtype=jnp.int32) - token_position)[:, None]
    cosine, sine = rotation_factors(token_position)
    first_parts, second_parts, out_top, first_row, cosine, sine = fence(
        (first_parts, second_parts, out_top, first_row, cosine, sine)
    )
    first_parts = gather_bits(first_parts, count, early[cut_bits:])
    second_parts = gather_bits(second_parts, count, late[cut_bits:])
    out_top = gather_top_rest(out_top, count)
    first_parts, second_parts, out_top = fence((first_parts, second_parts, out_top))
    first_parts = gather_bits(first_parts, count, [0])
    out_parts = gather_bits(lay_top(out_top, device, count), count, early[:cut_bits])
    first_parts, second_parts = fence((first_parts, second_parts))
    second_parts = gather_bits(second_parts, count, [0])
    first_weight = weight_parts(first_parts, device, count)

    normed_low, gain_one, gain_two, head_gains = prepare(device, first_weight, tokens, shard, head_shard)
    attended_first, *saved_first = attend(device, normed_low, first_weight, head_gains, cosine, sine, first_row)
    attended_first, second_parts, out_parts = fence((attended_first, second_parts, out_parts))
    out_parts = gather_bits(out_parts, count, early[cut_bits:])
    second_weight = weight_parts(second_parts, device, count)
    attended_second, *saved_second = attend(device, normed_low, second_weight, head_gains, cosine, sine, first_row)
    stages = sum_bits(count)
    orders = {name: row_order(count, bits) for name, bits in stages.items()}
    turned = dict(
        out=turn((attended_first, attended_second), device, orders["out"]),
        first=turn((normed_low,), device, orders["first"]),
        second=turn((normed_low,), device, orders["second"]),
    )
    attended_first, attended_second, out_parts, turned = fence((attended_first, attended_second, out_parts, turned))
    out_parts = gather_bits(out_parts, count, [0])
    residual, out_weight = project(
        device,
        [out_parts[mask] for mask in range(count // 4)],
        tokens,
        attended_first,
        attended_second,
    )
    (
        hidden, grad_gate, grad_up, gate_kept, gate_sent, turned_up, down_kept, down_sent
    ) = feed_forward(
        device, residual, gain_two, cotangent, ffn_weights, shard, orders["gate"], orders["up"]
    )

    live = dict(
        hidden=hidden, grad_gate=grad_gate, grad_up=grad_up, gate=gate_kept, down=down_kept, turned_up=turned_up,
    )
    flying = {}

    def cut():
        live.update(fence(dict(live)))

    def fly(**sent):
        live.update({name + "_sent": value for name, value in sent.items()})
        cut()
        for name in sent:
            flying[name] = exchange(live.pop(name + "_sent"), count, 1 << stages[name].pop(0))

    def land(*names):
        live.update({name + "_came": flying.pop(name) for name in names})
        cut()
        flying.update({name: live.pop(name + "_came") for name in names})

    def relay(*names, places=(0, 0, 0, 0, 0, 0)):
        for name, place in zip(names, places):
            live[name], sent = fold((live[name], flying[name], place))
            flying[name] = exchange(sent, count, 1 << stages[name].pop(0))

    def operands(name, saved):
        return *from_far(out_weight, *saved), head_gains, cosine, sine, first_row, *from_far(turned[name])

    live["turned"] = turned
    fly(down=down_sent, gate=gate_sent)
    live["up"], up_sent = product_halves(live.pop("turned_up"), live["grad_up"])
    fly(up=up_sent)
    relay("down", "gate", "up")
    cut()
    turned = live.pop("turned")
    (
        live["grad_residual"], live["low"], live["grad_gain_two"], live["out"], live["out_sent"], live["first"],
        live["first_sent"], live["head_sums"], live["normed_sum"],
    ) = back(
        device, residual, gain_two, cotangent, live.pop("grad_gate"), live.pop("grad_up"), ffn_weights, shard,
        turned["out"], operands("first", saved_first), first_weight,
    )
    land("down", "gate", "up")
    fly(first=live["first_sent"], out=live["out_sent"])
    relay("down")
    live["gate"], live["up"], sent = fold(
        (live["gate"], flying["gate"], 0), (live["up"], flying["up"], 0), merged=True
    )
    stages["gate"].pop(0)
    flying["both"] = exchange(sent, count, 1 << stages["up"].pop(0))
    relay("first", "out")
    cut()
    live["second"], live["second_sent"], live["grad_tokens"], live["mixed"] = attend_back_last(
        device, live.pop("low"), operands("second", saved_second), second_weight,
        (live.pop("head_sums"), live.pop("normed_sum")), tokens, gain_one, live.pop("grad_residual"),
        live.pop("grad_gain_two"), residual, live.pop("hidden"), ffn_weights, orders["second"], shard, head_shard,
    )
    land("down", "both")
    land("first", "out")
    fly(second=live["second_sent"])
    relay("second")
    both = flying.pop("both")
    flying.update(gate=both, up=both)
    mixed, grad_tokens = live.pop("mixed"), live.pop("grad_tokens")
    relay("up", "gate", places=(1, 0))
    relay("first", "out")
    relay("up", "gate")
    relay("second")
    relay("down")
    cut()
    while any(stages.values()):
        for name in ("second", "first", "out", "down", "gate", "up"):
            if stages[name]:
                relay(name)
    pairs = {name: (live.pop(name), flying.pop(name)) for name in stages}
    sum_down, sum_gate, sum_up, sum_out = (sum_end(pairs[name]) for name in ("down", "gate", "up", "out"))
    first, second = pairs["first"], pairs["second"]
    sum_query, sum_key, sum_value, *sum_gains = end_projections(first, second, head_shard)
    return (
        mixed,
        grad_tokens,
        sum_gains[0].reshape(-1),
        sum_query,
        sum_key,
        sum_value,
        sum_gains[2].reshape(-1),
        sum_gains[3].reshape(-1),
        sum_out,
        sum_gains[1].reshape(-1),
        sum_gate,
        sum_up,
        sum_down,
    )


def solution(mesh):
    return jax.shard_map(
        on_device,
        mesh=mesh,
        in_specs=(
            P("fsdp", None),
            P(),
            P(),
            P("fsdp"),
            P("fsdp", None),
            P("fsdp", None),
            P("fsdp", None),
            P("fsdp"),
            P("fsdp"),
            P("fsdp", None),
            P("fsdp"),
            P("fsdp", None),
            P("fsdp", None),
            P("fsdp", None),
            P("fsdp", None),
        ),
        out_specs=(
            P("fsdp", None),
            P("fsdp", None),
            P("fsdp"),
            P("fsdp", None),
            P("fsdp", None),
            P("fsdp", None),
            P("fsdp"),
            P("fsdp"),
            P("fsdp", None),
            P("fsdp"),
            P("fsdp", None),
            P("fsdp", None),
            P("fsdp", None),
        ),
        check_vma=False,
    )
```

```python
import functools
import math

import jax
import jax.numpy as jnp
from jax import lax
from jax.experimental import pallas as pl
from jax.experimental.pallas import tpu as pltpu
from jax.sharding import PartitionSpec as P

QUERY_HEADS = 16
KEY_VALUE_HEADS = 8
HEAD_SIZE = 128


SMALL = pl.CostEstimate(flops=1, bytes_accessed=1, transcendentals=0)


def far(shape, dtype):
    return pltpu.HBM(tuple(shape), dtype)


def from_far(*values):
    return [pltpu.with_memory_space_constraint(value, pltpu.HBM) for value in values]


epsilon = 1e-06
rope_base = 1000000.0


def layout(seq_lengths, seq_owner, device, row_total_count):
    seq_index = jnp.arange(seq_lengths.shape[0], dtype=jnp.int32)
    same_owner = seq_owner[:, None] == seq_owner[None, :]
    before = seq_index[None, :] < seq_index[:, None]
    starts = jnp.sum(jnp.where(same_owner & before, seq_lengths[None, :], 0), axis=1)
    places = jnp.arange(row_total_count, dtype=jnp.int32)
    member = (
        (seq_owner[None, :] == device)
        & (starts[None, :] <= places[:, None])
        & (places[:, None] < (starts + seq_lengths)[None, :])
    )
    seq_id = jnp.sum(jnp.where(member, seq_index[None, :], 0), axis=1)
    token_position = jnp.sum(jnp.where(member, places[:, None] - starts[None, :], 0), axis=1)
    return (seq_id, token_position)


def rotation_factors(token_position):
    half_width = HEAD_SIZE // 2
    frequency = jnp.exp(
        jnp.arange(half_width, dtype=jnp.float32) * (-2.0 * math.log(rope_base) / HEAD_SIZE)
    )
    angles = token_position.astype(jnp.float32)[:, None] * frequency[None, :]
    cosine = jnp.cos(angles)
    sine = jnp.sin(angles)
    return jnp.concatenate([cosine, cosine], axis=1), jnp.concatenate([-sine, sine], axis=1)


def norm_forward(values, gain):
    inverse = lax.rsqrt(jnp.mean(values * values, axis=-1, keepdims=True) + epsilon)
    unit_rows = values * inverse
    return (unit_rows * gain, unit_rows, inverse)


def exchange(values, count, mask):
    return lax.ppermute(values, "fsdp", [(source, source ^ mask) for source in range(count)])


def middle_bits(count, flip):
    bits = list(range(1, count.bit_length() - 3))
    return bits[::-1] if flip else bits


def sum_bits(count):
    bits = count.bit_length() - 1
    middle = list(range(1, bits - 2))
    low, high = bits - 2, bits - 1
    return dict(
        down=[0, middle[-1], high, low] + middle[-2::-1],
        gate=[0] + middle + [low, high],
        up=[0, low, middle[-1], high] + middle[-2::-1],
        out=[0] + middle + [low, high],
        first=[0, low] + middle[::-1] + [high],
        second=[0] + middle + [low, high],
    )


def row_order(count, sequence):
    bits = len(sequence)
    return [
        sum(((index >> (bits - 1 - step)) & 1) << bit for step, bit in enumerate(sequence)) for index in range(count)
    ]


def turn_body(device_ref, *refs, order):
    values, (out_ref, turned_ref) = refs[:-2], refs[-2:]
    start = 0
    for ref in values:
        turned_ref[start : start + ref.shape[1], :] = ref[...].astype(turned_ref.dtype).T
        start += ref.shape[1]
    device = device_ref[0]
    rows = out_ref.shape[0] // len(order)
    group = max(1, 16 // rows)
    for first in range(0, len(order), group):
        blocks = [
            turned_ref[pl.ds(pl.multiple_of((device ^ mask) * rows, rows), rows), :]
            for mask in order[first : first + group]
        ]
        block = blocks[0] if group == 1 else jnp.concatenate(blocks, axis=0)
        out_ref[first * rows : (first + group) * rows, :] = block.astype(out_ref.dtype)


def turn(values, device, order):
    count = len(order)
    rows = values[0].shape[0]
    columns = sum(value.shape[1] for value in values)
    held = jnp.bfloat16 if columns // count % 16 == 0 else jnp.float32
    return pl.pallas_call(
        functools.partial(turn_body, order=order),
        grid_spec=pltpu.PrefetchScalarGridSpec(
            num_scalar_prefetch=1,
            grid=(1,),
            in_specs=[pl.BlockSpec(value.shape, lambda i, d: (0, 0)) for value in values],
            out_specs=pl.BlockSpec((columns, rows), lambda i, d: (0, 0)),
            scratch_shapes=[pltpu.VMEM((columns, rows), held)],
        ),
        out_shape=far((columns, rows), values[0].dtype),
        compiler_params=pltpu.CompilerParams(vmem_limit_bytes=16 * 1024 * 1024),
        cost_estimate=SMALL,
        name="turn",
    )(device.reshape(1), *values)


def fold_body(*refs, pairs, merged):
    def add(first, second):
        return (first[...].astype(jnp.float32) + second[...].astype(jnp.float32)).astype(jnp.bfloat16)

    out_refs = refs[4 * pairs :]
    start = 0
    for index in range(pairs):
        kept_first, kept_second, came_first, came_second = refs[4 * index : 4 * index + 4]
        sent = add(kept_second, came_second)
        if merged:
            out_refs[pairs][:, start : start + sent.shape[1]] = sent
            start += sent.shape[1]
        else:
            out_refs[pairs + index][...] = sent
        out_refs[index][...] = add(kept_first, came_first)


def fold(*pairs, merged=False):
    halves = [kept.shape[0] // 2 for kept, *_ in pairs]
    steps = next(n for n in (2, 1) if n == 1 or all(rows % (16 * n) == 0 for rows in halves))
    in_specs, out_specs, out_shape, operands = [], [], [], []
    for rows, (kept, came, place) in zip(halves, pairs):
        columns = kept.shape[1]
        spec = lambda shift, place=0, rows=rows, columns=columns: pl.BlockSpec(
            (rows // steps, columns), lambda i: (i + shift, place)
        )
        in_specs += [spec(0), spec(steps), spec(0, place), spec(steps, place)]
        operands += [kept, kept, came, came]
        out_specs += [spec(0)]
        out_shape += [jax.ShapeDtypeStruct((rows, columns), jnp.bfloat16)]
    if merged:
        columns = sum(kept.shape[1] for kept, *_ in pairs)
        sent_specs = [pl.BlockSpec((halves[0] // steps, columns), lambda i: (i, 0))]
        sent_shape = [jax.ShapeDtypeStruct((halves[0], columns), jnp.bfloat16)]
    else:
        sent_specs, sent_shape = list(out_specs), list(out_shape)
    block_bytes = sum(6 * 2 * (rows // steps) * kept.shape[1] for rows, (kept, *_) in zip(halves, pairs))
    return pl.pallas_call(
        functools.partial(fold_body, pairs=len(pairs), merged=merged),
        grid=(steps,),
        in_specs=in_specs,
        out_specs=out_specs + sent_specs,
        out_shape=out_shape + sent_shape,
        compiler_params=pltpu.CompilerParams(vmem_limit_bytes=2 * block_bytes + 6 * 1024 * 1024),
        cost_estimate=SMALL,
        name="fold",
    )(*operands)


def sum_end(pair):
    return pair[0].astype(jnp.float32) + pair[1].astype(jnp.float32)


def place_body(device_ref, *refs):
    parts = refs[:-2]
    out_ref, semaphores = refs[-2:]
    device = device_ref[0]
    copies = [
        pltpu.make_async_copy(part, out_ref.at[:, device ^ mask], semaphores.at[mask])
        for mask, part in enumerate(parts)
    ]
    for copy in copies:
        copy.start()
    for copy in copies:
        copy.wait()


def place(parts, inner):
    top, rows, columns = parts[0].shape
    return pl.pallas_call(
        place_body,
        grid_spec=pltpu.PrefetchScalarGridSpec(
            num_scalar_prefetch=1,
            grid=(1,),
            in_specs=[pl.BlockSpec(memory_space=pl.ANY)] * len(parts),
            out_specs=pl.BlockSpec((top, len(parts), rows, columns), lambda i, d: (0, 0, 0, 0)),
            scratch_shapes=[pltpu.SemaphoreType.DMA((len(parts),))],
        ),
        out_shape=far((top, len(parts), rows, columns), parts[0].dtype)
        if top > 1
        else jax.ShapeDtypeStruct((top, len(parts), rows, columns), parts[0].dtype),
        compiler_params=pltpu.CompilerParams(vmem_limit_bytes=14 * 1024 * 1024),
        cost_estimate=SMALL,
        name="place",
    )(inner.reshape(1), *parts).reshape(top * len(parts) * rows, columns)


def gather_top(block, count):
    return [block, exchange(block, count, count // 4), exchange(block, count, count // 2)]


def gather_top_rest(blocks, count):
    return [block[None] for block in blocks + [exchange(blocks[2], count, count // 4)]]


def stack_body(gate_ref, up_ref, down_ref, out_ref):
    rows = gate_ref.shape[0]
    width = down_ref.shape[1]
    out_ref[:rows, :] = gate_ref[...]
    out_ref[rows : 2 * rows, :] = up_ref[...]
    for piece in range(down_ref.shape[0] // rows):
        columns = slice(piece * width, (piece + 1) * width)
        out_ref[2 * rows :, columns] = down_ref[piece * rows : (piece + 1) * rows, :]


def stack(w_gate, w_up, w_down):
    rows, columns = w_gate.shape
    pieces = w_down.shape[0] // rows
    if rows % 16:
        down = w_down.reshape(pieces, rows, -1).transpose(1, 0, 2).reshape(rows, -1)
        return jnp.concatenate([w_gate, w_up, down], axis=0)
    return pl.pallas_call(
        stack_body,
        out_shape=jax.ShapeDtypeStruct((3 * rows, columns), w_gate.dtype),
        cost_estimate=SMALL,
        name="stack",
    )(w_gate, w_up, w_down)


def join_body(query_ref, key_ref, value_ref, gains_ref, out_ref):
    groups = KEY_VALUE_HEADS
    pair = query_ref.shape[1] // groups
    one = key_ref.shape[1] // groups
    shift = 0
    for group in range(groups):
        for ref, size in ((query_ref, pair), (key_ref, one), (value_ref, one)):
            out_ref[:, shift : shift + size] = ref[:, group * size : (group + 1) * size]
            shift += size
        if group == groups // 2 - 1:
            out_ref[:, shift : shift + 128] = gains_ref[...]
            shift += 128


def join(w_query, key_projection, value_projection, gains):
    rows = w_query.shape[0]
    columns = w_query.shape[1] + 2 * key_projection.shape[1] + 128
    return pl.pallas_call(
        join_body,
        out_shape=jax.ShapeDtypeStruct((rows, columns), w_query.dtype),
        cost_estimate=SMALL,
        name="join",
    )(w_query, key_projection, value_projection, gains)


def lay_top(blocks, device, count):
    return {0: place(from_far(*blocks), device // (count // 4)).reshape((4,) + blocks[0].shape[1:])}


def split_body(device_ref, *refs):
    parts = refs[:4]
    left_ref, right_ref, semaphores = refs[4:]
    width = left_ref.shape[-1]
    copies = []
    for mask, part in enumerate(parts):
        target = device_ref[0] ^ mask
        copies += [
            pltpu.make_async_copy(part.at[:, :width], left_ref.at[target], semaphores.at[2 * mask]),
            pltpu.make_async_copy(part.at[:, width:], right_ref.at[target], semaphores.at[2 * mask + 1]),
        ]
    for copy in copies:
        copy.start()
    for copy in copies:
        copy.wait()


def lay_top_split(blocks, device, count, width):
    rows, columns = blocks[0].shape[1:]
    shapes = [(4, rows, width), (4, rows, columns - width)]
    return pl.pallas_call(
        split_body,
        grid_spec=pltpu.PrefetchScalarGridSpec(
            num_scalar_prefetch=1,
            grid=(1,),
            in_specs=[pl.BlockSpec(memory_space=pl.ANY)] * 4,
            out_specs=[pl.BlockSpec(shape, lambda i, d: (0, 0, 0)) for shape in shapes],
            scratch_shapes=[pltpu.SemaphoreType.DMA((8,))],
        ),
        out_shape=[jax.ShapeDtypeStruct(shape, blocks[0].dtype) for shape in shapes],
        compiler_params=pltpu.CompilerParams(vmem_limit_bytes=10 * 1024 * 1024),
        cost_estimate=SMALL,
        name="lay_top_split",
    )((device // (count // 4)).reshape(1), *from_far(*[block[0] for block in blocks]))


def gather_bits(parts, count, bits):
    parts = dict(parts)
    for bit in bits:
        for mask in list(parts):
            parts[mask | (1 << bit)] = exchange(parts[mask], count, 1 << bit)
    return parts


def lay(parts, device, count):
    return place([parts[mask] for mask in range(count // 4)], device & (count // 4 - 1))


def gain_columns(first, second, third, fourth, rows):
    columns = [jnp.pad(v, (0, rows - v.shape[0]))[:, None] for v in (first, second, third, fourth)]
    return jnp.pad(jnp.concatenate(columns, axis=1), ((0, 0), (0, 124)))


def swap_halves(head):
    return pltpu.roll(head, HEAD_SIZE // 2, 1)


def unit_head(raw):
    inverse = lax.rsqrt(jnp.mean(raw * raw, axis=-1, keepdims=True) + epsilon)
    return raw * inverse, inverse


def contract(left, right, left_axis, right_axis):
    return lax.dot_general(
        left, right, (((left_axis,), (right_axis,)), ((), ())), preferred_element_type=jnp.float32
    )


def block_scores(group, key_rows, first_row, row_start):
    scores = contract(group, key_rows, 1, 1) * (1.0 / math.sqrt(HEAD_SIZE))
    rows = lax.broadcasted_iota(jnp.int32, scores.shape, 0)
    half = scores.shape[0] // 2
    rows = jnp.where(rows >= half, rows - half, rows) + row_start
    columns = lax.broadcasted_iota(jnp.int32, scores.shape, 1)
    return jnp.where((columns <= rows) & (columns >= first_row), scores, -1e30)


def head_pair(ref, block):
    return jnp.concatenate([ref[block, :HEAD_SIZE], ref[block, HEAD_SIZE:]], axis=0)


def pair_rows(first_row_ref, block):
    rows = first_row_ref[block, :]
    return jnp.concatenate([rows, rows], axis=0)


GROUP = 4 * HEAD_SIZE


def weight_parts(parts, device, count):
    if parts[0].shape[1] % 16 == 0:
        return [parts[mask] for mask in range(count // 4)]
    weight = lay(parts, device, count)
    return [weight[None]]


def part_specs(parts, index):
    top, rows, _ = parts[0].shape
    return [pl.BlockSpec((top, rows, GROUP), lambda *j: (0, 0, index(*j))) for _ in parts]


def join_parts(device_ref, part_refs, weight_ref):
    inner = device_ref[0] & (len(part_refs) - 1)
    for mask, ref in enumerate(part_refs):
        weight_ref[:, inner ^ mask] = ref[...]
    top, count, rows, columns = weight_ref.shape
    return weight_ref[...].reshape(top * count * rows, columns)


def prepare_body(device_ref, *refs, shard, head_shard):
    (*part_refs, tokens_ref), (normed_ref, first_gain_ref, second_gain_ref, head_gains_ref, gains_ref) = refs[:-5], refs[-5:]
    lines = join_parts(device_ref, part_refs, gains_ref).astype(jnp.float32).T
    gain = lines[0:1, :]
    first_gain_ref[...] = gain
    second_gain_ref[...] = lines[1:2, :]
    width = lines.shape[1]
    source = lax.broadcasted_iota(jnp.int32, (width, HEAD_SIZE), 0)
    target = lax.broadcasted_iota(jnp.int32, (width, HEAD_SIZE), 1)
    pick = jnp.where(target // head_shard * shard + target % head_shard == source, 1.0, 0.0)
    head_gains_ref[...] = jnp.dot(
        lines[2:4, :], pick, precision=lax.Precision.HIGHEST, preferred_element_type=jnp.float32
    )
    unit, _ = unit_head(tokens_ref[...].astype(jnp.float32))
    normed_ref[...] = (unit * gain).astype(jnp.bfloat16)


def prepare(device, parts, tokens, shard, head_shard):
    rows, width = tokens.shape
    top, part_rows, columns = parts[0].shape
    whole = lambda *shape: pl.BlockSpec(shape, lambda i, d: (0, 0))
    line = jax.ShapeDtypeStruct((1, width), jnp.float32)
    return pl.pallas_call(
        functools.partial(prepare_body, shard=shard, head_shard=head_shard),
        grid_spec=pltpu.PrefetchScalarGridSpec(
            num_scalar_prefetch=1,
            grid=(1,),
            in_specs=[pl.BlockSpec((top, part_rows, 128), lambda i, d: (0, 0, columns // 128 - 1)) for _ in parts]
            + [whole(rows, width)],
            out_specs=[whole(rows, width), whole(1, width), whole(1, width), whole(2, HEAD_SIZE)],
            scratch_shapes=[pltpu.VMEM((top, len(parts), part_rows, 128), jnp.bfloat16)],
        ),
        out_shape=[
            jax.ShapeDtypeStruct((rows, width), jnp.bfloat16),
            line,
            line,
            jax.ShapeDtypeStruct((2, HEAD_SIZE), jnp.float32),
        ],
        compiler_params=pltpu.CompilerParams(vmem_limit_bytes=16 * 1024 * 1024),
        cost_estimate=SMALL,
        name="prepare",
    )(device.reshape(1), *parts, tokens)


def attend_body(device_ref, *refs):
    (*part_refs, normed_ref, gains_ref, cosine_ref, sine_ref, first_ref), out_refs = refs[:-7], refs[-7:]
    attended_ref, query_ref, key_ref, value_ref, raw_ref, total_ref, weight_ref = out_refs
    cosine = cosine_ref[...]
    sine = sine_ref[...]

    def turned(raw, gain):
        scaled = unit_head(raw)[0] * gain
        return (scaled * cosine + swap_halves(scaled) * sine).astype(jnp.bfloat16)

    weight = join_parts(device_ref, part_refs, weight_ref)
    raw = jnp.dot(normed_ref[...], weight, preferred_element_type=jnp.float32)
    raw_ref[...] = raw[:, : 3 * HEAD_SIZE]
    for head in range(2):
        part = slice(head * HEAD_SIZE, (head + 1) * HEAD_SIZE)
        query_ref[:, part] = turned(raw[:, part], gains_ref[0:1, :])
    key_ref[...] = turned(raw[:, 2 * HEAD_SIZE : 3 * HEAD_SIZE], gains_ref[1:2, :])
    value_ref[...] = raw[:, 3 * HEAD_SIZE :].astype(jnp.bfloat16)
    step = 128
    for start in range(0, raw.shape[0], step):
        block = slice(start, start + step)
        seen = slice(0, start + step)
        scores = block_scores(head_pair(query_ref, block), key_ref[seen, :], pair_rows(first_ref, block), start)
        top = jnp.max(scores, axis=-1, keepdims=True)
        log_total = top + jnp.log(jnp.sum(jnp.exp(scores - top), axis=-1, keepdims=True))
        probs_low = jnp.exp(scores - log_total).astype(jnp.bfloat16)
        out = jnp.dot(probs_low, value_ref[seen, :], preferred_element_type=jnp.float32).astype(jnp.bfloat16)
        attended_ref[block, :HEAD_SIZE] = out[:step]
        attended_ref[block, HEAD_SIZE:] = out[step:]
        total_ref[0, block, 0:1] = log_total[:step]
        total_ref[0, block, 1:2] = log_total[step:]


def attend(device, normed, parts, head_gains, cosine, sine, first_row):
    rows, width = normed.shape
    groups = KEY_VALUE_HEADS // 2
    whole = lambda *shape: pl.BlockSpec(shape, lambda h, d: (0, 0))
    columns = lambda size: pl.BlockSpec((rows, size), lambda h, d: (0, h))
    low = lambda size: far((rows, groups * size), jnp.bfloat16)
    pair = 2 * HEAD_SIZE
    return pl.pallas_call(
        attend_body,
        grid_spec=pltpu.PrefetchScalarGridSpec(
            num_scalar_prefetch=1,
            grid=(groups,),
            in_specs=part_specs(parts, lambda h, d: h)
            + [
                whole(rows, width),
                whole(2, HEAD_SIZE),
                whole(rows, HEAD_SIZE),
                whole(rows, HEAD_SIZE),
                whole(rows, 1),
            ],
            out_specs=[
                columns(pair),
                columns(pair),
                columns(HEAD_SIZE),
                columns(HEAD_SIZE),
                columns(3 * HEAD_SIZE),
                pl.BlockSpec((1, rows, 2), lambda h, d: (h, 0, 0)),
            ],
            scratch_shapes=[pltpu.VMEM((parts[0].shape[0], len(parts), parts[0].shape[1], GROUP), jnp.bfloat16)],
        ),
        out_shape=[
            jax.ShapeDtypeStruct((rows, groups * pair), jnp.bfloat16),
            low(pair),
            low(HEAD_SIZE),
            low(HEAD_SIZE),
            far((rows, groups * 3 * HEAD_SIZE), jnp.float32),
            far((groups, rows, 2), jnp.float32),
        ],
        compiler_params=pltpu.CompilerParams(vmem_limit_bytes=26 * 1024 * 1024),
        cost_estimate=SMALL,
        name="attend",
    )(device.reshape(1), *parts, normed, head_gains, cosine, sine, first_row)


def attend_back_body(
    device_ref, residual_ref, wo_ref, query_ref, key_ref, value_ref, raw_ref, total_ref,
    gains_ref, cosine_ref, sine_ref, first_ref, turned_ref, *refs,
    order, shard, head_shard, last, parts, head=None,
):
    part_refs, refs = refs[:parts], refs[parts:]
    if last:
        head_gains_in_ref, normed_in_ref = refs[:2]
        refs = refs[2:]
        tokens_ref, gain_ref, grad_residual_ref, gain_two_ref, hidden_ref, down_ref, ffn_in_ref = refs[:7]
        kept_ref, sent_ref, tokens_out_ref, mixed_ref = refs[7:11]
        head_gains_ref, normed_sum_ref, lines_ref, mixed_sum_ref, down_weight_ref = refs[11:16]
        scratch = refs[16:]
    else:
        kept_ref, sent_ref, head_gains_ref, normed_sum_ref = refs[:4]
        scratch = refs[4:]
    grad_out_ref, query_sum_ref, key_sum_ref, value_sum_ref, grads_ref, weight_ref = scratch
    scale = 1.0 / math.sqrt(HEAD_SIZE)
    heads = KEY_VALUE_HEADS // 2
    if head is None:
        head = pl.program_id(0)

    @pl.when(head == 0)
    def _():
        head_gains_ref[...] = head_gains_in_ref[...] if last else jnp.zeros_like(head_gains_ref)
        normed_sum_ref[...] = normed_in_ref[...] if last else jnp.zeros_like(normed_sum_ref)

    if last:
        gather_down(down_ref, down_weight_ref, down_weight_ref.shape[1])

        @pl.when(head == 0)
        def _():
            mixed_sum_ref[...] = ffn_in_ref[...]

        mixed_sum_ref[...] += jnp.dot(hidden_ref[...], down_weight_ref[...], preferred_element_type=jnp.float32)

        @pl.when(head == heads - 1)
        def _():
            mixed_ref[...] = mixed_sum_ref[...].astype(jnp.bfloat16)

    grad_out_ref[...] = contract(residual_ref[...], wo_ref[...], 1, 1).astype(jnp.bfloat16)
    key_sum_ref[...] = jnp.zeros_like(key_sum_ref)
    value_sum_ref[...] = jnp.zeros_like(value_sum_ref)
    step = 128
    for start in range(0, residual_ref.shape[0], step):
        block = slice(start, start + step)
        seen = slice(0, start + step)
        group = head_pair(query_ref, block)
        grad_out = head_pair(grad_out_ref, block)
        key_rows = key_ref[seen, :]
        scores = block_scores(group, key_rows, pair_rows(first_ref, block), start)
        log_total = jnp.concatenate([total_ref[0, block, 0:1], total_ref[0, block, 1:2]], axis=0)
        probs = jnp.exp(scores - log_total)
        grad_probs = contract(grad_out, value_ref[seen, :], 1, 1)
        value_sum_ref[seen, :] += contract(probs.astype(jnp.bfloat16), grad_out, 0, 0)
        inner = jnp.sum(probs * grad_probs, axis=-1, keepdims=True)
        grad_scores = (probs * (grad_probs - inner)).astype(jnp.bfloat16)
        grad_group = jnp.dot(grad_scores, key_rows, preferred_element_type=jnp.float32) * scale
        query_sum_ref[block, :HEAD_SIZE] = grad_group[:step]
        query_sum_ref[block, HEAD_SIZE:] = grad_group[step:]
        key_sum_ref[seen, :] += contract(grad_scores, group, 0, 0)
    grads_ref[:, 3 * HEAD_SIZE :] = value_sum_ref[...].astype(jnp.bfloat16)
    cosine = cosine_ref[...]
    sine = sine_ref[...]

    def back(grad, part, gain):
        turned = grad * cosine - swap_halves(grad) * sine
        unit, inverse = unit_head(raw_ref[:, part])
        product = turned * unit
        scaled = turned * gain
        grad_raw = inverse * (scaled - unit * jnp.mean(product * gain, axis=-1, keepdims=True))
        grads_ref[:, part] = grad_raw.astype(jnp.bfloat16)
        return jnp.sum(product, axis=0, keepdims=True)

    for index in range(2):
        part = slice(index * HEAD_SIZE, (index + 1) * HEAD_SIZE)
        head_gains_ref[0:1, :] += back(query_sum_ref[:, part], part, gains_ref[0:1, :])
    part = slice(2 * HEAD_SIZE, 3 * HEAD_SIZE)
    head_gains_ref[1:2, :] += back(key_sum_ref[...] * scale, part, gains_ref[1:2, :])

    grads = grads_ref[...]
    half = turned_ref.shape[0] // 2
    product = jnp.dot(turned_ref[...], grads, preferred_element_type=jnp.float32).astype(jnp.bfloat16)
    columns = pl.ds(pl.multiple_of(head * GROUP, GROUP), GROUP)
    kept_ref[:, columns] = product[:half]
    sent_ref[:, columns] = product[half:]
    normed_sum_ref[...] += contract(grads, join_parts(device_ref, part_refs, weight_ref), 1, 1)

    if not last:
        return

    @pl.when(head == heads - 1)
    def _():
        unit, inverse = unit_head(tokens_ref[...].astype(jnp.float32))
        grad = normed_sum_ref[...]
        scaled = grad * gain_ref[...]
        grad_first = inverse * (scaled - unit * jnp.mean(scaled * unit, axis=-1, keepdims=True))
        tokens_out_ref[...] = (grad_residual_ref[...] + grad_first).astype(jnp.bfloat16)
        width = grad.shape[1]
        source = lax.broadcasted_iota(jnp.int32, (HEAD_SIZE, width), 0)
        target = lax.broadcasted_iota(jnp.int32, (HEAD_SIZE, width), 1)
        spread = jnp.where(source // head_shard * shard + source % head_shard == target, 1.0, 0.0)
        heads = jnp.dot(
            head_gains_ref[...], spread, precision=lax.Precision.HIGHEST, preferred_element_type=jnp.float32
        )
        lines = jnp.concatenate(
            [
                jnp.sum(grad * unit, axis=0, keepdims=True),
                gain_two_ref[...],
                heads,
                jnp.zeros((124, width), jnp.float32),
            ],
            axis=0,
        )
        lines_ref[...] = lines.T
        device = device_ref[0]
        group = max(1, 16 // shard)
        end = slice(kept_ref.shape[1] - 128, None)
        for first in range(0, len(order), group):
            blocks = [
                lines_ref[pl.ds(pl.multiple_of((device ^ mask) * shard, shard), shard), :]
                for mask in order[first : first + group]
            ]
            block = (blocks[0] if group == 1 else jnp.concatenate(blocks, axis=0)).astype(jnp.bfloat16)
            row = first * shard
            target_ref = kept_ref if row < half else sent_ref
            target_ref[row % half : row % half + group * shard, end] = block


def attend_back_specs(rows, width, part, head, parts):
    first = part * KEY_VALUE_HEADS // 2
    whole = lambda *shape: pl.BlockSpec(shape, lambda *j: (0, 0))
    columns = lambda height, size: pl.BlockSpec((height, size), lambda *j: (0, head(*j)))
    pair = 2 * HEAD_SIZE
    return [
        pl.BlockSpec((pair, width), lambda *j: (head(*j) + first, 0)),
        columns(rows, pair),
        columns(rows, HEAD_SIZE),
        columns(rows, HEAD_SIZE),
        columns(rows, 3 * HEAD_SIZE),
        pl.BlockSpec((1, rows, 2), lambda *j: (head(*j), 0, 0)),
        whole(2, HEAD_SIZE),
        whole(rows, HEAD_SIZE),
        whole(rows, HEAD_SIZE),
        whole(rows, 1),
        whole(width, rows),
    ] + part_specs(parts, head)


def attend_back_scratch(rows, parts):
    pair = 2 * HEAD_SIZE
    return [
        pltpu.VMEM((rows, pair), jnp.bfloat16),
        pltpu.VMEM((rows, pair), jnp.float32),
        pltpu.VMEM((rows, HEAD_SIZE), jnp.float32),
        pltpu.VMEM((rows, HEAD_SIZE), jnp.float32),
        pltpu.VMEM((rows, GROUP), jnp.bfloat16),
        pltpu.VMEM((parts[0].shape[0], len(parts), parts[0].shape[1], GROUP), jnp.bfloat16),
    ]


def attend_back_last(
    device, residual_low, operands, parts, sums, tokens, gain, grad_residual, grad_gain_two, ffn_in, hidden, weights,
    order, shard, head_shard,
):
    rows, width = residual_low.shape
    whole = lambda *shape: pl.BlockSpec(shape, lambda *j: (0, 0))
    own_width = KEY_VALUE_HEADS * 2 * HEAD_SIZE + 128
    half = jax.ShapeDtypeStruct((width // 2, own_width), jnp.bfloat16)
    low = jax.ShapeDtypeStruct((rows, width), jnp.bfloat16)
    tiles = KEY_VALUE_HEADS // 2
    tile = weights.shape[2] // tiles
    weight_args, weight_specs = ffn_operands(weights, shard, width, tiles, lambda h, d: h)
    return pl.pallas_call(
        functools.partial(
            attend_back_body, order=order, shard=shard, head_shard=head_shard, last=True, parts=len(parts)
        ),
        grid_spec=pltpu.PrefetchScalarGridSpec(
            num_scalar_prefetch=1,
            grid=(KEY_VALUE_HEADS // 2,),
            in_specs=[whole(rows, width)]
            + attend_back_specs(rows, width, 1, lambda h, d: h, parts)
            + [whole(2, HEAD_SIZE), whole(rows, width)]
            + [whole(rows, width), whole(1, width), whole(rows, width), whole(1, width)]
            + [pl.BlockSpec((rows, tile), lambda h, d: (0, h)), weight_specs[2], whole(rows, width)],
            out_specs=[
                whole(width // 2, own_width), whole(width // 2, own_width), whole(rows, width), whole(rows, width)
            ],
            scratch_shapes=[
                pltpu.VMEM((2, HEAD_SIZE), jnp.float32),
                pltpu.VMEM((rows, width), jnp.float32),
                pltpu.VMEM((width, 128), jnp.float32),
                pltpu.VMEM((rows, width), jnp.float32),
                pltpu.VMEM((tile, width), jnp.bfloat16),
            ]
            + attend_back_scratch(rows, parts),
        ),
        out_shape=[half, half, low, low],
        compiler_params=pltpu.CompilerParams(vmem_limit_bytes=46 * 1024 * 1024),
        cost_estimate=SMALL,
        name="attend_back_last",
    )(
        device.reshape(1), residual_low, *operands, *parts, sums[0], *from_far(sums[1], tokens), gain, *from_far(grad_residual),
        grad_gain_two, *from_far(hidden, weight_args[2], ffn_in),
    )


def project_body(device_ref, *refs, top_steps):
    (*part_refs, tokens_ref, first_ref, second_ref), (residual_ref, weight_out_ref) = refs[:-2], refs[-2:]
    inner = device_ref[0] & (len(part_refs) - 1)

    @pl.when(pl.program_id(0) == 0)
    def _():
        residual_ref[...] = tokens_ref[...].astype(jnp.float32)

    for mask, ref in enumerate(part_refs):
        weight_out_ref[:, inner ^ mask] = ref[...]
    top, count, rows, columns = weight_out_ref.shape
    weight = weight_out_ref[...].reshape(top * count * rows, columns)
    for ref, part in ((first_ref, 0), (second_ref, 1)):

        @pl.when(pl.program_id(0) // (top_steps // 2) == part)
        def _():
            residual_ref[...] += jnp.dot(ref[...], weight, preferred_element_type=jnp.float32)


def project(device, parts, tokens, first, second):
    rows, width = tokens.shape
    top, part_rows, _ = parts[0].shape
    step_rows = len(parts) * part_rows
    whole = pl.BlockSpec((rows, width), lambda j, d: (0, 0))
    residual, weight = pl.pallas_call(
        functools.partial(project_body, top_steps=top),
        grid_spec=pltpu.PrefetchScalarGridSpec(
            num_scalar_prefetch=1,
            grid=(top,),
            in_specs=[pl.BlockSpec((1, part_rows, width), lambda j, d: (j, 0, 0)) for _ in parts]
            + [
                whole,
                pl.BlockSpec((rows, step_rows), lambda j, d: (0, jnp.minimum(j, top // 2 - 1))),
                pl.BlockSpec((rows, step_rows), lambda j, d: (0, jnp.maximum(j - top // 2, 0))),
            ],
            out_specs=[whole, pl.BlockSpec((1, len(parts), part_rows, width), lambda j, d: (j, 0, 0, 0))],
        ),
        out_shape=[
            far((rows, width), jnp.float32),
            far((top, len(parts), part_rows, width), jnp.bfloat16),
        ],
        compiler_params=pltpu.CompilerParams(vmem_limit_bytes=20 * 1024 * 1024),
        cost_estimate=SMALL,
        name="project",
    )(device.reshape(1), *parts, tokens, first, second)
    return residual, weight.reshape(top * step_rows, width)


def gather_down(down_ref, down_weight_ref, width):
    devices, rows, _ = down_ref.shape
    pieces = down_ref.shape[2] // width
    for index in range(devices):
        for piece in range(pieces):
            first = (index * pieces + piece) * rows
            down_weight_ref[first : first + rows, :] = down_ref[index, :, piece * width : (piece + 1) * width]


def feed_forward_body(
    device_ref, residual_ref, gain_ref, cotangent_ref, gate_ref, up_ref, down_ref,
    hidden_ref, grad_gate_ref, grad_up_ref, gate_kept_ref, gate_sent_ref, for_up_ref,
    down_kept_ref, down_sent_ref, normed_ref, down_weight_ref, turned_ref, for_gate_ref, product_ref,
    *, gate_order, up_order,
):
    device = device_ref[0]
    width = residual_ref.shape[1]

    @pl.when(pl.program_id(0) == 0)
    def _():
        unit, _ = unit_head(residual_ref[...])
        normed = (unit * gain_ref[...]).astype(jnp.bfloat16)
        normed_ref[...] = normed
        turned_ref[...] = normed.astype(turned_ref.dtype).T
        rows = width // len(gate_order)
        group = max(1, 16 // rows)
        for order, ref in ((gate_order, for_gate_ref), (up_order, for_up_ref)):
            for first in range(0, len(order), group):
                blocks = [
                    turned_ref[pl.ds(pl.multiple_of((device ^ mask) * rows, rows), rows), :]
                    for mask in order[first : first + group]
                ]
                block = blocks[0] if group == 1 else jnp.concatenate(blocks, axis=0)
                ref[first * rows : (first + group) * rows, :] = block.astype(jnp.bfloat16)

    normed = normed_ref[...]
    gather_down(down_ref, down_weight_ref, width)
    cotangent = cotangent_ref[...]
    gate = jnp.dot(normed, gate_ref[...].reshape(width, gate_ref.shape[-1]), preferred_element_type=jnp.float32)
    up = jnp.dot(normed, up_ref[...].reshape(width, up_ref.shape[-1]), preferred_element_type=jnp.float32)
    grad_hidden = contract(cotangent, down_weight_ref[...], 1, 1)
    sigmoid = jax.nn.sigmoid(gate)
    silu = gate * sigmoid
    hidden = (silu * up).astype(jnp.bfloat16)
    grad_gate = (grad_hidden * up * sigmoid * (1.0 + gate * (1.0 - sigmoid))).astype(jnp.bfloat16)
    hidden_ref[...] = hidden
    grad_gate_ref[...] = grad_gate
    grad_up = (grad_hidden * silu).astype(jnp.bfloat16)
    grad_up_ref[...] = grad_up

    product = jnp.dot(for_gate_ref[...], grad_gate, preferred_element_type=jnp.float32).astype(jnp.bfloat16)
    half = product.shape[0] // 2
    gate_kept_ref[...] = product[:half]
    gate_sent_ref[...] = product[half:]
    product_ref[...] = contract(hidden, cotangent, 0, 0).reshape(product_ref.shape)
    owners = product_ref.shape[0]
    low = device & (owners - 1)
    for target, core in ((down_kept_ref, 0), (down_sent_ref, 1)):
        blocks = [product_ref[low ^ (index | core)] for index in range(0, owners, 2)]
        target[...] = jnp.concatenate(blocks, axis=0).astype(jnp.bfloat16).reshape(target.shape)


def ffn_operands(weights, shard, width, tiles, at):
    count, _, hidden_width = weights.shape
    tile = hidden_width // tiles
    if shard % 16 == 0:
        return [weights, weights, weights], [
            pl.BlockSpec((count, shard, tile), lambda *j: (0, 0, at(*j))),
            pl.BlockSpec((count, shard, tile), lambda *j: (0, 1, at(*j))),
            pl.BlockSpec((count // tiles, shard, hidden_width), lambda *j: (at(*j), 2, 0)),
        ]
    gate, up, down = (weights[:, part * shard : (part + 1) * shard] for part in range(3))
    down = down.reshape(count, shard, -1, width).transpose(0, 2, 1, 3).reshape(tiles, tile, width)
    return [gate.reshape(width, hidden_width), up.reshape(width, hidden_width), down], [
        pl.BlockSpec((width, tile), lambda *j: (0, at(*j))),
        pl.BlockSpec((width, tile), lambda *j: (0, at(*j))),
        pl.BlockSpec((1, tile, width), lambda *j: (at(*j), 0, 0)),
    ]


def feed_forward(device, residual, gain, cotangent, weights, shard, gate_order, up_order):
    rows, width = residual.shape
    count, _, hidden_width = weights.shape
    tiles = 4
    tile = hidden_width // tiles
    owners = count // tiles
    at = lambda j, d: j ^ (d[0] // owners)
    whole = pl.BlockSpec((rows, width), lambda j, d: (0, 0))
    row = pl.BlockSpec((1, width), lambda j, d: (0, 0))
    low = lambda height, size: jax.ShapeDtypeStruct((height, size), jnp.bfloat16)
    low4 = jax.ShapeDtypeStruct((2, tiles, tile // 4, width), jnp.bfloat16)
    weight_args, weight_specs = ffn_operands(weights, shard, width, tiles, at)
    columns = lambda height: pl.BlockSpec((height, tile), lambda j, d: (0, at(j, d)))
    down_half = pl.BlockSpec((2, 1, tile // 4, width), lambda j, d: (0, j, 0, 0))
    *out, down_kept, down_sent = pl.pallas_call(
        functools.partial(feed_forward_body, gate_order=gate_order, up_order=up_order),
        grid_spec=pltpu.PrefetchScalarGridSpec(
            num_scalar_prefetch=1,
            grid=(tiles,),
            in_specs=[whole, row, whole] + weight_specs,
            out_specs=[
                columns(rows),
                columns(rows),
                columns(rows),
                columns(width // 2),
                columns(width // 2),
                pl.BlockSpec((width, rows), lambda j, d: (0, 0)),
                down_half,
                down_half,
            ],
            scratch_shapes=[
                pltpu.VMEM((rows, width), jnp.bfloat16),
                pltpu.VMEM((tile, width), jnp.bfloat16),
                pltpu.VMEM((width, rows), jnp.bfloat16 if shard % 16 == 0 else jnp.float32),
                pltpu.VMEM((width, rows), jnp.bfloat16),
                pltpu.VMEM((owners, tile // owners, width), jnp.float32),
            ],
        ),
        out_shape=[
            far((rows, hidden_width), jnp.bfloat16),
            far((rows, hidden_width), jnp.bfloat16),
            far((rows, hidden_width), jnp.bfloat16),
            low(width // 2, hidden_width),
            low(width // 2, hidden_width),
            low(width, rows),
            low4,
            low4,
        ],
        compiler_params=pltpu.CompilerParams(vmem_limit_bytes=56 * 1024 * 1024),
        cost_estimate=SMALL,
        name="feed_forward",
    )(device.reshape(1), residual, gain, *from_far(cotangent, *weight_args))
    return *out, down_kept.reshape(-1, width), down_sent.reshape(-1, width)


def product_body(left_ref, right_ref, kept_ref, sent_ref):
    product = jnp.dot(left_ref[...], right_ref[...], preferred_element_type=jnp.float32).astype(jnp.bfloat16)
    half = product.shape[0] // 2
    kept_ref[...] = product[:half]
    sent_ref[...] = product[half:]


def product_halves(left, right):
    rows, depth = left.shape
    columns = right.shape[1]
    tile = min(columns, 768)
    half = jax.ShapeDtypeStruct((rows // 2, columns), jnp.bfloat16)
    return pl.pallas_call(
        product_body,
        grid=(columns // tile,),
        in_specs=[pl.BlockSpec((rows, depth), lambda j: (0, 0)), pl.BlockSpec((depth, tile), lambda j: (0, j))],
        out_specs=[pl.BlockSpec((rows // 2, tile), lambda j: (0, j))] * 2,
        out_shape=[half, half],
        compiler_params=pltpu.CompilerParams(vmem_limit_bytes=20 * 1024 * 1024),
        cost_estimate=SMALL,
        name="product_halves",
    )(left, right)


FFN_STEPS = 4


def back_body(device_ref, *refs, parts):
    (
        residual_ref, gain_ref, cotangent_ref, grad_gate_ref, grad_up_ref, gate_ref, up_ref, turned_out_ref
    ), refs = refs[:8], refs[8:]
    operands, refs = refs[: 11 + parts], refs[11 + parts :]
    (
        grad_residual_ref, grad_low_ref, grad_gain_ref, out_kept_ref, out_sent_ref, kept_ref, sent_ref, head_gains_ref,
        normed_sum_ref, back_ref,
    ), scratch = refs[:10], refs[10:]
    step = pl.program_id(0)
    width = residual_ref.shape[1]

    @pl.when(step == 0)
    def _():
        back_ref[...] = jnp.zeros_like(back_ref)

    @pl.when(step < FFN_STEPS)
    def _():
        back_ref[...] += contract(
            grad_gate_ref[...], gate_ref[...].reshape(width, gate_ref.shape[-1]), 1, 1
        ) + contract(grad_up_ref[...], up_ref[...].reshape(width, up_ref.shape[-1]), 1, 1)

    @pl.when(step == FFN_STEPS - 1)
    def _():
        unit, inverse = unit_head(residual_ref[...])
        grad = back_ref[...]
        grad_gain_ref[...] = jnp.sum(grad * unit, axis=0, keepdims=True)
        scaled = grad * gain_ref[...]
        grad_mid = inverse * (scaled - unit * jnp.mean(scaled * unit, axis=-1, keepdims=True))
        grad_residual = cotangent_ref[...].astype(jnp.float32) + grad_mid
        grad_residual_ref[...] = grad_residual
        grad_low = grad_residual.astype(jnp.bfloat16)
        grad_low_ref[...] = grad_low
        half = out_kept_ref.shape[0]
        for start in range(0, half, 512):
            for ref, shift in ((out_kept_ref, 0), (out_sent_ref, half)):
                rows = slice(start + shift, start + shift + 512)
                ref[start : start + 512, :] = jnp.dot(
                    turned_out_ref[rows, :], grad_low, preferred_element_type=jnp.float32
                ).astype(jnp.bfloat16)

    @pl.when(step >= FFN_STEPS)
    def _():
        attend_back_body(
            device_ref, grad_low_ref, *operands, kept_ref, sent_ref, head_gains_ref, normed_sum_ref, *scratch,
            order=None, shard=None, head_shard=None, last=False, parts=parts, head=step - FFN_STEPS,
        )


def back(device, residual, gain, cotangent, grad_gate, grad_up, weights, shard, turned_out, operands, parts):
    rows, width = residual.shape
    tile = weights.shape[2] // FFN_STEPS
    at = lambda j, d: jnp.minimum(j, FFN_STEPS - 1)
    head = lambda j, d: jnp.maximum(j - FFN_STEPS, 0)
    whole = lambda *shape: pl.BlockSpec(shape, lambda *j: (0, 0))
    columns = pl.BlockSpec((rows, tile), lambda *j: (0, at(*j)))
    weight_args, weight_specs = ffn_operands(weights, shard, width, FFN_STEPS, at)
    out_rows = turned_out.shape[0]
    own_width = KEY_VALUE_HEADS * 2 * HEAD_SIZE
    low = lambda height, size: jax.ShapeDtypeStruct((height, size), jnp.bfloat16)
    wide = far((rows, width), jnp.float32)
    return pl.pallas_call(
        functools.partial(back_body, parts=len(parts)),
        grid_spec=pltpu.PrefetchScalarGridSpec(
            num_scalar_prefetch=1,
            grid=(FFN_STEPS + KEY_VALUE_HEADS // 2,),
            in_specs=[whole(rows, width), whole(1, width), whole(rows, width), columns, columns]
            + weight_specs[:2]
            + [whole(out_rows, rows)]
            + attend_back_specs(rows, width, 0, head, parts),
            out_specs=[
                whole(rows, width),
                whole(rows, width),
                whole(1, width),
                whole(out_rows // 2, width),
                whole(out_rows // 2, width),
                whole(width // 2, own_width),
                whole(width // 2, own_width),
                whole(2, HEAD_SIZE),
                whole(rows, width),
            ],
            scratch_shapes=[pltpu.VMEM((rows, width), jnp.float32)] + attend_back_scratch(rows, parts),
        ),
        out_shape=[
            wide,
            low(rows, width),
            jax.ShapeDtypeStruct((1, width), jnp.float32),
            low(out_rows // 2, width),
            low(out_rows // 2, width),
            low(width // 2, own_width),
            low(width // 2, own_width),
            jax.ShapeDtypeStruct((2, HEAD_SIZE), jnp.float32),
            wide,
        ],
        compiler_params=pltpu.CompilerParams(vmem_limit_bytes=50 * 1024 * 1024),
        cost_estimate=SMALL,
        name="back",
    )(
        device.reshape(1), residual, gain, *from_far(cotangent, grad_gate, grad_up, *weight_args[:2], turned_out), *operands, *parts
    )


def end_body(first_kept, first_came, second_kept, second_came, query_ref, key_ref, value_ref, *gain_refs):
    def part(kept, came, start, size):
        columns = slice(start, start + size)
        return kept[:, columns].astype(jnp.float32) + came[:, columns].astype(jnp.float32)

    group = 0
    for kept, came in ((first_kept, first_came), (second_kept, second_came)):
        for start in range(0, KEY_VALUE_HEADS // 2 * GROUP, GROUP):
            for ref, size in ((query_ref, 2 * HEAD_SIZE), (key_ref, HEAD_SIZE), (value_ref, HEAD_SIZE)):
                ref[:, group * size : (group + 1) * size] = part(kept, came, start, size)
                start += size
            group += 1
    gains = part(second_kept, second_came, KEY_VALUE_HEADS // 2 * GROUP, 128).T
    for index, ref in enumerate(gain_refs):
        ref[...] = gains[index : index + 1, : ref.shape[1]]


def end_projections(first, second, head_shard):
    rows = first[0].shape[0]
    query_width, key_width = QUERY_HEADS * HEAD_SIZE, KEY_VALUE_HEADS * HEAD_SIZE
    return pl.pallas_call(
        end_body,
        out_shape=[
            jax.ShapeDtypeStruct(shape, jnp.float32)
            for shape in (
                (rows, query_width), (rows, key_width), (rows, key_width), (1, rows), (1, rows), (1, head_shard),
                (1, head_shard),
            )
        ],
        cost_estimate=SMALL,
        name="end_projections",
    )(*first, *second)


def on_device(
    tokens,
    seq_lengths,
    seq_owner,
    g_attn,
    w_query,
    key_projection,
    value_projection,
    query_norm_gain,
    g_key,
    w_out,
    g_ffn,
    w_gate,
    w_up,
    w_down,
    cotangent,
):
    row_total_count = tokens.shape[0]
    fence = lax.optimization_barrier
    count = lax.axis_size("fsdp")
    device = lax.axis_index("fsdp")
    early = middle_bits(count, False)
    late = middle_bits(count, True)
    cut_bits = len(early) // 2
    shard = g_attn.shape[0]
    head_shard = query_norm_gain.shape[0]

    ffn_weights = lax.all_gather(stack(w_gate, w_up, w_down), "fsdp", axis=0, tiled=False)
    projections = join(
        w_query, key_projection, value_projection, gain_columns(g_attn, g_ffn, query_norm_gain, g_key, shard)
    )
    top = gather_top(projections, count)
    top, w_out = fence((top, w_out))
    top = gather_top_rest(top, count)
    top, w_out = fence((top, w_out))
    first_part, second_part = lay_top_split(top, device, count, KEY_VALUE_HEADS // 2 * GROUP + 128)
    first_parts = gather_bits({0: first_part}, count, early[:cut_bits])
    second_parts = gather_bits({0: second_part}, count, late[:cut_bits])
    out_top = gather_top(w_out, count)
    seq_id, token_position = layout(seq_lengths, seq_owner, device, row_total_count)
    first_row = (jnp.arange(row_total_count, dtype=jnp.int32) - token_position)[:, None]
    cosine, sine = rotation_factors(token_position)
    first_parts, second_parts, out_top, first_row, cosine, sine = fence(
        (first_parts, second_parts, out_top, first_row, cosine, sine)
    )
    first_parts = gather_bits(first_parts, count, early[cut_bits:])
    second_parts = gather_bits(second_parts, count, late[cut_bits:])
    out_top = gather_top_rest(out_top, count)
    first_parts, second_parts, out_top = fence((first_parts, second_parts, out_top))
    first_parts = gather_bits(first_parts, count, [0])
    out_parts = gather_bits(lay_top(out_top, device, count), count, early[:cut_bits])
    first_parts, second_parts = fence((first_parts, second_parts))
    second_parts = gather_bits(second_parts, count, [0])
    first_weight = weight_parts(first_parts, device, count)

    normed_low, gain_one, gain_two, head_gains = prepare(device, first_weight, tokens, shard, head_shard)
    attended_first, *saved_first = attend(device, normed_low, first_weight, head_gains, cosine, sine, first_row)
    attended_first, second_parts, out_parts = fence((attended_first, second_parts, out_parts))
    out_parts = gather_bits(out_parts, count, early[cut_bits:])
    second_weight = weight_parts(second_parts, device, count)
    attended_second, *saved_second = attend(device, normed_low, second_weight, head_gains, cosine, sine, first_row)
    stages = sum_bits(count)
    orders = {name: row_order(count, bits) for name, bits in stages.items()}
    turned = dict(
        out=turn((attended_first, attended_second), device, orders["out"]),
        first=turn((normed_low,), device, orders["first"]),
        second=turn((normed_low,), device, orders["second"]),
    )
    attended_first, attended_second, out_parts, turned = fence((attended_first, attended_second, out_parts, turned))
    out_parts = gather_bits(out_parts, count, [0])
    residual, out_weight = project(
        device,
        [out_parts[mask] for mask in range(count // 4)],
        tokens,
        attended_first,
        attended_second,
    )
    (
        hidden, grad_gate, grad_up, gate_kept, gate_sent, turned_up, down_kept, down_sent
    ) = feed_forward(
        device, residual, gain_two, cotangent, ffn_weights, shard, orders["gate"], orders["up"]
    )

    live = dict(
        hidden=hidden, grad_gate=grad_gate, grad_up=grad_up, gate=gate_kept, down=down_kept, turned_up=turned_up,
    )
    flying = {}

    def cut():
        live.update(fence(dict(live)))

    def fly(**sent):
        live.update({name + "_sent": value for name, value in sent.items()})
        cut()
        for name in sent:
            flying[name] = exchange(live.pop(name + "_sent"), count, 1 << stages[name].pop(0))

    def land(*names):
        live.update({name + "_came": flying.pop(name) for name in names})
        cut()
        flying.update({name: live.pop(name + "_came") for name in names})

    def relay(*names, places=(0, 0, 0, 0, 0, 0)):
        for name, place in zip(names, places):
            live[name], sent = fold((live[name], flying[name], place))
            flying[name] = exchange(sent, count, 1 << stages[name].pop(0))

    def operands(name, saved):
        return *from_far(out_weight, *saved), head_gains, cosine, sine, first_row, *from_far(turned[name])

    live["turned"] = turned
    fly(down=down_sent, gate=gate_sent)
    live["up"], up_sent = product_halves(live.pop("turned_up"), live["grad_up"])
    fly(up=up_sent)
    relay("down", "gate", "up")
    cut()
    turned = live.pop("turned")
    (
        live["grad_residual"], live["low"], live["grad_gain_two"], live["out"], live["out_sent"], live["first"],
        live["first_sent"], live["head_sums"], live["normed_sum"],
    ) = back(
        device, residual, gain_two, cotangent, live.pop("grad_gate"), live.pop("grad_up"), ffn_weights, shard,
        turned["out"], operands("first", saved_first), first_weight,
    )
    land("down", "gate", "up")
    fly(first=live["first_sent"], out=live["out_sent"])
    relay("down")
    live["gate"], live["up"], sent = fold(
        (live["gate"], flying["gate"], 0), (live["up"], flying["up"], 0), merged=True
    )
    stages["gate"].pop(0)
    flying["both"] = exchange(sent, count, 1 << stages["up"].pop(0))
    relay("first", "out")
    cut()
    live["second"], live["second_sent"], live["grad_tokens"], live["mixed"] = attend_back_last(
        device, live.pop("low"), operands("second", saved_second), second_weight,
        (live.pop("head_sums"), live.pop("normed_sum")), tokens, gain_one, live.pop("grad_residual"),
        live.pop("grad_gain_two"), residual, live.pop("hidden"), ffn_weights, orders["second"], shard, head_shard,
    )
    land("down", "both")
    land("first", "out")
    fly(second=live["second_sent"])
    relay("second")
    both = flying.pop("both")
    flying.update(gate=both, up=both)
    mixed, grad_tokens = live.pop("mixed"), live.pop("grad_tokens")
    relay("up", "gate", places=(1, 0))
    relay("first", "out")
    relay("up", "gate")
    relay("second")
    relay("down")
    cut()
    relay("first", "out")
    cut()
    relay("second")
    while any(stages.values()):
        for name in ("second", "first", "out", "down", "gate", "up"):
            if stages[name]:
                relay(name)
    pairs = {name: (live.pop(name), flying.pop(name)) for name in stages}
    sum_down, sum_gate, sum_up, sum_out = (sum_end(pairs[name]) for name in ("down", "gate", "up", "out"))
    first, second = pairs["first"], pairs["second"]
    sum_query, sum_key, sum_value, *sum_gains = end_projections(first, second, head_shard)
    return (
        mixed,
        grad_tokens,
        sum_gains[0].reshape(-1),
        sum_query,
        sum_key,
        sum_value,
        sum_gains[2].reshape(-1),
        sum_gains[3].reshape(-1),
        sum_out,
        sum_gains[1].reshape(-1),
        sum_gate,
        sum_up,
        sum_down,
    )


def solution(mesh):
    return jax.shard_map(
        on_device,
        mesh=mesh,
        in_specs=(
            P("fsdp", None),
            P(),
            P(),
            P("fsdp"),
            P("fsdp", None),
            P("fsdp", None),
            P("fsdp", None),
            P("fsdp"),
            P("fsdp"),
            P("fsdp", None),
            P("fsdp"),
            P("fsdp", None),
            P("fsdp", None),
            P("fsdp", None),
            P("fsdp", None),
        ),
        out_specs=(
            P("fsdp", None),
            P("fsdp", None),
            P("fsdp"),
            P("fsdp", None),
            P("fsdp", None),
            P("fsdp", None),
            P("fsdp"),
            P("fsdp"),
            P("fsdp", None),
            P("fsdp"),
            P("fsdp", None),
            P("fsdp", None),
            P("fsdp", None),
        ),
        check_vma=False,
    )
```
